256 devices in a mesh: frames: 128 (over y, z_hi, x, core), strip: 2 (over z_lo).
Axes of the slice: x: 4, y: 4, z: 8 (z_hi: 4, z_lo: 2; z = z_hi * 2 + z_lo), core: 2. Of those that a mesh axis runs over, the one named last changes fastest.
Arguments:
- queries: bfloat16 [65536, 1024], P(('frames', 'strip')), may hold values from -16 to 16
- keys: bfloat16 [65536, 1024], P(('frames', 'strip')), may hold values from -16 to 16
- values: bfloat16 [65536, 1024], P(('frames', 'strip')), may hold values from -6 to 6
- out_grad: bfloat16 [65536, 1024], P(('frames', 'strip')), may hold values from -6 to 6
- block_list: int32 [1024, 13], P(('frames', 'strip')), may hold values from 0 to 23, as said below
- block_count: int32 [1024], P(('frames', 'strip')), may hold values from 1 to 13
Outputs:
- attended: bfloat16 [65536, 1024], P(('frames', 'strip'))
- query_grad: bfloat16 [65536, 1024], P(('frames', 'strip'))
- key_grad: bfloat16 [65536, 1024], P(('frames', 'strip'))
- value_grad: bfloat16 [65536, 1024], P(('frames', 'strip'))
The draws below stay inside these ranges and needn't reach their ends.
Inputs may be any that keep to these rules, and one draw needn't show every extreme that they name: `block_list`: each row holds 13 different window block numbers; its first entry is 8 + (b mod (8)), the query block's own block.
All inputs are finite; a program needn't handle non-finite values.
Results may differ from the reference program's by a relative error of at most 0.025.
Values may be sent and summed in bfloat16 or wider, within the bound.
A program may use at most 128 MiB of HBM per device.

```python
import math
import jax
import jax.numpy as jnp
from jax import lax

D = 1024
HEADS = 16
HD = 64
BLOCK = 64
SEL = 13
FRAME_TOK = 512
TOKENS = 65536


def draw_queries(key, part):
    key = jax.random.fold_in(key, 1)
    result = jnp.clip(jax.random.normal(key, (TOKENS, D), jnp.float32), -6.0, 6.0)
    return result.astype(jnp.bfloat16)


def draw_keys(key, part):
    key = jax.random.fold_in(key, 2)
    result = jnp.clip(jax.random.normal(key, (TOKENS, D), jnp.float32), -6.0, 6.0)
    return result.astype(jnp.bfloat16)


def draw_block_list(key, part):
    key = jax.random.fold_in(key, 5)
    frame_blocks = FRAME_TOK // BLOCK
    window_blocks = 3 * frame_blocks
    all_blocks = TOKENS // BLOCK
    own_block = frame_blocks + jnp.arange(all_blocks, dtype=jnp.int32) % frame_blocks
    column_ids = jnp.arange(window_blocks, dtype=jnp.int32)
    ranking = jax.random.randint(key, (all_blocks, window_blocks), 0, 1048576, jnp.int32) * window_blocks + column_ids[None, :]
    ranking = jnp.where(column_ids[None, :] == own_block[:, None], -1, ranking)
    others = lax.top_k(ranking, SEL - 1)[1].astype(jnp.int32)
    return jnp.concatenate([own_block[:, None], others], axis=1)


def draw_block_count(key, part):
    key = jax.random.fold_in(key, 6)
    frame_blocks = FRAME_TOK // BLOCK
    frame_count = TOKENS // FRAME_TOK
    limit = jax.random.randint(jax.random.fold_in(key, 1), (frame_count, 1), SEL // 4, SEL + 1, jnp.int32)
    counts = jax.random.randint(jax.random.fold_in(key, 2), (frame_count, frame_blocks), 1, limit + 1, jnp.int32)
    counts = counts.reshape(-1)
    return counts.at[0].set(SEL).at[1].set(1)


def shard_levels(stream_key, extent, pieces, smallest, largest):
    gain, own = 1.0, jax.random.fold_in(stream_key, 6)
    for axis_at, blocks in pieces:
        draws = jnp.exp(jax.random.uniform(jax.random.fold_in(own, axis_at), (blocks,), jnp.float32, smallest / len(pieces), largest / len(pieces)))
        gain = gain * jnp.repeat(draws, extent[axis_at] // blocks).reshape([-1 if axis == axis_at else 1 for axis in range(len(extent))])
    return gain


def scatter_about(key, shape, deviation, bound, shards=(), kind=jnp.bfloat16):
    values = deviation * jax.random.normal(key, shape, jnp.float32)
    if shards:
        values = values * shard_levels(key, shape, shards, -0.22, 0.18)
    return jnp.clip(values, -bound, bound).astype(kind)


def setup_inputs(seed: int = 0) -> dict:
    seeds = jax.random.split(jax.random.key(seed), 7)
    return {
        "queries": draw_queries(jax.random.fold_in(seeds[6], 71), 0),
        "keys": draw_keys(jax.random.fold_in(seeds[6], 71), 0),
        "values": scatter_about(seeds[2], (TOKENS, D), 1.0, 6.0, ((0, 256),)),
        "out_grad": scatter_about(seeds[3], (TOKENS, D), 1.0, 6.0, ((0, 256),)),
        "block_list": draw_block_list(jax.random.fold_in(seeds[6], 71), 0),
        "block_count": draw_block_count(jax.random.fold_in(seeds[6], 71), 0),
    }


def attend_rows(query_part, grad_part, key_pick, value_pick, allowed, factor):
    scores = jnp.einsum('bqhd,bkhd->bhqk', query_part, key_pick) * factor
    scores = jnp.where(allowed, scores, -jnp.inf)
    peak = lax.optimization_barrier(jnp.max(scores, axis=-1, keepdims=True))
    powers = jnp.exp(scores - peak)
    weights = powers / lax.optimization_barrier(jnp.sum(powers, axis=-1, keepdims=True))
    weights_low = weights.astype(jnp.bfloat16).astype(jnp.float32)
    attended = jnp.einsum('bhqk,bkhd->bqhd', weights_low, value_pick).astype(jnp.bfloat16)
    row_dots = lax.optimization_barrier(jnp.sum(grad_part * attended.astype(jnp.float32), axis=-1))
    grad_weights = jnp.einsum('bqhd,bkhd->bhqk', grad_part, value_pick)
    grad_scores = (weights * (grad_weights - jnp.transpose(row_dots, (0, 2, 1))[..., None])).astype(jnp.bfloat16).astype(jnp.float32)
    query_grad = (factor * jnp.einsum('bhqk,bkhd->bqhd', grad_scores, key_pick)).astype(jnp.bfloat16)
    key_tiles = factor * jnp.einsum('bhqk,bqhd->bkhd', grad_scores, query_part)
    value_tiles = jnp.einsum('bhqk,bqhd->bkhd', weights_low, grad_part)
    return (attended, query_grad, key_tiles, value_tiles)

def reference(queries, keys, values, out_grad, block_list, block_count):
    frame_rows = FRAME_TOK
    frame_blocks = frame_rows // BLOCK
    window_blocks = 3 * frame_blocks
    frame_count = TOKENS // frame_rows
    factor = 1.0 / math.sqrt(HD)
    padding = jnp.zeros((frame_rows, D), keys.dtype)
    keys_padded = jnp.concatenate([padding, keys, padding], axis=0)
    values_padded = jnp.concatenate([padding, values, padding], axis=0)
    query_frames = queries.reshape(frame_count, frame_blocks, BLOCK, HEADS, HD)
    grad_frames = out_grad.reshape(frame_count, frame_blocks, BLOCK, HEADS, HD)
    list_frames = block_list.reshape(frame_count, frame_blocks, SEL)
    count_frames = block_count.reshape(frame_count, frame_blocks)
    block_ids = jnp.arange(window_blocks, dtype=jnp.int32)
    slot_ids = jnp.arange(SEL, dtype=jnp.int32)

    def window_terms(tiles, targets):
        summed = jnp.zeros((window_blocks, BLOCK, D), jnp.float32).at[targets].add(tiles.reshape(frame_blocks * SEL, BLOCK, D))
        rounded = lax.optimization_barrier(summed.astype(jnp.bfloat16)).astype(jnp.float32)
        return rounded.reshape(3 * frame_rows, D)

    def per_frame(carry, item):
        key_acc, value_acc = carry
        frame, query_part, grad_part, lists, counts = item
        start = (frame * frame_rows).astype(jnp.int32)
        key_window = lax.dynamic_slice_in_dim(keys_padded, start, 3 * frame_rows, 0).reshape(window_blocks, BLOCK, HEADS, HD)
        value_window = lax.dynamic_slice_in_dim(values_padded, start, 3 * frame_rows, 0).reshape(window_blocks, BLOCK, HEADS, HD)
        present = ((block_ids >= frame_blocks) | (frame > 0)) & ((block_ids < 2 * frame_blocks) | (frame < frame_count - 1))
        usable = (slot_ids[None, :] < counts[:, None]) & present[lists]
        allowed = jnp.repeat(usable, BLOCK, axis=1)[:, None, None, :]
        key_pick = key_window[lists].reshape(frame_blocks, SEL * BLOCK, HEADS, HD).astype(jnp.float32)
        value_pick = value_window[lists].reshape(frame_blocks, SEL * BLOCK, HEADS, HD).astype(jnp.float32)
        attended, query_grad, key_tiles, value_tiles = attend_rows(query_part.astype(jnp.float32), grad_part.astype(jnp.float32), key_pick, value_pick, allowed, factor)
        targets = lists.reshape(-1)
        key_terms = window_terms(key_tiles, targets)
        value_terms = window_terms(value_tiles, targets)
        key_acc = lax.dynamic_update_slice_in_dim(key_acc, lax.dynamic_slice_in_dim(key_acc, start, 3 * frame_rows, 0) + key_terms, start, 0)
        value_acc = lax.dynamic_update_slice_in_dim(value_acc, lax.dynamic_slice_in_dim(value_acc, start, 3 * frame_rows, 0) + value_terms, start, 0)
        return ((key_acc, value_acc), (attended, query_grad))
    empty = jnp.zeros(((frame_count + 2) * frame_rows, D), jnp.float32)
    frame_ids = jnp.arange(frame_count, dtype=jnp.int32)
    (key_acc, value_acc), (attended, query_grad) = lax.scan(per_frame, (empty, empty), (frame_ids, query_frames, grad_frames, list_frames, count_frames))
    key_grad = key_acc[frame_rows:frame_rows + TOKENS].astype(jnp.bfloat16)
    value_grad = value_acc[frame_rows:frame_rows + TOKENS].astype(jnp.bfloat16)
    return (attended.reshape(TOKENS, D), query_grad.reshape(TOKENS, D), key_grad, value_grad)
```

```python
import jax
import jax.numpy as jnp
from jax import lax
from jax.experimental import pallas as pl
from jax.experimental.pallas import tpu as pltpu
from jax.sharding import PartitionSpec as P

HD = 64
BLOCK = 64
SEL = 13
HALF = 4
FRAME = 8
WINDOW = 24
GROUPS = 4
LANES = 128
FACTOR = 0.125
MASKED = -1e30
PLACE_AT = 32
MESH = pl.DeviceIdType.MESH


def kernel(
    frames,
    block_list, block_count, queries, keys, values, out_grad,
    attended, query_grad, key_grad, value_grad,
    kv, qd, work, tiles, rows_out, give, take, own, final, meta_vm, meta_sm,
    in_send, in_recv, in_local, own_send, own_recv, fwd_send, fwd_recv,
    meta_send, meta_recv, meta_local, row_send, row_recv, row_local,
    term_send, term_recv, grad_send, grad_recv, grad_local,
):
    f, s = lax.axis_index("frames"), lax.axis_index("strip")
    o = 1 - s
    after, before = lax.rem(f + 1, frames), lax.rem(f + frames - 1, frames)
    partner, next_dev, prev_dev = (f, o), (after, s), (before, s)

    barrier = pltpu.get_barrier_semaphore()
    for device in (partner, next_dev, prev_dev):
        pl.semaphore_signal(barrier, inc=1, device_id=device, device_id_type=MESH)
    pl.semaphore_wait(barrier, 3)

    def remote(src, dst, send, recv, device):
        return pltpu.make_async_remote_copy(
            src_ref=src, dst_ref=dst, send_sem=send, recv_sem=recv,
            device_id=device, device_id_type=MESH,
        )

    def columns(half, g):
        return pl.ds(pl.multiple_of(half * (GROUPS * LANES) + g * LANES, LANES), LANES)

    sources = (keys, values, queries, out_grad)

    def landing(g, a):
        lanes = pl.ds((a % 2) * LANES, LANES)
        if a < 2:
            return kv.at[g, pl.ds(FRAME + HALF * s, HALF), :, lanes]
        return qd.at[g, pl.ds(HALF * s, HALF), :, lanes]

    def swap(g, a):
        return remote(
            sources[a].at[:, :, columns(o, g)], landing(g, a), in_send.at[g, a], in_recv.at[g, a], partner
        )

    def keep(g, a):
        return pltpu.make_async_copy(sources[a].at[:, :, columns(s, g)], landing(g, a), in_local.at[g, a])

    def pass_on(g, d, half, send, recv):
        return remote(
            kv.at[g, pl.ds(FRAME + HALF * half, HALF)],
            kv.at[g, pl.ds((0, 2 * FRAME)[d] + HALF * half, HALF)],
            send.at[g, d], recv.at[g, d], (next_dev, prev_dev)[d],
        )

    def pass_own(g, d):
        return pass_on(g, d, s, own_send, own_recv)

    def pass_other(g, d):
        return pass_on(g, d, o, fwd_send, fwd_recv)

    def send_terms(g, d):
        return remote(
            give.at[g, d], take.at[g, d], term_send.at[g, d], term_recv.at[g, d], (next_dev, prev_dev)[d]
        )

    def across(staged, targets, sends, recvs, g, a):
        return remote(
            staged.at[g, pl.ds(HALF * o, HALF), :, pl.ds(a * LANES, LANES)],
            targets[a].at[:, :, columns(s, g)], sends.at[g, a], recvs.at[g, a], partner,
        )

    def along(staged, targets, local, g, a):
        return pltpu.make_async_copy(
            staged.at[g, pl.ds(HALF * s, HALF), :, pl.ds(a * LANES, LANES)],
            targets[a].at[:, :, columns(s, g)], local.at[g, a],
        )

    row_targets, grad_targets = (query_grad, attended), (key_grad, value_grad)

    def rows_across(g, a):
        return across(rows_out, row_targets, row_send, row_recv, g, a)

    def rows_along(g, a):
        return along(rows_out, row_targets, row_local, g, a)

    def grads_across(g, a):
        return across(final, grad_targets, grad_send, grad_recv, g, a)

    def grads_along(g, a):
        return along(final, grad_targets, grad_local, g, a)

    share_meta = remote(meta_vm.at[s], meta_vm.at[s], meta_send, meta_recv, partner)

    def begin(g, carry):
        for a in range(4):
            swap(g, a).start()
        for a in range(4):
            keep(g, a).start()
        return carry

    lax.fori_loop(0, GROUPS, begin, 0)

    def begin_own(g, carry):
        for a in range(2):
            keep(g, a).wait()
        for d in range(2):
            pass_own(g, d).start()
        return carry

    lax.fori_loop(0, GROUPS, begin_own, 0)

    listed = block_list[...]
    row_at = lax.broadcasted_iota(jnp.int32, (HALF, LANES), 0)
    lane_at = lax.broadcasted_iota(jnp.int32, (HALF, LANES), 1)
    counts = jnp.zeros((HALF, LANES), jnp.int32)
    for row in range(HALF):
        counts = jnp.where(row_at == row, block_count[row], counts)
    edge_low = jnp.where(f > 0, 0, FRAME)
    edge_high = jnp.where(f < frames - 1, WINDOW, 2 * FRAME)
    usable = (listed >= edge_low) & (listed < edge_high) & (lane_at[:, :SEL] < counts[:, :SEL])
    slots = jnp.where(usable, listed, -1)
    place = jnp.full((HALF, LANES), SEL, jnp.int32)
    for j in range(SEL):
        place = jnp.where(lane_at - PLACE_AT == slots[:, j:j + 1], j, place)
    meta_vm[s, 0:HALF] = place
    meta_vm[s, 0:HALF, 0:SEL] = listed
    meta_vm[s, HALF:] = jnp.zeros((HALF, LANES), jnp.int32)
    meta_vm[s, HALF:, 0:SEL] = usable.astype(jnp.int32)
    share_meta.start()
    share_meta.wait()
    to_scalar = pltpu.make_async_copy(meta_vm, meta_sm, meta_local)
    to_scalar.start()
    to_scalar.wait()

    tiles[:, SEL] = jnp.zeros((FRAME, BLOCK, 2 * LANES), jnp.float32)

    def forward(g):
        for a in range(2):
            swap(g, a).wait_recv()
        for d in range(2):
            pass_other(g, d).start()

    forward(0)

    row_ids = lax.broadcasted_iota(jnp.int32, (4 * HD, 4 * HD), 0) // HD
    col_ids = lax.broadcasted_iota(jnp.int32, (4 * HD, 4 * HD), 1) // HD
    spread = jnp.where(
        row_ids == col_ids, jnp.where(col_ids < 2, FACTOR, 1.0), 0.0
    ).astype(jnp.bfloat16)
    first_head = lax.broadcasted_iota(jnp.int32, (BLOCK, LANES), 1) < HD

    def heads(full):
        return jnp.where(first_head, full[:HD], full[HD:])

    def fold(array, op):
        return op(array.reshape(array.shape[0] // 8, 8, LANES), axis=0)

    def attend(g, b):
        strip, row = b // HALF, lax.rem(b, HALF)
        part = qd[g, b]
        diagonal = jnp.concatenate([part] * 4, axis=0) * spread
        picked = jnp.concatenate(
            [work[meta_sm[strip, row, j]] for j in range(SEL)], axis=0
        )
        both = lax.dot_general(
            picked, diagonal, (((1,), (1,)), ((), ())), preferred_element_type=jnp.float32
        )
        bias = [
            jnp.where(meta_sm[strip, HALF + row, j] > 0, 0.0, MASKED).astype(jnp.float32)
            for j in range(SEL)
        ]
        parts = [both[j * BLOCK:(j + 1) * BLOCK, :LANES] for j in range(SEL)]
        peak = fold(parts[0], jnp.max) + bias[0]
        for j in range(1, SEL):
            peak = jnp.maximum(peak, fold(parts[j], jnp.max) + bias[j])
        peak = jnp.max(peak, axis=0, keepdims=True)
        powers = [jnp.exp(parts[j] - (peak - bias[j])) for j in range(SEL)]
        grad_weights = [both[j * BLOCK:(j + 1) * BLOCK, LANES:] for j in range(SEL)]
        total = fold(powers[0], jnp.sum)
        dots = fold(powers[0] * grad_weights[0], jnp.sum)
        for j in range(1, SEL):
            total = total + fold(powers[j], jnp.sum)
            dots = dots + fold(powers[j] * grad_weights[j], jnp.sum)
        scale = 1.0 / jnp.sum(total, axis=0, keepdims=True)
        row_dots = jnp.sum(dots, axis=0, keepdims=True) * scale
        slabs = []
        for j in range(SEL):
            weights = powers[j] * scale
            grad_scores = weights * (grad_weights[j] - row_dots)
            slabs.append(jnp.concatenate([grad_scores, weights], axis=1).astype(jnp.bfloat16))
        slab = jnp.concatenate(slabs, axis=0)
        terms = jnp.dot(slab, diagonal, preferred_element_type=jnp.float32)
        tiles[b, :SEL] = terms.reshape(SEL, BLOCK, 2 * LANES)
        mixed = lax.dot_general(
            slab, picked, (((0,), (0,)), ((), ())), preferred_element_type=jnp.float32
        )
        rows_out[g, b] = jnp.concatenate(
            [heads(mixed[:LANES, :LANES]) * FACTOR, heads(mixed[LANES:, LANES:])], axis=1
        ).astype(jnp.bfloat16)

    def finish(g):
        slot = lax.rem(g, 2)
        for d in range(2):
            send_terms(g, d).wait_recv()

        def add(w, carry):
            total = own[slot, w] + take[g, 0, w].astype(jnp.float32) + take[g, 1, w].astype(jnp.float32)
            final[g, w] = total.astype(jnp.bfloat16)
            return carry

        lax.fori_loop(0, FRAME, add, 0)
        for a in range(2):
            grads_across(g, a).start()
        for a in range(2):
            grads_along(g, a).start()

    def one_group(g, carry):
        @pl.when(g + 1 < GROUPS)
        def _():
            forward(g + 1)

        for a in range(2, 4):
            keep(g, a).wait()
            swap(g, a).wait_recv()
        for d in range(2):
            pass_own(g, d).wait_recv()
            pass_other(g, d).wait_recv()
        work[...] = kv[g]

        def one_block(i, inner):
            attend(g, lax.rem(HALF * o + i, FRAME))

            @pl.when(i == HALF - 1)
            def _():
                for a in range(2):
                    rows_across(g, a).start()

            return inner

        lax.fori_loop(0, FRAME, one_block, 0)
        for a in range(2):
            rows_along(g, a).start()

        def gather(w, base):
            acc = None
            for b in range(FRAME):
                place = meta_sm[b // HALF, b % HALF, PLACE_AT + base + w]
                tile = tiles[b, place]
                acc = tile if acc is None else acc + tile
            return acc

        def collect(w, inner):
            give[g, 1, w] = gather(w, 0).astype(jnp.bfloat16)
            give[g, 0, w] = gather(w, 2 * FRAME).astype(jnp.bfloat16)
            return inner

        lax.fori_loop(0, FRAME, collect, 0)
        for d in range(2):
            send_terms(g, d).start()

        def collect_own(w, inner):
            own[lax.rem(g, 2), w] = gather(w, FRAME)
            return inner

        lax.fori_loop(0, FRAME, collect_own, 0)

        @pl.when(g > 0)
        def _():
            finish(g - 1)

        return carry

    lax.fori_loop(0, GROUPS, one_group, 0)
    finish(GROUPS - 1)

    def drain(g, carry):
        for a in range(4):
            swap(g, a).wait_send()
        for d in range(2):
            pass_own(g, d).wait_send()
            pass_other(g, d).wait_send()
            send_terms(g, d).wait_send()
        for a in range(2):
            rows_across(g, a).wait()
            rows_along(g, a).wait()
            grads_across(g, a).wait()
            grads_along(g, a).wait()
        return carry

    lax.fori_loop(0, GROUPS, drain, 0)


def body(queries, keys, values, out_grad, block_list, block_count):
    rows, width = queries.shape
    frames = lax.axis_size("frames")
    blocked = [x.reshape(HALF, BLOCK, width) for x in (queries, keys, values, out_grad)]
    shape = jax.ShapeDtypeStruct((HALF, BLOCK, width), jnp.bfloat16)
    dma = pltpu.SemaphoreType.DMA
    flops = 6 * 2 * FRAME * SEL * BLOCK * 256 * 256 * GROUPS
    outs = pl.pallas_call(
        lambda *refs: kernel(frames, *refs),
        out_shape=[shape] * 4,
        in_specs=[pl.BlockSpec(memory_space=pltpu.VMEM), pl.BlockSpec(memory_space=pltpu.SMEM)] + [pl.BlockSpec(memory_space=pl.ANY)] * 4,
        out_specs=[pl.BlockSpec(memory_space=pl.ANY)] * 4,
        scratch_shapes=[
            pltpu.VMEM((GROUPS, WINDOW, BLOCK, 2 * LANES), jnp.bfloat16),
            pltpu.VMEM((GROUPS, FRAME, BLOCK, 2 * LANES), jnp.bfloat16),
            pltpu.VMEM((WINDOW, BLOCK, 2 * LANES), jnp.bfloat16),
            pltpu.VMEM((FRAME, SEL + 1, BLOCK, 2 * LANES), jnp.float32),
            pltpu.VMEM((GROUPS, FRAME, BLOCK, 2 * LANES), jnp.bfloat16),
            pltpu.VMEM((GROUPS, 2, FRAME, BLOCK, 2 * LANES), jnp.bfloat16),
            pltpu.VMEM((GROUPS, 2, FRAME, BLOCK, 2 * LANES), jnp.bfloat16),
            pltpu.VMEM((2, FRAME, BLOCK, 2 * LANES), jnp.float32),
            pltpu.VMEM((GROUPS, FRAME, BLOCK, 2 * LANES), jnp.bfloat16),
            pltpu.VMEM((2, 8, LANES), jnp.int32),
            pltpu.SMEM((2, 8, LANES), jnp.int32),
            dma((GROUPS, 4)), dma((GROUPS, 4)), dma((GROUPS, 4)),
            dma((GROUPS, 2)), dma((GROUPS, 2)), dma((GROUPS, 2)), dma((GROUPS, 2)),
            dma, dma, dma,
            dma((GROUPS, 2)), dma((GROUPS, 2)), dma((GROUPS, 2)),
            dma((GROUPS, 2)), dma((GROUPS, 2)),
            dma((GROUPS, 2)), dma((GROUPS, 2)), dma((GROUPS, 2)),
        ],
        cost_estimate=pl.CostEstimate(
            flops=flops, bytes_accessed=16 * rows * width, transcendentals=FRAME * SEL * BLOCK * LANES * GROUPS
        ),
        compiler_params=pltpu.CompilerParams(
            collective_id=0, has_side_effects=True, vmem_limit_bytes=60 * 1024 * 1024
        ),
    )(block_list, block_count, *blocked)
    return tuple(x.reshape(rows, width) for x in outs)


def solution(mesh):
    split = P(("frames", "strip"), None)
    in_specs = (split, split, split, split, split, P(("frames", "strip")))
    return jax.shard_map(
        body, mesh=mesh, in_specs=in_specs, out_specs=(split,) * 4, check_vma=False
    )
```

```python
import jax
import jax.numpy as jnp
from jax import lax
from jax.experimental import pallas as pl
from jax.experimental.pallas import tpu as pltpu
from jax.sharding import PartitionSpec as P

HD = 64
BLOCK = 64
SEL = 13
HALF = 4
FRAME = 8
WINDOW = 24
GROUPS = 4
LANES = 128
FACTOR = 0.125
MASKED = -1e30
PLACE_AT = 32
MESH = pl.DeviceIdType.MESH


def kernel(
    frames,
    block_list, block_count, queries, keys, values, out_grad,
    attended, query_grad, key_grad, value_grad,
    kv, qd, work, tiles, rows_out, give, take, own, final, meta_vm, meta_sm,
    in_send, in_recv, in_local, own_send, own_recv, fwd_send, fwd_recv,
    meta_send, meta_recv, meta_local, row_send, row_recv, row_local,
    term_send, term_recv, grad_send, grad_recv, grad_local,
):
    f, s = lax.axis_index("frames"), lax.axis_index("strip")
    o = 1 - s
    after, before = lax.rem(f + 1, frames), lax.rem(f + frames - 1, frames)
    partner, next_dev, prev_dev = (f, o), (after, s), (before, s)

    barrier = pltpu.get_barrier_semaphore()
    for device in (partner, next_dev, prev_dev):
        pl.semaphore_signal(barrier, inc=1, device_id=device, device_id_type=MESH)
    pl.semaphore_wait(barrier, 3)

    def remote(src, dst, send, recv, device):
        return pltpu.make_async_remote_copy(
            src_ref=src, dst_ref=dst, send_sem=send, recv_sem=recv,
            device_id=device, device_id_type=MESH,
        )

    def columns(half, g):
        return pl.ds(pl.multiple_of(half * (GROUPS * LANES) + g * LANES, LANES), LANES)

    sources = (keys, values, queries, out_grad)

    def landing(g, a):
        lanes = pl.ds((a % 2) * LANES, LANES)
        if a < 2:
            return kv.at[g, pl.ds(FRAME + HALF * s, HALF), :, lanes]
        return qd.at[g, pl.ds(HALF * s, HALF), :, lanes]

    def swap(g, a):
        return remote(
            sources[a].at[:, :, columns(o, g)], landing(g, a), in_send.at[g, a], in_recv.at[g, a], partner
        )

    def keep(g, a):
        return pltpu.make_async_copy(sources[a].at[:, :, columns(s, g)], landing(g, a), in_local.at[g, a])

    def pass_on(g, d, half, send, recv):
        return remote(
            kv.at[g, pl.ds(FRAME + HALF * half, HALF)],
            kv.at[g, pl.ds((0, 2 * FRAME)[d] + HALF * half, HALF)],
            send.at[g, d], recv.at[g, d], (next_dev, prev_dev)[d],
        )

    def pass_own(g, d):
        return pass_on(g, d, s, own_send, own_recv)

    def pass_other(g, d):
        return pass_on(g, d, o, fwd_send, fwd_recv)

    def send_terms(g, d):
        return remote(
            give.at[g, d], take.at[g, d], term_send.at[g, d], term_recv.at[g, d], (next_dev, prev_dev)[d]
        )

    def across(staged, targets, sends, recvs, g, a):
        return remote(
            staged.at[g, pl.ds(HALF * o, HALF), :, pl.ds(a * LANES, LANES)],
            targets[a].at[:, :, columns(s, g)], sends.at[g, a], recvs.at[g, a], partner,
        )

    def along(staged, targets, local, g, a):
        return pltpu.make_async_copy(
            staged.at[g, pl.ds(HALF * s, HALF), :, pl.ds(a * LANES, LANES)],
            targets[a].at[:, :, columns(s, g)], local.at[g, a],
        )

    row_targets, grad_targets = (query_grad, attended), (key_grad, value_grad)

    def rows_across(g, a):
        return across(rows_out, row_targets, row_send, row_recv, g, a)

    def rows_along(g, a):
        return along(rows_out, row_targets, row_local, g, a)

    def grads_across(g, a):
        return across(final, grad_targets, grad_send, grad_recv, g, a)

    def grads_along(g, a):
        return along(final, grad_targets, grad_local, g, a)

    share_meta = remote(meta_vm.at[s], meta_vm.at[s], meta_send, meta_recv, partner)

    def begin(g):
        for a in range(4):
            swap(g, a).start()

    def begin_own(g):
        for a in range(2):
            keep(g, a).wait()
        for d in range(2):
            pass_own(g, d).start()

    begin(0)

    def begin_keep(g, carry):
        for a in range(4):
            keep(g, a).start()
        return carry

    lax.fori_loop(0, GROUPS, begin_keep, 0)
    begin_own(0)

    listed = block_list[...]
    row_at = lax.broadcasted_iota(jnp.int32, (HALF, LANES), 0)
    lane_at = lax.broadcasted_iota(jnp.int32, (HALF, LANES), 1)
    counts = jnp.zeros((HALF, LANES), jnp.int32)
    for row in range(HALF):
        counts = jnp.where(row_at == row, block_count[row], counts)
    edge_low = jnp.where(f > 0, 0, FRAME)
    edge_high = jnp.where(f < frames - 1, WINDOW, 2 * FRAME)
    usable = (listed >= edge_low) & (listed < edge_high) & (lane_at[:, :SEL] < counts[:, :SEL])
    slots = jnp.where(usable, listed, -1)
    place = jnp.full((HALF, LANES), SEL, jnp.int32)
    for j in range(SEL):
        place = jnp.where(lane_at - PLACE_AT == slots[:, j:j + 1], j, place)
    meta_vm[s, 0:HALF] = place
    meta_vm[s, 0:HALF, 0:SEL] = listed
    meta_vm[s, HALF:] = jnp.zeros((HALF, LANES), jnp.int32)
    meta_vm[s, HALF:, 0:SEL] = usable.astype(jnp.int32)
    share_meta.start()
    share_meta.wait()
    to_scalar = pltpu.make_async_copy(meta_vm, meta_sm, meta_local)
    to_scalar.start()
    to_scalar.wait()

    tiles[:, SEL] = jnp.zeros((FRAME, BLOCK, 2 * LANES), jnp.float32)

    def forward(g):
        for a in range(2):
            swap(g, a).wait_recv()
        for d in range(2):
            pass_other(g, d).start()

    forward(0)
    begin(1)
    begin_own(1)

    row_ids = lax.broadcasted_iota(jnp.int32, (4 * HD, 4 * HD), 0) // HD
    col_ids = lax.broadcasted_iota(jnp.int32, (4 * HD, 4 * HD), 1) // HD
    spread = jnp.where(
        row_ids == col_ids, jnp.where(col_ids < 2, FACTOR, 1.0), 0.0
    ).astype(jnp.bfloat16)
    first_head = lax.broadcasted_iota(jnp.int32, (BLOCK, LANES), 1) < HD

    def heads(full):
        return jnp.where(first_head, full[:HD], full[HD:])

    def fold(array, op):
        return op(array.reshape(array.shape[0] // 8, 8, LANES), axis=0)

    def attend(g, b):
        strip, row = b // HALF, lax.rem(b, HALF)
        part = qd[g, b]
        diagonal = jnp.concatenate([part] * 4, axis=0) * spread
        picked = jnp.concatenate(
            [work[meta_sm[strip, row, j]] for j in range(SEL)], axis=0
        )
        both = lax.dot_general(
            picked, diagonal, (((1,), (1,)), ((), ())), preferred_element_type=jnp.float32
        )
        bias = [
            jnp.where(meta_sm[strip, HALF + row, j] > 0, 0.0, MASKED).astype(jnp.float32)
            for j in range(SEL)
        ]
        parts = [both[j * BLOCK:(j + 1) * BLOCK, :LANES] for j in range(SEL)]
        peak = fold(parts[0], jnp.max) + bias[0]
        for j in range(1, SEL):
            peak = jnp.maximum(peak, fold(parts[j], jnp.max) + bias[j])
        peak = jnp.max(peak, axis=0, keepdims=True)
        powers = [jnp.exp(parts[j] - (peak - bias[j])) for j in range(SEL)]
        grad_weights = [both[j * BLOCK:(j + 1) * BLOCK, LANES:] for j in range(SEL)]
        total = fold(powers[0], jnp.sum)
        dots = fold(powers[0] * grad_weights[0], jnp.sum)
        for j in range(1, SEL):
            total = total + fold(powers[j], jnp.sum)
            dots = dots + fold(powers[j] * grad_weights[j], jnp.sum)
        scale = 1.0 / jnp.sum(total, axis=0, keepdims=True)
        row_dots = jnp.sum(dots, axis=0, keepdims=True) * scale
        slabs = []
        for j in range(SEL):
            weights = powers[j] * scale
            grad_scores = weights * (grad_weights[j] - row_dots)
            slabs.append(jnp.concatenate([grad_scores, weights], axis=1).astype(jnp.bfloat16))
        slab = jnp.concatenate(slabs, axis=0)
        terms = jnp.dot(slab, diagonal, preferred_element_type=jnp.float32)
        tiles[b, :SEL] = terms.reshape(SEL, BLOCK, 2 * LANES)
        mixed = lax.dot_general(
            slab, picked, (((0,), (0,)), ((), ())), preferred_element_type=jnp.float32
        )
        rows_out[g, b] = jnp.concatenate(
            [heads(mixed[:LANES, :LANES]) * FACTOR, heads(mixed[LANES:, LANES:])], axis=1
        ).astype(jnp.bfloat16)

    def finish(g):
        slot = lax.rem(g, 2)
        for d in range(2):
            send_terms(g, d).wait_recv()

        def add(w, carry):
            total = own[slot, w] + take[g, 0, w].astype(jnp.float32) + take[g, 1, w].astype(jnp.float32)
            final[g, w] = total.astype(jnp.bfloat16)
            return carry

        lax.fori_loop(0, FRAME, add, 0)
        for a in range(2):
            grads_across(g, a).start()
        for a in range(2):
            grads_along(g, a).start()

    def one_group(g, carry):
        for a in range(2, 4):
            keep(g, a).wait()
            swap(g, a).wait_recv()
        for d in range(2):
            pass_own(g, d).wait_recv()
            pass_other(g, d).wait_recv()

        @pl.when(g + 2 < GROUPS)
        def _():
            begin(g + 2)
            begin_own(g + 2)

        work[...] = kv[g]

        def two_blocks(i, inner):
            b = lax.rem(HALF * o + 2 * i, FRAME)
            attend(g, b)
            attend(g, b + 1)

            @pl.when(i == HALF // 2 - 1)
            def _():
                for a in range(2):
                    rows_across(g, a).start()

                @pl.when(g + 1 < GROUPS)
                def _():
                    forward(g + 1)

            return inner

        lax.fori_loop(0, FRAME // 2, two_blocks, 0)
        for a in range(2):
            rows_along(g, a).start()

        def gather(w, base):
            acc = None
            for b in range(FRAME):
                place = meta_sm[b // HALF, b % HALF, PLACE_AT + base + w]
                tile = tiles[b, place]
                acc = tile if acc is None else acc + tile
            return acc

        def collect(w, inner):
            give[g, 1, w] = gather(w, 0).astype(jnp.bfloat16)
            give[g, 0, w] = gather(w, 2 * FRAME).astype(jnp.bfloat16)
            return inner

        lax.fori_loop(0, FRAME, collect, 0)
        for d in range(2):
            send_terms(g, d).start()

        def collect_own(w, inner):
            own[lax.rem(g, 2), w] = gather(w, FRAME)
            return inner

        lax.fori_loop(0, FRAME, collect_own, 0)

        @pl.when(g > 0)
        def _():
            finish(g - 1)

        return carry

    lax.fori_loop(0, GROUPS, one_group, 0)
    finish(GROUPS - 1)

    def drain(g, carry):
        for a in range(4):
            swap(g, a).wait_send()
        for d in range(2):
            pass_own(g, d).wait_send()
            pass_other(g, d).wait_send()
            send_terms(g, d).wait_send()
        for a in range(2):
            rows_across(g, a).wait()
            rows_along(g, a).wait()
            grads_across(g, a).wait()
            grads_along(g, a).wait()
        return carry

    lax.fori_loop(0, GROUPS, drain, 0)


def hand_over(*refs):
    sources, targets, sems = refs[:4], refs[4:8], refs[8]
    copies = [
        pltpu.make_async_copy(src.at[pl.ds(at * 2, 2)], dst.at[pl.ds(at * 2, 2)], sems.at[i, at])
        for i, (src, dst) in enumerate(zip(sources, targets))
        for at in range(2)
    ]
    for copy in copies:
        copy.start()
    for copy in copies:
        copy.wait()


def body(queries, keys, values, out_grad, block_list, block_count):
    rows, width = queries.shape
    frames = lax.axis_size("frames")
    blocked = [x.reshape(HALF, BLOCK, width) for x in (queries, keys, values, out_grad)]
    shape = jax.ShapeDtypeStruct((HALF, BLOCK, width), jnp.bfloat16)
    dma = pltpu.SemaphoreType.DMA
    flops = 6 * 2 * FRAME * SEL * BLOCK * 256 * 256 * GROUPS
    outs = pl.pallas_call(
        lambda *refs: kernel(frames, *refs),
        out_shape=[shape] * 4,
        in_specs=[pl.BlockSpec(memory_space=pltpu.VMEM), pl.BlockSpec(memory_space=pltpu.SMEM)] + [pl.BlockSpec(memory_space=pl.ANY)] * 4,
        out_specs=[pl.BlockSpec(memory_space=pl.ANY)] * 4,
        scratch_shapes=[
            pltpu.VMEM((GROUPS, WINDOW, BLOCK, 2 * LANES), jnp.bfloat16),
            pltpu.VMEM((GROUPS, FRAME, BLOCK, 2 * LANES), jnp.bfloat16),
            pltpu.VMEM((WINDOW, BLOCK, 2 * LANES), jnp.bfloat16),
            pltpu.VMEM((FRAME, SEL + 1, BLOCK, 2 * LANES), jnp.float32),
            pltpu.VMEM((GROUPS, FRAME, BLOCK, 2 * LANES), jnp.bfloat16),
            pltpu.VMEM((GROUPS, 2, FRAME, BLOCK, 2 * LANES), jnp.bfloat16),
            pltpu.VMEM((GROUPS, 2, FRAME, BLOCK, 2 * LANES), jnp.bfloat16),
            pltpu.VMEM((2, FRAME, BLOCK, 2 * LANES), jnp.float32),
            pltpu.VMEM((GROUPS, FRAME, BLOCK, 2 * LANES), jnp.bfloat16),
            pltpu.VMEM((2, 8, LANES), jnp.int32),
            pltpu.SMEM((2, 8, LANES), jnp.int32),
            dma((GROUPS, 4)), dma((GROUPS, 4)), dma((GROUPS, 4)),
            dma((GROUPS, 2)), dma((GROUPS, 2)), dma((GROUPS, 2)), dma((GROUPS, 2)),
            dma, dma, dma,
            dma((GROUPS, 2)), dma((GROUPS, 2)), dma((GROUPS, 2)),
            dma((GROUPS, 2)), dma((GROUPS, 2)),
            dma((GROUPS, 2)), dma((GROUPS, 2)), dma((GROUPS, 2)),
        ],
        cost_estimate=pl.CostEstimate(
            flops=flops, bytes_accessed=16 * rows * width, transcendentals=FRAME * SEL * BLOCK * LANES * GROUPS
        ),
        compiler_params=pltpu.CompilerParams(
            collective_id=0, has_side_effects=True, vmem_limit_bytes=60 * 1024 * 1024
        ),
    )(block_list, block_count, *blocked)
    outs = pl.pallas_call(
        hand_over,
        out_shape=[shape] * 4,
        in_specs=[pl.BlockSpec(memory_space=pl.ANY)] * 4,
        out_specs=[pl.BlockSpec(memory_space=pl.ANY)] * 4,
        scratch_shapes=[dma((4, 2))],
        compiler_params=pltpu.CompilerParams(vmem_limit_bytes=60 * 1024 * 1024),
    )(*outs)
    return tuple(x.reshape(rows, width) for x in outs)


def solution(mesh):
    split = P(("frames", "strip"), None)
    in_specs = (split, split, split, split, split, P(("frames", "strip")))
    return jax.shard_map(
        body, mesh=mesh, in_specs=in_specs, out_specs=(split,) * 4, check_vma=False
    )
```

```python
import jax
import jax.numpy as jnp
from jax import lax
from jax.experimental import pallas as pl
from jax.experimental.pallas import tpu as pltpu
from jax.sharding import PartitionSpec as P

HD = 64
BLOCK = 64
SEL = 13
HALF = 4
FRAME = 8
WINDOW = 24
GROUPS = 4
LANES = 128
FACTOR = 0.125
MASKED = -1e30
PLACE_AT = 32
RUN = 8
MESH = pl.DeviceIdType.MESH


def kernel(
    frames,
    block_list, block_count, queries, keys, values, out_grad,
    attended, query_grad, key_grad, value_grad,
    kv, qd, work, tiles, rows_out, give, take, own, final, relay, meta_vm, meta_sm,
    in_send, in_recv, in_local, pass_send, pass_recv,
    meta_send, meta_recv, meta_local, row_send, row_recv, row_local,
    term_send, term_recv, grad_send, grad_recv, grad_local, relay_send, relay_recv,
):
    f, s = lax.axis_index("frames"), lax.axis_index("strip")
    o = 1 - s
    after, before = lax.rem(f + 1, frames), lax.rem(f + frames - 1, frames)
    partner, next_dev, prev_dev = (f, o), (after, s), (before, s)

    place_in_run = lax.rem(f, RUN)
    edge = (place_in_run == RUN - 1, place_in_run == 0)
    part_column = (3 * s, 1 + s)

    def relay_of(d, column):
        if d == 0:
            return (lax.rem(f + 1 + 2 * column, frames), s)
        return (lax.rem(f + frames - 1 - 2 * column, frames), s)

    relay_back = lax.rem(place_in_run, 2)
    relay_column = lax.select(relay_back == 0, place_in_run // 2, (RUN - 1 - place_in_run) // 2)
    is_relay = ((relay_column == 1) & (s == 0)) | ((relay_column >= 2) & (s == 1))
    relay_half = lax.rem(relay_column, 2)
    relay_target_frame = f - place_in_run + relay_back * (RUN - 1)
    relay_source_frame = lax.rem(relay_target_frame + frames - 1 + 2 * relay_back, frames)
    relay_target, relay_source = (relay_target_frame, s), (relay_source_frame, s)

    def relay_in_run(d, column):
        return f - 2 * column if d == 0 else f + 2 * column

    barrier = pltpu.get_barrier_semaphore()

    def greet(device):
        pl.semaphore_signal(barrier, inc=1, device_id=device, device_id_type=MESH)

    for device in (partner, next_dev, prev_dev):
        greet(device)

    @pl.when(is_relay)
    def _():
        greet(relay_source)
        greet(relay_target)

    for d in range(2):
        for column in (1, 2, 3):
            @pl.when(edge[d] & (s == (0 if column == 1 else 1)))
            def _():
                greet(relay_of(d, column))
                greet((relay_in_run(d, column), s))

    at_end = (edge[0] | edge[1]).astype(jnp.int32)
    pl.semaphore_wait(barrier, 3 + 2 * is_relay.astype(jnp.int32) + at_end * (2 + 2 * s))

    def remote(src, dst, send, recv, device):
        return pltpu.make_async_remote_copy(
            src_ref=src, dst_ref=dst, send_sem=send, recv_sem=recv,
            device_id=device, device_id_type=MESH,
        )

    def columns(half, g):
        return pl.ds(pl.multiple_of(half * (GROUPS * LANES) + g * LANES, LANES), LANES)

    sources = (keys, values, queries, out_grad)

    def landing(g, a):
        lanes = pl.ds((a % 2) * LANES, LANES)
        if a < 2:
            return kv.at[g, pl.ds(FRAME + HALF * s, HALF), :, lanes]
        return qd.at[g, pl.ds(HALF * s, HALF), :, lanes]

    def swap(g, a):
        return remote(
            sources[a].at[:, :, columns(o, g)], landing(g, a), in_send.at[g, a], in_recv.at[g, a], partner
        )

    def keep(g, a):
        return pltpu.make_async_copy(sources[a].at[:, :, columns(s, g)], landing(g, a), in_local.at[g, a])

    neighbours = (next_dev, prev_dev)

    def start_part(d, part, src, dst, send, recv, phase, g):
        straight = remote(src, dst, send, recv, neighbours[d])
        if part == 0:
            bent = edge[d] & (s == 1)
        else:
            bent = edge[d]

        @pl.when(bent)
        def _():
            remote(
                src, relay.at[phase, g], send, relay_recv.at[phase, g], relay_of(d, part_column[part])
            ).start()

        @pl.when(jnp.logical_not(bent))
        def _():
            straight.start()

    def kv_window(g, base, half):
        return kv.at[g, pl.ds(base + HALF * half, HALF)]

    def pass_args(g, d, part):
        half = (s, o)[part]
        return (
            kv_window(g, FRAME, half), kv_window(g, (0, 2 * FRAME)[d], half),
            pass_send.at[g, d, half], pass_recv.at[g, d, half],
        )

    def start_pass(g, d, part):
        start_part(d, part, *pass_args(g, d, part), 0, g)

    def wait_pass(g, d, part):
        return remote(*pass_args(g, d, part), neighbours[d])

    def term_args(g, d, part):
        half = (s, o)[part]
        at = pl.ds(HALF * half, HALF)
        return (
            give.at[g, d, at], take.at[g, d, at], term_send.at[g, d, half], term_recv.at[g, d, half]
        )

    def start_terms(g, d, part):
        start_part(d, part, *term_args(g, d, part), 1, g)

    def wait_terms(g, d, part):
        return remote(*term_args(g, d, part), neighbours[d])

    def relay_on(g, phase):
        if phase == 0:
            target = kv_window(g, relay_back * (2 * FRAME), relay_half)
            recv = pass_recv.at[g, relay_back, relay_half]
        else:
            target = take.at[g, relay_back, pl.ds(HALF * relay_half, HALF)]
            recv = term_recv.at[g, relay_back, relay_half]
        return remote(relay.at[phase, g], target, relay_send.at[phase, g], recv, relay_target)

    def relay_step(g, phase):
        @pl.when(is_relay)
        def _():
            remote(
                relay.at[phase, g], relay.at[phase, g], relay_send.at[phase, g],
                relay_recv.at[phase, g], relay_target,
            ).wait_recv()
            relay_on(g, phase).start()

    def across(staged, targets, sends, recvs, g, a):
        return remote(
            staged.at[g, pl.ds(HALF * o, HALF), :, pl.ds(a * LANES, LANES)],
            targets[a].at[:, :, columns(s, g)], sends.at[g, a], recvs.at[g, a], partner,
        )

    def along(staged, targets, local, g, a):
        return pltpu.make_async_copy(
            staged.at[g, pl.ds(HALF * s, HALF), :, pl.ds(a * LANES, LANES)],
            targets[a].at[:, :, columns(s, g)], local.at[g, a],
        )

    row_targets, grad_targets = (query_grad, attended), (key_grad, value_grad)

    def rows_across(g, a):
        return across(rows_out, row_targets, row_send, row_recv, g, a)

    def rows_along(g, a):
        return along(rows_out, row_targets, row_local, g, a)

    def grads_across(g, a):
        return across(final, grad_targets, grad_send, grad_recv, g, a)

    def grads_along(g, a):
        return along(final, grad_targets, grad_local, g, a)

    share_meta = remote(meta_vm.at[s], meta_vm.at[s], meta_send, meta_recv, partner)

    def begin(g):
        for a in range(4):
            swap(g, a).start()

    def begin_own(g):
        for a in range(2):
            keep(g, a).wait()
        for d in range(2):
            start_pass(g, d, 0)

    begin(0)

    def begin_keep(g, carry):
        for a in range(4):
            keep(g, a).start()
        return carry

    lax.fori_loop(0, GROUPS, begin_keep, 0)
    begin_own(0)

    listed = block_list[...]
    row_at = lax.broadcasted_iota(jnp.int32, (HALF, LANES), 0)
    lane_at = lax.broadcasted_iota(jnp.int32, (HALF, LANES), 1)
    counts = jnp.zeros((HALF, LANES), jnp.int32)
    for row in range(HALF):
        counts = jnp.where(row_at == row, block_count[row], counts)
    edge_low = jnp.where(f > 0, 0, FRAME)
    edge_high = jnp.where(f < frames - 1, WINDOW, 2 * FRAME)
    usable = (listed >= edge_low) & (listed < edge_high) & (lane_at[:, :SEL] < counts[:, :SEL])
    slots = jnp.where(usable, listed, -1)
    place = jnp.full((HALF, LANES), SEL, jnp.int32)
    for j in range(SEL):
        place = jnp.where(lane_at - PLACE_AT == slots[:, j:j + 1], j, place)
    meta_vm[s, 0:HALF] = place
    meta_vm[s, 0:HALF, 0:SEL] = listed
    meta_vm[s, HALF:] = jnp.zeros((HALF, LANES), jnp.int32)
    meta_vm[s, HALF:, 0:SEL] = usable.astype(jnp.int32)
    share_meta.start()
    share_meta.wait()
    to_scalar = pltpu.make_async_copy(meta_vm, meta_sm, meta_local)
    to_scalar.start()
    to_scalar.wait()

    tiles[:, SEL] = jnp.zeros((FRAME, BLOCK, 2 * LANES), jnp.float32)

    def forward(g):
        for a in range(2):
            swap(g, a).wait_recv()
        for d in range(2):
            start_pass(g, d, 1)

    forward(0)
    begin(1)
    begin_own(1)
    relay_step(0, 0)

    row_ids = lax.broadcasted_iota(jnp.int32, (4 * HD, 4 * HD), 0) // HD
    col_ids = lax.broadcasted_iota(jnp.int32, (4 * HD, 4 * HD), 1) // HD
    spread = jnp.where(
        row_ids == col_ids, jnp.where(col_ids < 2, FACTOR, 1.0), 0.0
    ).astype(jnp.bfloat16)
    first_head = lax.broadcasted_iota(jnp.int32, (BLOCK, LANES), 1) < HD

    def heads(full):
        return jnp.where(first_head, full[:HD], full[HD:])

    def fold(array, op):
        return op(array.reshape(array.shape[0] // 8, 8, LANES), axis=0)

    def attend(g, b):
        strip, row = b // HALF, lax.rem(b, HALF)
        part = qd[g, b]
        diagonal = jnp.concatenate([part] * 4, axis=0) * spread
        picked = jnp.concatenate(
            [work[meta_sm[strip, row, j]] for j in range(SEL)], axis=0
        )
        both = lax.dot_general(
            picked, diagonal, (((1,), (1,)), ((), ())), preferred_element_type=jnp.float32
        )
        bias = [
            jnp.where(meta_sm[strip, HALF + row, j] > 0, 0.0, MASKED).astype(jnp.float32)
            for j in range(SEL)
        ]
        parts = [both[j * BLOCK:(j + 1) * BLOCK, :LANES] for j in range(SEL)]
        peak = fold(parts[0], jnp.max) + bias[0]
        for j in range(1, SEL):
            peak = jnp.maximum(peak, fold(parts[j], jnp.max) + bias[j])
        peak = jnp.max(peak, axis=0, keepdims=True)
        powers = [jnp.exp(parts[j] - (peak - bias[j])) for j in range(SEL)]
        grad_weights = [both[j * BLOCK:(j + 1) * BLOCK, LANES:] for j in range(SEL)]
        total = fold(powers[0], jnp.sum)
        dots = fold(powers[0] * grad_weights[0], jnp.sum)
        for j in range(1, SEL):
            total = total + fold(powers[j], jnp.sum)
            dots = dots + fold(powers[j] * grad_weights[j], jnp.sum)
        scale = 1.0 / jnp.sum(total, axis=0, keepdims=True)
        row_dots = jnp.sum(dots, axis=0, keepdims=True) * scale
        slabs = []
        for j in range(SEL):
            weights = powers[j] * scale
            grad_scores = weights * (grad_weights[j] - row_dots)
            slabs.append(jnp.concatenate([grad_scores, weights], axis=1).astype(jnp.bfloat16))
        slab = jnp.concatenate(slabs, axis=0)
        terms = jnp.dot(slab, diagonal, preferred_element_type=jnp.float32)
        tiles[b, :SEL] = terms.reshape(SEL, BLOCK, 2 * LANES)
        mixed = lax.dot_general(
            slab, picked, (((0,), (0,)), ((), ())), preferred_element_type=jnp.float32
        )
        rows_out[g, b] = jnp.concatenate(
            [heads(mixed[:LANES, :LANES]) * FACTOR, heads(mixed[LANES:, LANES:])], axis=1
        ).astype(jnp.bfloat16)

    def finish(g):
        slot = lax.rem(g, 2)
        for d in range(2):
            for part in range(2):
                wait_terms(g, d, part).wait_recv()

        def add(w, carry):
            total = own[slot, w] + take[g, 0, w].astype(jnp.float32) + take[g, 1, w].astype(jnp.float32)
            final[g, w] = total.astype(jnp.bfloat16)
            return carry

        lax.fori_loop(0, FRAME, add, 0)
        for a in range(2):
            grads_across(g, a).start()
        for a in range(2):
            grads_along(g, a).start()

    def one_group(g, carry):
        for a in range(2, 4):
            keep(g, a).wait()
            swap(g, a).wait_recv()
        for d in range(2):
            for part in range(2):
                wait_pass(g, d, part).wait_recv()

        @pl.when(g + 2 < GROUPS)
        def _():
            begin(g + 2)
            begin_own(g + 2)

        work[...] = kv[g]

        def two_blocks(i, inner):
            b = lax.rem(HALF * o + 2 * i, FRAME)
            attend(g, b)
            attend(g, b + 1)

            @pl.when((i == 0) & (g > 0))
            def _():
                relay_step(g - 1, 1)

            @pl.when(i == 1)
            def _():
                for a in range(2):
                    rows_across(g, a).start()

                @pl.when(g + 1 < GROUPS)
                def _():
                    forward(g + 1)

            @pl.when((i == 2) & (g + 1 < GROUPS))
            def _():
                relay_step(g + 1, 0)

            @pl.when((i == 2) & (g > 0))
            def _():
                finish(g - 1)

            return inner

        lax.fori_loop(0, FRAME // 2, two_blocks, 0)
        for a in range(2):
            rows_along(g, a).start()

        def gather(w, base):
            acc = None
            for b in range(FRAME):
                place = meta_sm[b // HALF, b % HALF, PLACE_AT + base + w]
                tile = tiles[b, place]
                acc = tile if acc is None else acc + tile
            return acc

        def collect(w, inner):
            give[g, 1, w] = gather(w, 0).astype(jnp.bfloat16)
            give[g, 0, w] = gather(w, 2 * FRAME).astype(jnp.bfloat16)
            return inner

        lax.fori_loop(0, FRAME, collect, 0)
        for d in range(2):
            for part in range(2):
                start_terms(g, d, part)

        def collect_own(w, inner):
            own[lax.rem(g, 2), w] = gather(w, FRAME)
            return inner

        lax.fori_loop(0, FRAME, collect_own, 0)

        return carry

    lax.fori_loop(0, GROUPS, one_group, 0)
    relay_step(GROUPS - 1, 1)
    finish(GROUPS - 1)

    def drain(g, carry):
        for a in range(4):
            swap(g, a).wait_send()
        for d in range(2):
            for part in range(2):
                wait_pass(g, d, part).wait_send()
                wait_terms(g, d, part).wait_send()

        @pl.when(is_relay)
        def _():
            for phase in range(2):
                relay_on(g, phase).wait_send()

        for a in range(2):
            rows_across(g, a).wait()
            rows_along(g, a).wait()
            grads_across(g, a).wait()
            grads_along(g, a).wait()
        return carry

    lax.fori_loop(0, GROUPS, drain, 0)


def hand_over(*refs):
    sources, targets, sems = refs[:4], refs[4:8], refs[8]
    copies = [
        pltpu.make_async_copy(src.at[pl.ds(at * 2, 2)], dst.at[pl.ds(at * 2, 2)], sems.at[i, at])
        for i, (src, dst) in enumerate(zip(sources, targets))
        for at in range(2)
    ]
    for copy in copies:
        copy.start()
    for copy in copies:
        copy.wait()


def body(queries, keys, values, out_grad, block_list, block_count):
    rows, width = queries.shape
    frames = lax.axis_size("frames")
    blocked = [x.reshape(HALF, BLOCK, width) for x in (queries, keys, values, out_grad)]
    shape = jax.ShapeDtypeStruct((HALF, BLOCK, width), jnp.bfloat16)
    dma = pltpu.SemaphoreType.DMA
    flops = 6 * 2 * FRAME * SEL * BLOCK * 256 * 256 * GROUPS
    outs = pl.pallas_call(
        lambda *refs: kernel(frames, *refs),
        out_shape=[shape] * 4,
        in_specs=[pl.BlockSpec(memory_space=pltpu.VMEM), pl.BlockSpec(memory_space=pltpu.SMEM)] + [pl.BlockSpec(memory_space=pl.ANY)] * 4,
        out_specs=[pl.BlockSpec(memory_space=pl.ANY)] * 4,
        scratch_shapes=[
            pltpu.VMEM((GROUPS, WINDOW, BLOCK, 2 * LANES), jnp.bfloat16),
            pltpu.VMEM((GROUPS, FRAME, BLOCK, 2 * LANES), jnp.bfloat16),
            pltpu.VMEM((WINDOW, BLOCK, 2 * LANES), jnp.bfloat16),
            pltpu.VMEM((FRAME, SEL + 1, BLOCK, 2 * LANES), jnp.float32),
            pltpu.VMEM((GROUPS, FRAME, BLOCK, 2 * LANES), jnp.bfloat16),
            pltpu.VMEM((GROUPS, 2, FRAME, BLOCK, 2 * LANES), jnp.bfloat16),
            pltpu.VMEM((GROUPS, 2, FRAME, BLOCK, 2 * LANES), jnp.bfloat16),
            pltpu.VMEM((2, FRAME, BLOCK, 2 * LANES), jnp.float32),
            pltpu.VMEM((GROUPS, FRAME, BLOCK, 2 * LANES), jnp.bfloat16),
            pltpu.VMEM((2, GROUPS, HALF, BLOCK, 2 * LANES), jnp.bfloat16),
            pltpu.VMEM((2, 8, LANES), jnp.int32),
            pltpu.SMEM((2, 8, LANES), jnp.int32),
            dma((GROUPS, 4)), dma((GROUPS, 4)), dma((GROUPS, 4)),
            dma((GROUPS, 2, 2)), dma((GROUPS, 2, 2)),
            dma, dma, dma,
            dma((GROUPS, 2)), dma((GROUPS, 2)), dma((GROUPS, 2)),
            dma((GROUPS, 2, 2)), dma((GROUPS, 2, 2)),
            dma((GROUPS, 2)), dma((GROUPS, 2)), dma((GROUPS, 2)),
            dma((2, GROUPS)), dma((2, GROUPS)),
        ],
        cost_estimate=pl.CostEstimate(
            flops=flops, bytes_accessed=16 * rows * width, transcendentals=FRAME * SEL * BLOCK * LANES * GROUPS
        ),
        compiler_params=pltpu.CompilerParams(
            collective_id=0, has_side_effects=True, vmem_limit_bytes=60 * 1024 * 1024
        ),
    )(block_list, block_count, *blocked)
    outs = pl.pallas_call(
        hand_over,
        out_shape=[shape] * 4,
        in_specs=[pl.BlockSpec(memory_space=pltpu.VMEM)] * 4,
        out_specs=[pl.BlockSpec(memory_space=pl.ANY)] * 4,
        scratch_shapes=[dma((4, 2))],
        compiler_params=pltpu.CompilerParams(vmem_limit_bytes=60 * 1024 * 1024),
    )(*outs)
    return tuple(x.reshape(rows, width) for x in outs)


def solution(mesh):
    split = P(("frames", "strip"), None)
    in_specs = (split, split, split, split, split, P(("frames", "strip")))
    return jax.shard_map(
        body, mesh=mesh, in_specs=in_specs, out_specs=(split,) * 4, check_vma=False
    )
```

```python
import jax
import jax.numpy as jnp
from jax import lax
from jax.experimental import pallas as pl
from jax.experimental.pallas import tpu as pltpu
from jax.sharding import PartitionSpec as P

HD = 64
BLOCK = 64
SEL = 13
HALF = 4
FRAME = 8
WINDOW = 24
GROUPS = 4
LANES = 128
FACTOR = 0.125
MASKED = -1e30
PLACE_AT = 32
RUN = 8
MESH = pl.DeviceIdType.MESH


def kernel(
    frames,
    block_list, block_count, queries, keys, values, out_grad,
    attended, query_grad, key_grad, value_grad,
    kv, qd, work, tiles, rows_out, give, take, own, final, relay, meta_vm, meta_sm,
    in_send, in_recv, in_local, pass_send, pass_recv,
    meta_send, meta_recv, meta_local, row_send, row_recv, row_local,
    term_send, term_recv, grad_send, grad_recv, grad_local, relay_send, relay_recv,
):
    f, s = lax.axis_index("frames"), lax.axis_index("strip")
    o = 1 - s
    after, before = lax.rem(f + 1, frames), lax.rem(f + frames - 1, frames)
    partner, next_dev, prev_dev = (f, o), (after, s), (before, s)

    place_in_run = lax.rem(f, RUN)
    edge = (place_in_run == RUN - 1, place_in_run == 0)
    part_column = (3 * s, 1 + s)

    def relay_of(d, column):
        if d == 0:
            return (lax.rem(f + 1 + 2 * column, frames), s)
        return (lax.rem(f + frames - 1 - 2 * column, frames), s)

    relay_back = lax.rem(place_in_run, 2)
    relay_column = lax.select(relay_back == 0, place_in_run // 2, (RUN - 1 - place_in_run) // 2)
    is_relay = ((relay_column == 1) & (s == 0)) | ((relay_column >= 2) & (s == 1))
    relay_half = lax.rem(relay_column, 2)
    relay_target_frame = f - place_in_run + relay_back * (RUN - 1)
    relay_source_frame = lax.rem(relay_target_frame + frames - 1 + 2 * relay_back, frames)
    relay_target, relay_source = (relay_target_frame, s), (relay_source_frame, s)

    def relay_in_run(d, column):
        return f - 2 * column if d == 0 else f + 2 * column

    barrier = pltpu.get_barrier_semaphore()

    def greet(device):
        pl.semaphore_signal(barrier, inc=1, device_id=device, device_id_type=MESH)

    for device in (partner, next_dev, prev_dev):
        greet(device)

    @pl.when(is_relay)
    def _():
        greet(relay_source)
        greet(relay_target)

    for d in range(2):
        for column in (1, 2, 3):
            @pl.when(edge[d] & (s == (0 if column == 1 else 1)))
            def _():
                greet(relay_of(d, column))
                greet((relay_in_run(d, column), s))

    at_end = (edge[0] | edge[1]).astype(jnp.int32)
    pl.semaphore_wait(barrier, 3 + 2 * is_relay.astype(jnp.int32) + at_end * (2 + 2 * s))

    def remote(src, dst, send, recv, device):
        return pltpu.make_async_remote_copy(
            src_ref=src, dst_ref=dst, send_sem=send, recv_sem=recv,
            device_id=device, device_id_type=MESH,
        )

    def columns(half, g):
        return pl.ds(pl.multiple_of(half * (GROUPS * LANES) + g * LANES, LANES), LANES)

    sources = (keys, values, queries, out_grad)

    def landing(g, a):
        lanes = pl.ds((a % 2) * LANES, LANES)
        if a < 2:
            return kv.at[g, pl.ds(FRAME + HALF * s, HALF), :, lanes]
        return qd.at[g, pl.ds(HALF * s, HALF), :, lanes]

    def swap(g, a):
        return remote(
            sources[a].at[:, :, columns(o, g)], landing(g, a), in_send.at[g, a], in_recv.at[g, a], partner
        )

    def keep(g, a):
        return pltpu.make_async_copy(sources[a].at[:, :, columns(s, g)], landing(g, a), in_local.at[g, a])

    neighbours = (next_dev, prev_dev)

    def start_part(d, part, src, dst, send, recv, phase, g):
        straight = remote(src, dst, send, recv, neighbours[d])
        if part == 0:
            bent = edge[d] & (s == 1)
        else:
            bent = edge[d]

        @pl.when(bent)
        def _():
            remote(
                src, relay.at[phase, g], send, relay_recv.at[phase, g], relay_of(d, part_column[part])
            ).start()

        @pl.when(jnp.logical_not(bent))
        def _():
            straight.start()

    def kv_window(g, base, half):
        return kv.at[g, pl.ds(base + HALF * half, HALF)]

    def pass_args(g, d, part):
        half = (s, o)[part]
        return (
            kv_window(g, FRAME, half), kv_window(g, (0, 2 * FRAME)[d], half),
            pass_send.at[g, d, half], pass_recv.at[g, d, half],
        )

    def start_pass(g, d, part):
        start_part(d, part, *pass_args(g, d, part), 0, g)

    def wait_pass(g, d, part):
        return remote(*pass_args(g, d, part), neighbours[d])

    def term_args(g, d, part):
        half = (s, o)[part]
        at = pl.ds(HALF * half, HALF)
        return (
            give.at[g, d, at], take.at[g, d, at], term_send.at[g, d, half], term_recv.at[g, d, half]
        )

    def start_terms(g, d, part):
        start_part(d, part, *term_args(g, d, part), 1, g)

    def wait_terms(g, d, part):
        return remote(*term_args(g, d, part), neighbours[d])

    def relay_on(g, phase):
        if phase == 0:
            target = kv_window(g, relay_back * (2 * FRAME), relay_half)
            recv = pass_recv.at[g, relay_back, relay_half]
        else:
            target = take.at[g, relay_back, pl.ds(HALF * relay_half, HALF)]
            recv = term_recv.at[g, relay_back, relay_half]
        return remote(relay.at[phase, g], target, relay_send.at[phase, g], recv, relay_target)

    def relay_step(g, phase):
        @pl.when(is_relay)
        def _():
            remote(
                relay.at[phase, g], relay.at[phase, g], relay_send.at[phase, g],
                relay_recv.at[phase, g], relay_target,
            ).wait_recv()
            relay_on(g, phase).start()

    def across(staged, targets, sends, recvs, g, a):
        return remote(
            staged.at[g, pl.ds(HALF * o, HALF), :, pl.ds(a * LANES, LANES)],
            targets[a].at[:, :, columns(s, g)], sends.at[g, a], recvs.at[g, a], partner,
        )

    def along(staged, targets, local, g, a):
        return pltpu.make_async_copy(
            staged.at[g, pl.ds(HALF * s, HALF), :, pl.ds(a * LANES, LANES)],
            targets[a].at[:, :, columns(s, g)], local.at[g, a],
        )

    row_targets, grad_targets = (query_grad, attended), (key_grad, value_grad)

    def rows_across(g, a):
        return across(rows_out, row_targets, row_send, row_recv, g, a)

    def rows_along(g, a):
        return along(rows_out, row_targets, row_local, g, a)

    def grads_across(g, a):
        return across(final, grad_targets, grad_send, grad_recv, g, a)

    def grads_along(g, a):
        return along(final, grad_targets, grad_local, g, a)

    share_meta = remote(meta_vm.at[s], meta_vm.at[s], meta_send, meta_recv, partner)

    def begin(g):
        for a in range(4):
            swap(g, a).start()

    def begin_own(g):
        for a in range(2):
            keep(g, a).wait()
        for d in range(2):
            start_pass(g, d, 0)

    begin(0)
    begin(1)

    def begin_keep(g, carry):
        for a in range(4):
            keep(g, a).start()
        return carry

    lax.fori_loop(0, GROUPS, begin_keep, 0)
    begin_own(0)
    begin_own(1)

    listed = block_list[...]
    row_at = lax.broadcasted_iota(jnp.int32, (HALF, LANES), 0)
    lane_at = lax.broadcasted_iota(jnp.int32, (HALF, LANES), 1)
    counts = jnp.zeros((HALF, LANES), jnp.int32)
    for row in range(HALF):
        counts = jnp.where(row_at == row, block_count[row], counts)
    edge_low = jnp.where(f > 0, 0, FRAME)
    edge_high = jnp.where(f < frames - 1, WINDOW, 2 * FRAME)
    usable = (listed >= edge_low) & (listed < edge_high) & (lane_at[:, :SEL] < counts[:, :SEL])
    slots = jnp.where(usable, listed, -1)
    place = jnp.full((HALF, LANES), SEL, jnp.int32)
    for j in range(SEL):
        place = jnp.where(lane_at - PLACE_AT == slots[:, j:j + 1], j, place)
    meta_vm[s, 0:HALF] = place
    meta_vm[s, 0:HALF, 0:SEL] = listed
    meta_vm[s, HALF:] = jnp.zeros((HALF, LANES), jnp.int32)
    meta_vm[s, HALF:, 0:SEL] = usable.astype(jnp.int32)
    share_meta.start()
    share_meta.wait()
    to_scalar = pltpu.make_async_copy(meta_vm, meta_sm, meta_local)
    to_scalar.start()
    to_scalar.wait()

    tiles[:, SEL] = jnp.zeros((FRAME, BLOCK, 2 * LANES), jnp.float32)

    def forward(g):
        for a in range(2):
            swap(g, a).wait_recv()
        for d in range(2):
            start_pass(g, d, 1)

    forward(0)
    begin(2)
    begin_own(2)
    relay_step(0, 0)
    forward(1)

    row_ids = lax.broadcasted_iota(jnp.int32, (4 * HD, 4 * HD), 0) // HD
    col_ids = lax.broadcasted_iota(jnp.int32, (4 * HD, 4 * HD), 1) // HD
    spread = jnp.where(
        row_ids == col_ids, jnp.where(col_ids < 2, FACTOR, 1.0), 0.0
    ).astype(jnp.bfloat16)
    first_head = lax.broadcasted_iota(jnp.int32, (BLOCK, LANES), 1) < HD

    def heads(full):
        return jnp.where(first_head, full[:HD], full[HD:])

    def fold(array, op):
        return op(array.reshape(array.shape[0] // 8, 8, LANES), axis=0)

    def attend(g, b):
        strip, row = b // HALF, lax.rem(b, HALF)
        part = qd[g, b]
        diagonal = jnp.concatenate([part] * 4, axis=0) * spread
        picked = jnp.concatenate(
            [work[meta_sm[strip, row, j]] for j in range(SEL)], axis=0
        )
        both = lax.dot_general(
            picked, diagonal, (((1,), (1,)), ((), ())), preferred_element_type=jnp.float32
        )
        bias = [
            jnp.where(meta_sm[strip, HALF + row, j] > 0, 0.0, MASKED).astype(jnp.float32)
            for j in range(SEL)
        ]
        parts = [both[j * BLOCK:(j + 1) * BLOCK, :LANES] for j in range(SEL)]
        peak = fold(parts[0], jnp.max) + bias[0]
        for j in range(1, SEL):
            peak = jnp.maximum(peak, fold(parts[j], jnp.max) + bias[j])
        peak = jnp.max(peak, axis=0, keepdims=True)
        powers = [jnp.exp(parts[j] - (peak - bias[j])) for j in range(SEL)]
        grad_weights = [both[j * BLOCK:(j + 1) * BLOCK, LANES:] for j in range(SEL)]
        total = fold(powers[0], jnp.sum)
        dots = fold(powers[0] * grad_weights[0], jnp.sum)
        for j in range(1, SEL):
            total = total + fold(powers[j], jnp.sum)
            dots = dots + fold(powers[j] * grad_weights[j], jnp.sum)
        scale = 1.0 / jnp.sum(total, axis=0, keepdims=True)
        row_dots = jnp.sum(dots, axis=0, keepdims=True) * scale
        slabs = []
        for j in range(SEL):
            weights = powers[j] * scale
            grad_scores = weights * (grad_weights[j] - row_dots)
            slabs.append(jnp.concatenate([grad_scores, weights], axis=1).astype(jnp.bfloat16))
        slab = jnp.concatenate(slabs, axis=0)
        terms = jnp.dot(slab, diagonal, preferred_element_type=jnp.float32)
        tiles[b, :SEL] = terms.reshape(SEL, BLOCK, 2 * LANES)
        mixed = lax.dot_general(
            slab, picked, (((0,), (0,)), ((), ())), preferred_element_type=jnp.float32
        )
        rows_out[g, b] = jnp.concatenate(
            [heads(mixed[:LANES, :LANES]) * FACTOR, heads(mixed[LANES:, LANES:])], axis=1
        ).astype(jnp.bfloat16)

    def finish(g):
        slot = lax.rem(g, 2)
        for d in range(2):
            for part in range(2):
                wait_terms(g, d, part).wait_recv()

        def add(w, carry):
            total = own[slot, w] + take[g, 0, w].astype(jnp.float32) + take[g, 1, w].astype(jnp.float32)
            final[g, w] = total.astype(jnp.bfloat16)
            return carry

        lax.fori_loop(0, FRAME, add, 0)
        for a in range(2):
            grads_across(g, a).start()
        for a in range(2):
            grads_along(g, a).start()

    def one_group(g, carry):
        for a in range(2, 4):
            keep(g, a).wait()
            swap(g, a).wait_recv()
        for d in range(2):
            for part in range(2):
                wait_pass(g, d, part).wait_recv()

        @pl.when(g + 3 < GROUPS)
        def _():
            begin(g + 3)
            begin_own(g + 3)

        work[...] = kv[g]

        def two_blocks(i, inner):
            b = lax.rem(HALF * o + 2 * i, FRAME)
            attend(g, b)
            attend(g, b + 1)

            @pl.when((i == 0) & (g > 1))
            def _():
                finish(g - 2)

            @pl.when((i == 0) & (g == 0))
            def _():
                relay_step(1, 0)

            @pl.when(i == 1)
            def _():
                for a in range(2):
                    rows_across(g, a).start()

                @pl.when(g + 2 < GROUPS)
                def _():
                    forward(g + 2)

            @pl.when((i == 2) & (g > 0))
            def _():
                relay_step(g - 1, 1)

            @pl.when((i == 3) & (g + 2 < GROUPS))
            def _():
                relay_step(g + 2, 0)

            return inner

        lax.fori_loop(0, FRAME // 2, two_blocks, 0)
        for a in range(2):
            rows_along(g, a).start()

        def gather(w, base):
            acc = None
            for b in range(FRAME):
                place = meta_sm[b // HALF, b % HALF, PLACE_AT + base + w]
                tile = tiles[b, place]
                acc = tile if acc is None else acc + tile
            return acc

        def collect(w, inner):
            give[g, 1, w] = gather(w, 0).astype(jnp.bfloat16)
            give[g, 0, w] = gather(w, 2 * FRAME).astype(jnp.bfloat16)
            return inner

        lax.fori_loop(0, FRAME, collect, 0)
        for d in range(2):
            for part in range(2):
                start_terms(g, d, part)

        def collect_own(w, inner):
            own[lax.rem(g, 2), w] = gather(w, FRAME)
            return inner

        lax.fori_loop(0, FRAME, collect_own, 0)

        return carry

    lax.fori_loop(0, GROUPS, one_group, 0)
    finish(GROUPS - 2)
    relay_step(GROUPS - 1, 1)
    finish(GROUPS - 1)

    def drain(g, carry):
        for a in range(4):
            swap(g, a).wait_send()
        for d in range(2):
            for part in range(2):
                wait_pass(g, d, part).wait_send()
                wait_terms(g, d, part).wait_send()

        @pl.when(is_relay)
        def _():
            for phase in range(2):
                relay_on(g, phase).wait_send()

        for a in range(2):
            rows_across(g, a).wait()
            rows_along(g, a).wait()
            grads_across(g, a).wait()
            grads_along(g, a).wait()
        return carry

    lax.fori_loop(0, GROUPS, drain, 0)


def hand_over(*refs):
    sources, targets, sems = refs[:4], refs[4:8], refs[8]
    copies = [
        pltpu.make_async_copy(src.at[pl.ds(at * 2, 2)], dst.at[pl.ds(at * 2, 2)], sems.at[i, at])
        for i, (src, dst) in enumerate(zip(sources, targets))
        for at in range(2)
    ]
    for copy in copies:
        copy.start()
    for copy in copies:
        copy.wait()


def body(queries, keys, values, out_grad, block_list, block_count):
    rows, width = queries.shape
    frames = lax.axis_size("frames")
    blocked = [x.reshape(HALF, BLOCK, width) for x in (queries, keys, values, out_grad)]
    shape = jax.ShapeDtypeStruct((HALF, BLOCK, width), jnp.bfloat16)
    dma = pltpu.SemaphoreType.DMA
    flops = 6 * 2 * FRAME * SEL * BLOCK * 256 * 256 * GROUPS
    outs = pl.pallas_call(
        lambda *refs: kernel(frames, *refs),
        out_shape=[shape] * 4,
        in_specs=[pl.BlockSpec(memory_space=pltpu.VMEM), pl.BlockSpec(memory_space=pltpu.SMEM)] + [pl.BlockSpec(memory_space=pl.ANY)] * 4,
        out_specs=[pl.BlockSpec(memory_space=pl.ANY)] * 4,
        scratch_shapes=[
            pltpu.VMEM((GROUPS, WINDOW, BLOCK, 2 * LANES), jnp.bfloat16),
            pltpu.VMEM((GROUPS, FRAME, BLOCK, 2 * LANES), jnp.bfloat16),
            pltpu.VMEM((WINDOW, BLOCK, 2 * LANES), jnp.bfloat16),
            pltpu.VMEM((FRAME, SEL + 1, BLOCK, 2 * LANES), jnp.float32),
            pltpu.VMEM((GROUPS, FRAME, BLOCK, 2 * LANES), jnp.bfloat16),
            pltpu.VMEM((GROUPS, 2, FRAME, BLOCK, 2 * LANES), jnp.bfloat16),
            pltpu.VMEM((GROUPS, 2, FRAME, BLOCK, 2 * LANES), jnp.bfloat16),
            pltpu.VMEM((2, FRAME, BLOCK, 2 * LANES), jnp.float32),
            pltpu.VMEM((GROUPS, FRAME, BLOCK, 2 * LANES), jnp.bfloat16),
            pltpu.VMEM((2, GROUPS, HALF, BLOCK, 2 * LANES), jnp.bfloat16),
            pltpu.VMEM((2, 8, LANES), jnp.int32),
            pltpu.SMEM((2, 8, LANES), jnp.int32),
            dma((GROUPS, 4)), dma((GROUPS, 4)), dma((GROUPS, 4)),
            dma((GROUPS, 2, 2)), dma((GROUPS, 2, 2)),
            dma, dma, dma,
            dma((GROUPS, 2)), dma((GROUPS, 2)), dma((GROUPS, 2)),
            dma((GROUPS, 2, 2)), dma((GROUPS, 2, 2)),
            dma((GROUPS, 2)), dma((GROUPS, 2)), dma((GROUPS, 2)),
            dma((2, GROUPS)), dma((2, GROUPS)),
        ],
        cost_estimate=pl.CostEstimate(
            flops=flops, bytes_accessed=16 * rows * width, transcendentals=FRAME * SEL * BLOCK * LANES * GROUPS
        ),
        compiler_params=pltpu.CompilerParams(
            collective_id=0, has_side_effects=True, vmem_limit_bytes=60 * 1024 * 1024
        ),
    )(block_list, block_count, *blocked)
    outs = pl.pallas_call(
        hand_over,
        out_shape=[shape] * 4,
        in_specs=[pl.BlockSpec(memory_space=pltpu.VMEM)] * 4,
        out_specs=[pl.BlockSpec(memory_space=pl.ANY)] * 4,
        scratch_shapes=[dma((4, 2))],
        compiler_params=pltpu.CompilerParams(vmem_limit_bytes=60 * 1024 * 1024),
    )(*outs)
    return tuple(x.reshape(rows, width) for x in outs)


def solution(mesh):
    split = P(("frames", "strip"), None)
    in_specs = (split, split, split, split, split, P(("frames", "strip")))
    return jax.shard_map(
        body, mesh=mesh, in_specs=in_specs, out_specs=(split,) * 4, check_vma=False
    )
```

```python
import jax
import jax.numpy as jnp
from jax import lax
from jax.experimental import pallas as pl
from jax.experimental.pallas import tpu as pltpu
from jax.sharding import PartitionSpec as P

HD = 64
BLOCK = 64
SEL = 13
HALF = 4
FRAME = 8
WINDOW = 24
GROUPS = 4
LANES = 128
FACTOR = 0.125
MASKED = -1e30
PLACE_AT = 32
RUN = 8
MESH = pl.DeviceIdType.MESH


def kernel(
    frames,
    block_list, block_count, queries, keys, values, out_grad,
    attended, query_grad, key_grad, value_grad,
    loaded, packed, kv, qd, work, tiles, rows_out, rows_in, give, take, own, final, final_in, relay, meta_vm, meta_sm,
    load_sem, in_send, in_recv, pass_send, pass_recv,
    meta_send, meta_recv, meta_local, row_send, row_recv, row_local,
    term_send, term_recv, grad_send, grad_recv, grad_local, relay_send, relay_recv,
):
    f, s = lax.axis_index("frames"), lax.axis_index("strip")
    o = 1 - s
    after, before = lax.rem(f + 1, frames), lax.rem(f + frames - 1, frames)
    partner, next_dev, prev_dev = (f, o), (after, s), (before, s)

    sources = (keys, values, queries, out_grad)
    loads = [pltpu.make_async_copy(sources[a], loaded.at[a], load_sem.at[a]) for a in range(4)]
    for load in loads:
        load.start()

    place_in_run = lax.rem(f, RUN)
    edge = (place_in_run == RUN - 1, place_in_run == 0)
    part_column = (3 * s, 1 + s)

    def relay_of(d, column):
        if d == 0:
            return (lax.rem(f + 1 + 2 * column, frames), s)
        return (lax.rem(f + frames - 1 - 2 * column, frames), s)

    relay_back = lax.rem(place_in_run, 2)
    relay_column = lax.select(relay_back == 0, place_in_run // 2, (RUN - 1 - place_in_run) // 2)
    is_relay = ((relay_column == 1) & (s == 0)) | ((relay_column >= 2) & (s == 1))
    relay_half = lax.rem(relay_column, 2)
    relay_target_frame = f - place_in_run + relay_back * (RUN - 1)
    relay_source_frame = lax.rem(relay_target_frame + frames - 1 + 2 * relay_back, frames)
    relay_target, relay_source = (relay_target_frame, s), (relay_source_frame, s)

    def relay_in_run(d, column):
        return f - 2 * column if d == 0 else f + 2 * column

    barrier = pltpu.get_barrier_semaphore()

    def greet(device):
        pl.semaphore_signal(barrier, inc=1, device_id=device, device_id_type=MESH)

    for device in (partner, next_dev, prev_dev):
        greet(device)

    @pl.when(is_relay)
    def _():
        greet(relay_source)
        greet(relay_target)

    for d in range(2):
        for column in (1, 2, 3):
            @pl.when(edge[d] & (s == (0 if column == 1 else 1)))
            def _():
                greet(relay_of(d, column))
                greet((relay_in_run(d, column), s))

    at_end = (edge[0] | edge[1]).astype(jnp.int32)
    pl.semaphore_wait(barrier, 3 + 2 * is_relay.astype(jnp.int32) + at_end * (2 + 2 * s))

    def remote(src, dst, send, recv, device):
        return pltpu.make_async_remote_copy(
            src_ref=src, dst_ref=dst, send_sem=send, recv_sem=recv,
            device_id=device, device_id_type=MESH,
        )

    def columns(half, g):
        return pl.ds(pl.multiple_of(half * (GROUPS * LANES) + g * LANES, LANES), LANES)

    def landing(g, pair, half):
        if pair == 0:
            return kv.at[g, pl.ds(FRAME + HALF * half, HALF)]
        return qd.at[g, pl.ds(HALF * half, HALF)]

    def swap(g, pair):
        return remote(
            packed.at[g, pair], landing(g, pair, s), in_send.at[g, pair], in_recv.at[g, pair], partner
        )

    def pack(g, pair):
        for a in range(2):
            lanes = slice(a * LANES, (a + 1) * LANES)
            packed[g, pair, :, :, lanes] = loaded[2 * pair + a, :, :, columns(o, g)]

    def keep(g, pair):
        own_rows = landing(g, pair, s)
        for a in range(2):
            lanes = slice(a * LANES, (a + 1) * LANES)
            own_rows[:, :, lanes] = loaded[2 * pair + a, :, :, columns(s, g)]

    neighbours = (next_dev, prev_dev)

    def start_part(d, part, src, dst, send, recv, phase, g):
        straight = remote(src, dst, send, recv, neighbours[d])
        if part == 0:
            bent = edge[d] & (s == 1)
        else:
            bent = edge[d]

        @pl.when(bent)
        def _():
            remote(
                src, relay.at[phase, g], send, relay_recv.at[phase, g], relay_of(d, part_column[part])
            ).start()

        @pl.when(jnp.logical_not(bent))
        def _():
            straight.start()

    def kv_window(g, base, half):
        return kv.at[g, pl.ds(base + HALF * half, HALF)]

    def pass_args(g, d, part):
        half = (s, o)[part]
        return (
            kv_window(g, FRAME, half), kv_window(g, (0, 2 * FRAME)[d], half),
            pass_send.at[g, d, half], pass_recv.at[g, d, half],
        )

    def start_pass(g, d, part):
        start_part(d, part, *pass_args(g, d, part), 0, g)

    def wait_pass(g, d, part):
        return remote(*pass_args(g, d, part), neighbours[d])

    def term_args(g, d, part):
        half = (s, o)[part]
        at = pl.ds(HALF * half, HALF)
        return (
            give.at[g, d, at], take.at[g, d, at], term_send.at[g, d, half], term_recv.at[g, d, half]
        )

    def start_terms(g, d, part):
        start_part(d, part, *term_args(g, d, part), 1, g)

    def wait_terms(g, d, part):
        return remote(*term_args(g, d, part), neighbours[d])

    def relay_on(g, phase):
        if phase == 0:
            target = kv_window(g, relay_back * (2 * FRAME), relay_half)
            recv = pass_recv.at[g, relay_back, relay_half]
        else:
            target = take.at[g, relay_back, pl.ds(HALF * relay_half, HALF)]
            recv = term_recv.at[g, relay_back, relay_half]
        return remote(relay.at[phase, g], target, relay_send.at[phase, g], recv, relay_target)

    def relay_step(g, phase):
        @pl.when(is_relay)
        def _():
            remote(
                relay.at[phase, g], relay.at[phase, g], relay_send.at[phase, g],
                relay_recv.at[phase, g], relay_target,
            ).wait_recv()
            relay_on(g, phase).start()

    def rows_across(g):
        return remote(
            rows_out.at[g, pl.ds(HALF * o, HALF)], rows_in.at[g], row_send.at[g], row_recv.at[g], partner
        )

    def grads_across(g):
        return remote(
            final.at[g, pl.ds(HALF * o, HALF)], final_in.at[g], grad_send.at[g], grad_recv.at[g], partner
        )

    row_targets, grad_targets = (query_grad, attended), (key_grad, value_grad)

    def place_copy(staged, targets, local, g, half, a):
        return pltpu.make_async_copy(
            staged.at[:, :, pl.ds(a * LANES, LANES)], targets[a].at[:, :, columns(half, g)], local.at[g, a]
        )

    def rows_along(g, a):
        return place_copy(rows_out.at[g, pl.ds(HALF * s, HALF)], row_targets, row_local, g, s, a)

    def grads_along(g, a):
        return place_copy(final.at[g, pl.ds(HALF * s, HALF)], grad_targets, grad_local, g, s, a)

    def rows_back(g, a):
        return place_copy(rows_in.at[g], row_targets, row_local.at[pl.ds(GROUPS, GROUPS)], g, o, a)

    def grads_back(g, a):
        return place_copy(final_in.at[g], grad_targets, grad_local.at[pl.ds(GROUPS, GROUPS)], g, o, a)

    share_meta = remote(meta_vm.at[s], meta_vm.at[s], meta_send, meta_recv, partner)

    def begin(g):
        for pair in range(2):
            pack(g, pair)
            swap(g, pair).start()

    def begin_own(g):
        keep(g, 0)
        for d in range(2):
            start_pass(g, d, 0)
        keep(g, 1)

    for load in loads:
        load.wait()
    begin(0)
    begin_own(0)
    begin(1)
    begin_own(1)

    listed = block_list[...]
    row_at = lax.broadcasted_iota(jnp.int32, (HALF, LANES), 0)
    lane_at = lax.broadcasted_iota(jnp.int32, (HALF, LANES), 1)
    counts = jnp.zeros((HALF, LANES), jnp.int32)
    for row in range(HALF):
        counts = jnp.where(row_at == row, block_count[row], counts)
    edge_low = jnp.where(f > 0, 0, FRAME)
    edge_high = jnp.where(f < frames - 1, WINDOW, 2 * FRAME)
    usable = (listed >= edge_low) & (listed < edge_high) & (lane_at[:, :SEL] < counts[:, :SEL])
    slots = jnp.where(usable, listed, -1)
    place = jnp.full((HALF, LANES), SEL, jnp.int32)
    for j in range(SEL):
        place = jnp.where(lane_at - PLACE_AT == slots[:, j:j + 1], j, place)
    meta_vm[s, 0:HALF] = place
    meta_vm[s, 0:HALF, 0:SEL] = listed
    meta_vm[s, HALF:] = jnp.zeros((HALF, LANES), jnp.int32)
    meta_vm[s, HALF:, 0:SEL] = usable.astype(jnp.int32)
    share_meta.start()
    share_meta.wait()
    to_scalar = pltpu.make_async_copy(meta_vm, meta_sm, meta_local)
    to_scalar.start()
    to_scalar.wait()

    tiles[:, SEL] = jnp.zeros((FRAME, BLOCK, 2 * LANES), jnp.float32)

    def forward(g):
        swap(g, 0).wait_recv()
        for d in range(2):
            start_pass(g, d, 1)

    forward(0)
    begin(2)
    begin_own(2)
    relay_step(0, 0)
    forward(1)

    row_ids = lax.broadcasted_iota(jnp.int32, (4 * HD, 4 * HD), 0) // HD
    col_ids = lax.broadcasted_iota(jnp.int32, (4 * HD, 4 * HD), 1) // HD
    spread = jnp.where(
        row_ids == col_ids, jnp.where(col_ids < 2, FACTOR, 1.0), 0.0
    ).astype(jnp.bfloat16)
    first_head = lax.broadcasted_iota(jnp.int32, (BLOCK, LANES), 1) < HD

    def heads(full):
        return jnp.where(first_head, full[:HD], full[HD:])

    def fold(array, op):
        return op(array.reshape(array.shape[0] // 8, 8, LANES), axis=0)

    def attend(g, b):
        strip, row = b // HALF, lax.rem(b, HALF)
        part = qd[g, b]
        diagonal = jnp.concatenate([part] * 4, axis=0) * spread
        picked = jnp.concatenate(
            [work[meta_sm[strip, row, j]] for j in range(SEL)], axis=0
        )
        both = lax.dot_general(
            picked, diagonal, (((1,), (1,)), ((), ())), preferred_element_type=jnp.float32
        )
        bias = [
            jnp.where(meta_sm[strip, HALF + row, j] > 0, 0.0, MASKED).astype(jnp.float32)
            for j in range(SEL)
        ]
        parts = [both[j * BLOCK:(j + 1) * BLOCK, :LANES] for j in range(SEL)]
        peak = fold(parts[0], jnp.max) + bias[0]
        for j in range(1, SEL):
            peak = jnp.maximum(peak, fold(parts[j], jnp.max) + bias[j])
        peak = jnp.max(peak, axis=0, keepdims=True)
        powers = [jnp.exp(parts[j] - (peak - bias[j])) for j in range(SEL)]
        grad_weights = [both[j * BLOCK:(j + 1) * BLOCK, LANES:] for j in range(SEL)]
        total = fold(powers[0], jnp.sum)
        dots = fold(powers[0] * grad_weights[0], jnp.sum)
        for j in range(1, SEL):
            total = total + fold(powers[j], jnp.sum)
            dots = dots + fold(powers[j] * grad_weights[j], jnp.sum)
        scale = 1.0 / jnp.sum(total, axis=0, keepdims=True)
        row_dots = jnp.sum(dots, axis=0, keepdims=True) * scale
        slabs = []
        for j in range(SEL):
            weights = powers[j] * scale
            grad_scores = weights * (grad_weights[j] - row_dots)
            slabs.append(jnp.concatenate([grad_scores, weights], axis=1).astype(jnp.bfloat16))
        slab = jnp.concatenate(slabs, axis=0)
        terms = jnp.dot(slab, diagonal, preferred_element_type=jnp.float32)
        tiles[b, :SEL] = terms.reshape(SEL, BLOCK, 2 * LANES)
        mixed = lax.dot_general(
            slab, picked, (((0,), (0,)), ((), ())), preferred_element_type=jnp.float32
        )
        rows_out[g, b] = jnp.concatenate(
            [heads(mixed[:LANES, :LANES]) * FACTOR, heads(mixed[LANES:, LANES:])], axis=1
        ).astype(jnp.bfloat16)

    def finish(g):
        slot = lax.rem(g, 2)
        for d in range(2):
            for part in range(2):
                wait_terms(g, d, part).wait_recv()

        def add(w, carry):
            total = own[slot, w] + take[g, 0, w].astype(jnp.float32) + take[g, 1, w].astype(jnp.float32)
            final[g, w] = total.astype(jnp.bfloat16)
            return carry

        lax.fori_loop(0, FRAME, add, 0)
        grads_across(g).start()
        for a in range(2):
            grads_along(g, a).start()

    def one_group(g, carry):
        swap(g, 1).wait_recv()
        for d in range(2):
            for part in range(2):
                wait_pass(g, d, part).wait_recv()

        @pl.when(g + 3 < GROUPS)
        def _():
            begin(g + 3)
            begin_own(g + 3)

        work[...] = kv[g]

        def two_blocks(i, inner):
            b = lax.rem(HALF * o + 2 * i, FRAME)
            attend(g, b)
            attend(g, b + 1)

            @pl.when((i == 0) & (g > 1))
            def _():
                finish(g - 2)

            @pl.when((i == 0) & (g == 0))
            def _():
                relay_step(1, 0)

            @pl.when(i == 1)
            def _():
                rows_across(g).start()

                @pl.when(g + 2 < GROUPS)
                def _():
                    forward(g + 2)

            @pl.when((i == 2) & (g > 0))
            def _():
                relay_step(g - 1, 1)

            @pl.when((i == 3) & (g + 2 < GROUPS))
            def _():
                relay_step(g + 2, 0)

            return inner

        lax.fori_loop(0, FRAME // 2, two_blocks, 0)
        for a in range(2):
            rows_along(g, a).start()

        def gather(w, base):
            acc = None
            for b in range(FRAME):
                place = meta_sm[b // HALF, b % HALF, PLACE_AT + base + w]
                tile = tiles[b, place]
                acc = tile if acc is None else acc + tile
            return acc

        def collect(w, inner):
            give[g, 1, w] = gather(w, 0).astype(jnp.bfloat16)
            give[g, 0, w] = gather(w, 2 * FRAME).astype(jnp.bfloat16)
            return inner

        lax.fori_loop(0, FRAME, collect, 0)
        for d in range(2):
            for part in range(2):
                start_terms(g, d, part)

        def collect_own(w, inner):
            own[lax.rem(g, 2), w] = gather(w, FRAME)
            return inner

        lax.fori_loop(0, FRAME, collect_own, 0)

        return carry

    lax.fori_loop(0, GROUPS, one_group, 0)
    finish(GROUPS - 2)
    relay_step(GROUPS - 1, 1)
    finish(GROUPS - 1)

    def land(g, carry):
        rows_across(g).wait_recv()
        for a in range(2):
            rows_back(g, a).start()
        grads_across(g).wait_recv()
        for a in range(2):
            grads_back(g, a).start()
        return carry

    lax.fori_loop(0, GROUPS, land, 0)

    def drain(g, carry):
        for pair in range(2):
            swap(g, pair).wait_send()
        for d in range(2):
            for part in range(2):
                wait_pass(g, d, part).wait_send()
                wait_terms(g, d, part).wait_send()

        @pl.when(is_relay)
        def _():
            for phase in range(2):
                relay_on(g, phase).wait_send()

        rows_across(g).wait_send()
        grads_across(g).wait_send()
        for a in range(2):
            rows_along(g, a).wait()
            grads_along(g, a).wait()
            rows_back(g, a).wait()
            grads_back(g, a).wait()
        return carry

    lax.fori_loop(0, GROUPS, drain, 0)


def hand_over(*refs):
    sources, targets, sems = refs[:4], refs[4:8], refs[8]
    copies = [
        pltpu.make_async_copy(src.at[pl.ds(at * 2, 2)], dst.at[pl.ds(at * 2, 2)], sems.at[i, at])
        for i, (src, dst) in enumerate(zip(sources, targets))
        for at in range(2)
    ]
    for copy in copies:
        copy.start()
    for copy in copies:
        copy.wait()


def body(queries, keys, values, out_grad, block_list, block_count):
    rows, width = queries.shape
    frames = lax.axis_size("frames")
    blocked = [x.reshape(HALF, BLOCK, width) for x in (queries, keys, values, out_grad)]
    shape = jax.ShapeDtypeStruct((HALF, BLOCK, width), jnp.bfloat16)
    dma = pltpu.SemaphoreType.DMA
    flops = 6 * 2 * FRAME * SEL * BLOCK * 256 * 256 * GROUPS
    outs = pl.pallas_call(
        lambda *refs: kernel(frames, *refs),
        out_shape=[shape] * 4,
        in_specs=[pl.BlockSpec(memory_space=pltpu.VMEM), pl.BlockSpec(memory_space=pltpu.SMEM)] + [pl.BlockSpec(memory_space=pl.ANY)] * 4,
        out_specs=[pl.BlockSpec(memory_space=pl.ANY)] * 4,
        scratch_shapes=[
            pltpu.VMEM((4, HALF, BLOCK, width), jnp.bfloat16),
            pltpu.VMEM((GROUPS, 2, HALF, BLOCK, 2 * LANES), jnp.bfloat16),
            pltpu.VMEM((GROUPS, WINDOW, BLOCK, 2 * LANES), jnp.bfloat16),
            pltpu.VMEM((GROUPS, FRAME, BLOCK, 2 * LANES), jnp.bfloat16),
            pltpu.VMEM((WINDOW, BLOCK, 2 * LANES), jnp.bfloat16),
            pltpu.VMEM((FRAME, SEL + 1, BLOCK, 2 * LANES), jnp.float32),
            pltpu.VMEM((GROUPS, FRAME, BLOCK, 2 * LANES), jnp.bfloat16),
            pltpu.VMEM((GROUPS, HALF, BLOCK, 2 * LANES), jnp.bfloat16),
            pltpu.VMEM((GROUPS, 2, FRAME, BLOCK, 2 * LANES), jnp.bfloat16),
            pltpu.VMEM((GROUPS, 2, FRAME, BLOCK, 2 * LANES), jnp.bfloat16),
            pltpu.VMEM((2, FRAME, BLOCK, 2 * LANES), jnp.float32),
            pltpu.VMEM((GROUPS, FRAME, BLOCK, 2 * LANES), jnp.bfloat16),
            pltpu.VMEM((GROUPS, HALF, BLOCK, 2 * LANES), jnp.bfloat16),
            pltpu.VMEM((2, GROUPS, HALF, BLOCK, 2 * LANES), jnp.bfloat16),
            pltpu.VMEM((2, 8, LANES), jnp.int32),
            pltpu.SMEM((2, 8, LANES), jnp.int32),
            dma((4,)), dma((GROUPS, 2)), dma((GROUPS, 2)),
            dma((GROUPS, 2, 2)), dma((GROUPS, 2, 2)),
            dma, dma, dma,
            dma((GROUPS,)), dma((GROUPS,)), dma((2 * GROUPS, 2)),
            dma((GROUPS, 2, 2)), dma((GROUPS, 2, 2)),
            dma((GROUPS,)), dma((GROUPS,)), dma((2 * GROUPS, 2)),
            dma((2, GROUPS)), dma((2, GROUPS)),
        ],
        cost_estimate=pl.CostEstimate(
            flops=flops, bytes_accessed=16 * rows * width, transcendentals=FRAME * SEL * BLOCK * LANES * GROUPS
        ),
        compiler_params=pltpu.CompilerParams(
            collective_id=0, has_side_effects=True, vmem_limit_bytes=60 * 1024 * 1024
        ),
    )(block_list, block_count, *blocked)
    outs = pl.pallas_call(
        hand_over,
        out_shape=[shape] * 4,
        in_specs=[pl.BlockSpec(memory_space=pltpu.VMEM)] * 4,
        out_specs=[pl.BlockSpec(memory_space=pl.ANY)] * 4,
        scratch_shapes=[dma((4, 2))],
        compiler_params=pltpu.CompilerParams(vmem_limit_bytes=60 * 1024 * 1024),
    )(*outs)
    return tuple(x.reshape(rows, width) for x in outs)


def solution(mesh):
    split = P(("frames", "strip"), None)
    in_specs = (split, split, split, split, split, P(("frames", "strip")))
    return jax.shard_map(
        body, mesh=mesh, in_specs=in_specs, out_specs=(split,) * 4, check_vma=False
    )
```

```python
import jax
import jax.numpy as jnp
from jax import lax
from jax.experimental import pallas as pl
from jax.experimental.pallas import tpu as pltpu
from jax.sharding import PartitionSpec as P

HD = 64
BLOCK = 64
SEL = 13
HALF = 4
FRAME = 8
WINDOW = 24
GROUPS = 4
LANES = 128
FACTOR = 0.125
MASKED = -1e30
PLACE_AT = 32
RUN = 8
MESH = pl.DeviceIdType.MESH


def kernel(
    frames,
    block_list, block_count, queries, keys, values, out_grad,
    attended, query_grad, key_grad, value_grad,
    loaded, packed, kv, qd, work, tiles, rows_out, rows_in, give, take, own, final, final_in, relay, meta_vm, meta_sm,
    load_sem, in_send, in_recv, pass_send, pass_recv,
    meta_send, meta_recv, meta_local, row_send, row_recv, row_local,
    term_send, term_recv, grad_send, grad_recv, grad_local, relay_send, relay_recv,
):
    f, s = lax.axis_index("frames"), lax.axis_index("strip")
    o = 1 - s
    after, before = lax.rem(f + 1, frames), lax.rem(f + frames - 1, frames)
    partner, next_dev, prev_dev = (f, o), (after, s), (before, s)

    sources = (keys, values, queries, out_grad)
    loads = [pltpu.make_async_copy(sources[a], loaded.at[a], load_sem.at[a]) for a in range(4)]
    for load in loads:
        load.start()

    place_in_run = lax.rem(f, RUN)
    edge = (place_in_run == RUN - 1, place_in_run == 0)
    part_column = (3 * s, 1 + s)

    def relay_of(d, column):
        return (f - 2 * column if d == 0 else f + 2 * column, s)

    def relay_to(d, column):
        if d == 0:
            return (lax.rem(f + 1 + 2 * column, frames), s)
        return (lax.rem(f + frames - 1 - 2 * column, frames), s)

    relay_back = 1 - lax.rem(place_in_run, 2)
    relay_column = lax.select(relay_back == 0, (RUN - 1 - place_in_run) // 2, place_in_run // 2)
    is_relay = ((relay_column == 1) & (s == 0)) | ((relay_column >= 2) & (s == 1))
    relay_half = lax.rem(relay_column, 2)
    relay_source_frame = f - place_in_run + (1 - relay_back) * (RUN - 1)
    relay_target_frame = lax.rem(relay_source_frame + frames + 1 - 2 * relay_back, frames)
    relay_target, relay_source = (relay_target_frame, s), (relay_source_frame, s)

    barrier = pltpu.get_barrier_semaphore()

    def greet(device):
        pl.semaphore_signal(barrier, inc=1, device_id=device, device_id_type=MESH)

    for device in (partner, next_dev, prev_dev):
        greet(device)

    @pl.when(is_relay)
    def _():
        greet(relay_source)
        greet(relay_target)

    for d in range(2):
        for column in (1, 2, 3):
            @pl.when(edge[d] & (s == (0 if column == 1 else 1)))
            def _():
                greet(relay_of(d, column))
                greet(relay_to(d, column))

    at_end = (edge[0] | edge[1]).astype(jnp.int32)
    pl.semaphore_wait(barrier, 3 + 2 * is_relay.astype(jnp.int32) + at_end * (2 + 2 * s))

    def remote(src, dst, send, recv, device):
        return pltpu.make_async_remote_copy(
            src_ref=src, dst_ref=dst, send_sem=send, recv_sem=recv,
            device_id=device, device_id_type=MESH,
        )

    def columns(half, g):
        return pl.ds(pl.multiple_of(half * (GROUPS * LANES) + g * LANES, LANES), LANES)

    def landing(g, pair, half):
        if pair == 0:
            return kv.at[g, pl.ds(FRAME + HALF * half, HALF)]
        return qd.at[g, pl.ds(HALF * half, HALF)]

    def swap(g, pair):
        return remote(
            packed.at[g, pair], landing(g, pair, s), in_send.at[g, pair], in_recv.at[g, pair], partner
        )

    def pack(g, pair):
        for a in range(2):
            lanes = slice(a * LANES, (a + 1) * LANES)
            packed[g, pair, :, :, lanes] = loaded[2 * pair + a, :, :, columns(o, g)]

    def keep(g, pair):
        own_rows = landing(g, pair, s)
        for a in range(2):
            lanes = slice(a * LANES, (a + 1) * LANES)
            own_rows[:, :, lanes] = loaded[2 * pair + a, :, :, columns(s, g)]

    neighbours = (next_dev, prev_dev)

    def start_part(d, part, src, dst, send, recv, phase, g):
        straight = remote(src, dst, send, recv, neighbours[d])
        if part == 0:
            bent = edge[d] & (s == 1)
        else:
            bent = edge[d]

        @pl.when(bent)
        def _():
            remote(
                src, relay.at[phase, g], send, relay_recv.at[phase, g], relay_of(d, part_column[part])
            ).start()

        @pl.when(jnp.logical_not(bent))
        def _():
            straight.start()

    def kv_window(g, base, half):
        return kv.at[g, pl.ds(base + HALF * half, HALF)]

    def pass_args(g, d, part):
        half = (s, o)[part]
        return (
            kv_window(g, FRAME, half), kv_window(g, (0, 2 * FRAME)[d], half),
            pass_send.at[g, d, half], pass_recv.at[g, d, half],
        )

    def start_pass(g, d, part):
        start_part(d, part, *pass_args(g, d, part), 0, g)

    def wait_pass(g, d, part):
        return remote(*pass_args(g, d, part), neighbours[d])

    def term_args(g, d, part):
        half = (s, o)[part]
        at = pl.ds(HALF * half, HALF)
        return (
            give.at[g, d, at], take.at[g, d, at], term_send.at[g, d, half], term_recv.at[g, d, half]
        )

    def start_terms(g, d, part):
        start_part(d, part, *term_args(g, d, part), 1, g)

    def wait_terms(g, d, part):
        return remote(*term_args(g, d, part), neighbours[d])

    def relay_on(g, phase):
        if phase == 0:
            target = kv_window(g, relay_back * (2 * FRAME), relay_half)
            recv = pass_recv.at[g, relay_back, relay_half]
        else:
            target = take.at[g, relay_back, pl.ds(HALF * relay_half, HALF)]
            recv = term_recv.at[g, relay_back, relay_half]
        return remote(relay.at[phase, g], target, relay_send.at[phase, g], recv, relay_target)

    def relay_step(g, phase):
        @pl.when(is_relay)
        def _():
            remote(
                relay.at[phase, g], relay.at[phase, g], relay_send.at[phase, g],
                relay_recv.at[phase, g], relay_target,
            ).wait_recv()
            relay_on(g, phase).start()

    def rows_across(g):
        return remote(
            rows_out.at[g, pl.ds(HALF * o, HALF)], rows_in.at[g], row_send.at[g], row_recv.at[g], partner
        )

    def grads_across(g):
        return remote(
            final.at[g, pl.ds(HALF * o, HALF)], final_in.at[g], grad_send.at[g], grad_recv.at[g], partner
        )

    row_targets, grad_targets = (query_grad, attended), (key_grad, value_grad)

    def place_copy(staged, targets, local, g, half, a):
        return pltpu.make_async_copy(
            staged.at[:, :, pl.ds(a * LANES, LANES)], targets[a].at[:, :, columns(half, g)], local.at[g, a]
        )

    def rows_along(g, a):
        return place_copy(rows_out.at[g, pl.ds(HALF * s, HALF)], row_targets, row_local, g, s, a)

    def grads_along(g, a):
        return place_copy(final.at[g, pl.ds(HALF * s, HALF)], grad_targets, grad_local, g, s, a)

    def rows_back(g, a):
        return place_copy(rows_in.at[g], row_targets, row_local.at[pl.ds(GROUPS, GROUPS)], g, o, a)

    def grads_back(g, a):
        return place_copy(final_in.at[g], grad_targets, grad_local.at[pl.ds(GROUPS, GROUPS)], g, o, a)

    share_meta = remote(meta_vm.at[s], meta_vm.at[s], meta_send, meta_recv, partner)

    def begin(g):
        for pair in range(2):
            pack(g, pair)
            swap(g, pair).start()

    def begin_own(g):
        keep(g, 0)
        for d in range(2):
            start_pass(g, d, 0)
        keep(g, 1)

    for load in loads:
        load.wait()
    begin(0)
    begin_own(0)
    begin(1)
    begin_own(1)

    listed = block_list[...]
    row_at = lax.broadcasted_iota(jnp.int32, (HALF, LANES), 0)
    lane_at = lax.broadcasted_iota(jnp.int32, (HALF, LANES), 1)
    counts = jnp.zeros((HALF, LANES), jnp.int32)
    for row in range(HALF):
        counts = jnp.where(row_at == row, block_count[row], counts)
    edge_low = jnp.where(f > 0, 0, FRAME)
    edge_high = jnp.where(f < frames - 1, WINDOW, 2 * FRAME)
    usable = (listed >= edge_low) & (listed < edge_high) & (lane_at[:, :SEL] < counts[:, :SEL])
    slots = jnp.where(usable, listed, -1)
    place = jnp.full((HALF, LANES), SEL, jnp.int32)
    for j in range(SEL):
        place = jnp.where(lane_at - PLACE_AT == slots[:, j:j + 1], j, place)
    meta_vm[s, 0:HALF] = place
    meta_vm[s, 0:HALF, 0:SEL] = listed
    meta_vm[s, HALF:] = jnp.zeros((HALF, LANES), jnp.int32)
    meta_vm[s, HALF:, 0:SEL] = usable.astype(jnp.int32)
    share_meta.start()
    share_meta.wait()
    to_scalar = pltpu.make_async_copy(meta_vm, meta_sm, meta_local)
    to_scalar.start()
    to_scalar.wait()

    tiles[:, SEL] = jnp.zeros((FRAME, BLOCK, 2 * LANES), jnp.float32)

    def forward(g):
        swap(g, 0).wait_recv()
        for d in range(2):
            start_pass(g, d, 1)

    forward(0)
    begin(2)
    begin_own(2)
    relay_step(0, 0)
    forward(1)

    row_ids = lax.broadcasted_iota(jnp.int32, (4 * HD, 4 * HD), 0) // HD
    col_ids = lax.broadcasted_iota(jnp.int32, (4 * HD, 4 * HD), 1) // HD
    spread = jnp.where(
        row_ids == col_ids, jnp.where(col_ids < 2, FACTOR, 1.0), 0.0
    ).astype(jnp.bfloat16)
    first_head = lax.broadcasted_iota(jnp.int32, (BLOCK, LANES), 1) < HD

    def heads(full):
        return jnp.where(first_head, full[:HD], full[HD:])

    def fold(array, op):
        return op(array.reshape(array.shape[0] // 8, 8, LANES), axis=0)

    def attend(g, b):
        strip, row = b // HALF, lax.rem(b, HALF)
        part = qd[g, b]
        diagonal = jnp.concatenate([part] * 4, axis=0) * spread
        picked = jnp.concatenate(
            [work[meta_sm[strip, row, j]] for j in range(SEL)], axis=0
        )
        both = lax.dot_general(
            picked, diagonal, (((1,), (1,)), ((), ())), preferred_element_type=jnp.float32
        )
        bias = [
            jnp.where(meta_sm[strip, HALF + row, j] > 0, 0.0, MASKED).astype(jnp.float32)
            for j in range(SEL)
        ]
        parts = [both[j * BLOCK:(j + 1) * BLOCK, :LANES] for j in range(SEL)]
        peak = fold(parts[0], jnp.max) + bias[0]
        for j in range(1, SEL):
            peak = jnp.maximum(peak, fold(parts[j], jnp.max) + bias[j])
        peak = jnp.max(peak, axis=0, keepdims=True)
        powers = [jnp.exp(parts[j] - (peak - bias[j])) for j in range(SEL)]
        grad_weights = [both[j * BLOCK:(j + 1) * BLOCK, LANES:] for j in range(SEL)]
        total = fold(powers[0], jnp.sum)
        dots = fold(powers[0] * grad_weights[0], jnp.sum)
        for j in range(1, SEL):
            total = total + fold(powers[j], jnp.sum)
            dots = dots + fold(powers[j] * grad_weights[j], jnp.sum)
        scale = 1.0 / jnp.sum(total, axis=0, keepdims=True)
        row_dots = jnp.sum(dots, axis=0, keepdims=True) * scale
        slabs = []
        for j in range(SEL):
            weights = powers[j] * scale
            grad_scores = weights * (grad_weights[j] - row_dots)
            slabs.append(jnp.concatenate([grad_scores, weights], axis=1).astype(jnp.bfloat16))
        slab = jnp.concatenate(slabs, axis=0)
        terms = jnp.dot(slab, diagonal, preferred_element_type=jnp.float32)
        tiles[b, :SEL] = terms.reshape(SEL, BLOCK, 2 * LANES)
        mixed = lax.dot_general(
            slab, picked, (((0,), (0,)), ((), ())), preferred_element_type=jnp.float32
        )
        rows_out[g, b] = jnp.concatenate(
            [heads(mixed[:LANES, :LANES]) * FACTOR, heads(mixed[LANES:, LANES:])], axis=1
        ).astype(jnp.bfloat16)

    def finish(g):
        slot = lax.rem(g, 2)
        for d in range(2):
            for part in range(2):
                wait_terms(g, d, part).wait_recv()

        def add(w, carry):
            total = own[slot, w] + take[g, 0, w].astype(jnp.float32) + take[g, 1, w].astype(jnp.float32)
            final[g, w] = total.astype(jnp.bfloat16)
            return carry

        lax.fori_loop(0, FRAME, add, 0)
        grads_across(g).start()
        for a in range(2):
            grads_along(g, a).start()

    def one_group(g, carry):
        swap(g, 1).wait_recv()
        for d in range(2):
            for part in range(2):
                wait_pass(g, d, part).wait_recv()

        @pl.when(g + 3 < GROUPS)
        def _():
            begin(g + 3)
            begin_own(g + 3)

        work[...] = kv[g]

        def two_blocks(i, inner):
            b = lax.rem(HALF * o + 2 * i, FRAME)
            attend(g, b)
            attend(g, b + 1)

            @pl.when((i == 0) & (g > 1))
            def _():
                finish(g - 2)

            @pl.when((i == 0) & (g == 0))
            def _():
                relay_step(1, 0)

            @pl.when(i == 1)
            def _():
                rows_across(g).start()

                @pl.when(g + 2 < GROUPS)
                def _():
                    forward(g + 2)

            @pl.when((i == 2) & (g > 0))
            def _():
                relay_step(g - 1, 1)

            @pl.when((i == 3) & (g + 2 < GROUPS))
            def _():
                relay_step(g + 2, 0)

            return inner

        lax.fori_loop(0, FRAME // 2, two_blocks, 0)
        for a in range(2):
            rows_along(g, a).start()

        def gather(w, base):
            acc = None
            for b in range(FRAME):
                place = meta_sm[b // HALF, b % HALF, PLACE_AT + base + w]
                tile = tiles[b, place]
                acc = tile if acc is None else acc + tile
            return acc

        def collect(w, inner):
            give[g, 1, w] = gather(w, 0).astype(jnp.bfloat16)
            give[g, 0, w] = gather(w, 2 * FRAME).astype(jnp.bfloat16)
            return inner

        lax.fori_loop(0, FRAME, collect, 0)
        for d in range(2):
            for part in range(2):
                start_terms(g, d, part)

        def collect_own(w, inner):
            own[lax.rem(g, 2), w] = gather(w, FRAME)
            return inner

        lax.fori_loop(0, FRAME, collect_own, 0)

        return carry

    lax.fori_loop(0, GROUPS, one_group, 0)
    finish(GROUPS - 2)
    relay_step(GROUPS - 1, 1)
    finish(GROUPS - 1)

    def land(g, carry):
        rows_across(g).wait_recv()
        for a in range(2):
            rows_back(g, a).start()
        grads_across(g).wait_recv()
        for a in range(2):
            grads_back(g, a).start()
        return carry

    lax.fori_loop(0, GROUPS, land, 0)

    def drain(g, carry):
        for pair in range(2):
            swap(g, pair).wait_send()
        for d in range(2):
            for part in range(2):
                wait_pass(g, d, part).wait_send()
                wait_terms(g, d, part).wait_send()

        @pl.when(is_relay)
        def _():
            for phase in range(2):
                relay_on(g, phase).wait_send()

        rows_across(g).wait_send()
        grads_across(g).wait_send()
        for a in range(2):
            rows_along(g, a).wait()
            grads_along(g, a).wait()
            rows_back(g, a).wait()
            grads_back(g, a).wait()
        return carry

    lax.fori_loop(0, GROUPS, drain, 0)


def hand_over(*refs):
    sources, targets, sems = refs[:4], refs[4:8], refs[8]
    copies = [
        pltpu.make_async_copy(src.at[pl.ds(at * 2, 2)], dst.at[pl.ds(at * 2, 2)], sems.at[i, at])
        for i, (src, dst) in enumerate(zip(sources, targets))
        for at in range(2)
    ]
    for copy in copies:
        copy.start()
    for copy in copies:
        copy.wait()


def body(queries, keys, values, out_grad, block_list, block_count):
    rows, width = queries.shape
    frames = lax.axis_size("frames")
    blocked = [x.reshape(HALF, BLOCK, width) for x in (queries, keys, values, out_grad)]
    shape = jax.ShapeDtypeStruct((HALF, BLOCK, width), jnp.bfloat16)
    dma = pltpu.SemaphoreType.DMA
    flops = 6 * 2 * FRAME * SEL * BLOCK * 256 * 256 * GROUPS
    outs = pl.pallas_call(
        lambda *refs: kernel(frames, *refs),
        out_shape=[shape] * 4,
        in_specs=[pl.BlockSpec(memory_space=pltpu.VMEM), pl.BlockSpec(memory_space=pltpu.SMEM)] + [pl.BlockSpec(memory_space=pl.ANY)] * 4,
        out_specs=[pl.BlockSpec(memory_space=pl.ANY)] * 4,
        scratch_shapes=[
            pltpu.VMEM((4, HALF, BLOCK, width), jnp.bfloat16),
            pltpu.VMEM((GROUPS, 2, HALF, BLOCK, 2 * LANES), jnp.bfloat16),
            pltpu.VMEM((GROUPS, WINDOW, BLOCK, 2 * LANES), jnp.bfloat16),
            pltpu.VMEM((GROUPS, FRAME, BLOCK, 2 * LANES), jnp.bfloat16),
            pltpu.VMEM((WINDOW, BLOCK, 2 * LANES), jnp.bfloat16),
            pltpu.VMEM((FRAME, SEL + 1, BLOCK, 2 * LANES), jnp.float32),
            pltpu.VMEM((GROUPS, FRAME, BLOCK, 2 * LANES), jnp.bfloat16),
            pltpu.VMEM((GROUPS, HALF, BLOCK, 2 * LANES), jnp.bfloat16),
            pltpu.VMEM((GROUPS, 2, FRAME, BLOCK, 2 * LANES), jnp.bfloat16),
            pltpu.VMEM((GROUPS, 2, FRAME, BLOCK, 2 * LANES), jnp.bfloat16),
            pltpu.VMEM((2, FRAME, BLOCK, 2 * LANES), jnp.float32),
            pltpu.VMEM((GROUPS, FRAME, BLOCK, 2 * LANES), jnp.bfloat16),
            pltpu.VMEM((GROUPS, HALF, BLOCK, 2 * LANES), jnp.bfloat16),
            pltpu.VMEM((2, GROUPS, HALF, BLOCK, 2 * LANES), jnp.bfloat16),
            pltpu.VMEM((2, 8, LANES), jnp.int32),
            pltpu.SMEM((2, 8, LANES), jnp.int32),
            dma((4,)), dma((GROUPS, 2)), dma((GROUPS, 2)),
            dma((GROUPS, 2, 2)), dma((GROUPS, 2, 2)),
            dma, dma, dma,
            dma((GROUPS,)), dma((GROUPS,)), dma((2 * GROUPS, 2)),
            dma((GROUPS, 2, 2)), dma((GROUPS, 2, 2)),
            dma((GROUPS,)), dma((GROUPS,)), dma((2 * GROUPS, 2)),
            dma((2, GROUPS)), dma((2, GROUPS)),
        ],
        cost_estimate=pl.CostEstimate(
            flops=flops, bytes_accessed=16 * rows * width, transcendentals=FRAME * SEL * BLOCK * LANES * GROUPS
        ),
        compiler_params=pltpu.CompilerParams(
            collective_id=0, has_side_effects=True, vmem_limit_bytes=60 * 1024 * 1024
        ),
    )(block_list, block_count, *blocked)
    outs = pl.pallas_call(
        hand_over,
        out_shape=[shape] * 4,
        in_specs=[pl.BlockSpec(memory_space=pltpu.VMEM)] * 4,
        out_specs=[pl.BlockSpec(memory_space=pl.ANY)] * 4,
        scratch_shapes=[dma((4, 2))],
        compiler_params=pltpu.CompilerParams(vmem_limit_bytes=60 * 1024 * 1024),
    )(*outs)
    return tuple(x.reshape(rows, width) for x in outs)


def solution(mesh):
    split = P(("frames", "strip"), None)
    in_specs = (split, split, split, split, split, P(("frames", "strip")))
    return jax.shard_map(
        body, mesh=mesh, in_specs=in_specs, out_specs=(split,) * 4, check_vma=False
    )
```

```python
import jax
import jax.numpy as jnp
from jax import lax
from jax.experimental import pallas as pl
from jax.experimental.pallas import tpu as pltpu
from jax.sharding import PartitionSpec as P

HD = 64
BLOCK = 64
SEL = 13
HALF = 4
FRAME = 8
WINDOW = 24
GROUPS = 4
LANES = 128
FACTOR = 0.125
MASKED = -1e30
PLACE_AT = 32
RUN = 8
MESH = pl.DeviceIdType.MESH


def kernel(
    frames,
    block_list, block_count, queries, keys, values, out_grad,
    attended, query_grad, key_grad, value_grad,
    loaded, packed, kv, qd, work, tiles, rows_out, rows_in, give, take, own, final, final_in, relay, meta_vm, meta_sm,
    load_sem, in_send, in_recv, pass_send, pass_recv,
    meta_send, meta_recv, meta_local, row_send, row_recv, row_local,
    term_send, term_recv, grad_send, grad_recv, grad_local, relay_send, relay_recv,
):
    f, s = lax.axis_index("frames"), lax.axis_index("strip")
    o = 1 - s
    after, before = lax.rem(f + 1, frames), lax.rem(f + frames - 1, frames)
    partner, next_dev, prev_dev = (f, o), (after, s), (before, s)

    sources = (keys, values, queries, out_grad)
    loads = [pltpu.make_async_copy(sources[a], loaded.at[a], load_sem.at[a]) for a in range(4)]
    for load in loads:
        load.start()

    place_in_run = lax.rem(f, RUN)
    edge = (place_in_run == RUN - 1, place_in_run == 0)
    part_column = (3 * s, 1 + s)

    def relay_of(d, column):
        return (f - 2 * column if d == 0 else f + 2 * column, s)

    def relay_to(d, column):
        if d == 0:
            return (lax.rem(f + 1 + 2 * column, frames), s)
        return (lax.rem(f + frames - 1 - 2 * column, frames), s)

    relay_back = 1 - lax.rem(place_in_run, 2)
    relay_column = lax.select(relay_back == 0, (RUN - 1 - place_in_run) // 2, place_in_run // 2)
    is_relay = ((relay_column == 1) & (s == 0)) | ((relay_column >= 2) & (s == 1))
    relay_half = lax.rem(relay_column, 2)
    relay_source_frame = f - place_in_run + (1 - relay_back) * (RUN - 1)
    relay_target_frame = lax.rem(relay_source_frame + frames + 1 - 2 * relay_back, frames)
    relay_target, relay_source = (relay_target_frame, s), (relay_source_frame, s)

    barrier = pltpu.get_barrier_semaphore()

    def greet(device):
        pl.semaphore_signal(barrier, inc=1, device_id=device, device_id_type=MESH)

    for device in (partner, next_dev, prev_dev):
        greet(device)

    @pl.when(is_relay)
    def _():
        greet(relay_source)
        greet(relay_target)

    for d in range(2):
        for column in (1, 2, 3):
            @pl.when(edge[d] & (s == (0 if column == 1 else 1)))
            def _():
                greet(relay_of(d, column))
                greet(relay_to(d, column))

    at_end = (edge[0] | edge[1]).astype(jnp.int32)
    pl.semaphore_wait(barrier, 3 + 2 * is_relay.astype(jnp.int32) + at_end * (2 + 2 * s))

    def remote(src, dst, send, recv, device):
        return pltpu.make_async_remote_copy(
            src_ref=src, dst_ref=dst, send_sem=send, recv_sem=recv,
            device_id=device, device_id_type=MESH,
        )

    def columns(half, g):
        return pl.ds(pl.multiple_of(half * (GROUPS * LANES) + g * LANES, LANES), LANES)

    def landing(g, pair, half):
        if pair == 0:
            return kv.at[g, pl.ds(FRAME + HALF * half, HALF)]
        return qd.at[g, pl.ds(HALF * half, HALF)]

    def swap(g, pair):
        return remote(
            packed.at[g, pair], landing(g, pair, s), in_send.at[g, pair], in_recv.at[g, pair], partner
        )

    def pack(g, pair):
        for a in range(2):
            lanes = slice(a * LANES, (a + 1) * LANES)
            packed[g, pair, :, :, lanes] = loaded[2 * pair + a, :, :, columns(o, g)]

    def keep(g, pair):
        own_rows = landing(g, pair, s)
        for a in range(2):
            lanes = slice(a * LANES, (a + 1) * LANES)
            own_rows[:, :, lanes] = loaded[2 * pair + a, :, :, columns(s, g)]

    neighbours = (next_dev, prev_dev)

    def start_part(d, part, src, dst, send, recv, phase, g):
        straight = remote(src, dst, send, recv, neighbours[d])
        if part == 0:
            bent = edge[d] & (s == 1)
        else:
            bent = edge[d]

        @pl.when(bent)
        def _():
            remote(
                src, relay.at[phase, g], send, relay_recv.at[phase, g], relay_of(d, part_column[part])
            ).start()

        @pl.when(jnp.logical_not(bent))
        def _():
            straight.start()

    def kv_window(g, base, half):
        return kv.at[g, pl.ds(base + HALF * half, HALF)]

    def pass_args(g, d, part):
        half = (s, o)[part]
        return (
            kv_window(g, FRAME, half), kv_window(g, (0, 2 * FRAME)[d], half),
            pass_send.at[g, d, half], pass_recv.at[g, d, half],
        )

    def start_pass(g, d, part):
        start_part(d, part, *pass_args(g, d, part), 0, g)

    def wait_pass(g, d, part):
        return remote(*pass_args(g, d, part), neighbours[d])

    def term_args(g, d, part):
        half = (s, o)[part]
        at = pl.ds(HALF * half, HALF)
        return (
            give.at[g, d, at], take.at[g, d, at], term_send.at[g, d, half], term_recv.at[g, d, half]
        )

    def start_terms(g, d, part):
        start_part(d, part, *term_args(g, d, part), 1, g)

    def wait_terms(g, d, part):
        return remote(*term_args(g, d, part), neighbours[d])

    def relay_on(g, phase):
        if phase == 0:
            target = kv_window(g, relay_back * (2 * FRAME), relay_half)
            recv = pass_recv.at[g, relay_back, relay_half]
        else:
            target = take.at[g, relay_back, pl.ds(HALF * relay_half, HALF)]
            recv = term_recv.at[g, relay_back, relay_half]
        return remote(relay.at[phase, g], target, relay_send.at[phase, g], recv, relay_target)

    def relay_step(g, phase):
        @pl.when(is_relay)
        def _():
            remote(
                relay.at[phase, g], relay.at[phase, g], relay_send.at[phase, g],
                relay_recv.at[phase, g], relay_target,
            ).wait_recv()
            relay_on(g, phase).start()

    def rows_across(g):
        return remote(
            rows_out.at[g, pl.ds(HALF * o, HALF)], rows_in.at[g], row_send.at[g], row_recv.at[g], partner
        )

    def grads_across(g):
        return remote(
            final.at[g, pl.ds(HALF * o, HALF)], final_in.at[g], grad_send.at[g], grad_recv.at[g], partner
        )

    row_targets, grad_targets = (query_grad, attended), (key_grad, value_grad)

    def place_copy(staged, targets, local, g, half, a):
        return pltpu.make_async_copy(
            staged.at[:, :, pl.ds(a * LANES, LANES)], targets[a].at[:, :, columns(half, g)], local.at[g, a]
        )

    def rows_along(g, a):
        return place_copy(rows_out.at[g, pl.ds(HALF * s, HALF)], row_targets, row_local, g, s, a)

    def grads_along(g, a):
        return place_copy(final.at[g, pl.ds(HALF * s, HALF)], grad_targets, grad_local, g, s, a)

    def rows_back(g, a):
        return place_copy(rows_in.at[g], row_targets, row_local.at[pl.ds(GROUPS, GROUPS)], g, o, a)

    def grads_back(g, a):
        return place_copy(final_in.at[g], grad_targets, grad_local.at[pl.ds(GROUPS, GROUPS)], g, o, a)

    share_meta = remote(meta_vm.at[s], meta_vm.at[s], meta_send, meta_recv, partner)

    def begin(g):
        for pair in range(2):
            pack(g, pair)
            swap(g, pair).start()

    def begin_own(g):
        keep(g, 0)
        for d in range(2):
            start_pass(g, d, 0)
        keep(g, 1)

    for pair in range(2):
        loads[2 * pair].wait()
        loads[2 * pair + 1].wait()
        pack(0, pair)
        swap(0, pair).start()
        keep(0, pair)
        if pair == 0:
            for d in range(2):
                start_pass(0, d, 0)

    listed = block_list[...]
    row_at = lax.broadcasted_iota(jnp.int32, (HALF, LANES), 0)
    lane_at = lax.broadcasted_iota(jnp.int32, (HALF, LANES), 1)
    counts = jnp.zeros((HALF, LANES), jnp.int32)
    for row in range(HALF):
        counts = jnp.where(row_at == row, block_count[row], counts)
    edge_low = jnp.where(f > 0, 0, FRAME)
    edge_high = jnp.where(f < frames - 1, WINDOW, 2 * FRAME)
    usable = (listed >= edge_low) & (listed < edge_high) & (lane_at[:, :SEL] < counts[:, :SEL])
    slots = jnp.where(usable, listed, -1)
    place = jnp.full((HALF, LANES), SEL, jnp.int32)
    for j in range(SEL):
        place = jnp.where(lane_at - PLACE_AT == slots[:, j:j + 1], j, place)
    meta_vm[s, 0:HALF] = place
    meta_vm[s, 0:HALF, 0:SEL] = listed
    meta_vm[s, HALF:] = jnp.zeros((HALF, LANES), jnp.int32)
    meta_vm[s, HALF:, 0:SEL] = usable.astype(jnp.int32)
    share_meta.start()
    begin(1)
    begin_own(1)
    tiles[:, SEL] = jnp.zeros((FRAME, BLOCK, 2 * LANES), jnp.float32)

    def forward(g):
        swap(g, 0).wait_recv()
        for d in range(2):
            start_pass(g, d, 1)

    forward(0)
    share_meta.wait()
    to_scalar = pltpu.make_async_copy(meta_vm, meta_sm, meta_local)
    to_scalar.start()
    relay_step(0, 0)
    begin(2)
    begin_own(2)
    to_scalar.wait()
    forward(1)

    row_ids = lax.broadcasted_iota(jnp.int32, (4 * HD, 4 * HD), 0) // HD
    col_ids = lax.broadcasted_iota(jnp.int32, (4 * HD, 4 * HD), 1) // HD
    spread = jnp.where(
        row_ids == col_ids, jnp.where(col_ids < 2, FACTOR, 1.0), 0.0
    ).astype(jnp.bfloat16)
    first_head = lax.broadcasted_iota(jnp.int32, (BLOCK, LANES), 1) < HD

    def heads(full):
        return jnp.where(first_head, full[:HD], full[HD:])

    def fold(array, op):
        return op(array.reshape(array.shape[0] // 8, 8, LANES), axis=0)

    def attend(g, b):
        strip, row = b // HALF, lax.rem(b, HALF)
        part = qd[g, b]
        diagonal = jnp.concatenate([part] * 4, axis=0) * spread
        picked = jnp.concatenate(
            [work[meta_sm[strip, row, j]] for j in range(SEL)], axis=0
        )
        both = lax.dot_general(
            picked, diagonal, (((1,), (1,)), ((), ())), preferred_element_type=jnp.float32
        )
        bias = [
            jnp.where(meta_sm[strip, HALF + row, j] > 0, 0.0, MASKED).astype(jnp.float32)
            for j in range(SEL)
        ]
        parts = [both[j * BLOCK:(j + 1) * BLOCK, :LANES] for j in range(SEL)]
        peak = fold(parts[0], jnp.max) + bias[0]
        for j in range(1, SEL):
            peak = jnp.maximum(peak, fold(parts[j], jnp.max) + bias[j])
        peak = jnp.max(peak, axis=0, keepdims=True)
        powers = [jnp.exp(parts[j] - (peak - bias[j])) for j in range(SEL)]
        grad_weights = [both[j * BLOCK:(j + 1) * BLOCK, LANES:] for j in range(SEL)]
        total = fold(powers[0], jnp.sum)
        dots = fold(powers[0] * grad_weights[0], jnp.sum)
        for j in range(1, SEL):
            total = total + fold(powers[j], jnp.sum)
            dots = dots + fold(powers[j] * grad_weights[j], jnp.sum)
        scale = 1.0 / jnp.sum(total, axis=0, keepdims=True)
        row_dots = jnp.sum(dots, axis=0, keepdims=True) * scale
        slabs = []
        for j in range(SEL):
            weights = powers[j] * scale
            grad_scores = weights * (grad_weights[j] - row_dots)
            slabs.append(jnp.concatenate([grad_scores, weights], axis=1).astype(jnp.bfloat16))
        slab = jnp.concatenate(slabs, axis=0)
        terms = jnp.dot(slab, diagonal, preferred_element_type=jnp.float32)
        tiles[b, :SEL] = terms.reshape(SEL, BLOCK, 2 * LANES)
        mixed = lax.dot_general(
            slab, picked, (((0,), (0,)), ((), ())), preferred_element_type=jnp.float32
        )
        rows_out[g, b] = jnp.concatenate(
            [heads(mixed[:LANES, :LANES]) * FACTOR, heads(mixed[LANES:, LANES:])], axis=1
        ).astype(jnp.bfloat16)

    def finish(g):
        slot = lax.rem(g, 2)
        for d in range(2):
            for part in range(2):
                wait_terms(g, d, part).wait_recv()

        def add(w, carry):
            total = own[slot, w] + take[g, 0, w].astype(jnp.float32) + take[g, 1, w].astype(jnp.float32)
            final[g, w] = total.astype(jnp.bfloat16)
            return carry

        lax.fori_loop(0, FRAME, add, 0)
        grads_across(g).start()
        for a in range(2):
            grads_along(g, a).start()
        rows_across(g).wait_recv()
        for a in range(2):
            rows_back(g, a).start()

    def one_group(g, carry):
        swap(g, 1).wait_recv()
        for d in range(2):
            for part in range(2):
                wait_pass(g, d, part).wait_recv()

        @pl.when(g + 3 < GROUPS)
        def _():
            begin(g + 3)
            begin_own(g + 3)

        work[...] = kv[g]

        def four_blocks(i, inner):
            first = lax.rem(HALF * o + HALF * i, FRAME)
            for b in range(HALF):
                attend(g, first + b)

            @pl.when((i == 0) & (g > 1))
            def _():
                finish(g - 2)

            @pl.when(i == 0)
            def _():
                rows_across(g).start()

                @pl.when(g + 2 < GROUPS)
                def _():
                    forward(g + 2)

            @pl.when((i == 0) & (g == 0))
            def _():
                relay_step(1, 0)

            @pl.when((i == 0) & (g > 0))
            def _():
                relay_step(g - 1, 1)

            @pl.when((i == 1) & (g + 2 < GROUPS))
            def _():
                relay_step(g + 2, 0)

            return inner

        lax.fori_loop(0, 2, four_blocks, 0)
        for a in range(2):
            rows_along(g, a).start()

        def gather(w, base):
            acc = None
            for b in range(FRAME):
                place = meta_sm[b // HALF, b % HALF, PLACE_AT + base + w]
                tile = tiles[b, place]
                acc = tile if acc is None else acc + tile
            return acc

        def collect(w, inner):
            give[g, 1, w] = gather(w, 0).astype(jnp.bfloat16)
            give[g, 0, w] = gather(w, 2 * FRAME).astype(jnp.bfloat16)
            return inner

        lax.fori_loop(0, FRAME, collect, 0)
        for d in range(2):
            for part in range(2):
                start_terms(g, d, part)

        def collect_own(w, inner):
            own[lax.rem(g, 2), w] = gather(w, FRAME)
            return inner

        lax.fori_loop(0, FRAME, collect_own, 0)

        return carry

    lax.fori_loop(0, GROUPS, one_group, 0)
    finish(GROUPS - 2)
    relay_step(GROUPS - 1, 1)
    finish(GROUPS - 1)

    def land(g, carry):
        grads_across(g).wait_recv()
        for a in range(2):
            grads_back(g, a).start()
        return carry

    lax.fori_loop(0, GROUPS, land, 0)

    def drain(g, carry):
        for pair in range(2):
            swap(g, pair).wait_send()
        for d in range(2):
            for part in range(2):
                wait_pass(g, d, part).wait_send()
                wait_terms(g, d, part).wait_send()

        @pl.when(is_relay)
        def _():
            for phase in range(2):
                relay_on(g, phase).wait_send()

        rows_across(g).wait_send()
        grads_across(g).wait_send()
        for a in range(2):
            rows_along(g, a).wait()
            grads_along(g, a).wait()
            rows_back(g, a).wait()
            grads_back(g, a).wait()
        return carry

    lax.fori_loop(0, GROUPS, drain, 0)


def hand_over(*refs):
    sources, targets, held, in_sems, out_sems = refs[:4], refs[4:8], refs[8], refs[9], refs[10]
    spots = [(i, at) for i in range(4) for at in range(HALF)]
    ins = [pltpu.make_async_copy(sources[i].at[at], held.at[i, at], in_sems.at[i, at]) for i, at in spots]
    outs = [pltpu.make_async_copy(held.at[i, at], targets[i].at[at], out_sems.at[i, at]) for i, at in spots]
    for copy in ins:
        copy.start()
    for arrives, leaves in zip(ins, outs):
        arrives.wait()
        leaves.start()
    for copy in outs:
        copy.wait()


def body(queries, keys, values, out_grad, block_list, block_count):
    rows, width = queries.shape
    frames = lax.axis_size("frames")
    blocked = [x.reshape(HALF, BLOCK, width) for x in (queries, keys, values, out_grad)]
    shape = jax.ShapeDtypeStruct((HALF, BLOCK, width), jnp.bfloat16)
    dma = pltpu.SemaphoreType.DMA
    flops = 6 * 2 * FRAME * SEL * BLOCK * 256 * 256 * GROUPS
    outs = pl.pallas_call(
        lambda *refs: kernel(frames, *refs),
        out_shape=[shape] * 4,
        in_specs=[pl.BlockSpec(memory_space=pltpu.VMEM), pl.BlockSpec(memory_space=pltpu.SMEM)] + [pl.BlockSpec(memory_space=pl.ANY)] * 4,
        out_specs=[pl.BlockSpec(memory_space=pl.ANY)] * 4,
        scratch_shapes=[
            pltpu.VMEM((4, HALF, BLOCK, width), jnp.bfloat16),
            pltpu.VMEM((GROUPS, 2, HALF, BLOCK, 2 * LANES), jnp.bfloat16),
            pltpu.VMEM((GROUPS, WINDOW, BLOCK, 2 * LANES), jnp.bfloat16),
            pltpu.VMEM((GROUPS, FRAME, BLOCK, 2 * LANES), jnp.bfloat16),
            pltpu.VMEM((WINDOW, BLOCK, 2 * LANES), jnp.bfloat16),
            pltpu.VMEM((FRAME, SEL + 1, BLOCK, 2 * LANES), jnp.float32),
            pltpu.VMEM((GROUPS, FRAME, BLOCK, 2 * LANES), jnp.bfloat16),
            pltpu.VMEM((GROUPS, HALF, BLOCK, 2 * LANES), jnp.bfloat16),
            pltpu.VMEM((GROUPS, 2, FRAME, BLOCK, 2 * LANES), jnp.bfloat16),
            pltpu.VMEM((GROUPS, 2, FRAME, BLOCK, 2 * LANES), jnp.bfloat16),
            pltpu.VMEM((2, FRAME, BLOCK, 2 * LANES), jnp.float32),
            pltpu.VMEM((GROUPS, FRAME, BLOCK, 2 * LANES), jnp.bfloat16),
            pltpu.VMEM((GROUPS, HALF, BLOCK, 2 * LANES), jnp.bfloat16),
            pltpu.VMEM((2, GROUPS, HALF, BLOCK, 2 * LANES), jnp.bfloat16),
            pltpu.VMEM((2, 8, LANES), jnp.int32),
            pltpu.SMEM((2, 8, LANES), jnp.int32),
            dma((4,)), dma((GROUPS, 2)), dma((GROUPS, 2)),
            dma((GROUPS, 2, 2)), dma((GROUPS, 2, 2)),
            dma, dma, dma,
            dma((GROUPS,)), dma((GROUPS,)), dma((2 * GROUPS, 2)),
            dma((GROUPS, 2, 2)), dma((GROUPS, 2, 2)),
            dma((GROUPS,)), dma((GROUPS,)), dma((2 * GROUPS, 2)),
            dma((2, GROUPS)), dma((2, GROUPS)),
        ],
        cost_estimate=pl.CostEstimate(
            flops=flops, bytes_accessed=16 * rows * width, transcendentals=FRAME * SEL * BLOCK * LANES * GROUPS
        ),
        compiler_params=pltpu.CompilerParams(
            collective_id=0, has_side_effects=True, vmem_limit_bytes=60 * 1024 * 1024
        ),
    )(block_list, block_count, *blocked)
    outs = pl.pallas_call(
        hand_over,
        out_shape=[shape] * 4,
        in_specs=[pl.BlockSpec(memory_space=pl.ANY)] * 4,
        out_specs=[pl.BlockSpec(memory_space=pl.ANY)] * 4,
        scratch_shapes=[
            pltpu.VMEM((4, HALF, BLOCK, width), jnp.bfloat16), dma((4, HALF)), dma((4, HALF)),
        ],
        compiler_params=pltpu.CompilerParams(vmem_limit_bytes=60 * 1024 * 1024),
    )(*outs)
    return tuple(x.reshape(rows, width) for x in outs)


def solution(mesh):
    split = P(("frames", "strip"), None)
    in_specs = (split, split, split, split, split, P(("frames", "strip")))
    return jax.shard_map(
        body, mesh=mesh, in_specs=in_specs, out_specs=(split,) * 4, check_vma=False
    )
```

```python
import jax
import jax.numpy as jnp
from jax import lax
from jax.experimental import pallas as pl
from jax.experimental.pallas import tpu as pltpu
from jax.sharding import PartitionSpec as P

HD = 64
BLOCK = 64
SEL = 13
HALF = 4
FRAME = 8
WINDOW = 24
GROUPS = 4
LANES = 128
FACTOR = 0.125
MASKED = -1e30
PLACE_AT = 32
RUN = 8
MESH = pl.DeviceIdType.MESH


def kernel(
    frames,
    block_list, block_count, queries, keys, values, out_grad,
    attended, query_grad, key_grad, value_grad,
    loaded, packed, kv, qd, work, low, high, tiles, rows_out, rows_in, give, take, own, final, final_in, relay, meta_vm, meta_sm,
    load_sem, in_send, in_recv, pass_send, pass_recv,
    meta_send, meta_recv, meta_local, row_send, row_recv, row_local,
    term_send, term_recv, grad_send, grad_recv, grad_local, relay_send, relay_recv,
):
    f, s = lax.axis_index("frames"), lax.axis_index("strip")
    o = 1 - s
    after, before = lax.rem(f + 1, frames), lax.rem(f + frames - 1, frames)
    partner, next_dev, prev_dev = (f, o), (after, s), (before, s)

    sources = (keys, values, queries, out_grad)
    loads = [pltpu.make_async_copy(sources[a], loaded.at[a], load_sem.at[a]) for a in range(4)]
    for load in loads:
        load.start()

    place_in_run = lax.rem(f, RUN)
    edge = (place_in_run == RUN - 1, place_in_run == 0)
    part_column = (3 * s, 1 + s)

    def relay_of(d, column):
        return (f - 2 * column if d == 0 else f + 2 * column, s)

    def relay_to(d, column):
        if d == 0:
            return (lax.rem(f + 1 + 2 * column, frames), s)
        return (lax.rem(f + frames - 1 - 2 * column, frames), s)

    relay_back = 1 - lax.rem(place_in_run, 2)
    relay_column = lax.select(relay_back == 0, (RUN - 1 - place_in_run) // 2, place_in_run // 2)
    is_relay = ((relay_column == 1) & (s == 0)) | ((relay_column >= 2) & (s == 1))
    relay_half = lax.rem(relay_column, 2)
    relay_source_frame = f - place_in_run + (1 - relay_back) * (RUN - 1)
    relay_target_frame = lax.rem(relay_source_frame + frames + 1 - 2 * relay_back, frames)
    relay_target, relay_source = (relay_target_frame, s), (relay_source_frame, s)

    barrier = pltpu.get_barrier_semaphore()

    def greet(device):
        pl.semaphore_signal(barrier, inc=1, device_id=device, device_id_type=MESH)

    for device in (partner, next_dev, prev_dev):
        greet(device)

    @pl.when(is_relay)
    def _():
        greet(relay_source)
        greet(relay_target)

    for d in range(2):
        for column in (1, 2, 3):
            @pl.when(edge[d] & (s == (0 if column == 1 else 1)))
            def _():
                greet(relay_of(d, column))
                greet(relay_to(d, column))

    at_end = (edge[0] | edge[1]).astype(jnp.int32)
    pl.semaphore_wait(barrier, 3 + 2 * is_relay.astype(jnp.int32) + at_end * (2 + 2 * s))

    def remote(src, dst, send, recv, device):
        return pltpu.make_async_remote_copy(
            src_ref=src, dst_ref=dst, send_sem=send, recv_sem=recv,
            device_id=device, device_id_type=MESH,
        )

    def columns(half, g):
        return pl.ds(pl.multiple_of(half * (GROUPS * LANES) + g * LANES, LANES), LANES)

    def landing(g, pair, half):
        if pair == 0:
            return kv.at[g, pl.ds(FRAME + HALF * half, HALF)]
        return qd.at[g, pl.ds(HALF * half, HALF)]

    def swap(g, pair):
        return remote(
            packed.at[g, pair], landing(g, pair, s), in_send.at[g, pair], in_recv.at[g, pair], partner
        )

    def pack(g, pair):
        for a in range(2):
            lanes = slice(a * LANES, (a + 1) * LANES)
            packed[g, pair, :, :, lanes] = loaded[2 * pair + a, :, :, columns(o, g)]

    def keep(g, pair):
        own_rows = landing(g, pair, s)
        for a in range(2):
            lanes = slice(a * LANES, (a + 1) * LANES)
            own_rows[:, :, lanes] = loaded[2 * pair + a, :, :, columns(s, g)]

    neighbours = (next_dev, prev_dev)

    def start_part(d, part, src, dst, send, recv, phase, g):
        straight = remote(src, dst, send, recv, neighbours[d])
        if part == 0:
            bent = edge[d] & (s == 1)
        else:
            bent = edge[d]

        @pl.when(bent)
        def _():
            remote(
                src, relay.at[phase, g], send, relay_recv.at[phase, g], relay_of(d, part_column[part])
            ).start()

        @pl.when(jnp.logical_not(bent))
        def _():
            straight.start()

    def kv_window(g, base, half):
        return kv.at[g, pl.ds(base + HALF * half, HALF)]

    def pass_args(g, d, part):
        half = (s, o)[part]
        return (
            kv_window(g, FRAME, half), kv_window(g, (0, 2 * FRAME)[d], half),
            pass_send.at[g, d, half], pass_recv.at[g, d, half],
        )

    def start_pass(g, d, part):
        start_part(d, part, *pass_args(g, d, part), 0, g)

    def wait_pass(g, d, part):
        return remote(*pass_args(g, d, part), neighbours[d])

    def term_args(g, d, part):
        half = (s, o)[part]
        at = pl.ds(HALF * half, HALF)
        return (
            give.at[g, d, at], take.at[g, d, at], term_send.at[g, d, half], term_recv.at[g, d, half]
        )

    def start_terms(g, d, part):
        start_part(d, part, *term_args(g, d, part), 1, g)

    def wait_terms(g, d, part):
        return remote(*term_args(g, d, part), neighbours[d])

    def relay_on(g, phase):
        if phase == 0:
            target = kv_window(g, relay_back * (2 * FRAME), relay_half)
            recv = pass_recv.at[g, relay_back, relay_half]
        else:
            target = take.at[g, relay_back, pl.ds(HALF * relay_half, HALF)]
            recv = term_recv.at[g, relay_back, relay_half]
        return remote(relay.at[phase, g], target, relay_send.at[phase, g], recv, relay_target)

    def relay_step(g, phase):
        @pl.when(is_relay)
        def _():
            remote(
                relay.at[phase, g], relay.at[phase, g], relay_send.at[phase, g],
                relay_recv.at[phase, g], relay_target,
            ).wait_recv()
            relay_on(g, phase).start()

    def rows_across(g):
        return remote(
            rows_out.at[g, pl.ds(HALF * o, HALF)], rows_in.at[g], row_send.at[g], row_recv.at[g], partner
        )

    def grads_across(g):
        return remote(
            final.at[g, pl.ds(HALF * o, HALF)], final_in.at[g], grad_send.at[g], grad_recv.at[g], partner
        )

    row_targets, grad_targets = (query_grad, attended), (key_grad, value_grad)

    def place_copy(staged, targets, local, g, half, a):
        return pltpu.make_async_copy(
            staged.at[:, :, pl.ds(a * LANES, LANES)], targets[a].at[:, :, columns(half, g)], local.at[g, a]
        )

    def rows_along(g, a):
        return place_copy(rows_out.at[g, pl.ds(HALF * s, HALF)], row_targets, row_local, g, s, a)

    def grads_along(g, a):
        return place_copy(final.at[g, pl.ds(HALF * s, HALF)], grad_targets, grad_local, g, s, a)

    def rows_back(g, a):
        return place_copy(rows_in.at[g], row_targets, row_local.at[pl.ds(GROUPS, GROUPS)], g, o, a)

    def grads_back(g, a):
        return place_copy(final_in.at[g], grad_targets, grad_local.at[pl.ds(GROUPS, GROUPS)], g, o, a)

    share_meta = remote(meta_vm.at[s], meta_vm.at[s], meta_send, meta_recv, partner)

    def begin(g):
        for pair in range(2):
            pack(g, pair)
            swap(g, pair).start()

    def begin_own(g):
        keep(g, 0)
        for d in range(2):
            start_pass(g, d, 0)
        keep(g, 1)

    for pair in range(2):
        loads[2 * pair].wait()
        loads[2 * pair + 1].wait()
        pack(0, pair)
        swap(0, pair).start()
        keep(0, pair)
        if pair == 0:
            for d in range(2):
                start_pass(0, d, 0)

    listed = block_list[...]
    row_at = lax.broadcasted_iota(jnp.int32, (HALF, LANES), 0)
    lane_at = lax.broadcasted_iota(jnp.int32, (HALF, LANES), 1)
    counts = jnp.zeros((HALF, LANES), jnp.int32)
    for row in range(HALF):
        counts = jnp.where(row_at == row, block_count[row], counts)
    edge_low = jnp.where(f > 0, 0, FRAME)
    edge_high = jnp.where(f < frames - 1, WINDOW, 2 * FRAME)
    usable = (listed >= edge_low) & (listed < edge_high) & (lane_at[:, :SEL] < counts[:, :SEL])
    slots = jnp.where(usable, listed, -1)
    place = jnp.full((HALF, LANES), SEL, jnp.int32)
    for j in range(SEL):
        place = jnp.where(lane_at - PLACE_AT == slots[:, j:j + 1], j, place)
    meta_vm[s, 0:HALF] = place
    meta_vm[s, 0:HALF, 0:SEL] = listed
    meta_vm[s, HALF:] = jnp.zeros((HALF, LANES), jnp.int32)
    meta_vm[s, HALF:, 0:SEL] = usable.astype(jnp.int32)
    share_meta.start()
    begin(1)
    begin_own(1)
    tiles[:, SEL] = jnp.zeros((FRAME, BLOCK, 2 * LANES), jnp.float32)

    def forward(g):
        swap(g, 0).wait_recv()
        for d in range(2):
            start_pass(g, d, 1)

    forward(0)
    share_meta.wait()
    to_scalar = pltpu.make_async_copy(meta_vm, meta_sm, meta_local)
    to_scalar.start()
    relay_step(0, 0)
    begin(2)
    begin_own(2)
    to_scalar.wait()
    forward(1)

    row_ids = lax.broadcasted_iota(jnp.int32, (4 * HD, 4 * HD), 0) // HD
    col_ids = lax.broadcasted_iota(jnp.int32, (4 * HD, 4 * HD), 1) // HD
    spread = jnp.where(
        row_ids == col_ids, jnp.where(col_ids < 2, FACTOR, 1.0), 0.0
    ).astype(jnp.bfloat16)
    apart = jnp.where(row_ids == col_ids, jnp.where(col_ids < 2, FACTOR, 1.0), 0.0)
    eye = (
        lax.broadcasted_iota(jnp.int32, (4 * HD, 4 * HD), 0)
        == lax.broadcasted_iota(jnp.int32, (4 * HD, 4 * HD), 1)
    ).astype(jnp.bfloat16)
    gather_rows = (
        lax.broadcasted_iota(jnp.int32, (BLOCK, 4 * HD), 0)
        == lax.rem(lax.broadcasted_iota(jnp.int32, (BLOCK, 4 * HD), 1), BLOCK)
    ).astype(jnp.bfloat16)
    left_half = lax.broadcasted_iota(jnp.int32, (4 * HD, LANES), 1) < BLOCK

    def across_lanes(left, right):
        return lax.dot_general(
            left, right, (((1,), (1,)), ((), ())), preferred_element_type=jnp.float32
        )

    def turn(step, carry):
        blocks = [work[4 * step + k] for k in range(4)]
        straight = across_lanes(eye, jnp.concatenate(blocks, axis=0))
        crossed = across_lanes(eye, jnp.concatenate([blocks[k ^ 1] for k in range(4)], axis=0))
        for k in range(4):
            lanes = slice((k // 2) * LANES, (k // 2 + 1) * LANES)
            left, right = (straight, crossed) if k % 2 == 0 else (crossed, straight)
            low[4 * step + k] = jnp.where(left_half, left[:, lanes], 0.0).astype(jnp.bfloat16)
            high[4 * step + k] = jnp.where(left_half, 0.0, right[:, lanes]).astype(jnp.bfloat16)
        return carry

    def fold(array, op):
        return op(array.reshape(array.shape[0] // 8, 8, LANES), axis=0)

    def attend(g, b):
        strip, row = b // HALF, lax.rem(b, HALF)
        part = qd[g, b]
        diagonal = jnp.concatenate([part] * 4, axis=0) * spread
        picked = jnp.concatenate(
            [work[meta_sm[strip, row, j]] for j in range(SEL)], axis=0
        )
        both = across_lanes(picked, diagonal)
        bias = [
            jnp.where(meta_sm[strip, HALF + row, j] > 0, 0.0, MASKED).astype(jnp.float32)
            for j in range(SEL)
        ]
        parts = [both[j * BLOCK:(j + 1) * BLOCK, :LANES] for j in range(SEL)]
        peak = fold(parts[0], jnp.max) + bias[0]
        for j in range(1, SEL):
            peak = jnp.maximum(peak, fold(parts[j], jnp.max) + bias[j])
        peak = jnp.max(peak, axis=0, keepdims=True)
        powers = [jnp.exp(parts[j] - (peak - bias[j])) for j in range(SEL)]
        grad_weights = [both[j * BLOCK:(j + 1) * BLOCK, LANES:] for j in range(SEL)]
        total = fold(powers[0], jnp.sum)
        dots = fold(powers[0] * grad_weights[0], jnp.sum)
        for j in range(1, SEL):
            total = total + fold(powers[j], jnp.sum)
            dots = dots + fold(powers[j] * grad_weights[j], jnp.sum)
        scale = 1.0 / jnp.sum(total, axis=0, keepdims=True)
        row_dots = jnp.sum(dots, axis=0, keepdims=True) * scale
        slabs = []
        for j in range(SEL):
            weights = powers[j] * scale
            grad_scores = weights * (grad_weights[j] - row_dots)
            slabs.append(jnp.concatenate([grad_scores, weights], axis=1).astype(jnp.bfloat16))
        slab = jnp.concatenate(slabs, axis=0)
        terms = jnp.dot(slab, diagonal, preferred_element_type=jnp.float32)
        tiles[b, :SEL] = terms.reshape(SEL, BLOCK, 2 * LANES)
        turned = []
        for j in range(0, SEL, 2):
            pair = low[meta_sm[strip, row, j]]
            if j + 1 < SEL:
                pair = pair + high[meta_sm[strip, row, j + 1]]
            turned.append(pair)
        padded = jnp.concatenate([slab, jnp.zeros((BLOCK, 2 * LANES), jnp.bfloat16)], axis=0)
        mixed = jnp.dot(
            jnp.concatenate(turned, axis=1), padded, preferred_element_type=jnp.float32
        )
        rows_out[g, b] = across_lanes(gather_rows, (mixed * apart).astype(jnp.bfloat16)).astype(jnp.bfloat16)

    def finish(g):
        slot = lax.rem(g, 2)
        for d in range(2):
            for part in range(2):
                wait_terms(g, d, part).wait_recv()

        def add(w, carry):
            total = own[slot, w] + take[g, 0, w].astype(jnp.float32) + take[g, 1, w].astype(jnp.float32)
            final[g, w] = total.astype(jnp.bfloat16)
            return carry

        lax.fori_loop(0, FRAME, add, 0)
        grads_across(g).start()
        for a in range(2):
            grads_along(g, a).start()
        rows_across(g).wait_recv()
        for a in range(2):
            rows_back(g, a).start()

    def one_group(g, carry):
        swap(g, 1).wait_recv()
        for d in range(2):
            for part in range(2):
                wait_pass(g, d, part).wait_recv()

        @pl.when(g + 3 < GROUPS)
        def _():
            begin(g + 3)
            begin_own(g + 3)

        work[...] = kv[g]
        lax.fori_loop(0, WINDOW // 4, turn, 0)

        def four_blocks(i, inner):
            first = lax.rem(HALF * o + HALF * i, FRAME)
            for b in range(HALF):
                attend(g, first + b)

            @pl.when((i == 0) & (g > 1))
            def _():
                finish(g - 2)

            @pl.when(i == 0)
            def _():
                rows_across(g).start()

                @pl.when(g + 2 < GROUPS)
                def _():
                    forward(g + 2)

            @pl.when((i == 0) & (g == 0))
            def _():
                relay_step(1, 0)

            @pl.when((i == 0) & (g > 0))
            def _():
                relay_step(g - 1, 1)

            @pl.when((i == 1) & (g + 2 < GROUPS))
            def _():
                relay_step(g + 2, 0)

            return inner

        lax.fori_loop(0, 2, four_blocks, 0)
        for a in range(2):
            rows_along(g, a).start()

        def gather(w, base):
            acc = None
            for b in range(FRAME):
                place = meta_sm[b // HALF, b % HALF, PLACE_AT + base + w]
                tile = tiles[b, place]
                acc = tile if acc is None else acc + tile
            return acc

        def collect(w, inner):
            give[g, 1, w] = gather(w, 0).astype(jnp.bfloat16)
            give[g, 0, w] = gather(w, 2 * FRAME).astype(jnp.bfloat16)
            return inner

        lax.fori_loop(0, FRAME, collect, 0)
        for d in range(2):
            for part in range(2):
                start_terms(g, d, part)

        def collect_own(w, inner):
            own[lax.rem(g, 2), w] = gather(w, FRAME)
            return inner

        lax.fori_loop(0, FRAME, collect_own, 0)

        return carry

    lax.fori_loop(0, GROUPS, one_group, 0)
    finish(GROUPS - 2)
    relay_step(GROUPS - 1, 1)
    finish(GROUPS - 1)

    def land(g, carry):
        grads_across(g).wait_recv()
        for a in range(2):
            grads_back(g, a).start()
        return carry

    lax.fori_loop(0, GROUPS, land, 0)

    def drain(g, carry):
        for pair in range(2):
            swap(g, pair).wait_send()
        for d in range(2):
            for part in range(2):
                wait_pass(g, d, part).wait_send()
                wait_terms(g, d, part).wait_send()

        @pl.when(is_relay)
        def _():
            for phase in range(2):
                relay_on(g, phase).wait_send()

        rows_across(g).wait_send()
        grads_across(g).wait_send()
        for a in range(2):
            rows_along(g, a).wait()
            grads_along(g, a).wait()
            rows_back(g, a).wait()
            grads_back(g, a).wait()
        return carry

    lax.fori_loop(0, GROUPS, drain, 0)


def hand_over(*refs):
    sources, targets, held, in_sems, out_sems = refs[:4], refs[4:8], refs[8], refs[9], refs[10]
    spots = [(i, at) for i in range(4) for at in range(HALF)]
    ins = [pltpu.make_async_copy(sources[i].at[at], held.at[i, at], in_sems.at[i, at]) for i, at in spots]
    outs = [pltpu.make_async_copy(held.at[i, at], targets[i].at[at], out_sems.at[i, at]) for i, at in spots]
    for copy in ins:
        copy.start()
    for arrives, leaves in zip(ins, outs):
        arrives.wait()
        leaves.start()
    for copy in outs:
        copy.wait()


def body(queries, keys, values, out_grad, block_list, block_count):
    rows, width = queries.shape
    frames = lax.axis_size("frames")
    blocked = [x.reshape(HALF, BLOCK, width) for x in (queries, keys, values, out_grad)]
    shape = jax.ShapeDtypeStruct((HALF, BLOCK, width), jnp.bfloat16)
    dma = pltpu.SemaphoreType.DMA
    flops = 6 * 2 * FRAME * SEL * BLOCK * 256 * 256 * GROUPS
    outs = pl.pallas_call(
        lambda *refs: kernel(frames, *refs),
        out_shape=[shape] * 4,
        in_specs=[pl.BlockSpec(memory_space=pltpu.VMEM), pl.BlockSpec(memory_space=pltpu.SMEM)] + [pl.BlockSpec(memory_space=pl.ANY)] * 4,
        out_specs=[pl.BlockSpec(memory_space=pl.ANY)] * 4,
        scratch_shapes=[
            pltpu.VMEM((4, HALF, BLOCK, width), jnp.bfloat16),
            pltpu.VMEM((GROUPS, 2, HALF, BLOCK, 2 * LANES), jnp.bfloat16),
            pltpu.VMEM((GROUPS, WINDOW, BLOCK, 2 * LANES), jnp.bfloat16),
            pltpu.VMEM((GROUPS, FRAME, BLOCK, 2 * LANES), jnp.bfloat16),
            pltpu.VMEM((WINDOW, BLOCK, 2 * LANES), jnp.bfloat16),
            pltpu.VMEM((WINDOW, 2 * LANES, LANES), jnp.bfloat16),
            pltpu.VMEM((WINDOW, 2 * LANES, LANES), jnp.bfloat16),
            pltpu.VMEM((FRAME, SEL + 1, BLOCK, 2 * LANES), jnp.float32),
            pltpu.VMEM((GROUPS, FRAME, BLOCK, 2 * LANES), jnp.bfloat16),
            pltpu.VMEM((GROUPS, HALF, BLOCK, 2 * LANES), jnp.bfloat16),
            pltpu.VMEM((GROUPS, 2, FRAME, BLOCK, 2 * LANES), jnp.bfloat16),
            pltpu.VMEM((GROUPS, 2, FRAME, BLOCK, 2 * LANES), jnp.bfloat16),
            pltpu.VMEM((2, FRAME, BLOCK, 2 * LANES), jnp.float32),
            pltpu.VMEM((GROUPS, FRAME, BLOCK, 2 * LANES), jnp.bfloat16),
            pltpu.VMEM((GROUPS, HALF, BLOCK, 2 * LANES), jnp.bfloat16),
            pltpu.VMEM((2, GROUPS, HALF, BLOCK, 2 * LANES), jnp.bfloat16),
            pltpu.VMEM((2, 8, LANES), jnp.int32),
            pltpu.SMEM((2, 8, LANES), jnp.int32),
            dma((4,)), dma((GROUPS, 2)), dma((GROUPS, 2)),
            dma((GROUPS, 2, 2)), dma((GROUPS, 2, 2)),
            dma, dma, dma,
            dma((GROUPS,)), dma((GROUPS,)), dma((2 * GROUPS, 2)),
            dma((GROUPS, 2, 2)), dma((GROUPS, 2, 2)),
            dma((GROUPS,)), dma((GROUPS,)), dma((2 * GROUPS, 2)),
            dma((2, GROUPS)), dma((2, GROUPS)),
        ],
        cost_estimate=pl.CostEstimate(
            flops=flops, bytes_accessed=16 * rows * width, transcendentals=FRAME * SEL * BLOCK * LANES * GROUPS
        ),
        compiler_params=pltpu.CompilerParams(
            collective_id=0, has_side_effects=True, vmem_limit_bytes=60 * 1024 * 1024
        ),
    )(block_list, block_count, *blocked)
    outs = pl.pallas_call(
        hand_over,
        out_shape=[shape] * 4,
        in_specs=[pl.BlockSpec(memory_space=pl.ANY)] * 4,
        out_specs=[pl.BlockSpec(memory_space=pl.ANY)] * 4,
        scratch_shapes=[
            pltpu.VMEM((4, HALF, BLOCK, width), jnp.bfloat16), dma((4, HALF)), dma((4, HALF)),
        ],
        compiler_params=pltpu.CompilerParams(vmem_limit_bytes=60 * 1024 * 1024),
    )(*outs)
    return tuple(x.reshape(rows, width) for x in outs)


def solution(mesh):
    split = P(("frames", "strip"), None)
    in_specs = (split, split, split, split, split, P(("frames", "strip")))
    return jax.shard_map(
        body, mesh=mesh, in_specs=in_specs, out_specs=(split,) * 4, check_vma=False
    )
```

```python
import jax
import jax.numpy as jnp
from jax import lax
from jax.experimental import pallas as pl
from jax.experimental.pallas import tpu as pltpu
from jax.sharding import PartitionSpec as P

HD = 64
BLOCK = 64
SEL = 13
HALF = 4
FRAME = 8
WINDOW = 24
GROUPS = 4
LANES = 128
FACTOR = 0.125
MASKED = -1e30
PLACE_AT = 32
RUN = 8
MESH = pl.DeviceIdType.MESH


def kernel(
    frames,
    block_list, block_count, queries, keys, values, out_grad,
    attended, query_grad, key_grad, value_grad,
    loaded, packed, kv, qd, work, tiles, rows_out, rows_in, give, take, own, final, final_in, relay, meta_vm, meta_sm,
    load_sem, in_send, in_recv, pass_send, pass_recv,
    meta_send, meta_recv, meta_local, row_send, row_recv, row_local,
    term_send, term_recv, grad_send, grad_recv, grad_local, relay_send, relay_recv,
):
    f, s = lax.axis_index("frames"), lax.axis_index("strip")
    o = 1 - s
    after, before = lax.rem(f + 1, frames), lax.rem(f + frames - 1, frames)
    partner, next_dev, prev_dev = (f, o), (after, s), (before, s)

    sources = (keys, values, queries, out_grad)
    loads = [pltpu.make_async_copy(sources[a], loaded.at[a], load_sem.at[a]) for a in range(4)]
    for load in loads:
        load.start()

    place_in_run = lax.rem(f, RUN)
    edge = (place_in_run == RUN - 1, place_in_run == 0)
    part_column = (3 * s, 1 + s)

    def relay_of(d, column):
        return (f - 2 * column if d == 0 else f + 2 * column, s)

    def relay_to(d, column):
        if d == 0:
            return (lax.rem(f + 1 + 2 * column, frames), s)
        return (lax.rem(f + frames - 1 - 2 * column, frames), s)

    relay_back = 1 - lax.rem(place_in_run, 2)
    relay_column = lax.select(relay_back == 0, (RUN - 1 - place_in_run) // 2, place_in_run // 2)
    is_relay = ((relay_column == 1) & (s == 0)) | ((relay_column >= 2) & (s == 1))
    relay_half = lax.rem(relay_column, 2)
    relay_source_frame = f - place_in_run + (1 - relay_back) * (RUN - 1)
    relay_target_frame = lax.rem(relay_source_frame + frames + 1 - 2 * relay_back, frames)
    relay_target, relay_source = (relay_target_frame, s), (relay_source_frame, s)

    barrier = pltpu.get_barrier_semaphore()

    def greet(device):
        pl.semaphore_signal(barrier, inc=1, device_id=device, device_id_type=MESH)

    for device in (partner, next_dev, prev_dev):
        greet(device)

    @pl.when(is_relay)
    def _():
        greet(relay_source)
        greet(relay_target)

    for d in range(2):
        for column in (1, 2, 3):
            @pl.when(edge[d] & (s == (0 if column == 1 else 1)))
            def _():
                greet(relay_of(d, column))
                greet(relay_to(d, column))

    at_end = (edge[0] | edge[1]).astype(jnp.int32)
    pl.semaphore_wait(barrier, 3 + 2 * is_relay.astype(jnp.int32) + at_end * (2 + 2 * s))

    def remote(src, dst, send, recv, device):
        return pltpu.make_async_remote_copy(
            src_ref=src, dst_ref=dst, send_sem=send, recv_sem=recv,
            device_id=device, device_id_type=MESH,
        )

    def columns(half, g):
        return pl.ds(pl.multiple_of(half * (GROUPS * LANES) + g * LANES, LANES), LANES)

    def landing(g, pair, half):
        if pair == 0:
            return kv.at[g, pl.ds(FRAME + HALF * half, HALF)]
        return qd.at[g, pl.ds(HALF * half, HALF)]

    def swap(g, pair):
        return remote(
            packed.at[g, pair], landing(g, pair, s), in_send.at[g, pair], in_recv.at[g, pair], partner
        )

    def pack(g, pair):
        for a in range(2):
            lanes = slice(a * LANES, (a + 1) * LANES)
            packed[g, pair, :, :, lanes] = loaded[2 * pair + a, :, :, columns(o, g)]

    def keep(g, pair):
        own_rows = landing(g, pair, s)
        for a in range(2):
            lanes = slice(a * LANES, (a + 1) * LANES)
            own_rows[:, :, lanes] = loaded[2 * pair + a, :, :, columns(s, g)]

    neighbours = (next_dev, prev_dev)

    def start_part(d, part, src, dst, send, recv, phase, g):
        straight = remote(src, dst, send, recv, neighbours[d])
        if part == 0:
            bent = edge[d] & (s == 1)
        else:
            bent = edge[d]

        @pl.when(bent)
        def _():
            remote(
                src, relay.at[phase, g], send, relay_recv.at[phase, g], relay_of(d, part_column[part])
            ).start()

        @pl.when(jnp.logical_not(bent))
        def _():
            straight.start()

    def kv_window(g, base, half):
        return kv.at[g, pl.ds(base + HALF * half, HALF)]

    def pass_args(g, d, part):
        half = (s, o)[part]
        return (
            kv_window(g, FRAME, half), kv_window(g, (0, 2 * FRAME)[d], half),
            pass_send.at[g, d, half], pass_recv.at[g, d, half],
        )

    def start_pass(g, d, part):
        start_part(d, part, *pass_args(g, d, part), 0, g)

    def wait_pass(g, d, part):
        return remote(*pass_args(g, d, part), neighbours[d])

    def term_args(g, d, part):
        half = (s, o)[part]
        at = pl.ds(HALF * half, HALF)
        return (
            give.at[g, d, at], take.at[g, d, at], term_send.at[g, d, half], term_recv.at[g, d, half]
        )

    def start_terms(g, d, part):
        start_part(d, part, *term_args(g, d, part), 1, g)

    def wait_terms(g, d, part):
        return remote(*term_args(g, d, part), neighbours[d])

    def relay_on(g, phase):
        if phase == 0:
            target = kv_window(g, relay_back * (2 * FRAME), relay_half)
            recv = pass_recv.at[g, relay_back, relay_half]
        else:
            target = take.at[g, relay_back, pl.ds(HALF * relay_half, HALF)]
            recv = term_recv.at[g, relay_back, relay_half]
        return remote(relay.at[phase, g], target, relay_send.at[phase, g], recv, relay_target)

    def relay_step(g, phase):
        @pl.when(is_relay)
        def _():
            remote(
                relay.at[phase, g], relay.at[phase, g], relay_send.at[phase, g],
                relay_recv.at[phase, g], relay_target,
            ).wait_recv()
            relay_on(g, phase).start()

    def rows_across(g):
        return remote(
            rows_out.at[g, pl.ds(HALF * o, HALF)], rows_in.at[g], row_send.at[g], row_recv.at[g], partner
        )

    def grads_across(g):
        return remote(
            final.at[g, pl.ds(HALF * o, HALF)], final_in.at[g], grad_send.at[g], grad_recv.at[g], partner
        )

    row_targets, grad_targets = (query_grad, attended), (key_grad, value_grad)

    def place_copy(staged, targets, local, g, half, a):
        return pltpu.make_async_copy(
            staged.at[:, :, pl.ds(a * LANES, LANES)], targets[a].at[:, :, columns(half, g)], local.at[g, a]
        )

    def rows_along(g, a):
        return place_copy(rows_out.at[g, pl.ds(HALF * s, HALF)], row_targets, row_local, g, s, a)

    def grads_along(g, a):
        return place_copy(final.at[g, pl.ds(HALF * s, HALF)], grad_targets, grad_local, g, s, a)

    def rows_back(g, a):
        return place_copy(rows_in.at[g], row_targets, row_local.at[pl.ds(GROUPS, GROUPS)], g, o, a)

    def grads_back(g, a):
        return place_copy(final_in.at[g], grad_targets, grad_local.at[pl.ds(GROUPS, GROUPS)], g, o, a)

    share_meta = remote(meta_vm.at[s], meta_vm.at[s], meta_send, meta_recv, partner)

    def begin(g):
        for pair in range(2):
            pack(g, pair)
            swap(g, pair).start()

    def begin_own(g):
        keep(g, 0)
        for d in range(2):
            start_pass(g, d, 0)
        keep(g, 1)

    for pair in range(2):
        loads[2 * pair].wait()
        loads[2 * pair + 1].wait()
        pack(0, pair)
        swap(0, pair).start()
        keep(0, pair)
        if pair == 0:
            for d in range(2):
                start_pass(0, d, 0)

    listed = block_list[...]
    row_at = lax.broadcasted_iota(jnp.int32, (HALF, LANES), 0)
    lane_at = lax.broadcasted_iota(jnp.int32, (HALF, LANES), 1)
    counts = jnp.zeros((HALF, LANES), jnp.int32)
    for row in range(HALF):
        counts = jnp.where(row_at == row, block_count[row], counts)
    edge_low = jnp.where(f > 0, 0, FRAME)
    edge_high = jnp.where(f < frames - 1, WINDOW, 2 * FRAME)
    usable = (listed >= edge_low) & (listed < edge_high) & (lane_at[:, :SEL] < counts[:, :SEL])
    slots = jnp.where(usable, listed, -1)
    place = jnp.full((HALF, LANES), SEL, jnp.int32)
    for j in range(SEL):
        place = jnp.where(lane_at - PLACE_AT == slots[:, j:j + 1], j, place)
    meta_vm[s, 0:HALF] = place
    meta_vm[s, 0:HALF, 0:SEL] = listed
    meta_vm[s, HALF:] = jnp.zeros((HALF, LANES), jnp.int32)
    meta_vm[s, HALF:, 0:SEL] = usable.astype(jnp.int32)
    share_meta.start()
    begin(1)
    begin_own(1)
    tiles[:, SEL] = jnp.zeros((FRAME, BLOCK, 2 * LANES), jnp.float32)

    def forward(g):
        swap(g, 0).wait_recv()
        for d in range(2):
            start_pass(g, d, 1)

    forward(0)
    share_meta.wait()
    to_scalar = pltpu.make_async_copy(meta_vm, meta_sm, meta_local)
    to_scalar.start()
    relay_step(0, 0)
    begin(2)
    begin_own(2)
    to_scalar.wait()
    forward(1)

    row_ids = lax.broadcasted_iota(jnp.int32, (4 * HD, 4 * HD), 0) // HD
    col_ids = lax.broadcasted_iota(jnp.int32, (4 * HD, 4 * HD), 1) // HD
    spread = jnp.where(
        row_ids == col_ids, jnp.where(col_ids < 2, FACTOR, 1.0), 0.0
    ).astype(jnp.bfloat16)
    first_head = lax.broadcasted_iota(jnp.int32, (BLOCK, LANES), 1) < HD

    def heads(full):
        return jnp.where(first_head, full[:HD], full[HD:])

    def fold(array, op):
        return op(array.reshape(array.shape[0] // 8, 8, LANES), axis=0)

    def attend(g, b):
        strip, row = b // HALF, lax.rem(b, HALF)
        chunks = ((0, 4), (4, 8), (8, SEL))
        keep = {"slabs": [None] * SEL, "powers": [None] * SEL}

        def diagonal():
            keep["diagonal"] = jnp.concatenate([qd[g, b]] * 4, axis=0) * spread
            keep["bias"] = [
                jnp.where(meta_sm[strip, HALF + row, j] > 0, 0.0, MASKED).astype(jnp.float32)
                for j in range(SEL)
            ]

        def products(c):
            low, high = chunks[c]
            picked = jnp.concatenate([work[meta_sm[strip, row, j]] for j in range(low, high)], axis=0)
            keep["picked", c] = picked
            both = lax.dot_general(
                picked, keep["diagonal"], (((1,), (1,)), ((), ())), preferred_element_type=jnp.float32
            )
            for j in range(low, high):
                at = slice((j - low) * BLOCK, (j - low + 1) * BLOCK)
                keep["scores", j] = both[at, :LANES]
                keep["grad_weights", j] = both[at, LANES:]

        def peak(c):
            for j in range(*chunks[c]):
                top = fold(keep["scores", j], jnp.max) + keep["bias"][j]
                keep["peak"] = jnp.maximum(keep["peak"], top) if j else top
            if c == len(chunks) - 1:
                keep["peak"] = jnp.max(keep["peak"], axis=0, keepdims=True)

        def power(j):
            powers = jnp.exp(keep["scores", j] - (keep["peak"] - keep["bias"][j]))
            keep["powers"][j] = powers
            total = fold(powers, jnp.sum)
            dots = fold(powers * keep["grad_weights", j], jnp.sum)
            keep["total"] = keep["total"] + total if j else total
            keep["dots"] = keep["dots"] + dots if j else dots
            if j == SEL - 1:
                keep["scale"] = 1.0 / jnp.sum(keep["total"], axis=0, keepdims=True)
                keep["row_dots"] = jnp.sum(keep["dots"], axis=0, keepdims=True) * keep["scale"]

        def slab(j):
            weights = keep["powers"][j] * keep["scale"]
            grad_scores = weights * (keep["grad_weights", j] - keep["row_dots"])
            keep["slabs"][j] = (grad_scores.astype(jnp.bfloat16), weights.astype(jnp.bfloat16))

        def terms(c):
            low, high = chunks[c]
            parts = [jnp.concatenate([pair[k] for pair in keep["slabs"][low:high]], axis=0) for k in range(2)]
            keep["parts", c] = parts
            result = jnp.dot(
                jnp.concatenate(parts, axis=1), keep["diagonal"], preferred_element_type=jnp.float32
            )
            tiles[b, low:high] = result.reshape(high - low, BLOCK, 2 * LANES)

        def mixed(c):
            for k in range(2):
                lanes = slice(k * LANES, (k + 1) * LANES)
                product = lax.dot_general(
                    keep["parts", c][k], keep["picked", c][:, lanes], (((0,), (0,)), ((), ())),
                    preferred_element_type=jnp.float32,
                )
                keep["mixed", k] = keep["mixed", k] + product if c else product
            if c == len(chunks) - 1:
                rows_out[g, b] = jnp.concatenate(
                    [heads(keep["mixed", 0]) * FACTOR, heads(keep["mixed", 1])], axis=1
                ).astype(jnp.bfloat16)

        def call(function, *args):
            return lambda: function(*args)

        count = range(len(chunks))
        return (
            [diagonal] + [call(products, c) for c in count],
            [call(peak, c) for c in count] + [call(power, j) for j in range(SEL)] + [call(slab, j) for j in range(SEL)],
            [call(step, c) for c in count for step in (terms, mixed)],
        )

    def interleave(stages):
        placed = [
            ((k + 0.5) / len(stage), n, step)
            for n, stage in enumerate(stages)
            for k, step in enumerate(stage)
        ]
        for _, _, step in sorted(placed, key=lambda item: item[:2]):
            step()

    def finish(g):
        slot = lax.rem(g, 2)
        for d in range(2):
            for part in range(2):
                wait_terms(g, d, part).wait_recv()

        def add(w, carry):
            total = own[slot, w] + take[g, 0, w].astype(jnp.float32) + take[g, 1, w].astype(jnp.float32)
            final[g, w] = total.astype(jnp.bfloat16)
            return carry

        lax.fori_loop(0, FRAME, add, 0)
        grads_across(g).start()
        for a in range(2):
            grads_along(g, a).start()
        rows_across(g).wait_recv()
        for a in range(2):
            rows_back(g, a).start()

    def one_group(g, carry):
        swap(g, 1).wait_recv()
        for d in range(2):
            for part in range(2):
                wait_pass(g, d, part).wait_recv()

        @pl.when(g + 3 < GROUPS)
        def _():
            begin(g + 3)
            begin_own(g + 3)

        work[...] = kv[g]

        blocks = [attend(g, lax.rem(HALF * o + i, FRAME)) for i in range(FRAME)]
        for turn in range(FRAME + 2):
            interleave([blocks[turn - k][k] for k in (2, 1, 0) if 0 <= turn - k < FRAME])
            if turn == HALF + 1:
                rows_across(g).start()

                @pl.when(g > 1)
                def _():
                    finish(g - 2)

                @pl.when(g + 2 < GROUPS)
                def _():
                    forward(g + 2)

                @pl.when(g == 0)
                def _():
                    relay_step(1, 0)

                @pl.when(g > 0)
                def _():
                    relay_step(g - 1, 1)

        @pl.when(g + 2 < GROUPS)
        def _():
            relay_step(g + 2, 0)

        for a in range(2):
            rows_along(g, a).start()

        def gather(w, base):
            acc = None
            for b in range(FRAME):
                place = meta_sm[b // HALF, b % HALF, PLACE_AT + base + w]
                tile = tiles[b, place]
                acc = tile if acc is None else acc + tile
            return acc

        def collect(w, inner):
            give[g, 1, w] = gather(w, 0).astype(jnp.bfloat16)
            give[g, 0, w] = gather(w, 2 * FRAME).astype(jnp.bfloat16)
            return inner

        lax.fori_loop(0, FRAME, collect, 0)
        for d in range(2):
            for part in range(2):
                start_terms(g, d, part)

        def collect_own(w, inner):
            own[lax.rem(g, 2), w] = gather(w, FRAME)
            return inner

        lax.fori_loop(0, FRAME, collect_own, 0)

        return carry

    lax.fori_loop(0, GROUPS, one_group, 0)
    finish(GROUPS - 2)
    relay_step(GROUPS - 1, 1)
    finish(GROUPS - 1)

    def land(g, carry):
        grads_across(g).wait_recv()
        for a in range(2):
            grads_back(g, a).start()
        return carry

    lax.fori_loop(0, GROUPS, land, 0)

    def drain(g, carry):
        for pair in range(2):
            swap(g, pair).wait_send()
        for d in range(2):
            for part in range(2):
                wait_pass(g, d, part).wait_send()
                wait_terms(g, d, part).wait_send()

        @pl.when(is_relay)
        def _():
            for phase in range(2):
                relay_on(g, phase).wait_send()

        rows_across(g).wait_send()
        grads_across(g).wait_send()
        for a in range(2):
            rows_along(g, a).wait()
            grads_along(g, a).wait()
            rows_back(g, a).wait()
            grads_back(g, a).wait()
        return carry

    lax.fori_loop(0, GROUPS, drain, 0)


def hand_over(*refs):
    sources, targets, held, in_sems, out_sems = refs[:4], refs[4:8], refs[8], refs[9], refs[10]
    spots = [(i, at) for i in range(4) for at in range(HALF)]
    ins = [pltpu.make_async_copy(sources[i].at[at], held.at[i, at], in_sems.at[i, at]) for i, at in spots]
    outs = [pltpu.make_async_copy(held.at[i, at], targets[i].at[at], out_sems.at[i, at]) for i, at in spots]
    for copy in ins:
        copy.start()
    for arrives, leaves in zip(ins, outs):
        arrives.wait()
        leaves.start()
    for copy in outs:
        copy.wait()


def body(queries, keys, values, out_grad, block_list, block_count):
    rows, width = queries.shape
    frames = lax.axis_size("frames")
    blocked = [x.reshape(HALF, BLOCK, width) for x in (queries, keys, values, out_grad)]
    shape = jax.ShapeDtypeStruct((HALF, BLOCK, width), jnp.bfloat16)
    dma = pltpu.SemaphoreType.DMA
    flops = 6 * 2 * FRAME * SEL * BLOCK * 256 * 256 * GROUPS
    outs = pl.pallas_call(
        lambda *refs: kernel(frames, *refs),
        out_shape=[shape] * 4,
        in_specs=[pl.BlockSpec(memory_space=pltpu.VMEM), pl.BlockSpec(memory_space=pltpu.SMEM)] + [pl.BlockSpec(memory_space=pl.ANY)] * 4,
        out_specs=[pl.BlockSpec(memory_space=pl.ANY)] * 4,
        scratch_shapes=[
            pltpu.VMEM((4, HALF, BLOCK, width), jnp.bfloat16),
            pltpu.VMEM((GROUPS, 2, HALF, BLOCK, 2 * LANES), jnp.bfloat16),
            pltpu.VMEM((GROUPS, WINDOW, BLOCK, 2 * LANES), jnp.bfloat16),
            pltpu.VMEM((GROUPS, FRAME, BLOCK, 2 * LANES), jnp.bfloat16),
            pltpu.VMEM((WINDOW, BLOCK, 2 * LANES), jnp.bfloat16),
            pltpu.VMEM((FRAME, SEL + 1, BLOCK, 2 * LANES), jnp.float32),
            pltpu.VMEM((GROUPS, FRAME, BLOCK, 2 * LANES), jnp.bfloat16),
            pltpu.VMEM((GROUPS, HALF, BLOCK, 2 * LANES), jnp.bfloat16),
            pltpu.VMEM((GROUPS, 2, FRAME, BLOCK, 2 * LANES), jnp.bfloat16),
            pltpu.VMEM((GROUPS, 2, FRAME, BLOCK, 2 * LANES), jnp.bfloat16),
            pltpu.VMEM((2, FRAME, BLOCK, 2 * LANES), jnp.float32),
            pltpu.VMEM((GROUPS, FRAME, BLOCK, 2 * LANES), jnp.bfloat16),
            pltpu.VMEM((GROUPS, HALF, BLOCK, 2 * LANES), jnp.bfloat16),
            pltpu.VMEM((2, GROUPS, HALF, BLOCK, 2 * LANES), jnp.bfloat16),
            pltpu.VMEM((2, 8, LANES), jnp.int32),
            pltpu.SMEM((2, 8, LANES), jnp.int32),
            dma((4,)), dma((GROUPS, 2)), dma((GROUPS, 2)),
            dma((GROUPS, 2, 2)), dma((GROUPS, 2, 2)),
            dma, dma, dma,
            dma((GROUPS,)), dma((GROUPS,)), dma((2 * GROUPS, 2)),
            dma((GROUPS, 2, 2)), dma((GROUPS, 2, 2)),
            dma((GROUPS,)), dma((GROUPS,)), dma((2 * GROUPS, 2)),
            dma((2, GROUPS)), dma((2, GROUPS)),
        ],
        cost_estimate=pl.CostEstimate(
            flops=flops, bytes_accessed=16 * rows * width, transcendentals=FRAME * SEL * BLOCK * LANES * GROUPS
        ),
        compiler_params=pltpu.CompilerParams(
            collective_id=0, has_side_effects=True, vmem_limit_bytes=60 * 1024 * 1024
        ),
    )(block_list, block_count, *blocked)
    outs = pl.pallas_call(
        hand_over,
        out_shape=[shape] * 4,
        in_specs=[pl.BlockSpec(memory_space=pl.ANY)] * 4,
        out_specs=[pl.BlockSpec(memory_space=pl.ANY)] * 4,
        scratch_shapes=[
            pltpu.VMEM((4, HALF, BLOCK, width), jnp.bfloat16), dma((4, HALF)), dma((4, HALF)),
        ],
        compiler_params=pltpu.CompilerParams(vmem_limit_bytes=60 * 1024 * 1024),
    )(*outs)
    return tuple(x.reshape(rows, width) for x in outs)


def solution(mesh):
    split = P(("frames", "strip"), None)
    in_specs = (split, split, split, split, split, P(("frames", "strip")))
    return jax.shard_map(
        body, mesh=mesh, in_specs=in_specs, out_specs=(split,) * 4, check_vma=False
    )
```

```python
import jax
import jax.numpy as jnp
from jax import lax
from jax.experimental import pallas as pl
from jax.experimental.pallas import tpu as pltpu
from jax.sharding import PartitionSpec as P

HD = 64
BLOCK = 64
SEL = 13
HALF = 4
FRAME = 8
WINDOW = 24
GROUPS = 4
LANES = 128
FACTOR = 0.125
MASKED = -1e30
PLACE_AT = 32
RUN = 8
MESH = pl.DeviceIdType.MESH


def kernel(
    frames,
    block_list, block_count, queries, keys, values, out_grad,
    attended, query_grad, key_grad, value_grad,
    loaded, packed, kv, qd, work, tiles, rows_out, rows_in, give, take, own, final, final_in, relay, meta_vm, meta_sm,
    load_sem, in_send, in_recv, pass_send, pass_recv,
    meta_send, meta_recv, meta_local, row_send, row_recv, row_local,
    term_send, term_recv, grad_send, grad_recv, grad_local, relay_send, relay_recv,
):
    f, s = lax.axis_index("frames"), lax.axis_index("strip")
    o = 1 - s
    partner, next_dev, prev_dev = (f, o), (f + 1, s), (f - 1, s)

    sources = (keys, values, queries, out_grad)
    loads = [pltpu.make_async_copy(sources[a], loaded.at[a], load_sem.at[a]) for a in range(4)]
    for load in loads:
        load.start()

    place_in_run = lax.rem(f, RUN)
    has_after, has_before = f < frames - 1, f > 0
    edge = ((place_in_run == RUN - 1) & has_after, (place_in_run == 0) & has_before)
    part_column = (3 * s, 1 + s)

    def relay_of(d, column):
        return (f - 2 * column if d == 0 else f + 2 * column, s)

    def relay_to(d, column):
        return (f + 1 + 2 * column if d == 0 else f - 1 - 2 * column, s)

    relay_back = 1 - lax.rem(place_in_run, 2)
    relay_column = lax.select(relay_back == 0, (RUN - 1 - place_in_run) // 2, place_in_run // 2)
    relay_half = lax.rem(relay_column, 2)
    relay_source_frame = f - place_in_run + (1 - relay_back) * (RUN - 1)
    relay_target_frame = relay_source_frame + 1 - 2 * relay_back
    is_relay = ((relay_column == 1) & (s == 0)) | ((relay_column >= 2) & (s == 1))
    is_relay = is_relay & (relay_target_frame >= 0) & (relay_target_frame < frames)
    relay_target, relay_source = (relay_target_frame, s), (relay_source_frame, s)

    barrier = pltpu.get_barrier_semaphore()

    def greet(device):
        pl.semaphore_signal(barrier, inc=1, device_id=device, device_id_type=MESH)

    greet(partner)

    @pl.when(has_after)
    def _():
        greet(next_dev)

    @pl.when(has_before)
    def _():
        greet(prev_dev)

    @pl.when(is_relay)
    def _():
        greet(relay_source)
        greet(relay_target)

    for d in range(2):
        for column in (1, 2, 3):
            @pl.when(edge[d] & (s == (0 if column == 1 else 1)))
            def _():
                greet(relay_of(d, column))
                greet(relay_to(d, column))

    at_end = (edge[0] | edge[1]).astype(jnp.int32)
    beside = has_after.astype(jnp.int32) + has_before.astype(jnp.int32)
    pl.semaphore_wait(barrier, 1 + beside + 2 * is_relay.astype(jnp.int32) + at_end * (2 + 2 * s))

    def remote(src, dst, send, recv, device):
        return pltpu.make_async_remote_copy(
            src_ref=src, dst_ref=dst, send_sem=send, recv_sem=recv,
            device_id=device, device_id_type=MESH,
        )

    def columns(half, g):
        return pl.ds(pl.multiple_of(half * (GROUPS * LANES) + g * LANES, LANES), LANES)

    def landing(g, pair, half):
        if pair == 0:
            return kv.at[g, pl.ds(FRAME + HALF * half, HALF)]
        return qd.at[g, pl.ds(HALF * half, HALF)]

    def swap(g, pair):
        return remote(
            packed.at[g, pair], landing(g, pair, s), in_send.at[g, pair], in_recv.at[g, pair], partner
        )

    def pack(g, pair):
        for a in range(2):
            lanes = slice(a * LANES, (a + 1) * LANES)
            packed[g, pair, :, :, lanes] = loaded[2 * pair + a, :, :, columns(o, g)]

    def keep(g, pair):
        own_rows = landing(g, pair, s)
        for a in range(2):
            lanes = slice(a * LANES, (a + 1) * LANES)
            own_rows[:, :, lanes] = loaded[2 * pair + a, :, :, columns(s, g)]

    neighbours = (next_dev, prev_dev)
    sends_to, hears_from = (has_after, has_before), (has_before, has_after)

    def start_part(d, part, src, dst, send, recv, phase, g):
        straight = remote(src, dst, send, recv, neighbours[d])
        if part == 0:
            bent = edge[d] & (s == 1)
        else:
            bent = edge[d]

        @pl.when(bent)
        def _():
            remote(
                src, relay.at[phase, g], send, relay_recv.at[phase, g], relay_of(d, part_column[part])
            ).start()

        @pl.when(sends_to[d] & jnp.logical_not(bent))
        def _():
            straight.start()

    def kv_window(g, base, half):
        return kv.at[g, pl.ds(base + HALF * half, HALF)]

    def pass_args(g, d, part):
        half = (s, o)[part]
        return (
            kv_window(g, FRAME, half), kv_window(g, (0, 2 * FRAME)[d], half),
            pass_send.at[g, d, half], pass_recv.at[g, d, half],
        )

    def start_pass(g, d, part):
        start_part(d, part, *pass_args(g, d, part), 0, g)

    def wait_pass(g, d, part):
        return remote(*pass_args(g, d, part), neighbours[d])

    def term_args(g, d, part):
        half = (s, o)[part]
        at = pl.ds(HALF * half, HALF)
        return (
            give.at[g, d, at], take.at[g, d, at], term_send.at[g, d, half], term_recv.at[g, d, half]
        )

    def start_terms(g, d, part):
        start_part(d, part, *term_args(g, d, part), 1, g)

    def wait_terms(g, d, part):
        return remote(*term_args(g, d, part), neighbours[d])

    def relay_on(g, phase):
        if phase == 0:
            target = kv_window(g, relay_back * (2 * FRAME), relay_half)
            recv = pass_recv.at[g, relay_back, relay_half]
        else:
            target = take.at[g, relay_back, pl.ds(HALF * relay_half, HALF)]
            recv = term_recv.at[g, relay_back, relay_half]
        return remote(relay.at[phase, g], target, relay_send.at[phase, g], recv, relay_target)

    def relay_step(g, phase):
        @pl.when(is_relay)
        def _():
            remote(
                relay.at[phase, g], relay.at[phase, g], relay_send.at[phase, g],
                relay_recv.at[phase, g], relay_target,
            ).wait_recv()
            relay_on(g, phase).start()

    def rows_across(g):
        return remote(
            rows_out.at[g, pl.ds(HALF * o, HALF)], rows_in.at[g], row_send.at[g], row_recv.at[g], partner
        )

    def grads_across(g):
        return remote(
            final.at[g, pl.ds(HALF * o, HALF)], final_in.at[g], grad_send.at[g], grad_recv.at[g], partner
        )

    row_targets, grad_targets = (query_grad, attended), (key_grad, value_grad)

    def place_copy(staged, targets, local, g, half, a):
        return pltpu.make_async_copy(
            staged.at[:, :, pl.ds(a * LANES, LANES)], targets[a].at[:, :, columns(half, g)], local.at[g, a]
        )

    def rows_along(g, a):
        return place_copy(rows_out.at[g, pl.ds(HALF * s, HALF)], row_targets, row_local, g, s, a)

    def grads_along(g, a):
        return place_copy(final.at[g, pl.ds(HALF * s, HALF)], grad_targets, grad_local, g, s, a)

    def rows_back(g, a):
        return place_copy(rows_in.at[g], row_targets, row_local.at[pl.ds(GROUPS, GROUPS)], g, o, a)

    def grads_back(g, a):
        return place_copy(final_in.at[g], grad_targets, grad_local.at[pl.ds(GROUPS, GROUPS)], g, o, a)

    share_meta = remote(meta_vm.at[s], meta_vm.at[s], meta_send, meta_recv, partner)

    def begin(g):
        for pair in range(2):
            swap(g, pair).start()
            if pair == 0:
                for d in range(2):
                    start_pass(g, d, 0)

    for pair in range(2):
        loads[2 * pair].wait()
        loads[2 * pair + 1].wait()
        pack(0, pair)
        swap(0, pair).start()
        keep(0, pair)
        if pair == 0:
            for d in range(2):
                start_pass(0, d, 0)

    listed = block_list[...]
    row_at = lax.broadcasted_iota(jnp.int32, (HALF, LANES), 0)
    lane_at = lax.broadcasted_iota(jnp.int32, (HALF, LANES), 1)
    counts = jnp.zeros((HALF, LANES), jnp.int32)
    for row in range(HALF):
        counts = jnp.where(row_at == row, block_count[row], counts)
    edge_low = jnp.where(f > 0, 0, FRAME)
    edge_high = jnp.where(f < frames - 1, WINDOW, 2 * FRAME)
    usable = (listed >= edge_low) & (listed < edge_high) & (lane_at[:, :SEL] < counts[:, :SEL])
    slots = jnp.where(usable, listed, -1)
    place = jnp.full((HALF, LANES), SEL, jnp.int32)
    for j in range(SEL):
        place = jnp.where(lane_at - PLACE_AT == slots[:, j:j + 1], j, place)
    meta_vm[s, 0:HALF] = place
    meta_vm[s, 0:HALF, 0:SEL] = listed
    meta_vm[s, HALF:] = jnp.zeros((HALF, LANES), jnp.int32)
    meta_vm[s, HALF:, 0:SEL] = usable.astype(jnp.int32)
    share_meta.start()
    tiles[:, SEL] = jnp.zeros((FRAME, BLOCK, 2 * LANES), jnp.float32)

    def forward(g):
        swap(g, 0).wait_recv()
        for d in range(2):
            start_pass(g, d, 1)

    def prepare(g, carry):
        for pair in range(2):
            pack(g, pair)
            keep(g, pair)
        return carry

    lax.fori_loop(1, GROUPS, prepare, 0)

    def clear(w, carry):
        @pl.when(jnp.logical_not(has_before))
        def _():
            for g in range(GROUPS):
                kv[g, w] = jnp.zeros((BLOCK, 2 * LANES), jnp.bfloat16)
                take[g, 0, w] = jnp.zeros((BLOCK, 2 * LANES), jnp.bfloat16)

        @pl.when(jnp.logical_not(has_after))
        def _():
            for g in range(GROUPS):
                kv[g, 2 * FRAME + w] = jnp.zeros((BLOCK, 2 * LANES), jnp.bfloat16)
                take[g, 1, w] = jnp.zeros((BLOCK, 2 * LANES), jnp.bfloat16)

        return carry

    lax.fori_loop(0, FRAME, clear, 0)
    forward(0)
    begin(1)
    share_meta.wait()
    to_scalar = pltpu.make_async_copy(meta_vm, meta_sm, meta_local)
    to_scalar.start()
    relay_step(0, 0)
    to_scalar.wait()

    row_ids = lax.broadcasted_iota(jnp.int32, (4 * HD, 4 * HD), 0) // HD
    col_ids = lax.broadcasted_iota(jnp.int32, (4 * HD, 4 * HD), 1) // HD
    spread = jnp.where(
        row_ids == col_ids, jnp.where(col_ids < 2, FACTOR, 1.0), 0.0
    ).astype(jnp.bfloat16)
    first_head = lax.broadcasted_iota(jnp.int32, (BLOCK, LANES), 1) < HD

    def heads(full):
        return jnp.where(first_head, full[:HD], full[HD:])

    def fold(array, op):
        return op(array.reshape(array.shape[0] // 8, 8, LANES), axis=0)

    def attend(g, b):
        strip, row = b // HALF, lax.rem(b, HALF)
        chunks = ((0, 4), (4, 8), (8, SEL))
        keep = {"slabs": [None] * SEL, "powers": [None] * SEL}

        def diagonal():
            keep["diagonal"] = jnp.concatenate([qd[g, b]] * 4, axis=0) * spread
            keep["bias"] = [
                jnp.where(meta_sm[strip, HALF + row, j] > 0, 0.0, MASKED).astype(jnp.float32)
                for j in range(SEL)
            ]

        def products(c):
            low, high = chunks[c]
            picked = jnp.concatenate([work[meta_sm[strip, row, j]] for j in range(low, high)], axis=0)
            keep["picked", c] = picked
            both = lax.dot_general(
                picked, keep["diagonal"], (((1,), (1,)), ((), ())), preferred_element_type=jnp.float32
            )
            for j in range(low, high):
                at = slice((j - low) * BLOCK, (j - low + 1) * BLOCK)
                keep["scores", j] = both[at, :LANES]
                keep["grad_weights", j] = both[at, LANES:]

        def peak(c):
            for j in range(*chunks[c]):
                top = fold(keep["scores", j], jnp.max) + keep["bias"][j]
                keep["peak"] = jnp.maximum(keep["peak"], top) if j else top
            if c == len(chunks) - 1:
                keep["peak"] = jnp.max(keep["peak"], axis=0, keepdims=True)

        def power(j):
            powers = jnp.exp(keep["scores", j] - (keep["peak"] - keep["bias"][j]))
            keep["powers"][j] = powers
            total = fold(powers, jnp.sum)
            dots = fold(powers * keep["grad_weights", j], jnp.sum)
            keep["total"] = keep["total"] + total if j else total
            keep["dots"] = keep["dots"] + dots if j else dots
            if j == SEL - 1:
                keep["scale"] = 1.0 / jnp.sum(keep["total"], axis=0, keepdims=True)
                keep["row_dots"] = jnp.sum(keep["dots"], axis=0, keepdims=True) * keep["scale"]

        def slab(j):
            weights = keep["powers"][j] * keep["scale"]
            grad_scores = weights * (keep["grad_weights", j] - keep["row_dots"])
            keep["slabs"][j] = (grad_scores.astype(jnp.bfloat16), weights.astype(jnp.bfloat16))

        def terms(c):
            low, high = chunks[c]
            parts = [jnp.concatenate([pair[k] for pair in keep["slabs"][low:high]], axis=0) for k in range(2)]
            keep["parts", c] = parts
            result = jnp.dot(
                jnp.concatenate(parts, axis=1), keep["diagonal"], preferred_element_type=jnp.float32
            )
            tiles[b, low:high] = result.reshape(high - low, BLOCK, 2 * LANES)

        def mixed(c):
            for k in range(2):
                lanes = slice(k * LANES, (k + 1) * LANES)
                product = lax.dot_general(
                    keep["parts", c][k], keep["picked", c][:, lanes], (((0,), (0,)), ((), ())),
                    preferred_element_type=jnp.float32,
                )
                keep["mixed", k] = keep["mixed", k] + product if c else product
            if c == len(chunks) - 1:
                rows_out[g, b] = jnp.concatenate(
                    [heads(keep["mixed", 0]) * FACTOR, heads(keep["mixed", 1])], axis=1
                ).astype(jnp.bfloat16)

        def call(function, *args):
            return lambda: function(*args)

        count = range(len(chunks))
        return (
            [diagonal] + [call(products, c) for c in count],
            [call(peak, c) for c in count] + [call(power, j) for j in range(SEL)] + [call(slab, j) for j in range(SEL)],
            [call(step, c) for c in count for step in (terms, mixed)],
        )

    def interleave(stages):
        placed = [
            ((k + 0.5) / len(stage), n, step)
            for n, stage in enumerate(stages)
            for k, step in enumerate(stage)
        ]
        for _, _, step in sorted(placed, key=lambda item: item[:2]):
            step()

    def finish(g):
        slot = lax.rem(g, 2)
        for d in range(2):
            @pl.when(hears_from[d])
            def _():
                for part in range(2):
                    wait_terms(g, d, part).wait_recv()

        def add(w, carry):
            total = own[slot, w] + take[g, 0, w].astype(jnp.float32) + take[g, 1, w].astype(jnp.float32)
            final[g, w] = total.astype(jnp.bfloat16)
            return carry

        lax.fori_loop(0, FRAME, add, 0)
        grads_across(g).start()
        for a in range(2):
            grads_along(g, a).start()
        rows_across(g).wait_recv()
        for a in range(2):
            rows_back(g, a).start()

    def one_group(g, carry):
        swap(g, 1).wait_recv()
        for d in range(2):
            @pl.when(hears_from[d])
            def _():
                for part in range(2):
                    wait_pass(g, d, part).wait_recv()

        @pl.when(g == 1)
        def _():
            begin(3)

        work[...] = kv[g]

        blocks = [attend(g, lax.rem(HALF * o + i, FRAME)) for i in range(FRAME)]
        for turn in range(FRAME + 2):
            interleave([blocks[turn - k][k] for k in (2, 1, 0) if 0 <= turn - k < FRAME])
            if turn == 3:
                @pl.when(g == 0)
                def _():
                    forward(1)
                    begin(2)

                @pl.when(g > 0)
                def _():
                    relay_step(g - 1, 1)

            if turn == HALF + 1:
                rows_across(g).start()
            if turn == 7:
                @pl.when(g + 2 < GROUPS)
                def _():
                    forward(g + 2)

                @pl.when(g == 0)
                def _():
                    relay_step(1, 0)

                @pl.when(g > 0)
                def _():
                    finish(g - 1)

        @pl.when(g + 2 < GROUPS)
        def _():
            relay_step(g + 2, 0)

        for a in range(2):
            rows_along(g, a).start()

        def gather(w, base):
            acc = None
            for b in range(FRAME):
                place = meta_sm[b // HALF, b % HALF, PLACE_AT + base + w]
                tile = tiles[b, place]
                acc = tile if acc is None else acc + tile
            return acc

        def collect(w, inner):
            give[g, 1, w] = gather(w, 0).astype(jnp.bfloat16)
            give[g, 0, w] = gather(w, 2 * FRAME).astype(jnp.bfloat16)
            return inner

        lax.fori_loop(0, FRAME, collect, 0)
        for d in range(2):
            for part in range(2):
                start_terms(g, d, part)

        def collect_own(w, inner):
            own[lax.rem(g, 2), w] = gather(w, FRAME)
            return inner

        lax.fori_loop(0, FRAME, collect_own, 0)

        return carry

    lax.fori_loop(0, GROUPS, one_group, 0)
    relay_step(GROUPS - 1, 1)
    finish(GROUPS - 1)

    def land(g, carry):
        grads_across(g).wait_recv()
        for a in range(2):
            grads_back(g, a).start()
        return carry

    lax.fori_loop(0, GROUPS, land, 0)

    def drain(g, carry):
        for pair in range(2):
            swap(g, pair).wait_send()
        for d in range(2):
            @pl.when(sends_to[d])
            def _():
                for part in range(2):
                    wait_pass(g, d, part).wait_send()
                    wait_terms(g, d, part).wait_send()

        @pl.when(is_relay)
        def _():
            for phase in range(2):
                relay_on(g, phase).wait_send()

        rows_across(g).wait_send()
        grads_across(g).wait_send()
        for a in range(2):
            rows_along(g, a).wait()
            grads_along(g, a).wait()
            rows_back(g, a).wait()
            grads_back(g, a).wait()
        return carry

    lax.fori_loop(0, GROUPS, drain, 0)


def hand_over(*refs):
    sources, targets, held, in_sems, out_sems = refs[:4], refs[4:8], refs[8], refs[9], refs[10]
    spots = [(i, at) for i in range(4) for at in range(HALF)]
    ins = [pltpu.make_async_copy(sources[i].at[at], held.at[i, at], in_sems.at[i, at]) for i, at in spots]
    outs = [pltpu.make_async_copy(held.at[i, at], targets[i].at[at], out_sems.at[i, at]) for i, at in spots]
    for copy in ins:
        copy.start()
    for arrives, leaves in zip(ins, outs):
        arrives.wait()
        leaves.start()
    for copy in outs:
        copy.wait()


def body(queries, keys, values, out_grad, block_list, block_count):
    rows, width = queries.shape
    frames = lax.axis_size("frames")
    blocked = [x.reshape(HALF, BLOCK, width) for x in (queries, keys, values, out_grad)]
    shape = jax.ShapeDtypeStruct((HALF, BLOCK, width), jnp.bfloat16)
    dma = pltpu.SemaphoreType.DMA
    flops = 6 * 2 * FRAME * SEL * BLOCK * 256 * 256 * GROUPS
    outs = pl.pallas_call(
        lambda *refs: kernel(frames, *refs),
        out_shape=[shape] * 4,
        in_specs=[pl.BlockSpec(memory_space=pltpu.VMEM), pl.BlockSpec(memory_space=pltpu.SMEM)] + [pl.BlockSpec(memory_space=pl.ANY)] * 4,
        out_specs=[pl.BlockSpec(memory_space=pl.ANY)] * 4,
        scratch_shapes=[
            pltpu.VMEM((4, HALF, BLOCK, width), jnp.bfloat16),
            pltpu.VMEM((GROUPS, 2, HALF, BLOCK, 2 * LANES), jnp.bfloat16),
            pltpu.VMEM((GROUPS, WINDOW, BLOCK, 2 * LANES), jnp.bfloat16),
            pltpu.VMEM((GROUPS, FRAME, BLOCK, 2 * LANES), jnp.bfloat16),
            pltpu.VMEM((WINDOW, BLOCK, 2 * LANES), jnp.bfloat16),
            pltpu.VMEM((FRAME, SEL + 1, BLOCK, 2 * LANES), jnp.float32),
            pltpu.VMEM((GROUPS, FRAME, BLOCK, 2 * LANES), jnp.bfloat16),
            pltpu.VMEM((GROUPS, HALF, BLOCK, 2 * LANES), jnp.bfloat16),
            pltpu.VMEM((GROUPS, 2, FRAME, BLOCK, 2 * LANES), jnp.bfloat16),
            pltpu.VMEM((GROUPS, 2, FRAME, BLOCK, 2 * LANES), jnp.bfloat16),
            pltpu.VMEM((2, FRAME, BLOCK, 2 * LANES), jnp.float32),
            pltpu.VMEM((GROUPS, FRAME, BLOCK, 2 * LANES), jnp.bfloat16),
            pltpu.VMEM((GROUPS, HALF, BLOCK, 2 * LANES), jnp.bfloat16),
            pltpu.VMEM((2, GROUPS, HALF, BLOCK, 2 * LANES), jnp.bfloat16),
            pltpu.VMEM((2, 8, LANES), jnp.int32),
            pltpu.SMEM((2, 8, LANES), jnp.int32),
            dma((4,)), dma((GROUPS, 2)), dma((GROUPS, 2)),
            dma((GROUPS, 2, 2)), dma((GROUPS, 2, 2)),
            dma, dma, dma,
            dma((GROUPS,)), dma((GROUPS,)), dma((2 * GROUPS, 2)),
            dma((GROUPS, 2, 2)), dma((GROUPS, 2, 2)),
            dma((GROUPS,)), dma((GROUPS,)), dma((2 * GROUPS, 2)),
            dma((2, GROUPS)), dma((2, GROUPS)),
        ],
        cost_estimate=pl.CostEstimate(
            flops=flops, bytes_accessed=16 * rows * width, transcendentals=FRAME * SEL * BLOCK * LANES * GROUPS
        ),
        compiler_params=pltpu.CompilerParams(
            collective_id=0, has_side_effects=True, vmem_limit_bytes=60 * 1024 * 1024
        ),
    )(block_list, block_count, *blocked)
    outs = pl.pallas_call(
        hand_over,
        out_shape=[shape] * 4,
        in_specs=[pl.BlockSpec(memory_space=pl.ANY)] * 4,
        out_specs=[pl.BlockSpec(memory_space=pl.ANY)] * 4,
        scratch_shapes=[
            pltpu.VMEM((4, HALF, BLOCK, width), jnp.bfloat16), dma((4, HALF)), dma((4, HALF)),
        ],
        compiler_params=pltpu.CompilerParams(vmem_limit_bytes=60 * 1024 * 1024),
    )(*outs)
    return tuple(x.reshape(rows, width) for x in outs)


def solution(mesh):
    split = P(("frames", "strip"), None)
    in_specs = (split, split, split, split, split, P(("frames", "strip")))
    return jax.shard_map(
        body, mesh=mesh, in_specs=in_specs, out_specs=(split,) * 4, check_vma=False
    )
```

```python
import jax
import jax.numpy as jnp
from jax import lax
from jax.experimental import pallas as pl
from jax.experimental.pallas import tpu as pltpu
from jax.sharding import PartitionSpec as P

HD = 64
BLOCK = 64
SEL = 13
HALF = 4
FRAME = 8
WINDOW = 24
GROUPS = 4
LANES = 128
FACTOR = 0.125
MASKED = -1e30
PLACE_AT = 32
RUN = 8
MESH = pl.DeviceIdType.MESH


def kernel(
    frames,
    block_list, block_count, queries, keys, values, out_grad,
    attended, query_grad, key_grad, value_grad,
    loaded, packed, kv, qd, work, tiles, rows_out, rows_in, give, take, own, final, final_in, relay, meta_vm, meta_sm,
    load_sem, in_send, in_recv, pass_send, pass_recv,
    meta_send, meta_recv, meta_local, row_send, row_recv, row_local,
    term_send, term_recv, grad_send, grad_recv, grad_local, relay_send, relay_recv,
):
    f, s = lax.axis_index("frames"), lax.axis_index("strip")
    o = 1 - s
    partner, next_dev, prev_dev = (f, o), (f + 1, s), (f - 1, s)

    sources = (keys, values, queries, out_grad)
    loads = [pltpu.make_async_copy(sources[a], loaded.at[a], load_sem.at[a]) for a in range(4)]
    for load in loads:
        load.start()

    place_in_run = lax.rem(f, RUN)
    has_after, has_before = f < frames - 1, f > 0
    edge = ((place_in_run == RUN - 1) & has_after, (place_in_run == 0) & has_before)
    part_column = (3 * s, 1 + s)

    def relay_of(d, column):
        return (f - 2 * column if d == 0 else f + 2 * column, s)

    def relay_to(d, column):
        return (f + 1 + 2 * column if d == 0 else f - 1 - 2 * column, s)

    relay_back = 1 - lax.rem(place_in_run, 2)
    relay_column = lax.select(relay_back == 0, (RUN - 1 - place_in_run) // 2, place_in_run // 2)
    relay_half = lax.rem(relay_column, 2)
    relay_source_frame = f - place_in_run + (1 - relay_back) * (RUN - 1)
    relay_target_frame = relay_source_frame + 1 - 2 * relay_back
    is_relay = ((relay_column == 1) & (s == 0)) | ((relay_column >= 2) & (s == 1))
    is_relay = is_relay & (relay_target_frame >= 0) & (relay_target_frame < frames)
    relay_target, relay_source = (relay_target_frame, s), (relay_source_frame, s)

    barrier = pltpu.get_barrier_semaphore()

    def greet(device):
        pl.semaphore_signal(barrier, inc=1, device_id=device, device_id_type=MESH)

    greet(partner)

    @pl.when(has_after)
    def _():
        greet(next_dev)

    @pl.when(has_before)
    def _():
        greet(prev_dev)

    @pl.when(is_relay)
    def _():
        greet(relay_source)
        greet(relay_target)

    for d in range(2):
        for column in (1, 2, 3):
            @pl.when(edge[d] & (s == (0 if column == 1 else 1)))
            def _():
                greet(relay_of(d, column))
                greet(relay_to(d, column))

    at_end = (edge[0] | edge[1]).astype(jnp.int32)
    beside = has_after.astype(jnp.int32) + has_before.astype(jnp.int32)
    pl.semaphore_wait(barrier, 1 + beside + 2 * is_relay.astype(jnp.int32) + at_end * (2 + 2 * s))

    def remote(src, dst, send, recv, device):
        return pltpu.make_async_remote_copy(
            src_ref=src, dst_ref=dst, send_sem=send, recv_sem=recv,
            device_id=device, device_id_type=MESH,
        )

    def columns(half, g):
        return pl.ds(pl.multiple_of(half * (GROUPS * LANES) + g * LANES, LANES), LANES)

    def landing(g, pair, half):
        if pair == 0:
            return kv.at[g, pl.ds(FRAME + HALF * half, HALF)]
        return qd.at[g, pl.ds(HALF * half, HALF)]

    def swap(g, pair):
        return remote(
            packed.at[g, pair], landing(g, pair, s), in_send.at[g, pair], in_recv.at[g, pair], partner
        )

    def pack(g, pair):
        for a in range(2):
            lanes = slice(a * LANES, (a + 1) * LANES)
            packed[g, pair, :, :, lanes] = loaded[2 * pair + a, :, :, columns(o, g)]

    def keep(g, pair):
        own_rows = landing(g, pair, s)
        for a in range(2):
            lanes = slice(a * LANES, (a + 1) * LANES)
            own_rows[:, :, lanes] = loaded[2 * pair + a, :, :, columns(s, g)]

    neighbours = (next_dev, prev_dev)
    sends_to, hears_from = (has_after, has_before), (has_before, has_after)

    def start_part(d, part, src, dst, send, recv, phase, g):
        straight = remote(src, dst, send, recv, neighbours[d])
        if part == 0:
            bent = edge[d] & (s == 1)
        else:
            bent = edge[d]

        @pl.when(bent)
        def _():
            remote(
                src, relay.at[phase, g], send, relay_recv.at[phase, g], relay_of(d, part_column[part])
            ).start()

        @pl.when(sends_to[d] & jnp.logical_not(bent))
        def _():
            straight.start()

    def kv_window(g, base, half):
        return kv.at[g, pl.ds(base + HALF * half, HALF)]

    def pass_args(g, d, part):
        half = (s, o)[part]
        return (
            kv_window(g, FRAME, half), kv_window(g, (0, 2 * FRAME)[d], half),
            pass_send.at[g, d, half], pass_recv.at[g, d, half],
        )

    def start_pass(g, d, part):
        start_part(d, part, *pass_args(g, d, part), 0, g)

    def wait_pass(g, d, part):
        return remote(*pass_args(g, d, part), neighbours[d])

    def term_args(g, d, part):
        half = (s, o)[part]
        at = pl.ds(HALF * half, HALF)
        return (
            give.at[g, d, at], take.at[g, d, at], term_send.at[g, d, half], term_recv.at[g, d, half]
        )

    def start_terms(g, d, part):
        start_part(d, part, *term_args(g, d, part), 1, g)

    def wait_terms(g, d, part):
        return remote(*term_args(g, d, part), neighbours[d])

    def relay_on(g, phase):
        if phase == 0:
            target = kv_window(g, relay_back * (2 * FRAME), relay_half)
            recv = pass_recv.at[g, relay_back, relay_half]
        else:
            target = take.at[g, relay_back, pl.ds(HALF * relay_half, HALF)]
            recv = term_recv.at[g, relay_back, relay_half]
        return remote(relay.at[phase, g], target, relay_send.at[phase, g], recv, relay_target)

    def relay_step(g, phase):
        @pl.when(is_relay)
        def _():
            remote(
                relay.at[phase, g], relay.at[phase, g], relay_send.at[phase, g],
                relay_recv.at[phase, g], relay_target,
            ).wait_recv()
            relay_on(g, phase).start()

    def rows_across(g):
        return remote(
            rows_out.at[g, pl.ds(HALF * o, HALF)], rows_in.at[g], row_send.at[g], row_recv.at[g], partner
        )

    def grads_across(g):
        return remote(
            final.at[g, pl.ds(HALF * o, HALF)], final_in.at[g], grad_send.at[g], grad_recv.at[g], partner
        )

    row_targets, grad_targets = (query_grad, attended), (key_grad, value_grad)

    def place_copy(staged, targets, local, g, half, a):
        return pltpu.make_async_copy(
            staged.at[:, :, pl.ds(a * LANES, LANES)], targets[a].at[:, :, columns(half, g)], local.at[g, a]
        )

    def rows_along(g, a):
        return place_copy(rows_out.at[g, pl.ds(HALF * s, HALF)], row_targets, row_local, g, s, a)

    def grads_along(g, a):
        return place_copy(final.at[g, pl.ds(HALF * s, HALF)], grad_targets, grad_local, g, s, a)

    def rows_back(g, a):
        return place_copy(rows_in.at[g], row_targets, row_local.at[pl.ds(GROUPS, GROUPS)], g, o, a)

    def grads_back(g, a):
        return place_copy(final_in.at[g], grad_targets, grad_local.at[pl.ds(GROUPS, GROUPS)], g, o, a)

    share_meta = remote(meta_vm.at[s], meta_vm.at[s], meta_send, meta_recv, partner)

    def begin(g):
        for pair in range(2):
            swap(g, pair).start()
            if pair == 0:
                for d in range(2):
                    start_pass(g, d, 0)

    def pack_keep(g):
        for pair in range(2):
            pack(g, pair)
            keep(g, pair)

    for pair in range(2):
        loads[2 * pair].wait()
        loads[2 * pair + 1].wait()
        pack(0, pair)
        swap(0, pair).start()
        keep(0, pair)
        if pair == 0:
            for d in range(2):
                start_pass(0, d, 0)

    listed = block_list[...]
    row_at = lax.broadcasted_iota(jnp.int32, (HALF, LANES), 0)
    lane_at = lax.broadcasted_iota(jnp.int32, (HALF, LANES), 1)
    counts = jnp.zeros((HALF, LANES), jnp.int32)
    for row in range(HALF):
        counts = jnp.where(row_at == row, block_count[row], counts)
    edge_low = jnp.where(f > 0, 0, FRAME)
    edge_high = jnp.where(f < frames - 1, WINDOW, 2 * FRAME)
    usable = (listed >= edge_low) & (listed < edge_high) & (lane_at[:, :SEL] < counts[:, :SEL])
    slots = jnp.where(usable, listed, -1)
    place = jnp.full((HALF, LANES), SEL, jnp.int32)
    for j in range(SEL):
        place = jnp.where(lane_at - PLACE_AT == slots[:, j:j + 1], j, place)
    meta_vm[s, 0:HALF] = place
    meta_vm[s, 0:HALF, 0:SEL] = listed
    meta_vm[s, HALF:] = jnp.zeros((HALF, LANES), jnp.int32)
    meta_vm[s, HALF:, 0:SEL] = usable.astype(jnp.int32)
    share_meta.start()
    pack_keep(1)
    begin(1)
    tiles[:, SEL] = jnp.zeros((FRAME, BLOCK, 2 * LANES), jnp.float32)

    def forward(g):
        swap(g, 0).wait_recv()
        for d in range(2):
            start_pass(g, d, 1)

    def clear(w, carry):
        @pl.when(jnp.logical_not(has_before))
        def _():
            for g in range(GROUPS):
                kv[g, w] = jnp.zeros((BLOCK, 2 * LANES), jnp.bfloat16)
                take[g, 0, w] = jnp.zeros((BLOCK, 2 * LANES), jnp.bfloat16)

        @pl.when(jnp.logical_not(has_after))
        def _():
            for g in range(GROUPS):
                kv[g, 2 * FRAME + w] = jnp.zeros((BLOCK, 2 * LANES), jnp.bfloat16)
                take[g, 1, w] = jnp.zeros((BLOCK, 2 * LANES), jnp.bfloat16)

        return carry

    lax.fori_loop(0, FRAME, clear, 0)
    forward(0)
    pack_keep(2)
    begin(2)
    share_meta.wait()
    to_scalar = pltpu.make_async_copy(meta_vm, meta_sm, meta_local)
    to_scalar.start()
    relay_step(0, 0)
    to_scalar.wait()
    pack_keep(3)
    forward(1)

    row_ids = lax.broadcasted_iota(jnp.int32, (4 * HD, 4 * HD), 0) // HD
    col_ids = lax.broadcasted_iota(jnp.int32, (4 * HD, 4 * HD), 1) // HD
    spread = jnp.where(
        row_ids == col_ids, jnp.where(col_ids < 2, FACTOR, 1.0), 0.0
    ).astype(jnp.bfloat16)
    first_head = lax.broadcasted_iota(jnp.int32, (BLOCK, LANES), 1) < HD

    def heads(full):
        return jnp.where(first_head, full[:HD], full[HD:])

    def fold(array, op):
        return op(array.reshape(array.shape[0] // 8, 8, LANES), axis=0)

    def attend(g, b):
        strip, row = b // HALF, lax.rem(b, HALF)
        chunks = ((0, 4), (4, 8), (8, SEL))
        keep = {"slabs": [None] * SEL, "powers": [None] * SEL}

        def diagonal():
            keep["diagonal"] = jnp.concatenate([qd[g, b]] * 4, axis=0) * spread
            keep["bias"] = [
                jnp.where(meta_sm[strip, HALF + row, j] > 0, 0.0, MASKED).astype(jnp.float32)
                for j in range(SEL)
            ]

        def products(c):
            low, high = chunks[c]
            picked = jnp.concatenate([work[meta_sm[strip, row, j]] for j in range(low, high)], axis=0)
            keep["picked", c] = picked
            both = lax.dot_general(
                picked, keep["diagonal"], (((1,), (1,)), ((), ())), preferred_element_type=jnp.float32
            )
            for j in range(low, high):
                at = slice((j - low) * BLOCK, (j - low + 1) * BLOCK)
                keep["scores", j] = both[at, :LANES]
                keep["grad_weights", j] = both[at, LANES:]

        def peak(c):
            for j in range(*chunks[c]):
                top = fold(keep["scores", j], jnp.max) + keep["bias"][j]
                keep["peak"] = jnp.maximum(keep["peak"], top) if j else top
            if c == len(chunks) - 1:
                keep["peak"] = jnp.max(keep["peak"], axis=0, keepdims=True)

        def power(j):
            powers = jnp.exp(keep["scores", j] - (keep["peak"] - keep["bias"][j]))
            keep["powers"][j] = powers
            total = fold(powers, jnp.sum)
            dots = fold(powers * keep["grad_weights", j], jnp.sum)
            keep["total"] = keep["total"] + total if j else total
            keep["dots"] = keep["dots"] + dots if j else dots
            if j == SEL - 1:
                keep["scale"] = 1.0 / jnp.sum(keep["total"], axis=0, keepdims=True)
                keep["row_dots"] = jnp.sum(keep["dots"], axis=0, keepdims=True) * keep["scale"]

        def slab(j):
            weights = keep["powers"][j] * keep["scale"]
            grad_scores = weights * (keep["grad_weights", j] - keep["row_dots"])
            keep["slabs"][j] = (grad_scores.astype(jnp.bfloat16), weights.astype(jnp.bfloat16))

        def terms(c):
            low, high = chunks[c]
            parts = [jnp.concatenate([pair[k] for pair in keep["slabs"][low:high]], axis=0) for k in range(2)]
            keep["parts", c] = parts
            result = jnp.dot(
                jnp.concatenate(parts, axis=1), keep["diagonal"], preferred_element_type=jnp.float32
            )
            tiles[b, low:high] = result.reshape(high - low, BLOCK, 2 * LANES)

        def mixed(c):
            for k in range(2):
                lanes = slice(k * LANES, (k + 1) * LANES)
                product = lax.dot_general(
                    keep["parts", c][k], keep["picked", c][:, lanes], (((0,), (0,)), ((), ())),
                    preferred_element_type=jnp.float32,
                )
                keep["mixed", k] = keep["mixed", k] + product if c else product
            if c == len(chunks) - 1:
                rows_out[g, b] = jnp.concatenate(
                    [heads(keep["mixed", 0]) * FACTOR, heads(keep["mixed", 1])], axis=1
                ).astype(jnp.bfloat16)

        def call(function, *args):
            return lambda: function(*args)

        count = range(len(chunks))
        return (
            [diagonal] + [call(products, c) for c in count],
            [call(peak, c) for c in count] + [call(power, j) for j in range(SEL)] + [call(slab, j) for j in range(SEL)],
            [call(step, c) for c in count for step in (terms, mixed)],
        )

    def interleave(stages):
        placed = [
            ((k + 0.5) / len(stage), n, step)
            for n, stage in enumerate(stages)
            for k, step in enumerate(stage)
        ]
        for _, _, step in sorted(placed, key=lambda item: item[:2]):
            step()

    def finish(g):
        slot = lax.rem(g, 2)
        for d in range(2):
            @pl.when(hears_from[d])
            def _():
                for part in range(2):
                    wait_terms(g, d, part).wait_recv()

        def add(w, carry):
            total = own[slot, w] + take[g, 0, w].astype(jnp.float32) + take[g, 1, w].astype(jnp.float32)
            final[g, w] = total.astype(jnp.bfloat16)
            return carry

        lax.fori_loop(0, FRAME, add, 0)
        grads_across(g).start()
        for a in range(2):
            grads_along(g, a).start()
        rows_across(g).wait_recv()
        for a in range(2):
            rows_back(g, a).start()

    def one_group(g, carry):
        swap(g, 1).wait_recv()
        for d in range(2):
            @pl.when(hears_from[d])
            def _():
                for part in range(2):
                    wait_pass(g, d, part).wait_recv()

        @pl.when(g == 0)
        def _():
            begin(3)

        work[...] = kv[g]

        blocks = [attend(g, lax.rem(HALF * o + i, FRAME)) for i in range(FRAME)]
        for turn in range(FRAME + 2):
            interleave([blocks[turn - k][k] for k in (2, 1, 0) if 0 <= turn - k < FRAME])
            if turn == HALF + 1:
                rows_across(g).start()

                @pl.when(g > 1)
                def _():
                    finish(g - 2)

                @pl.when(g + 2 < GROUPS)
                def _():
                    forward(g + 2)

                @pl.when(g == 0)
                def _():
                    relay_step(1, 0)

            if turn == FRAME:
                @pl.when(g > 0)
                def _():
                    relay_step(g - 1, 1)

        @pl.when(g + 2 < GROUPS)
        def _():
            relay_step(g + 2, 0)

        for a in range(2):
            rows_along(g, a).start()

        def gather(w, base):
            acc = None
            for b in range(FRAME):
                place = meta_sm[b // HALF, b % HALF, PLACE_AT + base + w]
                tile = tiles[b, place]
                acc = tile if acc is None else acc + tile
            return acc

        def collect(w, inner):
            give[g, 1, w] = gather(w, 0).astype(jnp.bfloat16)
            give[g, 0, w] = gather(w, 2 * FRAME).astype(jnp.bfloat16)
            return inner

        lax.fori_loop(0, FRAME, collect, 0)
        for d in range(2):
            for part in range(2):
                start_terms(g, d, part)

        def collect_own(w, inner):
            own[lax.rem(g, 2), w] = gather(w, FRAME)
            return inner

        lax.fori_loop(0, FRAME, collect_own, 0)

        return carry

    lax.fori_loop(0, GROUPS, one_group, 0)
    finish(GROUPS - 2)
    relay_step(GROUPS - 1, 1)
    finish(GROUPS - 1)

    def land(g, carry):
        grads_across(g).wait_recv()
        for a in range(2):
            grads_back(g, a).start()
        return carry

    lax.fori_loop(0, GROUPS, land, 0)

    def drain(g, carry):
        for pair in range(2):
            swap(g, pair).wait_send()
        for d in range(2):
            @pl.when(sends_to[d])
            def _():
                for part in range(2):
                    wait_pass(g, d, part).wait_send()
                    wait_terms(g, d, part).wait_send()

        @pl.when(is_relay)
        def _():
            for phase in range(2):
                relay_on(g, phase).wait_send()

        rows_across(g).wait_send()
        grads_across(g).wait_send()
        for a in range(2):
            rows_along(g, a).wait()
            grads_along(g, a).wait()
            rows_back(g, a).wait()
            grads_back(g, a).wait()
        return carry

    lax.fori_loop(0, GROUPS, drain, 0)


def hand_over(*refs):
    sources, targets, held, in_sems, out_sems = refs[:4], refs[4:8], refs[8], refs[9], refs[10]
    spots = [(i, at) for i in range(4) for at in range(HALF)]
    ins = [pltpu.make_async_copy(sources[i].at[at], held.at[i, at], in_sems.at[i, at]) for i, at in spots]
    outs = [pltpu.make_async_copy(held.at[i, at], targets[i].at[at], out_sems.at[i, at]) for i, at in spots]
    for copy in ins:
        copy.start()
    for arrives, leaves in zip(ins, outs):
        arrives.wait()
        leaves.start()
    for copy in outs:
        copy.wait()


def body(queries, keys, values, out_grad, block_list, block_count):
    rows, width = queries.shape
    frames = lax.axis_size("frames")
    blocked = [x.reshape(HALF, BLOCK, width) for x in (queries, keys, values, out_grad)]
    shape = jax.ShapeDtypeStruct((HALF, BLOCK, width), jnp.bfloat16)
    dma = pltpu.SemaphoreType.DMA
    flops = 6 * 2 * FRAME * SEL * BLOCK * 256 * 256 * GROUPS
    outs = pl.pallas_call(
        lambda *refs: kernel(frames, *refs),
        out_shape=[shape] * 4,
        in_specs=[pl.BlockSpec(memory_space=pltpu.VMEM), pl.BlockSpec(memory_space=pltpu.SMEM)] + [pl.BlockSpec(memory_space=pl.ANY)] * 4,
        out_specs=[pl.BlockSpec(memory_space=pl.ANY)] * 4,
        scratch_shapes=[
            pltpu.VMEM((4, HALF, BLOCK, width), jnp.bfloat16),
            pltpu.VMEM((GROUPS, 2, HALF, BLOCK, 2 * LANES), jnp.bfloat16),
            pltpu.VMEM((GROUPS, WINDOW, BLOCK, 2 * LANES), jnp.bfloat16),
            pltpu.VMEM((GROUPS, FRAME, BLOCK, 2 * LANES), jnp.bfloat16),
            pltpu.VMEM((WINDOW, BLOCK, 2 * LANES), jnp.bfloat16),
            pltpu.VMEM((FRAME, SEL + 1, BLOCK, 2 * LANES), jnp.float32),
            pltpu.VMEM((GROUPS, FRAME, BLOCK, 2 * LANES), jnp.bfloat16),
            pltpu.VMEM((GROUPS, HALF, BLOCK, 2 * LANES), jnp.bfloat16),
            pltpu.VMEM((GROUPS, 2, FRAME, BLOCK, 2 * LANES), jnp.bfloat16),
            pltpu.VMEM((GROUPS, 2, FRAME, BLOCK, 2 * LANES), jnp.bfloat16),
            pltpu.VMEM((2, FRAME, BLOCK, 2 * LANES), jnp.float32),
            pltpu.VMEM((GROUPS, FRAME, BLOCK, 2 * LANES), jnp.bfloat16),
            pltpu.VMEM((GROUPS, HALF, BLOCK, 2 * LANES), jnp.bfloat16),
            pltpu.VMEM((2, GROUPS, HALF, BLOCK, 2 * LANES), jnp.bfloat16),
            pltpu.VMEM((2, 8, LANES), jnp.int32),
            pltpu.SMEM((2, 8, LANES), jnp.int32),
            dma((4,)), dma((GROUPS, 2)), dma((GROUPS, 2)),
            dma((GROUPS, 2, 2)), dma((GROUPS, 2, 2)),
            dma, dma, dma,
            dma((GROUPS,)), dma((GROUPS,)), dma((2 * GROUPS, 2)),
            dma((GROUPS, 2, 2)), dma((GROUPS, 2, 2)),
            dma((GROUPS,)), dma((GROUPS,)), dma((2 * GROUPS, 2)),
            dma((2, GROUPS)), dma((2, GROUPS)),
        ],
        cost_estimate=pl.CostEstimate(
            flops=flops, bytes_accessed=16 * rows * width, transcendentals=FRAME * SEL * BLOCK * LANES * GROUPS
        ),
        compiler_params=pltpu.CompilerParams(
            collective_id=0, has_side_effects=True, vmem_limit_bytes=60 * 1024 * 1024
        ),
    )(block_list, block_count, *blocked)
    outs = pl.pallas_call(
        hand_over,
        out_shape=[shape] * 4,
        in_specs=[pl.BlockSpec(memory_space=pl.ANY)] * 4,
        out_specs=[pl.BlockSpec(memory_space=pl.ANY)] * 4,
        scratch_shapes=[
            pltpu.VMEM((4, HALF, BLOCK, width), jnp.bfloat16), dma((4, HALF)), dma((4, HALF)),
        ],
        compiler_params=pltpu.CompilerParams(vmem_limit_bytes=60 * 1024 * 1024),
    )(*outs)
    return tuple(x.reshape(rows, width) for x in outs)


def solution(mesh):
    split = P(("frames", "strip"), None)
    in_specs = (split, split, split, split, split, P(("frames", "strip")))
    return jax.shard_map(
        body, mesh=mesh, in_specs=in_specs, out_specs=(split,) * 4, check_vma=False
    )
```

```python
import jax
import jax.numpy as jnp
from jax import lax
from jax.experimental import pallas as pl
from jax.experimental.pallas import tpu as pltpu
from jax.sharding import PartitionSpec as P

HD = 64
BLOCK = 64
SEL = 13
HALF = 4
FRAME = 8
WINDOW = 24
GROUPS = 4
LANES = 128
FACTOR = 0.125
MASKED = -1e30
PLACE_AT = 32
RUN = 8
MESH = pl.DeviceIdType.MESH


def kernel(
    frames,
    block_list, block_count, queries, keys, values, out_grad,
    attended, query_grad, key_grad, value_grad,
    loaded, packed, kv, qd, work, tiles, rows_out, rows_in, give, take, own, final, final_in, relay, meta_vm, meta_sm,
    load_sem, in_send, in_recv, pass_send, pass_recv,
    meta_send, meta_recv, meta_local, row_send, row_recv, row_local,
    term_send, term_recv, grad_send, grad_recv, grad_local, relay_send, relay_recv,
):
    f, s = lax.axis_index("frames"), lax.axis_index("strip")
    o = 1 - s
    partner, next_dev, prev_dev = (f, o), (f + 1, s), (f - 1, s)

    sources = (keys, values, queries, out_grad)
    loads = [pltpu.make_async_copy(sources[a], loaded.at[a], load_sem.at[a]) for a in range(4)]
    for load in loads:
        load.start()

    place_in_run = lax.rem(f, RUN)
    has_after, has_before = f < frames - 1, f > 0
    edge = ((place_in_run == RUN - 1) & has_after, (place_in_run == 0) & has_before)
    part_column = (3 * s, 1 + s)

    def relay_of(d, column):
        return (f - 2 * column if d == 0 else f + 2 * column, s)

    def relay_to(d, column):
        return (f + 1 + 2 * column if d == 0 else f - 1 - 2 * column, s)

    relay_back = 1 - lax.rem(place_in_run, 2)
    relay_column = lax.select(relay_back == 0, (RUN - 1 - place_in_run) // 2, place_in_run // 2)
    relay_half = lax.rem(relay_column, 2)
    relay_source_frame = f - place_in_run + (1 - relay_back) * (RUN - 1)
    relay_target_frame = relay_source_frame + 1 - 2 * relay_back
    is_relay = ((relay_column == 1) & (s == 0)) | ((relay_column >= 2) & (s == 1))
    is_relay = is_relay & (relay_target_frame >= 0) & (relay_target_frame < frames)
    relay_target, relay_source = (relay_target_frame, s), (relay_source_frame, s)

    barrier = pltpu.get_barrier_semaphore()

    def greet(device):
        pl.semaphore_signal(barrier, inc=1, device_id=device, device_id_type=MESH)

    greet(partner)

    @pl.when(has_after)
    def _():
        greet(next_dev)

    @pl.when(has_before)
    def _():
        greet(prev_dev)

    @pl.when(is_relay)
    def _():
        greet(relay_source)
        greet(relay_target)

    for d in range(2):
        for column in (1, 2, 3):
            @pl.when(edge[d] & (s == (0 if column == 1 else 1)))
            def _():
                greet(relay_of(d, column))
                greet(relay_to(d, column))

    at_end = (edge[0] | edge[1]).astype(jnp.int32)
    beside = has_after.astype(jnp.int32) + has_before.astype(jnp.int32)
    pl.semaphore_wait(barrier, 1 + beside + 2 * is_relay.astype(jnp.int32) + at_end * (2 + 2 * s))

    def remote(src, dst, send, recv, device):
        return pltpu.make_async_remote_copy(
            src_ref=src, dst_ref=dst, send_sem=send, recv_sem=recv,
            device_id=device, device_id_type=MESH,
        )

    def columns(half, g):
        return pl.ds(pl.multiple_of(half * (GROUPS * LANES) + g * LANES, LANES), LANES)

    def landing(g, pair, half):
        if pair == 0:
            return kv.at[g, pl.ds(FRAME + HALF * half, HALF)]
        return qd.at[g, pl.ds(HALF * half, HALF)]

    def swap(g, pair):
        return remote(
            packed.at[g, pair], landing(g, pair, s), in_send.at[g, pair], in_recv.at[g, pair], partner
        )

    def pack(g, pair):
        for a in range(2):
            lanes = slice(a * LANES, (a + 1) * LANES)
            packed[g, pair, :, :, lanes] = loaded[2 * pair + a, :, :, columns(o, g)]

    def keep(g, pair):
        own_rows = landing(g, pair, s)
        for a in range(2):
            lanes = slice(a * LANES, (a + 1) * LANES)
            own_rows[:, :, lanes] = loaded[2 * pair + a, :, :, columns(s, g)]

    neighbours = (next_dev, prev_dev)
    sends_to, hears_from = (has_after, has_before), (has_before, has_after)

    def start_part(d, part, src, dst, send, recv, phase, g):
        straight = remote(src, dst, send, recv, neighbours[d])
        if part == 0:
            bent = edge[d] & (s == 1)
        else:
            bent = edge[d]

        @pl.when(bent)
        def _():
            remote(
                src, relay.at[phase, g], send, relay_recv.at[phase, g], relay_of(d, part_column[part])
            ).start()

        @pl.when(sends_to[d] & jnp.logical_not(bent))
        def _():
            straight.start()

    def kv_window(g, base, half):
        return kv.at[g, pl.ds(base + HALF * half, HALF)]

    def pass_args(g, d, part):
        half = (s, o)[part]
        return (
            kv_window(g, FRAME, half), kv_window(g, (0, 2 * FRAME)[d], half),
            pass_send.at[g, d, half], pass_recv.at[g, d, half],
        )

    def start_pass(g, d, part):
        start_part(d, part, *pass_args(g, d, part), 0, g)

    def wait_pass(g, d, part):
        return remote(*pass_args(g, d, part), neighbours[d])

    def term_args(g, d, part):
        half = (s, o)[part]
        at = pl.ds(HALF * half, HALF)
        return (
            give.at[g, d, at], take.at[g, d, at], term_send.at[g, d, half], term_recv.at[g, d, half]
        )

    def start_terms(g, d, part):
        start_part(d, part, *term_args(g, d, part), 1, g)

    def wait_terms(g, d, part):
        return remote(*term_args(g, d, part), neighbours[d])

    def relay_on(g, phase):
        if phase == 0:
            target = kv_window(g, relay_back * (2 * FRAME), relay_half)
            recv = pass_recv.at[g, relay_back, relay_half]
        else:
            target = take.at[g, relay_back, pl.ds(HALF * relay_half, HALF)]
            recv = term_recv.at[g, relay_back, relay_half]
        return remote(relay.at[phase, g], target, relay_send.at[phase, g], recv, relay_target)

    def relay_step(g, phase):
        @pl.when(is_relay)
        def _():
            remote(
                relay.at[phase, g], relay.at[phase, g], relay_send.at[phase, g],
                relay_recv.at[phase, g], relay_target,
            ).wait_recv()
            relay_on(g, phase).start()

    def rows_across(g):
        return remote(
            rows_out.at[g, pl.ds(HALF * o, HALF)], rows_in.at[g], row_send.at[g], row_recv.at[g], partner
        )

    def grads_across(g):
        return remote(
            final.at[g, pl.ds(HALF * o, HALF)], final_in.at[g], grad_send.at[g], grad_recv.at[g], partner
        )

    row_targets, grad_targets = (query_grad, attended), (key_grad, value_grad)

    def place_copy(staged, targets, local, g, half, a):
        return pltpu.make_async_copy(
            staged.at[:, :, pl.ds(a * LANES, LANES)], targets[a].at[:, :, columns(half, g)], local.at[g, a]
        )

    def rows_along(g, a):
        return place_copy(rows_out.at[g, pl.ds(HALF * s, HALF)], row_targets, row_local, g, s, a)

    def grads_along(g, a):
        return place_copy(final.at[g, pl.ds(HALF * s, HALF)], grad_targets, grad_local, g, s, a)

    def rows_back(g, a):
        return place_copy(rows_in.at[g], row_targets, row_local.at[pl.ds(GROUPS, GROUPS)], g, o, a)

    def grads_back(g, a):
        return place_copy(final_in.at[g], grad_targets, grad_local.at[pl.ds(GROUPS, GROUPS)], g, o, a)

    share_meta = remote(meta_vm.at[s], meta_vm.at[s], meta_send, meta_recv, partner)

    def begin_keys(g):
        swap(g, 0).start()
        for d in range(2):
            start_pass(g, d, 0)

    def begin_queries(g):
        swap(g, 1).start()

    def pack_keep(g):
        for pair in range(2):
            pack(g, pair)
            keep(g, pair)

    for pair in range(2):
        loads[2 * pair].wait()
        loads[2 * pair + 1].wait()
        pack(0, pair)
        keep(0, pair)
        if pair == 0:
            begin_keys(0)
        else:
            begin_queries(0)

    listed = block_list[...]
    row_at = lax.broadcasted_iota(jnp.int32, (HALF, LANES), 0)
    lane_at = lax.broadcasted_iota(jnp.int32, (HALF, LANES), 1)
    counts = jnp.zeros((HALF, LANES), jnp.int32)
    for row in range(HALF):
        counts = jnp.where(row_at == row, block_count[row], counts)
    edge_low = jnp.where(f > 0, 0, FRAME)
    edge_high = jnp.where(f < frames - 1, WINDOW, 2 * FRAME)
    usable = (listed >= edge_low) & (listed < edge_high) & (lane_at[:, :SEL] < counts[:, :SEL])
    slots = jnp.where(usable, listed, -1)
    place = jnp.full((HALF, LANES), SEL, jnp.int32)
    for j in range(SEL):
        place = jnp.where(lane_at - PLACE_AT == slots[:, j:j + 1], j, place)
    meta_vm[s, 0:HALF] = place
    meta_vm[s, 0:HALF, 0:SEL] = listed
    meta_vm[s, HALF:] = jnp.zeros((HALF, LANES), jnp.int32)
    meta_vm[s, HALF:, 0:SEL] = usable.astype(jnp.int32)
    share_meta.start()
    pack_keep(1)
    begin_keys(1)
    pack_keep(2)
    tiles[:, SEL] = jnp.zeros((FRAME, BLOCK, 2 * LANES), jnp.float32)

    def forward(g):
        swap(g, 0).wait_recv()
        for d in range(2):
            start_pass(g, d, 1)

    def clear(w, carry):
        @pl.when(jnp.logical_not(has_before))
        def _():
            for g in range(GROUPS):
                kv[g, w] = jnp.zeros((BLOCK, 2 * LANES), jnp.bfloat16)
                take[g, 0, w] = jnp.zeros((BLOCK, 2 * LANES), jnp.bfloat16)

        @pl.when(jnp.logical_not(has_after))
        def _():
            for g in range(GROUPS):
                kv[g, 2 * FRAME + w] = jnp.zeros((BLOCK, 2 * LANES), jnp.bfloat16)
                take[g, 1, w] = jnp.zeros((BLOCK, 2 * LANES), jnp.bfloat16)

        return carry

    lax.fori_loop(0, FRAME, clear, 0)
    forward(0)
    begin_keys(2)
    begin_queries(1)
    share_meta.wait()
    to_scalar = pltpu.make_async_copy(meta_vm, meta_sm, meta_local)
    to_scalar.start()
    relay_step(0, 0)
    to_scalar.wait()
    pack_keep(3)

    row_ids = lax.broadcasted_iota(jnp.int32, (4 * HD, 4 * HD), 0) // HD
    col_ids = lax.broadcasted_iota(jnp.int32, (4 * HD, 4 * HD), 1) // HD
    spread = jnp.where(
        row_ids == col_ids, jnp.where(col_ids < 2, FACTOR, 1.0), 0.0
    ).astype(jnp.bfloat16)
    first_head = lax.broadcasted_iota(jnp.int32, (BLOCK, LANES), 1) < HD

    def heads(full):
        return jnp.where(first_head, full[:HD], full[HD:])

    def fold(array, op):
        return op(array.reshape(array.shape[0] // 8, 8, LANES), axis=0)

    def attend(g, b):
        strip, row = b // HALF, lax.rem(b, HALF)
        chunks = ((0, 4), (4, 8), (8, SEL))
        keep = {"slabs": [None] * SEL, "powers": [None] * SEL}

        def diagonal():
            keep["diagonal"] = jnp.concatenate([qd[g, b]] * 4, axis=0) * spread
            keep["bias"] = [
                jnp.where(meta_sm[strip, HALF + row, j] > 0, 0.0, MASKED).astype(jnp.float32)
                for j in range(SEL)
            ]

        def products(c):
            low, high = chunks[c]
            picked = jnp.concatenate([work[meta_sm[strip, row, j]] for j in range(low, high)], axis=0)
            keep["picked", c] = picked
            both = lax.dot_general(
                picked, keep["diagonal"], (((1,), (1,)), ((), ())), preferred_element_type=jnp.float32
            )
            for j in range(low, high):
                at = slice((j - low) * BLOCK, (j - low + 1) * BLOCK)
                keep["scores", j] = both[at, :LANES]
                keep["grad_weights", j] = both[at, LANES:]

        def peak(c):
            for j in range(*chunks[c]):
                top = fold(keep["scores", j], jnp.max) + keep["bias"][j]
                keep["peak"] = jnp.maximum(keep["peak"], top) if j else top
            if c == len(chunks) - 1:
                keep["peak"] = jnp.max(keep["peak"], axis=0, keepdims=True)

        def power(j):
            powers = jnp.exp(keep["scores", j] - (keep["peak"] - keep["bias"][j]))
            keep["powers"][j] = powers
            total = fold(powers, jnp.sum)
            dots = fold(powers * keep["grad_weights", j], jnp.sum)
            keep["total"] = keep["total"] + total if j else total
            keep["dots"] = keep["dots"] + dots if j else dots
            if j == SEL - 1:
                keep["scale"] = 1.0 / jnp.sum(keep["total"], axis=0, keepdims=True)
                keep["row_dots"] = jnp.sum(keep["dots"], axis=0, keepdims=True) * keep["scale"]

        def slab(j):
            weights = keep["powers"][j] * keep["scale"]
            grad_scores = weights * (keep["grad_weights", j] - keep["row_dots"])
            keep["slabs"][j] = (grad_scores.astype(jnp.bfloat16), weights.astype(jnp.bfloat16))

        def terms(c):
            low, high = chunks[c]
            parts = [jnp.concatenate([pair[k] for pair in keep["slabs"][low:high]], axis=0) for k in range(2)]
            keep["parts", c] = parts
            result = jnp.dot(
                jnp.concatenate(parts, axis=1), keep["diagonal"], preferred_element_type=jnp.float32
            )
            tiles[b, low:high] = result.reshape(high - low, BLOCK, 2 * LANES)

        def mixed(c):
            for k in range(2):
                lanes = slice(k * LANES, (k + 1) * LANES)
                product = lax.dot_general(
                    keep["parts", c][k], keep["picked", c][:, lanes], (((0,), (0,)), ((), ())),
                    preferred_element_type=jnp.float32,
                )
                keep["mixed", k] = keep["mixed", k] + product if c else product
            if c == len(chunks) - 1:
                rows_out[g, b] = jnp.concatenate(
                    [heads(keep["mixed", 0]) * FACTOR, heads(keep["mixed", 1])], axis=1
                ).astype(jnp.bfloat16)

        def call(function, *args):
            return lambda: function(*args)

        count = range(len(chunks))
        return (
            [diagonal] + [call(products, c) for c in count],
            [call(peak, c) for c in count] + [call(power, j) for j in range(SEL)] + [call(slab, j) for j in range(SEL)],
            [call(step, c) for c in count for step in (terms, mixed)],
        )

    def interleave(stages):
        placed = [
            ((k + 0.5) / len(stage), n, step)
            for n, stage in enumerate(stages)
            for k, step in enumerate(stage)
        ]
        for _, _, step in sorted(placed, key=lambda item: item[:2]):
            step()

    def finish(g):
        slot = lax.rem(g, 2)
        for d in range(2):
            @pl.when(hears_from[d])
            def _():
                for part in range(2):
                    wait_terms(g, d, part).wait_recv()

        def add(w, carry):
            total = own[slot, w] + take[g, 0, w].astype(jnp.float32) + take[g, 1, w].astype(jnp.float32)
            final[g, w] = total.astype(jnp.bfloat16)
            return carry

        lax.fori_loop(0, FRAME, add, 0)
        grads_across(g).start()
        for a in range(2):
            grads_along(g, a).start()
        rows_across(g).wait_recv()
        for a in range(2):
            rows_back(g, a).start()

    def one_group(g, carry):
        swap(g, 1).wait_recv()
        for d in range(2):
            @pl.when(hears_from[d])
            def _():
                for part in range(2):
                    wait_pass(g, d, part).wait_recv()

        work[...] = kv[g]

        blocks = [attend(g, lax.rem(HALF * o + i, FRAME)) for i in range(FRAME)]
        for turn in range(FRAME + 2):
            interleave([blocks[turn - k][k] for k in (2, 1, 0) if 0 <= turn - k < FRAME])
            if turn == 3:
                @pl.when(g == 0)
                def _():
                    forward(1)
                    begin_keys(3)
                    begin_queries(2)

                @pl.when((g > 0) & (g + 1 < GROUPS))
                def _():
                    relay_step(g + 1, 0)

            if turn == HALF + 1:
                rows_across(g).start()
            if turn == 7:
                @pl.when(g == 0)
                def _():
                    begin_queries(3)
                    relay_step(1, 0)

                @pl.when(g + 2 < GROUPS)
                def _():
                    forward(g + 2)

                @pl.when(g > 0)
                def _():
                    relay_step(g - 1, 1)

                @pl.when(g > 1)
                def _():
                    finish(g - 2)

        for a in range(2):
            rows_along(g, a).start()

        def gather(w, base):
            acc = None
            for b in range(FRAME):
                place = meta_sm[b // HALF, b % HALF, PLACE_AT + base + w]
                tile = tiles[b, place]
                acc = tile if acc is None else acc + tile
            return acc

        def collect(w, inner):
            give[g, 1, w] = gather(w, 0).astype(jnp.bfloat16)
            give[g, 0, w] = gather(w, 2 * FRAME).astype(jnp.bfloat16)
            return inner

        lax.fori_loop(0, FRAME, collect, 0)
        for d in range(2):
            for part in range(2):
                start_terms(g, d, part)

        def collect_own(w, inner):
            own[lax.rem(g, 2), w] = gather(w, FRAME)
            return inner

        lax.fori_loop(0, FRAME, collect_own, 0)

        return carry

    lax.fori_loop(0, GROUPS, one_group, 0)
    finish(GROUPS - 2)
    relay_step(GROUPS - 1, 1)
    finish(GROUPS - 1)

    def land(g, carry):
        grads_across(g).wait_recv()
        for a in range(2):
            grads_back(g, a).start()
        return carry

    lax.fori_loop(0, GROUPS, land, 0)

    def drain(g, carry):
        for pair in range(2):
            swap(g, pair).wait_send()
        for d in range(2):
            @pl.when(sends_to[d])
            def _():
                for part in range(2):
                    wait_pass(g, d, part).wait_send()
                    wait_terms(g, d, part).wait_send()

        @pl.when(is_relay)
        def _():
            for phase in range(2):
                relay_on(g, phase).wait_send()

        rows_across(g).wait_send()
        grads_across(g).wait_send()
        for a in range(2):
            rows_along(g, a).wait()
            grads_along(g, a).wait()
            rows_back(g, a).wait()
            grads_back(g, a).wait()
        return carry

    lax.fori_loop(0, GROUPS, drain, 0)


def hand_over(*refs):
    sources, targets, held, in_sems, out_sems = refs[:4], refs[4:8], refs[8], refs[9], refs[10]
    spots = [(i, at) for i in range(4) for at in range(HALF)]
    ins = [pltpu.make_async_copy(sources[i].at[at], held.at[i, at], in_sems.at[i, at]) for i, at in spots]
    outs = [pltpu.make_async_copy(held.at[i, at], targets[i].at[at], out_sems.at[i, at]) for i, at in spots]
    for copy in ins:
        copy.start()
    for arrives, leaves in zip(ins, outs):
        arrives.wait()
        leaves.start()
    for copy in outs:
        copy.wait()


def body(queries, keys, values, out_grad, block_list, block_count):
    rows, width = queries.shape
    frames = lax.axis_size("frames")
    blocked = [x.reshape(HALF, BLOCK, width) for x in (queries, keys, values, out_grad)]
    shape = jax.ShapeDtypeStruct((HALF, BLOCK, width), jnp.bfloat16)
    dma = pltpu.SemaphoreType.DMA
    flops = 6 * 2 * FRAME * SEL * BLOCK * 256 * 256 * GROUPS
    outs = pl.pallas_call(
        lambda *refs: kernel(frames, *refs),
        out_shape=[shape] * 4,
        in_specs=[pl.BlockSpec(memory_space=pltpu.VMEM), pl.BlockSpec(memory_space=pltpu.SMEM)] + [pl.BlockSpec(memory_space=pl.ANY)] * 4,
        out_specs=[pl.BlockSpec(memory_space=pl.ANY)] * 4,
        scratch_shapes=[
            pltpu.VMEM((4, HALF, BLOCK, width), jnp.bfloat16),
            pltpu.VMEM((GROUPS, 2, HALF, BLOCK, 2 * LANES), jnp.bfloat16),
            pltpu.VMEM((GROUPS, WINDOW, BLOCK, 2 * LANES), jnp.bfloat16),
            pltpu.VMEM((GROUPS, FRAME, BLOCK, 2 * LANES), jnp.bfloat16),
            pltpu.VMEM((WINDOW, BLOCK, 2 * LANES), jnp.bfloat16),
            pltpu.VMEM((FRAME, SEL + 1, BLOCK, 2 * LANES), jnp.float32),
            pltpu.VMEM((GROUPS, FRAME, BLOCK, 2 * LANES), jnp.bfloat16),
            pltpu.VMEM((GROUPS, HALF, BLOCK, 2 * LANES), jnp.bfloat16),
            pltpu.VMEM((GROUPS, 2, FRAME, BLOCK, 2 * LANES), jnp.bfloat16),
            pltpu.VMEM((GROUPS, 2, FRAME, BLOCK, 2 * LANES), jnp.bfloat16),
            pltpu.VMEM((2, FRAME, BLOCK, 2 * LANES), jnp.float32),
            pltpu.VMEM((GROUPS, FRAME, BLOCK, 2 * LANES), jnp.bfloat16),
            pltpu.VMEM((GROUPS, HALF, BLOCK, 2 * LANES), jnp.bfloat16),
            pltpu.VMEM((2, GROUPS, HALF, BLOCK, 2 * LANES), jnp.bfloat16),
            pltpu.VMEM((2, 8, LANES), jnp.int32),
            pltpu.SMEM((2, 8, LANES), jnp.int32),
            dma((4,)), dma((GROUPS, 2)), dma((GROUPS, 2)),
            dma((GROUPS, 2, 2)), dma((GROUPS, 2, 2)),
            dma, dma, dma,
            dma((GROUPS,)), dma((GROUPS,)), dma((2 * GROUPS, 2)),
            dma((GROUPS, 2, 2)), dma((GROUPS, 2, 2)),
            dma((GROUPS,)), dma((GROUPS,)), dma((2 * GROUPS, 2)),
            dma((2, GROUPS)), dma((2, GROUPS)),
        ],
        cost_estimate=pl.CostEstimate(
            flops=flops, bytes_accessed=16 * rows * width, transcendentals=FRAME * SEL * BLOCK * LANES * GROUPS
        ),
        compiler_params=pltpu.CompilerParams(
            collective_id=0, has_side_effects=True, vmem_limit_bytes=60 * 1024 * 1024
        ),
    )(block_list, block_count, *blocked)
    outs = pl.pallas_call(
        hand_over,
        out_shape=[shape] * 4,
        in_specs=[pl.BlockSpec(memory_space=pl.ANY)] * 4,
        out_specs=[pl.BlockSpec(memory_space=pl.ANY)] * 4,
        scratch_shapes=[
            pltpu.VMEM((4, HALF, BLOCK, width), jnp.bfloat16), dma((4, HALF)), dma((4, HALF)),
        ],
        compiler_params=pltpu.CompilerParams(vmem_limit_bytes=60 * 1024 * 1024),
    )(*outs)
    return tuple(x.reshape(rows, width) for x in outs)


def solution(mesh):
    split = P(("frames", "strip"), None)
    in_specs = (split, split, split, split, split, P(("frames", "strip")))
    return jax.shard_map(
        body, mesh=mesh, in_specs=in_specs, out_specs=(split,) * 4, check_vma=False
    )
```

```python
import jax
import jax.numpy as jnp
from jax import lax
from jax.experimental import pallas as pl
from jax.experimental.pallas import tpu as pltpu
from jax.sharding import PartitionSpec as P

HD = 64
BLOCK = 64
SEL = 13
HALF = 4
FRAME = 8
WINDOW = 24
GROUPS = 4
LANES = 128
FACTOR = 0.125
MASKED = -1e30
PLACE_AT = 32
RUN = 8
MESH = pl.DeviceIdType.MESH


def kernel(
    frames,
    block_list, block_count, queries, keys, values, out_grad,
    attended, query_grad, key_grad, value_grad,
    loaded, packed, kv, qd, work, tiles, rows_out, rows_in, give, take, own, final, final_in, relay, meta_vm, meta_sm,
    load_sem, in_send, in_recv, pass_send, pass_recv,
    meta_send, meta_recv, meta_local, row_send, row_recv, row_local,
    term_send, term_recv, grad_send, grad_recv, grad_local, relay_send, relay_recv,
):
    f, s = lax.axis_index("frames"), lax.axis_index("strip")
    o = 1 - s
    partner, next_dev, prev_dev = (f, o), (f + 1, s), (f - 1, s)

    sources = (keys, values, queries, out_grad)
    loads = [pltpu.make_async_copy(sources[a], loaded.at[a], load_sem.at[a]) for a in range(4)]
    for load in loads:
        load.start()

    place_in_run = lax.rem(f, RUN)
    has_after, has_before = f < frames - 1, f > 0
    edge = ((place_in_run == RUN - 1) & has_after, (place_in_run == 0) & has_before)
    part_column = (3 * s, 1 + s)

    def relay_of(d, column):
        return (f - 2 * column if d == 0 else f + 2 * column, s)

    def relay_to(d, column):
        return (f + 1 + 2 * column if d == 0 else f - 1 - 2 * column, s)

    relay_back = 1 - lax.rem(place_in_run, 2)
    relay_column = lax.select(relay_back == 0, (RUN - 1 - place_in_run) // 2, place_in_run // 2)
    relay_half = lax.rem(relay_column, 2)
    relay_source_frame = f - place_in_run + (1 - relay_back) * (RUN - 1)
    relay_target_frame = relay_source_frame + 1 - 2 * relay_back
    is_relay = ((relay_column == 1) & (s == 0)) | ((relay_column >= 2) & (s == 1))
    is_relay = is_relay & (relay_target_frame >= 0) & (relay_target_frame < frames)
    relay_target, relay_source = (relay_target_frame, s), (relay_source_frame, s)

    barrier = pltpu.get_barrier_semaphore()

    def greet(device):
        pl.semaphore_signal(barrier, inc=1, device_id=device, device_id_type=MESH)

    greet(partner)

    @pl.when(has_after)
    def _():
        greet(next_dev)

    @pl.when(has_before)
    def _():
        greet(prev_dev)

    @pl.when(is_relay)
    def _():
        greet(relay_source)
        greet(relay_target)

    for d in range(2):
        for column in (1, 2, 3):
            @pl.when(edge[d] & (s == (0 if column == 1 else 1)))
            def _():
                greet(relay_of(d, column))
                greet(relay_to(d, column))

    at_end = (edge[0] | edge[1]).astype(jnp.int32)
    beside = has_after.astype(jnp.int32) + has_before.astype(jnp.int32)
    pl.semaphore_wait(barrier, 1 + beside + 2 * is_relay.astype(jnp.int32) + at_end * (2 + 2 * s))

    def remote(src, dst, send, recv, device):
        return pltpu.make_async_remote_copy(
            src_ref=src, dst_ref=dst, send_sem=send, recv_sem=recv,
            device_id=device, device_id_type=MESH,
        )

    def columns(half, g):
        return pl.ds(pl.multiple_of(half * (GROUPS * LANES) + g * LANES, LANES), LANES)

    def landing(g, pair, half):
        if pair == 0:
            return kv.at[g, pl.ds(FRAME + HALF * half, HALF)]
        return qd.at[g, pl.ds(HALF * half, HALF)]

    def swap(g, pair):
        return remote(
            packed.at[g, pair], landing(g, pair, s), in_send.at[g, pair], in_recv.at[g, pair], partner
        )

    def pack(g, pair):
        for a in range(2):
            lanes = slice(a * LANES, (a + 1) * LANES)
            packed[g, pair, :, :, lanes] = loaded[2 * pair + a, :, :, columns(o, g)]

    def keep(g, pair):
        own_rows = landing(g, pair, s)
        for a in range(2):
            lanes = slice(a * LANES, (a + 1) * LANES)
            own_rows[:, :, lanes] = loaded[2 * pair + a, :, :, columns(s, g)]

    neighbours = (next_dev, prev_dev)
    sends_to, hears_from = (has_after, has_before), (has_before, has_after)

    def start_part(d, part, src, dst, send, recv, phase, g):
        straight = remote(src, dst, send, recv, neighbours[d])
        if part == 0:
            bent = edge[d] & (s == 1)
        else:
            bent = edge[d]

        @pl.when(bent)
        def _():
            remote(
                src, relay.at[phase, g], send, relay_recv.at[phase, g], relay_of(d, part_column[part])
            ).start()

        @pl.when(sends_to[d] & jnp.logical_not(bent))
        def _():
            straight.start()

    def kv_window(g, base, half):
        return kv.at[g, pl.ds(base + HALF * half, HALF)]

    def pass_args(g, d, part):
        half = (s, o)[part]
        return (
            kv_window(g, FRAME, half), kv_window(g, (0, 2 * FRAME)[d], half),
            pass_send.at[g, d, half], pass_recv.at[g, d, half],
        )

    def start_pass(g, d, part):
        start_part(d, part, *pass_args(g, d, part), 0, g)

    def wait_pass(g, d, part):
        return remote(*pass_args(g, d, part), neighbours[d])

    def term_args(g, d, part):
        half = (s, o)[part]
        at = pl.ds(HALF * half, HALF)
        return (
            give.at[g, d, at], take.at[g, d, at], term_send.at[g, d, half], term_recv.at[g, d, half]
        )

    def start_terms(g, d, part):
        start_part(d, part, *term_args(g, d, part), 1, g)

    def wait_terms(g, d, part):
        return remote(*term_args(g, d, part), neighbours[d])

    def relay_on(g, phase):
        if phase == 0:
            target = kv_window(g, relay_back * (2 * FRAME), relay_half)
            recv = pass_recv.at[g, relay_back, relay_half]
        else:
            target = take.at[g, relay_back, pl.ds(HALF * relay_half, HALF)]
            recv = term_recv.at[g, relay_back, relay_half]
        return remote(relay.at[phase, g], target, relay_send.at[phase, g], recv, relay_target)

    def relay_step(g, phase):
        @pl.when(is_relay)
        def _():
            remote(
                relay.at[phase, g], relay.at[phase, g], relay_send.at[phase, g],
                relay_recv.at[phase, g], relay_target,
            ).wait_recv()
            relay_on(g, phase).start()

    def rows_across(g):
        return remote(
            rows_out.at[g, pl.ds(HALF * o, HALF)], rows_in.at[g], row_send.at[g], row_recv.at[g], partner
        )

    def grads_across(g):
        return remote(
            final.at[g, pl.ds(HALF * o, HALF)], final_in.at[g], grad_send.at[g], grad_recv.at[g], partner
        )

    row_targets, grad_targets = (query_grad, attended), (key_grad, value_grad)

    def place_copy(staged, targets, local, g, half, a):
        return pltpu.make_async_copy(
            staged.at[:, :, pl.ds(a * LANES, LANES)], targets[a].at[:, :, columns(half, g)], local.at[g, a]
        )

    def rows_along(g, a):
        return place_copy(rows_out.at[g, pl.ds(HALF * s, HALF)], row_targets, row_local, g, s, a)

    def grads_along(g, a):
        return place_copy(final.at[g, pl.ds(HALF * s, HALF)], grad_targets, grad_local, g, s, a)

    def rows_back(g, a):
        return place_copy(rows_in.at[g], row_targets, row_local.at[pl.ds(GROUPS, GROUPS)], g, o, a)

    def grads_back(g, a):
        return place_copy(final_in.at[g], grad_targets, grad_local.at[pl.ds(GROUPS, GROUPS)], g, o, a)

    share_meta = remote(meta_vm.at[s], meta_vm.at[s], meta_send, meta_recv, partner)

    def begin_keys(g):
        swap(g, 0).start()
        for d in range(2):
            start_pass(g, d, 0)

    def begin_queries(g):
        swap(g, 1).start()

    def pack_keep(g):
        for pair in range(2):
            pack(g, pair)
            keep(g, pair)

    for pair in range(2):
        loads[2 * pair].wait()
        loads[2 * pair + 1].wait()
        pack(0, pair)
        keep(0, pair)
        if pair == 0:
            begin_keys(0)
        else:
            begin_queries(0)

    listed = block_list[...]
    row_at = lax.broadcasted_iota(jnp.int32, (HALF, LANES), 0)
    lane_at = lax.broadcasted_iota(jnp.int32, (HALF, LANES), 1)
    counts = jnp.zeros((HALF, LANES), jnp.int32)
    for row in range(HALF):
        counts = jnp.where(row_at == row, block_count[row], counts)
    edge_low = jnp.where(f > 0, 0, FRAME)
    edge_high = jnp.where(f < frames - 1, WINDOW, 2 * FRAME)
    usable = (listed >= edge_low) & (listed < edge_high) & (lane_at[:, :SEL] < counts[:, :SEL])
    slots = jnp.where(usable, listed, -1)
    place = jnp.full((HALF, LANES), SEL, jnp.int32)
    for j in range(SEL):
        place = jnp.where(lane_at - PLACE_AT == slots[:, j:j + 1], j, place)
    meta_vm[s, 0:HALF] = place
    meta_vm[s, 0:HALF, 0:SEL] = listed
    meta_vm[s, HALF:] = jnp.zeros((HALF, LANES), jnp.int32)
    meta_vm[s, HALF:, 0:SEL] = usable.astype(jnp.int32)
    share_meta.start()
    pack_keep(1)
    begin_keys(1)
    pack_keep(2)
    tiles[:, SEL] = jnp.zeros((FRAME, BLOCK, 2 * LANES), jnp.float32)

    def forward(g):
        swap(g, 0).wait_recv()
        for d in range(2):
            start_pass(g, d, 1)

    def clear(w, carry):
        @pl.when(jnp.logical_not(has_before))
        def _():
            for g in range(GROUPS):
                kv[g, w] = jnp.zeros((BLOCK, 2 * LANES), jnp.bfloat16)
                take[g, 0, w] = jnp.zeros((BLOCK, 2 * LANES), jnp.bfloat16)

        @pl.when(jnp.logical_not(has_after))
        def _():
            for g in range(GROUPS):
                kv[g, 2 * FRAME + w] = jnp.zeros((BLOCK, 2 * LANES), jnp.bfloat16)
                take[g, 1, w] = jnp.zeros((BLOCK, 2 * LANES), jnp.bfloat16)

        return carry

    lax.fori_loop(0, FRAME, clear, 0)
    forward(0)
    begin_keys(2)
    begin_queries(1)
    share_meta.wait()
    to_scalar = pltpu.make_async_copy(meta_vm, meta_sm, meta_local)
    to_scalar.start()
    relay_step(0, 0)
    to_scalar.wait()
    pack_keep(3)

    row_ids = lax.broadcasted_iota(jnp.int32, (4 * HD, 4 * HD), 0) // HD
    col_ids = lax.broadcasted_iota(jnp.int32, (4 * HD, 4 * HD), 1) // HD
    spread = jnp.where(
        row_ids == col_ids, jnp.where(col_ids < 2, FACTOR, 1.0), 0.0
    ).astype(jnp.bfloat16)
    first_head = lax.broadcasted_iota(jnp.int32, (BLOCK, LANES), 1) < HD

    def heads(full):
        return jnp.where(first_head, full[:HD], full[HD:])

    def fold(array, op):
        return op(array.reshape(array.shape[0] // 8, 8, LANES), axis=0)

    def attend(g, b):
        strip, row = b // HALF, lax.rem(b, HALF)
        chunks = ((0, 4), (4, 8), (8, SEL))
        keep = {"slabs": [None] * SEL, "powers": [None] * SEL}

        def diagonal():
            keep["diagonal"] = jnp.concatenate([qd[g, b]] * 4, axis=0) * spread
            keep["bias"] = [
                jnp.where(meta_sm[strip, HALF + row, j] > 0, 0.0, MASKED).astype(jnp.float32)
                for j in range(SEL)
            ]

        def products(c):
            low, high = chunks[c]
            picked = jnp.concatenate([work[meta_sm[strip, row, j]] for j in range(low, high)], axis=0)
            keep["picked", c] = picked
            both = lax.dot_general(
                picked, keep["diagonal"], (((1,), (1,)), ((), ())), preferred_element_type=jnp.float32
            )
            for j in range(low, high):
                at = slice((j - low) * BLOCK, (j - low + 1) * BLOCK)
                keep["scores", j] = both[at, :LANES]
                keep["grad_weights", j] = both[at, LANES:]

        def peak(c):
            for j in range(*chunks[c]):
                top = fold(keep["scores", j], jnp.max) + keep["bias"][j]
                keep["peak"] = jnp.maximum(keep["peak"], top) if j else top
            if c == len(chunks) - 1:
                keep["peak"] = jnp.max(keep["peak"], axis=0, keepdims=True)

        def power(j):
            powers = jnp.exp(keep["scores", j] - (keep["peak"] - keep["bias"][j]))
            keep["powers"][j] = powers
            total = fold(powers, jnp.sum)
            dots = fold(powers * keep["grad_weights", j], jnp.sum)
            keep["total"] = keep["total"] + total if j else total
            keep["dots"] = keep["dots"] + dots if j else dots
            if j == SEL - 1:
                keep["scale"] = 1.0 / jnp.sum(keep["total"], axis=0, keepdims=True)
                keep["row_dots"] = jnp.sum(keep["dots"], axis=0, keepdims=True) * keep["scale"]

        def slab(j):
            weights = keep["powers"][j] * keep["scale"]
            grad_scores = weights * (keep["grad_weights", j] - keep["row_dots"])
            keep["slabs"][j] = (grad_scores.astype(jnp.bfloat16), weights.astype(jnp.bfloat16))

        def terms(c):
            low, high = chunks[c]
            parts = [jnp.concatenate([pair[k] for pair in keep["slabs"][low:high]], axis=0) for k in range(2)]
            keep["parts", c] = parts
            result = jnp.dot(
                jnp.concatenate(parts, axis=1), keep["diagonal"], preferred_element_type=jnp.float32
            )
            tiles[b, low:high] = result.reshape(high - low, BLOCK, 2 * LANES)

        def mixed(c):
            for k in range(2):
                lanes = slice(k * LANES, (k + 1) * LANES)
                product = lax.dot_general(
                    keep["parts", c][k], keep["picked", c][:, lanes], (((0,), (0,)), ((), ())),
                    preferred_element_type=jnp.float32,
                )
                keep["mixed", k] = keep["mixed", k] + product if c else product
            if c == len(chunks) - 1:
                rows_out[g, b] = jnp.concatenate(
                    [heads(keep["mixed", 0]) * FACTOR, heads(keep["mixed", 1])], axis=1
                ).astype(jnp.bfloat16)

        def call(function, *args):
            return lambda: function(*args)

        count = range(len(chunks))
        return (
            [diagonal] + [call(products, c) for c in count],
            [call(peak, c) for c in count] + [call(power, j) for j in range(SEL)] + [call(slab, j) for j in range(SEL)],
            [call(step, c) for c in count for step in (terms, mixed)],
        )

    def interleave(stages):
        placed = [
            ((k + 0.5) / len(stage), n, step)
            for n, stage in enumerate(stages)
            for k, step in enumerate(stage)
        ]
        for _, _, step in sorted(placed, key=lambda item: item[:2]):
            step()

    def finish(g):
        slot = lax.rem(g, 2)
        for d in range(2):
            @pl.when(hears_from[d])
            def _():
                for part in range(2):
                    wait_terms(g, d, part).wait_recv()

        def add(w, carry):
            total = own[slot, w] + take[g, 0, w].astype(jnp.float32) + take[g, 1, w].astype(jnp.float32)
            final[g, w] = total.astype(jnp.bfloat16)
            return carry

        lax.fori_loop(0, FRAME, add, 0)
        grads_across(g).start()
        for a in range(2):
            grads_along(g, a).start()
        rows_across(g).wait_recv()
        for a in range(2):
            rows_back(g, a).start()

    def one_group(g, carry):
        swap(g, 1).wait_recv()
        for d in range(2):
            @pl.when(hears_from[d])
            def _():
                for part in range(2):
                    wait_pass(g, d, part).wait_recv()

        work[...] = kv[g]

        blocks = [attend(g, lax.rem(HALF * o + i, FRAME)) for i in range(FRAME)]
        for turn in range(FRAME + 2):
            interleave([blocks[turn - k][k] for k in (2, 1, 0) if 0 <= turn - k < FRAME])
            if turn == 3:
                @pl.when(g == 0)
                def _():
                    forward(1)
                    begin_keys(3)
                    begin_queries(2)

                @pl.when((g > 0) & (g + 1 < GROUPS))
                def _():
                    relay_step(g + 1, 0)

                @pl.when(g == GROUPS - 1)
                def _():
                    rows_across(GROUPS - 2).start()

            if turn == 7:
                @pl.when(g == 0)
                def _():
                    begin_queries(3)
                    relay_step(1, 0)

                @pl.when(g + 2 < GROUPS)
                def _():
                    forward(g + 2)

                @pl.when(g > 0)
                def _():
                    relay_step(g - 1, 1)

                @pl.when((g > 0) & (g < GROUPS - 1))
                def _():
                    rows_across(g - 1).start()

                @pl.when(g > 1)
                def _():
                    finish(g - 2)

        for a in range(2):
            rows_along(g, a).start()

        def gather(w, base):
            acc = None
            for b in range(FRAME):
                place = meta_sm[b // HALF, b % HALF, PLACE_AT + base + w]
                tile = tiles[b, place]
                acc = tile if acc is None else acc + tile
            return acc

        def collect(w, inner):
            give[g, 1, w] = gather(w, 0).astype(jnp.bfloat16)
            give[g, 0, w] = gather(w, 2 * FRAME).astype(jnp.bfloat16)
            return inner

        lax.fori_loop(0, FRAME, collect, 0)
        for d in range(2):
            for part in range(2):
                start_terms(g, d, part)

        def collect_own(w, inner):
            own[lax.rem(g, 2), w] = gather(w, FRAME)
            return inner

        lax.fori_loop(0, FRAME, collect_own, 0)

        return carry

    lax.fori_loop(0, GROUPS, one_group, 0)
    relay_step(GROUPS - 1, 1)
    rows_across(GROUPS - 1).start()
    finish(GROUPS - 2)
    finish(GROUPS - 1)

    def land(g, carry):
        grads_across(g).wait_recv()
        for a in range(2):
            grads_back(g, a).start()
        return carry

    lax.fori_loop(0, GROUPS, land, 0)

    def drain(g, carry):
        for pair in range(2):
            swap(g, pair).wait_send()
        for d in range(2):
            @pl.when(sends_to[d])
            def _():
                for part in range(2):
                    wait_pass(g, d, part).wait_send()
                    wait_terms(g, d, part).wait_send()

        @pl.when(is_relay)
        def _():
            for phase in range(2):
                relay_on(g, phase).wait_send()

        rows_across(g).wait_send()
        grads_across(g).wait_send()
        for a in range(2):
            rows_along(g, a).wait()
            grads_along(g, a).wait()
            rows_back(g, a).wait()
            grads_back(g, a).wait()
        return carry

    lax.fori_loop(0, GROUPS, drain, 0)


def hand_over(*refs):
    sources, targets, held, in_sems, out_sems = refs[:4], refs[4:8], refs[8], refs[9], refs[10]
    spots = [(i, at) for i in range(4) for at in range(HALF)]
    ins = [pltpu.make_async_copy(sources[i].at[at], held.at[i, at], in_sems.at[i, at]) for i, at in spots]
    outs = [pltpu.make_async_copy(held.at[i, at], targets[i].at[at], out_sems.at[i, at]) for i, at in spots]
    for copy in ins:
        copy.start()
    for arrives, leaves in zip(ins, outs):
        arrives.wait()
        leaves.start()
    for copy in outs:
        copy.wait()


def body(queries, keys, values, out_grad, block_list, block_count):
    rows, width = queries.shape
    frames = lax.axis_size("frames")
    blocked = [x.reshape(HALF, BLOCK, width) for x in (queries, keys, values, out_grad)]
    shape = jax.ShapeDtypeStruct((HALF, BLOCK, width), jnp.bfloat16)
    dma = pltpu.SemaphoreType.DMA
    flops = 6 * 2 * FRAME * SEL * BLOCK * 256 * 256 * GROUPS
    outs = pl.pallas_call(
        lambda *refs: kernel(frames, *refs),
        out_shape=[shape] * 4,
        in_specs=[pl.BlockSpec(memory_space=pltpu.VMEM), pl.BlockSpec(memory_space=pltpu.SMEM)] + [pl.BlockSpec(memory_space=pl.ANY)] * 4,
        out_specs=[pl.BlockSpec(memory_space=pl.ANY)] * 4,
        scratch_shapes=[
            pltpu.VMEM((4, HALF, BLOCK, width), jnp.bfloat16),
            pltpu.VMEM((GROUPS, 2, HALF, BLOCK, 2 * LANES), jnp.bfloat16),
            pltpu.VMEM((GROUPS, WINDOW, BLOCK, 2 * LANES), jnp.bfloat16),
            pltpu.VMEM((GROUPS, FRAME, BLOCK, 2 * LANES), jnp.bfloat16),
            pltpu.VMEM((WINDOW, BLOCK, 2 * LANES), jnp.bfloat16),
            pltpu.VMEM((FRAME, SEL + 1, BLOCK, 2 * LANES), jnp.float32),
            pltpu.VMEM((GROUPS, FRAME, BLOCK, 2 * LANES), jnp.bfloat16),
            pltpu.VMEM((GROUPS, HALF, BLOCK, 2 * LANES), jnp.bfloat16),
            pltpu.VMEM((GROUPS, 2, FRAME, BLOCK, 2 * LANES), jnp.bfloat16),
            pltpu.VMEM((GROUPS, 2, FRAME, BLOCK, 2 * LANES), jnp.bfloat16),
            pltpu.VMEM((2, FRAME, BLOCK, 2 * LANES), jnp.float32),
            pltpu.VMEM((GROUPS, FRAME, BLOCK, 2 * LANES), jnp.bfloat16),
            pltpu.VMEM((GROUPS, HALF, BLOCK, 2 * LANES), jnp.bfloat16),
            pltpu.VMEM((2, GROUPS, HALF, BLOCK, 2 * LANES), jnp.bfloat16),
            pltpu.VMEM((2, 8, LANES), jnp.int32),
            pltpu.SMEM((2, 8, LANES), jnp.int32),
            dma((4,)), dma((GROUPS, 2)), dma((GROUPS, 2)),
            dma((GROUPS, 2, 2)), dma((GROUPS, 2, 2)),
            dma, dma, dma,
            dma((GROUPS,)), dma((GROUPS,)), dma((2 * GROUPS, 2)),
            dma((GROUPS, 2, 2)), dma((GROUPS, 2, 2)),
            dma((GROUPS,)), dma((GROUPS,)), dma((2 * GROUPS, 2)),
            dma((2, GROUPS)), dma((2, GROUPS)),
        ],
        cost_estimate=pl.CostEstimate(
            flops=flops, bytes_accessed=16 * rows * width, transcendentals=FRAME * SEL * BLOCK * LANES * GROUPS
        ),
        compiler_params=pltpu.CompilerParams(
            collective_id=0, has_side_effects=True, vmem_limit_bytes=60 * 1024 * 1024
        ),
    )(block_list, block_count, *blocked)
    outs = pl.pallas_call(
        hand_over,
        out_shape=[shape] * 4,
        in_specs=[pl.BlockSpec(memory_space=pl.ANY)] * 4,
        out_specs=[pl.BlockSpec(memory_space=pl.ANY)] * 4,
        scratch_shapes=[
            pltpu.VMEM((4, HALF, BLOCK, width), jnp.bfloat16), dma((4, HALF)), dma((4, HALF)),
        ],
        compiler_params=pltpu.CompilerParams(vmem_limit_bytes=60 * 1024 * 1024),
    )(*outs)
    return tuple(x.reshape(rows, width) for x in outs)


def solution(mesh):
    split = P(("frames", "strip"), None)
    in_specs = (split, split, split, split, split, P(("frames", "strip")))
    return jax.shard_map(
        body, mesh=mesh, in_specs=in_specs, out_specs=(split,) * 4, check_vma=False
    )
```

```python
import jax
import jax.numpy as jnp
from jax import lax
from jax.experimental import pallas as pl
from jax.experimental.pallas import tpu as pltpu
from jax.sharding import PartitionSpec as P

HD = 64
BLOCK = 64
SEL = 13
HALF = 4
FRAME = 8
WINDOW = 24
GROUPS = 4
LANES = 128
FACTOR = 0.125
MASKED = -1e30
PLACE_AT = 32
RUN = 8
MESH = pl.DeviceIdType.MESH


def kernel(
    frames,
    block_list, block_count, queries, keys, values, out_grad,
    attended, query_grad, key_grad, value_grad,
    loaded, packed, kv, qd, work, tiles, rows_out, rows_in, give, take, own, final, final_in, relay, meta_vm, meta_sm,
    load_sem, in_send, in_recv, pass_send, pass_recv,
    meta_send, meta_recv, meta_local, row_send, row_recv, row_local,
    term_send, term_recv, grad_send, grad_recv, grad_local, relay_send, relay_recv,
):
    f, s = lax.axis_index("frames"), lax.axis_index("strip")
    o = 1 - s
    partner, next_dev, prev_dev = (f, o), (f + 1, s), (f - 1, s)

    sources = (keys, values, queries, out_grad)
    loads = [pltpu.make_async_copy(sources[a], loaded.at[a], load_sem.at[a]) for a in range(4)]
    for load in loads:
        load.start()

    place_in_run = lax.rem(f, RUN)
    has_after, has_before = f < frames - 1, f > 0
    edge = ((place_in_run == RUN - 1) & has_after, (place_in_run == 0) & has_before)
    part_column = (3 * s, 1 + s)

    def relay_of(d, column):
        return (f - 2 * column if d == 0 else f + 2 * column, s)

    def relay_to(d, column):
        return (f + 1 + 2 * column if d == 0 else f - 1 - 2 * column, s)

    relay_back = 1 - lax.rem(place_in_run, 2)
    relay_column = lax.select(relay_back == 0, (RUN - 1 - place_in_run) // 2, place_in_run // 2)
    relay_half = lax.rem(relay_column, 2)
    relay_source_frame = f - place_in_run + (1 - relay_back) * (RUN - 1)
    relay_target_frame = relay_source_frame + 1 - 2 * relay_back
    is_relay = ((relay_column == 1) & (s == 0)) | ((relay_column >= 2) & (s == 1))
    is_relay = is_relay & (relay_target_frame >= 0) & (relay_target_frame < frames)
    relay_target, relay_source = (relay_target_frame, s), (relay_source_frame, s)

    barrier = pltpu.get_barrier_semaphore()

    def greet(device):
        pl.semaphore_signal(barrier, inc=1, device_id=device, device_id_type=MESH)

    greet(partner)

    @pl.when(has_after)
    def _():
        greet(next_dev)

    @pl.when(has_before)
    def _():
        greet(prev_dev)

    @pl.when(is_relay)
    def _():
        greet(relay_source)
        greet(relay_target)

    for d in range(2):
        for column in (1, 2, 3):
            @pl.when(edge[d] & (s == (0 if column == 1 else 1)))
            def _():
                greet(relay_of(d, column))
                greet(relay_to(d, column))

    at_end = (edge[0] | edge[1]).astype(jnp.int32)
    beside = has_after.astype(jnp.int32) + has_before.astype(jnp.int32)
    pl.semaphore_wait(barrier, 1 + beside + 2 * is_relay.astype(jnp.int32) + at_end * (2 + 2 * s))

    def remote(src, dst, send, recv, device):
        return pltpu.make_async_remote_copy(
            src_ref=src, dst_ref=dst, send_sem=send, recv_sem=recv,
            device_id=device, device_id_type=MESH,
        )

    def columns(half, g):
        return pl.ds(pl.multiple_of(half * (GROUPS * LANES) + g * LANES, LANES), LANES)

    def landing(g, pair, half):
        if pair == 0:
            return kv.at[g, pl.ds(FRAME + HALF * half, HALF)]
        return qd.at[g, pl.ds(HALF * half, HALF)]

    def swap(g, pair):
        return remote(
            packed.at[g, pair], landing(g, pair, s), in_send.at[g, pair], in_recv.at[g, pair], partner
        )

    def pack(g, pair):
        for a in range(2):
            lanes = slice(a * LANES, (a + 1) * LANES)
            packed[g, pair, :, :, lanes] = loaded[2 * pair + a, :, :, columns(o, g)]

    def keep(g, pair):
        own_rows = landing(g, pair, s)
        for a in range(2):
            lanes = slice(a * LANES, (a + 1) * LANES)
            own_rows[:, :, lanes] = loaded[2 * pair + a, :, :, columns(s, g)]

    neighbours = (next_dev, prev_dev)
    sends_to, hears_from = (has_after, has_before), (has_before, has_after)

    def start_part(d, part, src, dst, send, recv, phase, g):
        straight = remote(src, dst, send, recv, neighbours[d])
        if part == 0:
            bent = edge[d] & (s == 1)
        else:
            bent = edge[d]

        @pl.when(bent)
        def _():
            remote(
                src, relay.at[phase, g], send, relay_recv.at[phase, g], relay_of(d, part_column[part])
            ).start()

        @pl.when(sends_to[d] & jnp.logical_not(bent))
        def _():
            straight.start()

    def kv_window(g, base, half):
        return kv.at[g, pl.ds(base + HALF * half, HALF)]

    def pass_args(g, d, part):
        half = (s, o)[part]
        return (
            kv_window(g, FRAME, half), kv_window(g, (0, 2 * FRAME)[d], half),
            pass_send.at[g, d, half], pass_recv.at[g, d, half],
        )

    def start_pass(g, d, part):
        start_part(d, part, *pass_args(g, d, part), 0, g)

    def wait_pass(g, d, part):
        return remote(*pass_args(g, d, part), neighbours[d])

    def term_args(g, d, part):
        half = (s, o)[part]
        at = pl.ds(HALF * half, HALF)
        return (
            give.at[g, d, at], take.at[g, d, at], term_send.at[g, d, half], term_recv.at[g, d, half]
        )

    def start_terms(g, d, part):
        start_part(d, part, *term_args(g, d, part), 1, g)

    def wait_terms(g, d, part):
        return remote(*term_args(g, d, part), neighbours[d])

    def relay_on(g, phase):
        if phase == 0:
            target = kv_window(g, relay_back * (2 * FRAME), relay_half)
            recv = pass_recv.at[g, relay_back, relay_half]
        else:
            target = take.at[g, relay_back, pl.ds(HALF * relay_half, HALF)]
            recv = term_recv.at[g, relay_back, relay_half]
        return remote(relay.at[phase, g], target, relay_send.at[phase, g], recv, relay_target)

    def relay_step(g, phase):
        @pl.when(is_relay)
        def _():
            remote(
                relay.at[phase, g], relay.at[phase, g], relay_send.at[phase, g],
                relay_recv.at[phase, g], relay_target,
            ).wait_recv()
            relay_on(g, phase).start()

    def rows_across(g):
        return remote(
            rows_out.at[g, pl.ds(HALF * o, HALF)], rows_in.at[g], row_send.at[g], row_recv.at[g], partner
        )

    def grads_across(g):
        return remote(
            final.at[g, pl.ds(HALF * o, HALF)], final_in.at[g], grad_send.at[g], grad_recv.at[g], partner
        )

    row_targets, grad_targets = (query_grad, attended), (key_grad, value_grad)

    def place_copy(staged, targets, local, g, half, a):
        return pltpu.make_async_copy(
            staged.at[:, :, pl.ds(a * LANES, LANES)], targets[a].at[:, :, columns(half, g)], local.at[g, a]
        )

    def rows_along(g, a):
        return place_copy(rows_out.at[g, pl.ds(HALF * s, HALF)], row_targets, row_local, g, s, a)

    def grads_along(g, a):
        return place_copy(final.at[g, pl.ds(HALF * s, HALF)], grad_targets, grad_local, g, s, a)

    def rows_back(g, a):
        return place_copy(rows_in.at[g], row_targets, row_local.at[pl.ds(GROUPS, GROUPS)], g, o, a)

    def grads_back(g, a):
        return place_copy(final_in.at[g], grad_targets, grad_local.at[pl.ds(GROUPS, GROUPS)], g, o, a)

    share_meta = remote(meta_vm.at[s], meta_vm.at[s], meta_send, meta_recv, partner)

    def begin_keys(g):
        swap(g, 0).start()
        for d in range(2):
            start_pass(g, d, 0)

    def begin_queries(g):
        swap(g, 1).start()

    def pack_keep(g):
        for pair in range(2):
            pack(g, pair)
            keep(g, pair)

    for pair in range(2):
        loads[2 * pair].wait()
        loads[2 * pair + 1].wait()
        pack(0, pair)
        keep(0, pair)
        if pair == 0:
            begin_keys(0)
        else:
            begin_queries(0)

    listed = block_list[...]
    row_at = lax.broadcasted_iota(jnp.int32, (HALF, LANES), 0)
    lane_at = lax.broadcasted_iota(jnp.int32, (HALF, LANES), 1)
    counts = jnp.zeros((HALF, LANES), jnp.int32)
    for row in range(HALF):
        counts = jnp.where(row_at == row, block_count[row], counts)
    edge_low = jnp.where(f > 0, 0, FRAME)
    edge_high = jnp.where(f < frames - 1, WINDOW, 2 * FRAME)
    usable = (listed >= edge_low) & (listed < edge_high) & (lane_at[:, :SEL] < counts[:, :SEL])
    slots = jnp.where(usable, listed, -1)
    place = jnp.full((HALF, LANES), SEL, jnp.int32)
    for j in range(SEL):
        place = jnp.where(lane_at - PLACE_AT == slots[:, j:j + 1], j, place)
    meta_vm[s, 0:HALF] = place
    meta_vm[s, 0:HALF, 0:SEL] = listed
    meta_vm[s, HALF:] = jnp.zeros((HALF, LANES), jnp.int32)
    meta_vm[s, HALF:, 0:SEL] = usable.astype(jnp.int32)
    share_meta.start()
    pack_keep(1)
    begin_keys(1)
    pack_keep(2)
    tiles[:, SEL] = jnp.zeros((FRAME, BLOCK, 2 * LANES), jnp.float32)

    def forward(g):
        swap(g, 0).wait_recv()
        for d in range(2):
            start_pass(g, d, 1)

    def clear(w, carry):
        @pl.when(jnp.logical_not(has_before))
        def _():
            for g in range(GROUPS):
                kv[g, w] = jnp.zeros((BLOCK, 2 * LANES), jnp.bfloat16)
                take[g, 0, w] = jnp.zeros((BLOCK, 2 * LANES), jnp.bfloat16)

        @pl.when(jnp.logical_not(has_after))
        def _():
            for g in range(GROUPS):
                kv[g, 2 * FRAME + w] = jnp.zeros((BLOCK, 2 * LANES), jnp.bfloat16)
                take[g, 1, w] = jnp.zeros((BLOCK, 2 * LANES), jnp.bfloat16)

        return carry

    lax.fori_loop(0, FRAME, clear, 0)
    forward(0)
    begin_keys(2)
    begin_queries(1)
    share_meta.wait()
    to_scalar = pltpu.make_async_copy(meta_vm, meta_sm, meta_local)
    to_scalar.start()
    relay_step(0, 0)
    to_scalar.wait()
    pack_keep(3)

    row_ids = lax.broadcasted_iota(jnp.int32, (4 * HD, 4 * HD), 0) // HD
    col_ids = lax.broadcasted_iota(jnp.int32, (4 * HD, 4 * HD), 1) // HD
    spread = jnp.where(
        row_ids == col_ids, jnp.where(col_ids < 2, FACTOR, 1.0), 0.0
    ).astype(jnp.bfloat16)
    first_head = lax.broadcasted_iota(jnp.int32, (BLOCK, LANES), 1) < HD

    def heads(full):
        return jnp.where(first_head, full[:HD], full[HD:])

    def fold(array, op):
        return op(array.reshape(array.shape[0] // 8, 8, LANES), axis=0)

    def attend(g, b):
        strip, row = b // HALF, lax.rem(b, HALF)
        chunks = ((0, 4), (4, 8), (8, SEL))
        keep = {"slabs": [None] * SEL, "powers": [None] * SEL}

        def diagonal():
            keep["diagonal"] = jnp.concatenate([qd[g, b]] * 4, axis=0) * spread
            keep["bias"] = [
                jnp.where(meta_sm[strip, HALF + row, j] > 0, 0.0, MASKED).astype(jnp.float32)
                for j in range(SEL)
            ]

        def products(c):
            low, high = chunks[c]
            picked = jnp.concatenate([work[meta_sm[strip, row, j]] for j in range(low, high)], axis=0)
            keep["picked", c] = picked
            both = lax.dot_general(
                picked, keep["diagonal"], (((1,), (1,)), ((), ())), preferred_element_type=jnp.float32
            )
            for j in range(low, high):
                at = slice((j - low) * BLOCK, (j - low + 1) * BLOCK)
                keep["scores", j] = both[at, :LANES]
                keep["grad_weights", j] = both[at, LANES:]

        def peak(c):
            for j in range(*chunks[c]):
                top = fold(keep["scores", j], jnp.max) + keep["bias"][j]
                keep["peak"] = jnp.maximum(keep["peak"], top) if j else top
            if c == len(chunks) - 1:
                keep["peak"] = jnp.max(keep["peak"], axis=0, keepdims=True)

        def power(j):
            powers = jnp.exp(keep["scores", j] - (keep["peak"] - keep["bias"][j]))
            keep["powers"][j] = powers
            total = fold(powers, jnp.sum)
            dots = fold(powers * keep["grad_weights", j], jnp.sum)
            keep["total"] = keep["total"] + total if j else total
            keep["dots"] = keep["dots"] + dots if j else dots
            if j == SEL - 1:
                keep["scale"] = 1.0 / jnp.sum(keep["total"], axis=0, keepdims=True)
                keep["row_dots"] = jnp.sum(keep["dots"], axis=0, keepdims=True) * keep["scale"]

        def slab(j):
            weights = keep["powers"][j] * keep["scale"]
            grad_scores = weights * (keep["grad_weights", j] - keep["row_dots"])
            keep["slabs"][j] = (grad_scores.astype(jnp.bfloat16), weights.astype(jnp.bfloat16))

        def terms(c):
            low, high = chunks[c]
            parts = [jnp.concatenate([pair[k] for pair in keep["slabs"][low:high]], axis=0) for k in range(2)]
            keep["parts", c] = parts
            result = jnp.dot(
                jnp.concatenate(parts, axis=1), keep["diagonal"], preferred_element_type=jnp.float32
            )
            tiles[b, low:high] = result.reshape(high - low, BLOCK, 2 * LANES)

        def mixed(c):
            for k in range(2):
                lanes = slice(k * LANES, (k + 1) * LANES)
                product = lax.dot_general(
                    keep["parts", c][k], keep["picked", c][:, lanes], (((0,), (0,)), ((), ())),
                    preferred_element_type=jnp.float32,
                )
                keep["mixed", k] = keep["mixed", k] + product if c else product
            if c == len(chunks) - 1:
                rows_out[g, b] = jnp.concatenate(
                    [heads(keep["mixed", 0]) * FACTOR, heads(keep["mixed", 1])], axis=1
                ).astype(jnp.bfloat16)

        def call(function, *args):
            return lambda: function(*args)

        count = range(len(chunks))
        return (
            [diagonal] + [call(products, c) for c in count],
            [call(peak, c) for c in count] + [call(power, j) for j in range(SEL)] + [call(slab, j) for j in range(SEL)],
            [call(step, c) for c in count for step in (terms, mixed)],
        )

    def interleave(stages):
        placed = [
            ((k + 0.5) / len(stage), n, step)
            for n, stage in enumerate(stages)
            for k, step in enumerate(stage)
        ]
        for _, _, step in sorted(placed, key=lambda item: item[:2]):
            step()

    def finish(g):
        slot = lax.rem(g, 2)
        for d in range(2):
            @pl.when(hears_from[d])
            def _():
                for part in range(2):
                    wait_terms(g, d, part).wait_recv()

        def add(w, carry):
            total = own[slot, w] + take[g, 0, w].astype(jnp.float32) + take[g, 1, w].astype(jnp.float32)
            final[g, w] = total.astype(jnp.bfloat16)
            return carry

        lax.fori_loop(0, FRAME, add, 0)
        grads_across(g).start()
        for a in range(2):
            grads_along(g, a).start()
        rows_across(g).wait_recv()
        for a in range(2):
            rows_back(g, a).start()

    def one_group(g, carry):
        swap(g, 1).wait_recv()
        for d in range(2):
            @pl.when(hears_from[d])
            def _():
                for part in range(2):
                    wait_pass(g, d, part).wait_recv()

        work[...] = kv[g]

        blocks = [attend(g, lax.rem(HALF * o + i, FRAME)) for i in range(FRAME)]
        for turn in range(FRAME + 2):
            interleave([blocks[turn - k][k] for k in (2, 1, 0) if 0 <= turn - k < FRAME])
            if turn == 3:
                @pl.when(g == 0)
                def _():
                    forward(1)
                    begin_keys(3)
                    begin_queries(2)

                @pl.when((g > 0) & (g + 1 < GROUPS))
                def _():
                    relay_step(g + 1, 0)

                @pl.when(g == 1)
                def _():
                    rows_across(0).start()

                @pl.when(g > 1)
                def _():
                    finish(g - 2)

            if turn == 7:
                @pl.when(g == 0)
                def _():
                    begin_queries(3)
                    relay_step(1, 0)

                @pl.when(g + 2 < GROUPS)
                def _():
                    forward(g + 2)

                @pl.when(g > 0)
                def _():
                    relay_step(g - 1, 1)

        for a in range(2):
            rows_along(g, a).start()

        def gather(w, base):
            acc = None
            for b in range(FRAME):
                place = meta_sm[b // HALF, b % HALF, PLACE_AT + base + w]
                tile = tiles[b, place]
                acc = tile if acc is None else acc + tile
            return acc

        def collect(w, inner):
            give[g, 1, w] = gather(w, 0).astype(jnp.bfloat16)
            give[g, 0, w] = gather(w, 2 * FRAME).astype(jnp.bfloat16)
            return inner

        lax.fori_loop(0, FRAME, collect, 0)
        for d in range(2):
            for part in range(2):
                start_terms(g, d, part)

        @pl.when((g > 0) & (g < GROUPS - 1))
        def _():
            rows_across(g).start()

        def collect_own(w, inner):
            own[lax.rem(g, 2), w] = gather(w, FRAME)
            return inner

        lax.fori_loop(0, FRAME, collect_own, 0)

        return carry

    lax.fori_loop(0, GROUPS, one_group, 0)
    relay_step(GROUPS - 1, 1)
    rows_across(GROUPS - 1).start()
    finish(GROUPS - 2)
    finish(GROUPS - 1)

    def land(g, carry):
        grads_across(g).wait_recv()
        for a in range(2):
            grads_back(g, a).start()
        return carry

    lax.fori_loop(0, GROUPS, land, 0)

    def drain(g, carry):
        for pair in range(2):
            swap(g, pair).wait_send()
        for d in range(2):
            @pl.when(sends_to[d])
            def _():
                for part in range(2):
                    wait_pass(g, d, part).wait_send()
                    wait_terms(g, d, part).wait_send()

        @pl.when(is_relay)
        def _():
            for phase in range(2):
                relay_on(g, phase).wait_send()

        rows_across(g).wait_send()
        grads_across(g).wait_send()
        for a in range(2):
            rows_along(g, a).wait()
            grads_along(g, a).wait()
            rows_back(g, a).wait()
            grads_back(g, a).wait()
        return carry

    lax.fori_loop(0, GROUPS, drain, 0)


def hand_over(*refs):
    sources, targets, held, in_sems, out_sems = refs[:4], refs[4:8], refs[8], refs[9], refs[10]
    spots = [(i, at) for i in range(4) for at in range(HALF)]
    ins = [pltpu.make_async_copy(sources[i].at[at], held.at[i, at], in_sems.at[i, at]) for i, at in spots]
    outs = [pltpu.make_async_copy(held.at[i, at], targets[i].at[at], out_sems.at[i, at]) for i, at in spots]
    for copy in ins:
        copy.start()
    for arrives, leaves in zip(ins, outs):
        arrives.wait()
        leaves.start()
    for copy in outs:
        copy.wait()


def body(queries, keys, values, out_grad, block_list, block_count):
    rows, width = queries.shape
    frames = lax.axis_size("frames")
    blocked = [x.reshape(HALF, BLOCK, width) for x in (queries, keys, values, out_grad)]
    shape = jax.ShapeDtypeStruct((HALF, BLOCK, width), jnp.bfloat16)
    dma = pltpu.SemaphoreType.DMA
    flops = 6 * 2 * FRAME * SEL * BLOCK * 256 * 256 * GROUPS
    outs = pl.pallas_call(
        lambda *refs: kernel(frames, *refs),
        out_shape=[shape] * 4,
        in_specs=[pl.BlockSpec(memory_space=pltpu.VMEM), pl.BlockSpec(memory_space=pltpu.SMEM)] + [pl.BlockSpec(memory_space=pl.ANY)] * 4,
        out_specs=[pl.BlockSpec(memory_space=pl.ANY)] * 4,
        scratch_shapes=[
            pltpu.VMEM((4, HALF, BLOCK, width), jnp.bfloat16),
            pltpu.VMEM((GROUPS, 2, HALF, BLOCK, 2 * LANES), jnp.bfloat16),
            pltpu.VMEM((GROUPS, WINDOW, BLOCK, 2 * LANES), jnp.bfloat16),
            pltpu.VMEM((GROUPS, FRAME, BLOCK, 2 * LANES), jnp.bfloat16),
            pltpu.VMEM((WINDOW, BLOCK, 2 * LANES), jnp.bfloat16),
            pltpu.VMEM((FRAME, SEL + 1, BLOCK, 2 * LANES), jnp.float32),
            pltpu.VMEM((GROUPS, FRAME, BLOCK, 2 * LANES), jnp.bfloat16),
            pltpu.VMEM((GROUPS, HALF, BLOCK, 2 * LANES), jnp.bfloat16),
            pltpu.VMEM((GROUPS, 2, FRAME, BLOCK, 2 * LANES), jnp.bfloat16),
            pltpu.VMEM((GROUPS, 2, FRAME, BLOCK, 2 * LANES), jnp.bfloat16),
            pltpu.VMEM((2, FRAME, BLOCK, 2 * LANES), jnp.float32),
            pltpu.VMEM((GROUPS, FRAME, BLOCK, 2 * LANES), jnp.bfloat16),
            pltpu.VMEM((GROUPS, HALF, BLOCK, 2 * LANES), jnp.bfloat16),
            pltpu.VMEM((2, GROUPS, HALF, BLOCK, 2 * LANES), jnp.bfloat16),
            pltpu.VMEM((2, 8, LANES), jnp.int32),
            pltpu.SMEM((2, 8, LANES), jnp.int32),
            dma((4,)), dma((GROUPS, 2)), dma((GROUPS, 2)),
            dma((GROUPS, 2, 2)), dma((GROUPS, 2, 2)),
            dma, dma, dma,
            dma((GROUPS,)), dma((GROUPS,)), dma((2 * GROUPS, 2)),
            dma((GROUPS, 2, 2)), dma((GROUPS, 2, 2)),
            dma((GROUPS,)), dma((GROUPS,)), dma((2 * GROUPS, 2)),
            dma((2, GROUPS)), dma((2, GROUPS)),
        ],
        cost_estimate=pl.CostEstimate(
            flops=flops, bytes_accessed=16 * rows * width, transcendentals=FRAME * SEL * BLOCK * LANES * GROUPS
        ),
        compiler_params=pltpu.CompilerParams(
            collective_id=0, has_side_effects=True, vmem_limit_bytes=60 * 1024 * 1024
        ),
    )(block_list, block_count, *blocked)
    outs = pl.pallas_call(
        hand_over,
        out_shape=[shape] * 4,
        in_specs=[pl.BlockSpec(memory_space=pl.ANY)] * 4,
        out_specs=[pl.BlockSpec(memory_space=pl.ANY)] * 4,
        scratch_shapes=[
            pltpu.VMEM((4, HALF, BLOCK, width), jnp.bfloat16), dma((4, HALF)), dma((4, HALF)),
        ],
        compiler_params=pltpu.CompilerParams(vmem_limit_bytes=60 * 1024 * 1024),
    )(*outs)
    return tuple(x.reshape(rows, width) for x in outs)


def solution(mesh):
    split = P(("frames", "strip"), None)
    in_specs = (split, split, split, split, split, P(("frames", "strip")))
    return jax.shard_map(
        body, mesh=mesh, in_specs=in_specs, out_specs=(split,) * 4, check_vma=False
    )
```

```python
import jax
import jax.numpy as jnp
from jax import lax
from jax.experimental import pallas as pl
from jax.experimental.pallas import tpu as pltpu
from jax.sharding import PartitionSpec as P

HD = 64
BLOCK = 64
SEL = 13
HALF = 4
FRAME = 8
WINDOW = 24
GROUPS = 4
LANES = 128
FACTOR = 0.125
MASKED = -1e30
PLACE_AT = 32
RUN = 8
MESH = pl.DeviceIdType.MESH


def kernel(
    frames,
    block_list, block_count, queries, keys, values, out_grad,
    attended, query_grad, key_grad, value_grad,
    loaded, packed, kv, qd, work, tiles, rows_out, rows_in, give, take, own, final, final_in, relay, meta_vm, meta_sm,
    load_sem, in_send, in_recv, pass_send, pass_recv,
    meta_send, meta_recv, meta_local, row_send, row_recv, row_local,
    term_send, term_recv, grad_send, grad_recv, grad_local, relay_send, relay_recv, slant_send,
):
    f, s = lax.axis_index("frames"), lax.axis_index("strip")
    o = 1 - s
    partner, next_dev, prev_dev = (f, o), (f + 1, s), (f - 1, s)

    sources = (keys, values, queries, out_grad)
    loads = [pltpu.make_async_copy(sources[a], loaded.at[a], load_sem.at[a]) for a in range(4)]
    for load in loads:
        load.start()

    place_in_run = lax.rem(f, RUN)
    has_after, has_before = f < frames - 1, f > 0
    edge = ((place_in_run == RUN - 1) & has_after, (place_in_run == 0) & has_before)
    part_column = (3 * s, 1 + s)

    def relay_of(d, column):
        return (f - 2 * column if d == 0 else f + 2 * column, s)

    def relay_to(d, column):
        return (f + 1 + 2 * column if d == 0 else f - 1 - 2 * column, s)

    relay_back = 1 - lax.rem(place_in_run, 2)
    relay_column = lax.select(relay_back == 0, (RUN - 1 - place_in_run) // 2, place_in_run // 2)
    relay_half = lax.rem(relay_column, 2)
    relay_source_frame = f - place_in_run + (1 - relay_back) * (RUN - 1)
    relay_target_frame = relay_source_frame + 1 - 2 * relay_back
    is_relay = ((relay_column == 1) & (s == 0)) | ((relay_column >= 2) & (s == 1))
    is_relay = is_relay & (relay_target_frame >= 0) & (relay_target_frame < frames)
    relay_target, relay_source = (relay_target_frame, s), (relay_source_frame, s)

    barrier = pltpu.get_barrier_semaphore()

    def greet(device):
        pl.semaphore_signal(barrier, inc=1, device_id=device, device_id_type=MESH)

    greet(partner)

    @pl.when(has_after)
    def _():
        greet(next_dev)

    @pl.when(has_before)
    def _():
        greet(prev_dev)

    @pl.when(is_relay)
    def _():
        greet(relay_source)
        greet(relay_target)

    for d in range(2):
        for column in (1, 2, 3):
            @pl.when(edge[d] & (s == (0 if column == 1 else 1)))
            def _():
                greet(relay_of(d, column))
                greet(relay_to(d, column))

    slant = (edge[0] & (s == 1), edge[1] & (s == 0))
    slant_to = ((f + 1, 0), (f - 1, 1))
    for d in range(2):
        @pl.when(slant[d])
        def _():
            greet(slant_to[d])

    at_end = (edge[0] | edge[1]).astype(jnp.int32)
    slants = (slant[0] | slant[1]).astype(jnp.int32)
    beside = has_after.astype(jnp.int32) + has_before.astype(jnp.int32)
    pl.semaphore_wait(barrier, 1 + beside + slants + 2 * is_relay.astype(jnp.int32) + at_end * (2 + 2 * s))

    def remote(src, dst, send, recv, device):
        return pltpu.make_async_remote_copy(
            src_ref=src, dst_ref=dst, send_sem=send, recv_sem=recv,
            device_id=device, device_id_type=MESH,
        )

    def columns(half, g):
        return pl.ds(pl.multiple_of(half * (GROUPS * LANES) + g * LANES, LANES), LANES)

    def landing(g, pair, half):
        if pair == 0:
            return kv.at[g, pl.ds(FRAME + HALF * half, HALF)]
        return qd.at[g, pl.ds(HALF * half, HALF)]

    def swap(g, pair):
        return remote(
            packed.at[g, pair], landing(g, pair, s), in_send.at[g, pair], in_recv.at[g, pair], partner
        )

    def pack(g, pair):
        for a in range(2):
            lanes = slice(a * LANES, (a + 1) * LANES)
            packed[g, pair, :, :, lanes] = loaded[2 * pair + a, :, :, columns(o, g)]

    def keep(g, pair):
        own_rows = landing(g, pair, s)
        for a in range(2):
            lanes = slice(a * LANES, (a + 1) * LANES)
            own_rows[:, :, lanes] = loaded[2 * pair + a, :, :, columns(s, g)]

    neighbours = (next_dev, prev_dev)
    sends_to, hears_from = (has_after, has_before), (has_before, has_after)

    def skipped(d, g):
        return edge[d] & (s == d) & (g == 0)

    def start_part(d, part, src, dst, send, recv, phase, g):
        straight = remote(src, dst, send, recv, neighbours[d])
        starts = sends_to[d]
        if part == 0:
            bent = edge[d] & (s == 1)
        elif phase == 0:
            bent = edge[d] & (g > 0)
            starts = starts & jnp.logical_not(skipped(d, g))
        else:
            bent = edge[d]

        @pl.when(bent)
        def _():
            remote(
                src, relay.at[phase, g], send, relay_recv.at[phase, g], relay_of(d, part_column[part])
            ).start()

        @pl.when(starts & jnp.logical_not(bent))
        def _():
            straight.start()

    def kv_window(g, base, half):
        return kv.at[g, pl.ds(base + HALF * half, HALF)]

    def pass_args(g, d, part):
        half = (s, o)[part]
        return (
            kv_window(g, FRAME, half), kv_window(g, (0, 2 * FRAME)[d], half),
            pass_send.at[g, d, half], pass_recv.at[g, d, half],
        )

    def start_pass(g, d, part):
        start_part(d, part, *pass_args(g, d, part), 0, g)

    def wait_pass(g, d, part):
        return remote(*pass_args(g, d, part), neighbours[d])

    def term_args(g, d, part):
        half = (s, o)[part]
        at = pl.ds(HALF * half, HALF)
        return (
            give.at[g, d, at], take.at[g, d, at], term_send.at[g, d, half], term_recv.at[g, d, half]
        )

    def start_terms(g, d, part):
        start_part(d, part, *term_args(g, d, part), 1, g)

    def wait_terms(g, d, part):
        return remote(*term_args(g, d, part), neighbours[d])

    def relay_on(g, phase):
        if phase == 0:
            target = kv_window(g, relay_back * (2 * FRAME), relay_half)
            recv = pass_recv.at[g, relay_back, relay_half]
        else:
            target = take.at[g, relay_back, pl.ds(HALF * relay_half, HALF)]
            recv = term_recv.at[g, relay_back, relay_half]
        return remote(relay.at[phase, g], target, relay_send.at[phase, g], recv, relay_target)

    def relays(g, phase):
        return is_relay & ((relay_column == 3) | (g > 0)) if phase == 0 else is_relay

    def slant_copy(d):
        base = (0, 2 * FRAME)[d]
        return remote(
            packed.at[0, 0], kv_window(0, base, s), slant_send, pass_recv.at[0, d, s], slant_to[d]
        )

    def relay_step(g, phase):
        @pl.when(relays(g, phase))
        def _():
            remote(
                relay.at[phase, g], relay.at[phase, g], relay_send.at[phase, g],
                relay_recv.at[phase, g], relay_target,
            ).wait_recv()
            relay_on(g, phase).start()

    def rows_across(g):
        return remote(
            rows_out.at[g, pl.ds(HALF * o, HALF)], rows_in.at[g], row_send.at[g], row_recv.at[g], partner
        )

    def grads_across(g):
        return remote(
            final.at[g, pl.ds(HALF * o, HALF)], final_in.at[g], grad_send.at[g], grad_recv.at[g], partner
        )

    row_targets, grad_targets = (query_grad, attended), (key_grad, value_grad)

    def place_copy(staged, targets, local, g, half, a):
        return pltpu.make_async_copy(
            staged.at[:, :, pl.ds(a * LANES, LANES)], targets[a].at[:, :, columns(half, g)], local.at[g, a]
        )

    def rows_along(g, a):
        return place_copy(rows_out.at[g, pl.ds(HALF * s, HALF)], row_targets, row_local, g, s, a)

    def grads_along(g, a):
        return place_copy(final.at[g, pl.ds(HALF * s, HALF)], grad_targets, grad_local, g, s, a)

    def rows_back(g, a):
        return place_copy(rows_in.at[g], row_targets, row_local.at[pl.ds(GROUPS, GROUPS)], g, o, a)

    def grads_back(g, a):
        return place_copy(final_in.at[g], grad_targets, grad_local.at[pl.ds(GROUPS, GROUPS)], g, o, a)

    share_meta = remote(meta_vm.at[s], meta_vm.at[s], meta_send, meta_recv, partner)

    def begin_keys(g):
        swap(g, 0).start()
        for d in range(2):
            start_pass(g, d, 0)

    def begin_queries(g):
        swap(g, 1).start()

    def pack_keep(g):
        for pair in range(2):
            pack(g, pair)
            keep(g, pair)

    for pair in range(2):
        loads[2 * pair].wait()
        loads[2 * pair + 1].wait()
        pack(0, pair)
        keep(0, pair)
        if pair == 0:
            begin_keys(0)
            for d in range(2):
                @pl.when(slant[d])
                def _():
                    slant_copy(d).start()
        else:
            begin_queries(0)

    listed = block_list[...]
    row_at = lax.broadcasted_iota(jnp.int32, (HALF, LANES), 0)
    lane_at = lax.broadcasted_iota(jnp.int32, (HALF, LANES), 1)
    counts = jnp.zeros((HALF, LANES), jnp.int32)
    for row in range(HALF):
        counts = jnp.where(row_at == row, block_count[row], counts)
    edge_low = jnp.where(f > 0, 0, FRAME)
    edge_high = jnp.where(f < frames - 1, WINDOW, 2 * FRAME)
    usable = (listed >= edge_low) & (listed < edge_high) & (lane_at[:, :SEL] < counts[:, :SEL])
    slots = jnp.where(usable, listed, -1)
    place = jnp.full((HALF, LANES), SEL, jnp.int32)
    for j in range(SEL):
        place = jnp.where(lane_at - PLACE_AT == slots[:, j:j + 1], j, place)
    meta_vm[s, 0:HALF] = place
    meta_vm[s, 0:HALF, 0:SEL] = listed
    meta_vm[s, HALF:] = jnp.zeros((HALF, LANES), jnp.int32)
    meta_vm[s, HALF:, 0:SEL] = usable.astype(jnp.int32)
    share_meta.start()
    pack_keep(1)
    begin_keys(1)
    pack_keep(2)
    tiles[:, SEL] = jnp.zeros((FRAME, BLOCK, 2 * LANES), jnp.float32)

    def forward(g):
        swap(g, 0).wait_recv()
        for d in range(2):
            start_pass(g, d, 1)

    def clear(w, carry):
        @pl.when(jnp.logical_not(has_before))
        def _():
            for g in range(GROUPS):
                kv[g, w] = jnp.zeros((BLOCK, 2 * LANES), jnp.bfloat16)
                take[g, 0, w] = jnp.zeros((BLOCK, 2 * LANES), jnp.bfloat16)

        @pl.when(jnp.logical_not(has_after))
        def _():
            for g in range(GROUPS):
                kv[g, 2 * FRAME + w] = jnp.zeros((BLOCK, 2 * LANES), jnp.bfloat16)
                take[g, 1, w] = jnp.zeros((BLOCK, 2 * LANES), jnp.bfloat16)

        return carry

    lax.fori_loop(0, FRAME, clear, 0)
    relay_step(0, 0)
    forward(0)
    begin_keys(2)
    begin_queries(1)
    share_meta.wait()
    to_scalar = pltpu.make_async_copy(meta_vm, meta_sm, meta_local)
    to_scalar.start()
    to_scalar.wait()
    pack_keep(3)

    row_ids = lax.broadcasted_iota(jnp.int32, (4 * HD, 4 * HD), 0) // HD
    col_ids = lax.broadcasted_iota(jnp.int32, (4 * HD, 4 * HD), 1) // HD
    spread = jnp.where(
        row_ids == col_ids, jnp.where(col_ids < 2, FACTOR, 1.0), 0.0
    ).astype(jnp.bfloat16)
    first_head = lax.broadcasted_iota(jnp.int32, (BLOCK, LANES), 1) < HD

    def heads(full):
        return jnp.where(first_head, full[:HD], full[HD:])

    def fold(array, op):
        return op(array.reshape(array.shape[0] // 8, 8, LANES), axis=0)

    def attend(g, b):
        strip, row = b // HALF, lax.rem(b, HALF)
        chunks = ((0, 4), (4, 8), (8, SEL))
        keep = {"slabs": [None] * SEL, "powers": [None] * SEL}

        def diagonal():
            keep["diagonal"] = jnp.concatenate([qd[g, b]] * 4, axis=0) * spread
            keep["bias"] = [
                jnp.where(meta_sm[strip, HALF + row, j] > 0, 0.0, MASKED).astype(jnp.float32)
                for j in range(SEL)
            ]

        def products(c):
            low, high = chunks[c]
            picked = jnp.concatenate([work[meta_sm[strip, row, j]] for j in range(low, high)], axis=0)
            keep["picked", c] = picked
            both = lax.dot_general(
                picked, keep["diagonal"], (((1,), (1,)), ((), ())), preferred_element_type=jnp.float32
            )
            for j in range(low, high):
                at = slice((j - low) * BLOCK, (j - low + 1) * BLOCK)
                keep["scores", j] = both[at, :LANES]
                keep["grad_weights", j] = both[at, LANES:]

        def peak(c):
            for j in range(*chunks[c]):
                top = fold(keep["scores", j], jnp.max) + keep["bias"][j]
                keep["peak"] = jnp.maximum(keep["peak"], top) if j else top
            if c == len(chunks) - 1:
                keep["peak"] = jnp.max(keep["peak"], axis=0, keepdims=True)

        def power(j):
            powers = jnp.exp(keep["scores", j] - (keep["peak"] - keep["bias"][j]))
            keep["powers"][j] = powers
            total = fold(powers, jnp.sum)
            dots = fold(powers * keep["grad_weights", j], jnp.sum)
            keep["total"] = keep["total"] + total if j else total
            keep["dots"] = keep["dots"] + dots if j else dots
            if j == SEL - 1:
                keep["scale"] = 1.0 / jnp.sum(keep["total"], axis=0, keepdims=True)
                keep["row_dots"] = jnp.sum(keep["dots"], axis=0, keepdims=True) * keep["scale"]

        def slab(j):
            weights = keep["powers"][j] * keep["scale"]
            grad_scores = weights * (keep["grad_weights", j] - keep["row_dots"])
            keep["slabs"][j] = (grad_scores.astype(jnp.bfloat16), weights.astype(jnp.bfloat16))

        def terms(c):
            low, high = chunks[c]
            parts = [jnp.concatenate([pair[k] for pair in keep["slabs"][low:high]], axis=0) for k in range(2)]
            keep["parts", c] = parts
            result = jnp.dot(
                jnp.concatenate(parts, axis=1), keep["diagonal"], preferred_element_type=jnp.float32
            )
            tiles[b, low:high] = result.reshape(high - low, BLOCK, 2 * LANES)

        def mixed(c):
            for k in range(2):
                lanes = slice(k * LANES, (k + 1) * LANES)
                product = lax.dot_general(
                    keep["parts", c][k], keep["picked", c][:, lanes], (((0,), (0,)), ((), ())),
                    preferred_element_type=jnp.float32,
                )
                keep["mixed", k] = keep["mixed", k] + product if c else product
            if c == len(chunks) - 1:
                rows_out[g, b] = jnp.concatenate(
                    [heads(keep["mixed", 0]) * FACTOR, heads(keep["mixed", 1])], axis=1
                ).astype(jnp.bfloat16)

        def call(function, *args):
            return lambda: function(*args)

        count = range(len(chunks))
        return (
            [diagonal] + [call(products, c) for c in count],
            [call(peak, c) for c in count] + [call(power, j) for j in range(SEL)] + [call(slab, j) for j in range(SEL)],
            [call(step, c) for c in count for step in (terms, mixed)],
        )

    def interleave(stages):
        placed = [
            ((k + 0.5) / len(stage), n, step)
            for n, stage in enumerate(stages)
            for k, step in enumerate(stage)
        ]
        for _, _, step in sorted(placed, key=lambda item: item[:2]):
            step()

    def finish(g):
        slot = lax.rem(g, 2)
        for d in range(2):
            @pl.when(hears_from[d])
            def _():
                for part in range(2):
                    wait_terms(g, d, part).wait_recv()

        def add(w, carry):
            total = own[slot, w] + take[g, 0, w].astype(jnp.float32) + take[g, 1, w].astype(jnp.float32)
            final[g, w] = total.astype(jnp.bfloat16)
            return carry

        lax.fori_loop(0, FRAME, add, 0)
        grads_across(g).start()
        for a in range(2):
            grads_along(g, a).start()
        rows_across(g).wait_recv()
        for a in range(2):
            rows_back(g, a).start()

    def one_group(g, carry):
        swap(g, 1).wait_recv()
        for d in range(2):
            @pl.when(hears_from[d])
            def _():
                for part in range(2):
                    wait_pass(g, d, part).wait_recv()

        work[...] = kv[g]

        blocks = [attend(g, lax.rem(HALF * o + i, FRAME)) for i in range(FRAME)]
        for turn in range(FRAME + 2):
            interleave([blocks[turn - k][k] for k in (2, 1, 0) if 0 <= turn - k < FRAME])
            if turn == 3:
                @pl.when(g == 0)
                def _():
                    forward(1)
                    begin_keys(3)
                    begin_queries(2)

                @pl.when((g > 0) & (g + 1 < GROUPS))
                def _():
                    relay_step(g + 1, 0)

                @pl.when(g == GROUPS - 1)
                def _():
                    rows_across(GROUPS - 2).start()

            if turn == 7:
                @pl.when(g == 0)
                def _():
                    begin_queries(3)
                    relay_step(1, 0)

                @pl.when(g + 2 < GROUPS)
                def _():
                    forward(g + 2)

                @pl.when(g > 0)
                def _():
                    relay_step(g - 1, 1)

                @pl.when((g > 0) & (g < GROUPS - 1))
                def _():
                    rows_across(g - 1).start()

                @pl.when(g > 1)
                def _():
                    finish(g - 2)

        for a in range(2):
            rows_along(g, a).start()

        def gather(w, base):
            acc = None
            for b in range(FRAME):
                place = meta_sm[b // HALF, b % HALF, PLACE_AT + base + w]
                tile = tiles[b, place]
                acc = tile if acc is None else acc + tile
            return acc

        def collect(w, inner):
            give[g, 1, w] = gather(w, 0).astype(jnp.bfloat16)
            give[g, 0, w] = gather(w, 2 * FRAME).astype(jnp.bfloat16)
            return inner

        lax.fori_loop(0, FRAME, collect, 0)
        for d in range(2):
            for part in range(2):
                start_terms(g, d, part)

        def collect_own(w, inner):
            own[lax.rem(g, 2), w] = gather(w, FRAME)
            return inner

        lax.fori_loop(0, FRAME, collect_own, 0)

        return carry

    lax.fori_loop(0, GROUPS, one_group, 0)
    relay_step(GROUPS - 1, 1)
    rows_across(GROUPS - 1).start()
    finish(GROUPS - 2)
    finish(GROUPS - 1)

    def land(g, carry):
        grads_across(g).wait_recv()
        for a in range(2):
            grads_back(g, a).start()
        return carry

    lax.fori_loop(0, GROUPS, land, 0)

    def drain(g, carry):
        for pair in range(2):
            swap(g, pair).wait_send()
        for d in range(2):
            @pl.when(sends_to[d])
            def _():
                for part in range(2):
                    wait_terms(g, d, part).wait_send()
                wait_pass(g, d, 0).wait_send()

                @pl.when(jnp.logical_not(skipped(d, g)))
                def _():
                    wait_pass(g, d, 1).wait_send()

        for phase in range(2):
            @pl.when(relays(g, phase))
            def _():
                relay_on(g, phase).wait_send()

        rows_across(g).wait_send()
        grads_across(g).wait_send()
        for a in range(2):
            rows_along(g, a).wait()
            grads_along(g, a).wait()
            rows_back(g, a).wait()
            grads_back(g, a).wait()
        return carry

    lax.fori_loop(0, GROUPS, drain, 0)
    for d in range(2):
        @pl.when(slant[d])
        def _():
            slant_copy(d).wait_send()


def hand_over(*refs):
    sources, targets, held, in_sems, out_sems = refs[:4], refs[4:8], refs[8], refs[9], refs[10]
    spots = [(i, at) for i in range(4) for at in range(HALF)]
    ins = [pltpu.make_async_copy(sources[i].at[at], held.at[i, at], in_sems.at[i, at]) for i, at in spots]
    outs = [pltpu.make_async_copy(held.at[i, at], targets[i].at[at], out_sems.at[i, at]) for i, at in spots]
    for copy in ins:
        copy.start()
    for arrives, leaves in zip(ins, outs):
        arrives.wait()
        leaves.start()
    for copy in outs:
        copy.wait()


def body(queries, keys, values, out_grad, block_list, block_count):
    rows, width = queries.shape
    frames = lax.axis_size("frames")
    blocked = [x.reshape(HALF, BLOCK, width) for x in (queries, keys, values, out_grad)]
    shape = jax.ShapeDtypeStruct((HALF, BLOCK, width), jnp.bfloat16)
    dma = pltpu.SemaphoreType.DMA
    flops = 6 * 2 * FRAME * SEL * BLOCK * 256 * 256 * GROUPS
    outs = pl.pallas_call(
        lambda *refs: kernel(frames, *refs),
        out_shape=[shape] * 4,
        in_specs=[pl.BlockSpec(memory_space=pltpu.VMEM), pl.BlockSpec(memory_space=pltpu.SMEM)] + [pl.BlockSpec(memory_space=pl.ANY)] * 4,
        out_specs=[pl.BlockSpec(memory_space=pl.ANY)] * 4,
        scratch_shapes=[
            pltpu.VMEM((4, HALF, BLOCK, width), jnp.bfloat16),
            pltpu.VMEM((GROUPS, 2, HALF, BLOCK, 2 * LANES), jnp.bfloat16),
            pltpu.VMEM((GROUPS, WINDOW, BLOCK, 2 * LANES), jnp.bfloat16),
            pltpu.VMEM((GROUPS, FRAME, BLOCK, 2 * LANES), jnp.bfloat16),
            pltpu.VMEM((WINDOW, BLOCK, 2 * LANES), jnp.bfloat16),
            pltpu.VMEM((FRAME, SEL + 1, BLOCK, 2 * LANES), jnp.float32),
            pltpu.VMEM((GROUPS, FRAME, BLOCK, 2 * LANES), jnp.bfloat16),
            pltpu.VMEM((GROUPS, HALF, BLOCK, 2 * LANES), jnp.bfloat16),
            pltpu.VMEM((GROUPS, 2, FRAME, BLOCK, 2 * LANES), jnp.bfloat16),
            pltpu.VMEM((GROUPS, 2, FRAME, BLOCK, 2 * LANES), jnp.bfloat16),
            pltpu.VMEM((2, FRAME, BLOCK, 2 * LANES), jnp.float32),
            pltpu.VMEM((GROUPS, FRAME, BLOCK, 2 * LANES), jnp.bfloat16),
            pltpu.VMEM((GROUPS, HALF, BLOCK, 2 * LANES), jnp.bfloat16),
            pltpu.VMEM((2, GROUPS, HALF, BLOCK, 2 * LANES), jnp.bfloat16),
            pltpu.VMEM((2, 8, LANES), jnp.int32),
            pltpu.SMEM((2, 8, LANES), jnp.int32),
            dma((4,)), dma((GROUPS, 2)), dma((GROUPS, 2)),
            dma((GROUPS, 2, 2)), dma((GROUPS, 2, 2)),
            dma, dma, dma,
            dma((GROUPS,)), dma((GROUPS,)), dma((2 * GROUPS, 2)),
            dma((GROUPS, 2, 2)), dma((GROUPS, 2, 2)),
            dma((GROUPS,)), dma((GROUPS,)), dma((2 * GROUPS, 2)),
            dma((2, GROUPS)), dma((2, GROUPS)), dma,
        ],
        cost_estimate=pl.CostEstimate(
            flops=flops, bytes_accessed=16 * rows * width, transcendentals=FRAME * SEL * BLOCK * LANES * GROUPS
        ),
        compiler_params=pltpu.CompilerParams(
            collective_id=0, has_side_effects=True, vmem_limit_bytes=60 * 1024 * 1024
        ),
    )(block_list, block_count, *blocked)
    outs = pl.pallas_call(
        hand_over,
        out_shape=[shape] * 4,
        in_specs=[pl.BlockSpec(memory_space=pl.ANY)] * 4,
        out_specs=[pl.BlockSpec(memory_space=pl.ANY)] * 4,
        scratch_shapes=[
            pltpu.VMEM((4, HALF, BLOCK, width), jnp.bfloat16), dma((4, HALF)), dma((4, HALF)),
        ],
        compiler_params=pltpu.CompilerParams(vmem_limit_bytes=60 * 1024 * 1024),
    )(*outs)
    return tuple(x.reshape(rows, width) for x in outs)


def solution(mesh):
    split = P(("frames", "strip"), None)
    in_specs = (split, split, split, split, split, P(("frames", "strip")))
    return jax.shard_map(
        body, mesh=mesh, in_specs=in_specs, out_specs=(split,) * 4, check_vma=False
    )
```

```python
import jax
import jax.numpy as jnp
from jax import lax
from jax.experimental import pallas as pl
from jax.experimental.pallas import tpu as pltpu
from jax.sharding import PartitionSpec as P

HD = 64
BLOCK = 64
SEL = 13
HALF = 4
FRAME = 8
WINDOW = 24
GROUPS = 4
LANES = 128
FACTOR = 0.125
MASKED = -1e30
PLACE_AT = 32
RUN = 8
MESH = pl.DeviceIdType.MESH


def kernel(
    frames,
    block_list, block_count, queries, keys, values, out_grad,
    attended, query_grad, key_grad, value_grad,
    loaded, packed, kv, qd, work, tiles, rows_out, rows_in, give, take, own, final, final_in, relay, meta_vm, meta_sm,
    load_sem, in_send, in_recv, pass_send, pass_recv,
    meta_send, meta_recv, meta_local, row_send, row_recv, row_local,
    term_send, term_recv, grad_send, grad_recv, grad_local, relay_send, relay_recv, slant_send,
):
    f, s = lax.axis_index("frames"), lax.axis_index("strip")
    o = 1 - s
    partner, next_dev, prev_dev = (f, o), (f + 1, s), (f - 1, s)

    sources = (keys, values, queries, out_grad)
    loads = [pltpu.make_async_copy(sources[a], loaded.at[a], load_sem.at[a]) for a in range(4)]
    for load in loads:
        load.start()

    place_in_run = lax.rem(f, RUN)
    has_after, has_before = f < frames - 1, f > 0
    edge = ((place_in_run == RUN - 1) & has_after, (place_in_run == 0) & has_before)
    part_column = (3 * s, 1 + s)

    def relay_of(d, column):
        return (f - 2 * column if d == 0 else f + 2 * column, s)

    def relay_to(d, column):
        return (f + 1 + 2 * column if d == 0 else f - 1 - 2 * column, s)

    relay_back = 1 - lax.rem(place_in_run, 2)
    relay_column = lax.select(relay_back == 0, (RUN - 1 - place_in_run) // 2, place_in_run // 2)
    relay_half = lax.rem(relay_column, 2)
    relay_source_frame = f - place_in_run + (1 - relay_back) * (RUN - 1)
    relay_target_frame = relay_source_frame + 1 - 2 * relay_back
    is_relay = ((relay_column == 1) & (s == 0)) | ((relay_column >= 2) & (s == 1))
    is_relay = is_relay & (relay_target_frame >= 0) & (relay_target_frame < frames)
    relay_target, relay_source = (relay_target_frame, s), (relay_source_frame, s)

    barrier = pltpu.get_barrier_semaphore()

    def greet(device):
        pl.semaphore_signal(barrier, inc=1, device_id=device, device_id_type=MESH)

    greet(partner)

    @pl.when(has_after)
    def _():
        greet(next_dev)

    @pl.when(has_before)
    def _():
        greet(prev_dev)

    @pl.when(is_relay)
    def _():
        greet(relay_source)
        greet(relay_target)

    for d in range(2):
        for column in (1, 2, 3):
            @pl.when(edge[d] & (s == (0 if column == 1 else 1)))
            def _():
                greet(relay_of(d, column))
                greet(relay_to(d, column))

    slant = (edge[0] & (s == 1), edge[1] & (s == 0))
    slant_to = ((f + 1, 0), (f - 1, 1))
    for d in range(2):
        @pl.when(slant[d])
        def _():
            greet(slant_to[d])

    at_end = (edge[0] | edge[1]).astype(jnp.int32)
    slants = (slant[0] | slant[1]).astype(jnp.int32)
    beside = has_after.astype(jnp.int32) + has_before.astype(jnp.int32)
    pl.semaphore_wait(barrier, 1 + beside + slants + 2 * is_relay.astype(jnp.int32) + at_end * (2 + 2 * s))

    def remote(src, dst, send, recv, device):
        return pltpu.make_async_remote_copy(
            src_ref=src, dst_ref=dst, send_sem=send, recv_sem=recv,
            device_id=device, device_id_type=MESH,
        )

    def columns(half, g):
        return pl.ds(pl.multiple_of(half * (GROUPS * LANES) + g * LANES, LANES), LANES)

    def landing(g, pair, half):
        if pair == 0:
            return kv.at[g, pl.ds(FRAME + HALF * half, HALF)]
        return qd.at[g, pl.ds(HALF * half, HALF)]

    def swap(g, pair):
        return remote(
            packed.at[g, pair], landing(g, pair, s), in_send.at[g, pair], in_recv.at[g, pair], partner
        )

    def pack(g, pair):
        for a in range(2):
            lanes = slice(a * LANES, (a + 1) * LANES)
            packed[g, pair, :, :, lanes] = loaded[2 * pair + a, :, :, columns(o, g)]

    def keep(g, pair):
        own_rows = landing(g, pair, s)
        for a in range(2):
            lanes = slice(a * LANES, (a + 1) * LANES)
            own_rows[:, :, lanes] = loaded[2 * pair + a, :, :, columns(s, g)]

    neighbours = (next_dev, prev_dev)
    sends_to, hears_from = (has_after, has_before), (has_before, has_after)

    def skipped(d, g):
        return edge[d] & (s == d) & (g == 0)

    def start_part(d, part, src, dst, send, recv, phase, g):
        straight = remote(src, dst, send, recv, neighbours[d])
        starts = sends_to[d]
        if part == 0:
            bent = edge[d] & (s == 1)
        elif phase == 0:
            bent = edge[d] & (g > 0)
            starts = starts & jnp.logical_not(skipped(d, g))
        else:
            bent = edge[d]

        @pl.when(bent)
        def _():
            remote(
                src, relay.at[phase, g], send, relay_recv.at[phase, g], relay_of(d, part_column[part])
            ).start()

        @pl.when(starts & jnp.logical_not(bent))
        def _():
            straight.start()

    def kv_window(g, base, half):
        return kv.at[g, pl.ds(base + HALF * half, HALF)]

    def pass_args(g, d, part):
        half = (s, o)[part]
        return (
            kv_window(g, FRAME, half), kv_window(g, (0, 2 * FRAME)[d], half),
            pass_send.at[g, d, half], pass_recv.at[g, d, half],
        )

    def start_pass(g, d, part):
        start_part(d, part, *pass_args(g, d, part), 0, g)

    def wait_pass(g, d, part):
        return remote(*pass_args(g, d, part), neighbours[d])

    def term_args(g, d, part):
        half = (s, o)[part]
        at = pl.ds(HALF * half, HALF)
        return (
            give.at[g, d, at], take.at[g, d, at], term_send.at[g, d, half], term_recv.at[g, d, half]
        )

    def start_terms(g, d, part):
        start_part(d, part, *term_args(g, d, part), 1, g)

    def wait_terms(g, d, part):
        return remote(*term_args(g, d, part), neighbours[d])

    def relay_on(g, phase):
        if phase == 0:
            target = kv_window(g, relay_back * (2 * FRAME), relay_half)
            recv = pass_recv.at[g, relay_back, relay_half]
        else:
            target = take.at[g, relay_back, pl.ds(HALF * relay_half, HALF)]
            recv = term_recv.at[g, relay_back, relay_half]
        return remote(relay.at[phase, g], target, relay_send.at[phase, g], recv, relay_target)

    def relays(g, phase):
        return is_relay & ((relay_column == 3) | (g > 0)) if phase == 0 else is_relay

    def slant_copy(d):
        base = (0, 2 * FRAME)[d]
        return remote(
            packed.at[0, 0], kv_window(0, base, s), slant_send, pass_recv.at[0, d, s], slant_to[d]
        )

    def relay_step(g, phase):
        @pl.when(relays(g, phase))
        def _():
            remote(
                relay.at[phase, g], relay.at[phase, g], relay_send.at[phase, g],
                relay_recv.at[phase, g], relay_target,
            ).wait_recv()
            relay_on(g, phase).start()

    def rows_across(g):
        return remote(
            rows_out.at[g, pl.ds(HALF * o, HALF)], rows_in.at[g], row_send.at[g], row_recv.at[g], partner
        )

    def grads_across(g):
        return remote(
            final.at[g, pl.ds(HALF * o, HALF)], final_in.at[g], grad_send.at[g], grad_recv.at[g], partner
        )

    row_targets, grad_targets = (query_grad, attended), (key_grad, value_grad)

    def place_copy(staged, targets, local, g, half, a):
        return pltpu.make_async_copy(
            staged.at[:, :, pl.ds(a * LANES, LANES)], targets[a].at[:, :, columns(half, g)], local.at[g, a]
        )

    def rows_along(g, a):
        return place_copy(rows_out.at[g, pl.ds(HALF * s, HALF)], row_targets, row_local, g, s, a)

    def grads_along(g, a):
        return place_copy(final.at[g, pl.ds(HALF * s, HALF)], grad_targets, grad_local, g, s, a)

    def rows_back(g, a):
        return place_copy(rows_in.at[g], row_targets, row_local.at[pl.ds(GROUPS, GROUPS)], g, o, a)

    def grads_back(g, a):
        return place_copy(final_in.at[g], grad_targets, grad_local.at[pl.ds(GROUPS, GROUPS)], g, o, a)

    share_meta = remote(meta_vm.at[s], meta_vm.at[s], meta_send, meta_recv, partner)

    def begin_keys(g):
        swap(g, 0).start()
        for d in range(2):
            start_pass(g, d, 0)

    def begin_queries(g):
        swap(g, 1).start()

    def pack_keep(g):
        for pair in range(2):
            pack(g, pair)
            keep(g, pair)

    for pair in range(2):
        loads[2 * pair].wait()
        loads[2 * pair + 1].wait()
        pack(0, pair)
        keep(0, pair)
        if pair == 0:
            begin_keys(0)
            for d in range(2):
                @pl.when(slant[d])
                def _():
                    slant_copy(d).start()
        else:
            begin_queries(0)

    listed = block_list[...]
    row_at = lax.broadcasted_iota(jnp.int32, (HALF, LANES), 0)
    lane_at = lax.broadcasted_iota(jnp.int32, (HALF, LANES), 1)
    counts = jnp.zeros((HALF, LANES), jnp.int32)
    for row in range(HALF):
        counts = jnp.where(row_at == row, block_count[row], counts)
    edge_low = jnp.where(f > 0, 0, FRAME)
    edge_high = jnp.where(f < frames - 1, WINDOW, 2 * FRAME)
    usable = (listed >= edge_low) & (listed < edge_high) & (lane_at[:, :SEL] < counts[:, :SEL])
    slots = jnp.where(usable, listed, -1)
    place = jnp.full((HALF, LANES), SEL, jnp.int32)
    for j in range(SEL):
        place = jnp.where(lane_at - PLACE_AT == slots[:, j:j + 1], j, place)
    meta_vm[s, 0:HALF] = place
    meta_vm[s, 0:HALF, 0:SEL] = listed
    meta_vm[s, HALF:] = jnp.zeros((HALF, LANES), jnp.int32)
    meta_vm[s, HALF:, 0:SEL] = usable.astype(jnp.int32)
    share_meta.start()
    pack_keep(1)
    begin_keys(1)
    pack_keep(2)
    tiles[:, SEL] = jnp.zeros((FRAME, BLOCK, 2 * LANES), jnp.float32)

    def forward(g):
        swap(g, 0).wait_recv()
        for d in range(2):
            start_pass(g, d, 1)

    def clear(w, carry):
        @pl.when(jnp.logical_not(has_before))
        def _():
            for g in range(GROUPS):
                kv[g, w] = jnp.zeros((BLOCK, 2 * LANES), jnp.bfloat16)
                take[g, 0, w] = jnp.zeros((BLOCK, 2 * LANES), jnp.bfloat16)

        @pl.when(jnp.logical_not(has_after))
        def _():
            for g in range(GROUPS):
                kv[g, 2 * FRAME + w] = jnp.zeros((BLOCK, 2 * LANES), jnp.bfloat16)
                take[g, 1, w] = jnp.zeros((BLOCK, 2 * LANES), jnp.bfloat16)

        return carry

    lax.fori_loop(0, FRAME, clear, 0)
    relay_step(0, 0)
    forward(0)
    begin_keys(2)
    begin_queries(1)
    share_meta.wait()
    to_scalar = pltpu.make_async_copy(meta_vm, meta_sm, meta_local)
    to_scalar.start()
    to_scalar.wait()
    pack_keep(3)

    row_ids = lax.broadcasted_iota(jnp.int32, (4 * HD, 4 * HD), 0) // HD
    col_ids = lax.broadcasted_iota(jnp.int32, (4 * HD, 4 * HD), 1) // HD
    spread = jnp.where(
        row_ids == col_ids, jnp.where(col_ids < 2, FACTOR, 1.0), 0.0
    ).astype(jnp.bfloat16)
    first_head = lax.broadcasted_iota(jnp.int32, (BLOCK, LANES), 1) < HD

    def heads(full):
        return jnp.where(first_head, full[:HD], full[HD:])

    def fold(array, op):
        return op(array.reshape(array.shape[0] // 8, 8, LANES), axis=0)

    def attend(g, b):
        strip, row = b // HALF, lax.rem(b, HALF)
        chunks = ((0, 4), (4, 8), (8, SEL))
        keep = {"slabs": [None] * SEL, "powers": [None] * SEL}

        def diagonal():
            keep["diagonal"] = jnp.concatenate([qd[g, b]] * 4, axis=0) * spread
            keep["bias"] = [
                jnp.where(meta_sm[strip, HALF + row, j] > 0, 0.0, MASKED).astype(jnp.float32)
                for j in range(SEL)
            ]

        def products(c):
            low, high = chunks[c]
            picked = jnp.concatenate([work[meta_sm[strip, row, j]] for j in range(low, high)], axis=0)
            keep["picked", c] = picked
            both = lax.dot_general(
                picked, keep["diagonal"], (((1,), (1,)), ((), ())), preferred_element_type=jnp.float32
            )
            for j in range(low, high):
                at = slice((j - low) * BLOCK, (j - low + 1) * BLOCK)
                keep["scores", j] = both[at, :LANES]
                keep["grad_weights", j] = both[at, LANES:]

        def peak(c):
            for j in range(*chunks[c]):
                top = fold(keep["scores", j], jnp.max) + keep["bias"][j]
                keep["peak"] = jnp.maximum(keep["peak"], top) if j else top
            if c == len(chunks) - 1:
                keep["peak"] = jnp.max(keep["peak"], axis=0, keepdims=True)

        def power(j):
            powers = jnp.exp(keep["scores", j] - (keep["peak"] - keep["bias"][j]))
            keep["powers"][j] = powers
            total = fold(powers, jnp.sum)
            dots = fold(powers * keep["grad_weights", j], jnp.sum)
            keep["total"] = keep["total"] + total if j else total
            keep["dots"] = keep["dots"] + dots if j else dots
            if j == SEL - 1:
                keep["scale"] = 1.0 / jnp.sum(keep["total"], axis=0, keepdims=True)
                keep["row_dots"] = jnp.sum(keep["dots"], axis=0, keepdims=True) * keep["scale"]

        def slab(j):
            weights = keep["powers"][j] * keep["scale"]
            grad_scores = weights * (keep["grad_weights", j] - keep["row_dots"])
            keep["slabs"][j] = (grad_scores.astype(jnp.bfloat16), weights.astype(jnp.bfloat16))

        def terms(c):
            low, high = chunks[c]
            parts = [jnp.concatenate([pair[k] for pair in keep["slabs"][low:high]], axis=0) for k in range(2)]
            keep["parts", c] = parts
            result = jnp.dot(
                jnp.concatenate(parts, axis=1), keep["diagonal"], preferred_element_type=jnp.float32
            )
            tiles[b, low:high] = result.reshape(high - low, BLOCK, 2 * LANES)

        def mixed(c):
            for k in range(2):
                lanes = slice(k * LANES, (k + 1) * LANES)
                product = lax.dot_general(
                    keep["parts", c][k], keep["picked", c][:, lanes], (((0,), (0,)), ((), ())),
                    preferred_element_type=jnp.float32,
                )
                keep["mixed", k] = keep["mixed", k] + product if c else product
            if c == len(chunks) - 1:
                rows_out[g, b] = jnp.concatenate(
                    [heads(keep["mixed", 0]) * FACTOR, heads(keep["mixed", 1])], axis=1
                ).astype(jnp.bfloat16)

        def call(function, *args):
            return lambda: function(*args)

        count = range(len(chunks))
        return (
            [diagonal] + [call(products, c) for c in count],
            [call(peak, c) for c in count] + [call(power, j) for j in range(SEL)] + [call(slab, j) for j in range(SEL)],
            [call(step, c) for c in count for step in (terms, mixed)],
        )

    def interleave(stages):
        placed = [
            ((k + 0.5) / len(stage), n, step)
            for n, stage in enumerate(stages)
            for k, step in enumerate(stage)
        ]
        for _, _, step in sorted(placed, key=lambda item: item[:2]):
            step()

    def finish(g):
        slot = lax.rem(g, 2)
        for d in range(2):
            @pl.when(hears_from[d])
            def _():
                for part in range(2):
                    wait_terms(g, d, part).wait_recv()

        def add(w, carry):
            total = own[slot, w] + take[g, 0, w].astype(jnp.float32) + take[g, 1, w].astype(jnp.float32)
            final[g, w] = total.astype(jnp.bfloat16)
            return carry

        lax.fori_loop(HALF * o, HALF * o + HALF, add, 0)
        grads_across(g).start()
        lax.fori_loop(HALF * s, HALF * s + HALF, add, 0)
        for a in range(2):
            grads_along(g, a).start()
        rows_across(g).wait_recv()
        for a in range(2):
            rows_back(g, a).start()

    def one_group(g, carry):
        swap(g, 1).wait_recv()
        for d in range(2):
            @pl.when(hears_from[d])
            def _():
                for part in range(2):
                    wait_pass(g, d, part).wait_recv()

        work[...] = kv[g]

        blocks = [attend(g, lax.rem(HALF * o + i, FRAME)) for i in range(FRAME)]
        for turn in range(FRAME + 2):
            interleave([blocks[turn - k][k] for k in (2, 1, 0) if 0 <= turn - k < FRAME])
            if turn == 3:
                @pl.when(g == 0)
                def _():
                    forward(1)
                    begin_keys(3)
                    begin_queries(2)

                @pl.when((g > 0) & (g + 1 < GROUPS))
                def _():
                    relay_step(g + 1, 0)

                @pl.when(g == GROUPS - 1)
                def _():
                    rows_across(GROUPS - 2).start()
                    finish(GROUPS - 3)

            if turn == 7:
                @pl.when(g == 0)
                def _():
                    begin_queries(3)
                    relay_step(1, 0)

                @pl.when(g + 2 < GROUPS)
                def _():
                    forward(g + 2)

                @pl.when(g > 0)
                def _():
                    relay_step(g - 1, 1)

                @pl.when((g > 0) & (g < GROUPS - 1))
                def _():
                    rows_across(g - 1).start()

                @pl.when(g == GROUPS - 1)
                def _():
                    rows_across(g).start()

                @pl.when(g == GROUPS - 2)
                def _():
                    finish(g - 2)

        for a in range(2):
            rows_along(g, a).start()

        def gather(w, base):
            acc = None
            for b in range(FRAME):
                place = meta_sm[b // HALF, b % HALF, PLACE_AT + base + w]
                tile = tiles[b, place]
                acc = tile if acc is None else acc + tile
            return acc

        def collect(w, inner):
            give[g, 1, w] = gather(w, 0).astype(jnp.bfloat16)
            give[g, 0, w] = gather(w, 2 * FRAME).astype(jnp.bfloat16)
            return inner

        for part, half in ((1, o), (0, s)):
            lax.fori_loop(HALF * half, HALF * half + HALF, collect, 0)
            for d in range(2):
                start_terms(g, d, part)

        def collect_own(w, inner):
            own[lax.rem(g, 2), w] = gather(w, FRAME)
            return inner

        lax.fori_loop(0, FRAME, collect_own, 0)

        return carry

    lax.fori_loop(0, GROUPS, one_group, 0)
    finish(GROUPS - 2)
    relay_step(GROUPS - 1, 1)
    finish(GROUPS - 1)

    def land(g, carry):
        grads_across(g).wait_recv()
        for a in range(2):
            grads_back(g, a).start()
        return carry

    lax.fori_loop(0, GROUPS, land, 0)

    def drain(g, carry):
        for pair in range(2):
            swap(g, pair).wait_send()
        for d in range(2):
            @pl.when(sends_to[d])
            def _():
                for part in range(2):
                    wait_terms(g, d, part).wait_send()
                wait_pass(g, d, 0).wait_send()

                @pl.when(jnp.logical_not(skipped(d, g)))
                def _():
                    wait_pass(g, d, 1).wait_send()

        for phase in range(2):
            @pl.when(relays(g, phase))
            def _():
                relay_on(g, phase).wait_send()

        rows_across(g).wait_send()
        grads_across(g).wait_send()
        for a in range(2):
            rows_along(g, a).wait()
            grads_along(g, a).wait()
            rows_back(g, a).wait()
            grads_back(g, a).wait()
        return carry

    lax.fori_loop(0, GROUPS, drain, 0)
    for d in range(2):
        @pl.when(slant[d])
        def _():
            slant_copy(d).wait_send()


def hand_over(*refs):
    sources, targets, held, in_sems, out_sems = refs[:4], refs[4:8], refs[8], refs[9], refs[10]
    spots = [(i, at) for i in range(4) for at in range(HALF)]
    ins = [pltpu.make_async_copy(sources[i].at[at], held.at[i, at], in_sems.at[i, at]) for i, at in spots]
    outs = [pltpu.make_async_copy(held.at[i, at], targets[i].at[at], out_sems.at[i, at]) for i, at in spots]
    for copy in ins:
        copy.start()
    for arrives, leaves in zip(ins, outs):
        arrives.wait()
        leaves.start()
    for copy in outs:
        copy.wait()


def body(queries, keys, values, out_grad, block_list, block_count):
    rows, width = queries.shape
    frames = lax.axis_size("frames")
    blocked = [x.reshape(HALF, BLOCK, width) for x in (queries, keys, values, out_grad)]
    shape = jax.ShapeDtypeStruct((HALF, BLOCK, width), jnp.bfloat16)
    dma = pltpu.SemaphoreType.DMA
    flops = 6 * 2 * FRAME * SEL * BLOCK * 256 * 256 * GROUPS
    outs = pl.pallas_call(
        lambda *refs: kernel(frames, *refs),
        out_shape=[shape] * 4,
        in_specs=[pl.BlockSpec(memory_space=pltpu.VMEM), pl.BlockSpec(memory_space=pltpu.SMEM)] + [pl.BlockSpec(memory_space=pl.ANY)] * 4,
        out_specs=[pl.BlockSpec(memory_space=pl.ANY)] * 4,
        scratch_shapes=[
            pltpu.VMEM((4, HALF, BLOCK, width), jnp.bfloat16),
            pltpu.VMEM((GROUPS, 2, HALF, BLOCK, 2 * LANES), jnp.bfloat16),
            pltpu.VMEM((GROUPS, WINDOW, BLOCK, 2 * LANES), jnp.bfloat16),
            pltpu.VMEM((GROUPS, FRAME, BLOCK, 2 * LANES), jnp.bfloat16),
            pltpu.VMEM((WINDOW, BLOCK, 2 * LANES), jnp.bfloat16),
            pltpu.VMEM((FRAME, SEL + 1, BLOCK, 2 * LANES), jnp.float32),
            pltpu.VMEM((GROUPS, FRAME, BLOCK, 2 * LANES), jnp.bfloat16),
            pltpu.VMEM((GROUPS, HALF, BLOCK, 2 * LANES), jnp.bfloat16),
            pltpu.VMEM((GROUPS, 2, FRAME, BLOCK, 2 * LANES), jnp.bfloat16),
            pltpu.VMEM((GROUPS, 2, FRAME, BLOCK, 2 * LANES), jnp.bfloat16),
            pltpu.VMEM((2, FRAME, BLOCK, 2 * LANES), jnp.float32),
            pltpu.VMEM((GROUPS, FRAME, BLOCK, 2 * LANES), jnp.bfloat16),
            pltpu.VMEM((GROUPS, HALF, BLOCK, 2 * LANES), jnp.bfloat16),
            pltpu.VMEM((2, GROUPS, HALF, BLOCK, 2 * LANES), jnp.bfloat16),
            pltpu.VMEM((2, 8, LANES), jnp.int32),
            pltpu.SMEM((2, 8, LANES), jnp.int32),
            dma((4,)), dma((GROUPS, 2)), dma((GROUPS, 2)),
            dma((GROUPS, 2, 2)), dma((GROUPS, 2, 2)),
            dma, dma, dma,
            dma((GROUPS,)), dma((GROUPS,)), dma((2 * GROUPS, 2)),
            dma((GROUPS, 2, 2)), dma((GROUPS, 2, 2)),
            dma((GROUPS,)), dma((GROUPS,)), dma((2 * GROUPS, 2)),
            dma((2, GROUPS)), dma((2, GROUPS)), dma,
        ],
        cost_estimate=pl.CostEstimate(
            flops=flops, bytes_accessed=16 * rows * width, transcendentals=FRAME * SEL * BLOCK * LANES * GROUPS
        ),
        compiler_params=pltpu.CompilerParams(
            collective_id=0, has_side_effects=True, vmem_limit_bytes=60 * 1024 * 1024
        ),
    )(block_list, block_count, *blocked)
    outs = pl.pallas_call(
        hand_over,
        out_shape=[shape] * 4,
        in_specs=[pl.BlockSpec(memory_space=pl.ANY)] * 4,
        out_specs=[pl.BlockSpec(memory_space=pl.ANY)] * 4,
        scratch_shapes=[
            pltpu.VMEM((4, HALF, BLOCK, width), jnp.bfloat16), dma((4, HALF)), dma((4, HALF)),
        ],
        compiler_params=pltpu.CompilerParams(vmem_limit_bytes=60 * 1024 * 1024),
    )(*outs)
    return tuple(x.reshape(rows, width) for x in outs)


def solution(mesh):
    split = P(("frames", "strip"), None)
    in_specs = (split, split, split, split, split, P(("frames", "strip")))
    return jax.shard_map(
        body, mesh=mesh, in_specs=in_specs, out_specs=(split,) * 4, check_vma=False
    )
```

```python
import jax
import jax.numpy as jnp
from jax import lax
from jax.experimental import pallas as pl
from jax.experimental.pallas import tpu as pltpu
from jax.sharding import PartitionSpec as P

HD = 64
BLOCK = 64
SEL = 13
HALF = 4
FRAME = 8
WINDOW = 24
GROUPS = 4
LANES = 128
FACTOR = 0.125
MASKED = -1e30
PLACE_AT = 32
RUN = 8
MESH = pl.DeviceIdType.MESH


def kernel(
    frames,
    block_list, block_count, queries, keys, values, out_grad,
    attended, query_grad, key_grad, value_grad,
    loaded, packed, kv, qd, work, tiles, rows_out, rows_in, give, take, own, final, final_in, relay, meta_vm, meta_sm,
    load_sem, in_send, in_recv, pass_send, pass_recv,
    meta_send, meta_recv, meta_local, row_send, row_recv, row_local,
    term_send, term_recv, grad_send, grad_recv, grad_local, relay_send, relay_recv, slant_send,
):
    f, s = lax.axis_index("frames"), lax.axis_index("strip")
    o = 1 - s
    partner, next_dev, prev_dev = (f, o), (f + 1, s), (f - 1, s)

    sources = (keys, values, queries, out_grad)
    loads = [pltpu.make_async_copy(sources[a], loaded.at[a], load_sem.at[a]) for a in range(4)]
    for load in loads:
        load.start()

    place_in_run = lax.rem(f, RUN)
    has_after, has_before = f < frames - 1, f > 0
    edge = ((place_in_run == RUN - 1) & has_after, (place_in_run == 0) & has_before)
    part_column = (3 * s, 1 + s)

    def relay_of(d, column):
        return (f - 2 * column if d == 0 else f + 2 * column, s)

    def relay_to(d, column):
        return (f + 1 + 2 * column if d == 0 else f - 1 - 2 * column, s)

    relay_back = 1 - lax.rem(place_in_run, 2)
    relay_column = lax.select(relay_back == 0, (RUN - 1 - place_in_run) // 2, place_in_run // 2)
    relay_half = lax.rem(relay_column, 2)
    relay_source_frame = f - place_in_run + (1 - relay_back) * (RUN - 1)
    relay_target_frame = relay_source_frame + 1 - 2 * relay_back
    is_relay = ((relay_column == 1) & (s == 0)) | ((relay_column >= 2) & (s == 1))
    is_relay = is_relay & (relay_target_frame >= 0) & (relay_target_frame < frames)
    relay_target, relay_source = (relay_target_frame, s), (relay_source_frame, s)

    barrier = pltpu.get_barrier_semaphore()

    def greet(device):
        pl.semaphore_signal(barrier, inc=1, device_id=device, device_id_type=MESH)

    greet(partner)

    @pl.when(has_after)
    def _():
        greet(next_dev)

    @pl.when(has_before)
    def _():
        greet(prev_dev)

    @pl.when(is_relay)
    def _():
        greet(relay_source)
        greet(relay_target)

    for d in range(2):
        for column in (1, 2, 3):
            @pl.when(edge[d] & (s == (0 if column == 1 else 1)))
            def _():
                greet(relay_of(d, column))
                greet(relay_to(d, column))

    slant = (edge[0] & (s == 1), edge[1] & (s == 0))
    slant_to = ((f + 1, 0), (f - 1, 1))
    for d in range(2):
        @pl.when(slant[d])
        def _():
            greet(slant_to[d])

    at_end = (edge[0] | edge[1]).astype(jnp.int32)
    slants = (slant[0] | slant[1]).astype(jnp.int32)
    beside = has_after.astype(jnp.int32) + has_before.astype(jnp.int32)
    pl.semaphore_wait(barrier, 1 + beside + slants + 2 * is_relay.astype(jnp.int32) + at_end * (2 + 2 * s))

    def remote(src, dst, send, recv, device):
        return pltpu.make_async_remote_copy(
            src_ref=src, dst_ref=dst, send_sem=send, recv_sem=recv,
            device_id=device, device_id_type=MESH,
        )

    def columns(half, g):
        return pl.ds(pl.multiple_of(half * (GROUPS * LANES) + g * LANES, LANES), LANES)

    def landing(g, pair, half):
        if pair == 0:
            return kv.at[g, pl.ds(FRAME + HALF * half, HALF)]
        return qd.at[g, pl.ds(HALF * half, HALF)]

    def swap(g, pair):
        return remote(
            packed.at[g, pair], landing(g, pair, s), in_send.at[g, pair], in_recv.at[g, pair], partner
        )

    def pack(g, pair):
        for a in range(2):
            lanes = slice(a * LANES, (a + 1) * LANES)
            packed[g, pair, :, :, lanes] = loaded[2 * pair + a, :, :, columns(o, g)]

    def keep(g, pair):
        own_rows = landing(g, pair, s)
        for a in range(2):
            lanes = slice(a * LANES, (a + 1) * LANES)
            own_rows[:, :, lanes] = loaded[2 * pair + a, :, :, columns(s, g)]

    neighbours = (next_dev, prev_dev)
    sends_to, hears_from = (has_after, has_before), (has_before, has_after)

    def skipped(d, g):
        return edge[d] & (s == d) & (g == 0)

    def start_part(d, part, src, dst, send, recv, phase, g):
        straight = remote(src, dst, send, recv, neighbours[d])
        starts = sends_to[d]
        if part == 0:
            bent = edge[d] & (s == 1)
        elif phase == 0:
            bent = edge[d] & (g > 0)
            starts = starts & jnp.logical_not(skipped(d, g))
        else:
            bent = edge[d]

        @pl.when(bent)
        def _():
            remote(
                src, relay.at[phase, g], send, relay_recv.at[phase, g], relay_of(d, part_column[part])
            ).start()

        @pl.when(starts & jnp.logical_not(bent))
        def _():
            straight.start()

    def kv_window(g, base, half):
        return kv.at[g, pl.ds(base + HALF * half, HALF)]

    def pass_args(g, d, part):
        half = (s, o)[part]
        return (
            kv_window(g, FRAME, half), kv_window(g, (0, 2 * FRAME)[d], half),
            pass_send.at[g, d, half], pass_recv.at[g, d, half],
        )

    def start_pass(g, d, part):
        start_part(d, part, *pass_args(g, d, part), 0, g)

    def wait_pass(g, d, part):
        return remote(*pass_args(g, d, part), neighbours[d])

    def term_args(g, d, part):
        half = (s, o)[part]
        at = pl.ds(HALF * half, HALF)
        return (
            give.at[g, d, at], take.at[g, d, at], term_send.at[g, d, half], term_recv.at[g, d, half]
        )

    def start_terms(g, d, part):
        start_part(d, part, *term_args(g, d, part), 1, g)

    def wait_terms(g, d, part):
        return remote(*term_args(g, d, part), neighbours[d])

    def relay_on(g, phase):
        if phase == 0:
            target = kv_window(g, relay_back * (2 * FRAME), relay_half)
            recv = pass_recv.at[g, relay_back, relay_half]
        else:
            target = take.at[g, relay_back, pl.ds(HALF * relay_half, HALF)]
            recv = term_recv.at[g, relay_back, relay_half]
        return remote(relay.at[phase, g], target, relay_send.at[phase, g], recv, relay_target)

    def relays(g, phase):
        return is_relay & ((relay_column == 3) | (g > 0)) if phase == 0 else is_relay

    def slant_copy(d):
        base = (0, 2 * FRAME)[d]
        return remote(
            packed.at[0, 0], kv_window(0, base, s), slant_send, pass_recv.at[0, d, s], slant_to[d]
        )

    def relay_step(g, phase):
        @pl.when(relays(g, phase))
        def _():
            remote(
                relay.at[phase, g], relay.at[phase, g], relay_send.at[phase, g],
                relay_recv.at[phase, g], relay_target,
            ).wait_recv()
            relay_on(g, phase).start()

    def rows_across(g):
        return remote(
            rows_out.at[g, pl.ds(HALF * o, HALF)], rows_in.at[g], row_send.at[g], row_recv.at[g], partner
        )

    def grads_across(g):
        return remote(
            final.at[g, pl.ds(HALF * o, HALF)], final_in.at[g], grad_send.at[g], grad_recv.at[g], partner
        )

    row_targets, grad_targets = (query_grad, attended), (key_grad, value_grad)

    def place_copy(staged, targets, local, g, half, a):
        return pltpu.make_async_copy(
            staged.at[:, :, pl.ds(a * LANES, LANES)], targets[a].at[:, :, columns(half, g)], local.at[g, a]
        )

    def rows_along(g, a):
        return place_copy(rows_out.at[g, pl.ds(HALF * s, HALF)], row_targets, row_local, g, s, a)

    def grads_along(g, a):
        return place_copy(final.at[g, pl.ds(HALF * s, HALF)], grad_targets, grad_local, g, s, a)

    def rows_back(g, a):
        return place_copy(rows_in.at[g], row_targets, row_local.at[pl.ds(GROUPS, GROUPS)], g, o, a)

    def grads_back(g, a):
        return place_copy(final_in.at[g], grad_targets, grad_local.at[pl.ds(GROUPS, GROUPS)], g, o, a)

    share_meta = remote(meta_vm.at[s], meta_vm.at[s], meta_send, meta_recv, partner)

    def begin_keys(g):
        swap(g, 0).start()
        for d in range(2):
            start_pass(g, d, 0)

    def begin_queries(g):
        swap(g, 1).start()

    def pack_keep(g):
        for pair in range(2):
            pack(g, pair)
            keep(g, pair)

    for pair in range(2):
        loads[2 * pair].wait()
        loads[2 * pair + 1].wait()
        pack(0, pair)
        keep(0, pair)
        if pair == 0:
            begin_keys(0)
            for d in range(2):
                @pl.when(slant[d])
                def _():
                    slant_copy(d).start()
        else:
            begin_queries(0)

    listed = block_list[...]
    row_at = lax.broadcasted_iota(jnp.int32, (HALF, LANES), 0)
    lane_at = lax.broadcasted_iota(jnp.int32, (HALF, LANES), 1)
    counts = jnp.zeros((HALF, LANES), jnp.int32)
    for row in range(HALF):
        counts = jnp.where(row_at == row, block_count[row], counts)
    edge_low = jnp.where(f > 0, 0, FRAME)
    edge_high = jnp.where(f < frames - 1, WINDOW, 2 * FRAME)
    usable = (listed >= edge_low) & (listed < edge_high) & (lane_at[:, :SEL] < counts[:, :SEL])
    slots = jnp.where(usable, listed, -1)
    place = jnp.full((HALF, LANES), SEL, jnp.int32)
    for j in range(SEL):
        place = jnp.where(lane_at - PLACE_AT == slots[:, j:j + 1], j, place)
    meta_vm[s, 0:HALF] = place
    meta_vm[s, 0:HALF, 0:SEL] = listed
    meta_vm[s, HALF:] = jnp.zeros((HALF, LANES), jnp.int32)
    meta_vm[s, HALF:, 0:SEL] = usable.astype(jnp.int32)
    share_meta.start()
    pack_keep(1)
    pack_keep(2)
    tiles[:, SEL] = jnp.zeros((FRAME, BLOCK, 2 * LANES), jnp.float32)

    def forward(g):
        swap(g, 0).wait_recv()
        for d in range(2):
            start_pass(g, d, 1)

    def clear(w, carry):
        @pl.when(jnp.logical_not(has_before))
        def _():
            for g in range(GROUPS):
                kv[g, w] = jnp.zeros((BLOCK, 2 * LANES), jnp.bfloat16)
                take[g, 0, w] = jnp.zeros((BLOCK, 2 * LANES), jnp.bfloat16)

        @pl.when(jnp.logical_not(has_after))
        def _():
            for g in range(GROUPS):
                kv[g, 2 * FRAME + w] = jnp.zeros((BLOCK, 2 * LANES), jnp.bfloat16)
                take[g, 1, w] = jnp.zeros((BLOCK, 2 * LANES), jnp.bfloat16)

        return carry

    lax.fori_loop(0, FRAME, clear, 0)
    relay_step(0, 0)
    forward(0)
    begin_keys(1)
    share_meta.wait()
    to_scalar = pltpu.make_async_copy(meta_vm, meta_sm, meta_local)
    to_scalar.start()
    to_scalar.wait()
    pack_keep(3)

    row_ids = lax.broadcasted_iota(jnp.int32, (4 * HD, 4 * HD), 0) // HD
    col_ids = lax.broadcasted_iota(jnp.int32, (4 * HD, 4 * HD), 1) // HD
    spread = jnp.where(
        row_ids == col_ids, jnp.where(col_ids < 2, FACTOR, 1.0), 0.0
    ).astype(jnp.bfloat16)
    first_head = lax.broadcasted_iota(jnp.int32, (BLOCK, LANES), 1) < HD

    def heads(full):
        return jnp.where(first_head, full[:HD], full[HD:])

    def fold(array, op):
        return op(array.reshape(array.shape[0] // 8, 8, LANES), axis=0)

    def attend(g, b):
        strip, row = b // HALF, lax.rem(b, HALF)
        chunks = ((0, 4), (4, 8), (8, SEL))
        keep = {"slabs": [None] * SEL, "powers": [None] * SEL}

        def diagonal():
            keep["diagonal"] = jnp.concatenate([qd[g, b]] * 4, axis=0) * spread
            keep["bias"] = [
                jnp.where(meta_sm[strip, HALF + row, j] > 0, 0.0, MASKED).astype(jnp.float32)
                for j in range(SEL)
            ]

        def products(c):
            low, high = chunks[c]
            picked = jnp.concatenate([work[meta_sm[strip, row, j]] for j in range(low, high)], axis=0)
            keep["picked", c] = picked
            both = lax.dot_general(
                picked, keep["diagonal"], (((1,), (1,)), ((), ())), preferred_element_type=jnp.float32
            )
            for j in range(low, high):
                at = slice((j - low) * BLOCK, (j - low + 1) * BLOCK)
                keep["scores", j] = both[at, :LANES]
                keep["grad_weights", j] = both[at, LANES:]

        def peak(c):
            for j in range(*chunks[c]):
                top = fold(keep["scores", j], jnp.max) + keep["bias"][j]
                keep["peak"] = jnp.maximum(keep["peak"], top) if j else top
            if c == len(chunks) - 1:
                keep["peak"] = jnp.max(keep["peak"], axis=0, keepdims=True)

        def power(j):
            powers = jnp.exp(keep["scores", j] - (keep["peak"] - keep["bias"][j]))
            keep["powers"][j] = powers
            total = fold(powers, jnp.sum)
            dots = fold(powers * keep["grad_weights", j], jnp.sum)
            keep["total"] = keep["total"] + total if j else total
            keep["dots"] = keep["dots"] + dots if j else dots
            if j == SEL - 1:
                keep["scale"] = 1.0 / jnp.sum(keep["total"], axis=0, keepdims=True)
                keep["row_dots"] = jnp.sum(keep["dots"], axis=0, keepdims=True) * keep["scale"]

        def slab(j):
            weights = keep["powers"][j] * keep["scale"]
            grad_scores = weights * (keep["grad_weights", j] - keep["row_dots"])
            keep["slabs"][j] = (grad_scores.astype(jnp.bfloat16), weights.astype(jnp.bfloat16))

        def terms(c):
            low, high = chunks[c]
            parts = [jnp.concatenate([pair[k] for pair in keep["slabs"][low:high]], axis=0) for k in range(2)]
            keep["parts", c] = parts
            result = jnp.dot(
                jnp.concatenate(parts, axis=1), keep["diagonal"], preferred_element_type=jnp.float32
            )
            tiles[b, low:high] = result.reshape(high - low, BLOCK, 2 * LANES)

        def mixed(c):
            for k in range(2):
                lanes = slice(k * LANES, (k + 1) * LANES)
                product = lax.dot_general(
                    keep["parts", c][k], keep["picked", c][:, lanes], (((0,), (0,)), ((), ())),
                    preferred_element_type=jnp.float32,
                )
                keep["mixed", k] = keep["mixed", k] + product if c else product
            if c == len(chunks) - 1:
                rows_out[g, b] = jnp.concatenate(
                    [heads(keep["mixed", 0]) * FACTOR, heads(keep["mixed", 1])], axis=1
                ).astype(jnp.bfloat16)

        def call(function, *args):
            return lambda: function(*args)

        count = range(len(chunks))
        return (
            [diagonal] + [call(products, c) for c in count],
            [call(peak, c) for c in count] + [call(power, j) for j in range(SEL)] + [call(slab, j) for j in range(SEL)],
            [call(step, c) for c in count for step in (terms, mixed)],
        )

    def interleave(stages):
        placed = [
            ((k + 0.5) / len(stage), n, step)
            for n, stage in enumerate(stages)
            for k, step in enumerate(stage)
        ]
        for _, _, step in sorted(placed, key=lambda item: item[:2]):
            step()

    def finish(g):
        slot = lax.rem(g, 2)
        for d in range(2):
            @pl.when(hears_from[d])
            def _():
                for part in range(2):
                    wait_terms(g, d, part).wait_recv()

        def add(w, carry):
            total = own[slot, w] + take[g, 0, w].astype(jnp.float32) + take[g, 1, w].astype(jnp.float32)
            final[g, w] = total.astype(jnp.bfloat16)
            return carry

        lax.fori_loop(0, FRAME, add, 0)
        grads_across(g).start()
        for a in range(2):
            grads_along(g, a).start()
        rows_across(g).wait_recv()
        for a in range(2):
            rows_back(g, a).start()

    def one_group(g, carry):
        swap(g, 1).wait_recv()
        for d in range(2):
            @pl.when(hears_from[d])
            def _():
                for part in range(2):
                    wait_pass(g, d, part).wait_recv()

        @pl.when(g == 0)
        def _():
            begin_keys(2)
            begin_queries(1)

        work[...] = kv[g]

        blocks = [attend(g, lax.rem(HALF * o + i, FRAME)) for i in range(FRAME)]
        for turn in range(FRAME + 2):
            interleave([blocks[turn - k][k] for k in (2, 1, 0) if 0 <= turn - k < FRAME])
            if turn == 3:
                @pl.when(g == 0)
                def _():
                    forward(1)
                    begin_keys(3)
                    begin_queries(2)

                @pl.when((g > 0) & (g + 1 < GROUPS))
                def _():
                    relay_step(g + 1, 0)

                @pl.when(g == GROUPS - 1)
                def _():
                    rows_across(GROUPS - 2).start()

            if turn == 7:
                @pl.when(g == 0)
                def _():
                    begin_queries(3)
                    relay_step(1, 0)

                @pl.when(g + 2 < GROUPS)
                def _():
                    forward(g + 2)

                @pl.when(g > 0)
                def _():
                    relay_step(g - 1, 1)

                @pl.when((g > 0) & (g < GROUPS - 1))
                def _():
                    rows_across(g - 1).start()

                @pl.when(g > 1)
                def _():
                    finish(g - 2)

        for a in range(2):
            rows_along(g, a).start()

        def gather(w, base):
            acc = None
            for b in range(FRAME):
                place = meta_sm[b // HALF, b % HALF, PLACE_AT + base + w]
                tile = tiles[b, place]
                acc = tile if acc is None else acc + tile
            return acc

        def collect(w, inner):
            give[g, 1, w] = gather(w, 0).astype(jnp.bfloat16)
            give[g, 0, w] = gather(w, 2 * FRAME).astype(jnp.bfloat16)
            return inner

        for part, half in ((1, o), (0, s)):
            lax.fori_loop(HALF * half, HALF * half + HALF, collect, 0)
            for d in range(2):
                start_terms(g, d, part)

        def collect_own(w, inner):
            own[lax.rem(g, 2), w] = gather(w, FRAME)
            return inner

        lax.fori_loop(0, FRAME, collect_own, 0)

        return carry

    lax.fori_loop(0, GROUPS, one_group, 0)
    relay_step(GROUPS - 1, 1)
    rows_across(GROUPS - 1).start()

    @pl.when(at_end > 0)
    def _():
        finish(GROUPS - 2)

    finish(GROUPS - 1)

    @pl.when(at_end == 0)
    def _():
        finish(GROUPS - 2)

    def land(g, carry):
        grads_across(g).wait_recv()
        for a in range(2):
            grads_back(g, a).start()
        return carry

    lax.fori_loop(0, GROUPS, land, 0)

    def drain(g, carry):
        for pair in range(2):
            swap(g, pair).wait_send()
        for d in range(2):
            @pl.when(sends_to[d])
            def _():
                for part in range(2):
                    wait_terms(g, d, part).wait_send()
                wait_pass(g, d, 0).wait_send()

                @pl.when(jnp.logical_not(skipped(d, g)))
                def _():
                    wait_pass(g, d, 1).wait_send()

        for phase in range(2):
            @pl.when(relays(g, phase))
            def _():
                relay_on(g, phase).wait_send()

        rows_across(g).wait_send()
        grads_across(g).wait_send()
        for a in range(2):
            rows_along(g, a).wait()
            grads_along(g, a).wait()
            rows_back(g, a).wait()
            grads_back(g, a).wait()
        return carry

    lax.fori_loop(0, GROUPS, drain, 0)
    for d in range(2):
        @pl.when(slant[d])
        def _():
            slant_copy(d).wait_send()


def hand_over(*refs):
    sources, targets, held, in_sems, out_sems = refs[:4], refs[4:8], refs[8], refs[9], refs[10]
    spots = [(i, at) for i in range(4) for at in range(HALF)]
    ins = [pltpu.make_async_copy(sources[i].at[at], held.at[i, at], in_sems.at[i, at]) for i, at in spots]
    outs = [pltpu.make_async_copy(held.at[i, at], targets[i].at[at], out_sems.at[i, at]) for i, at in spots]
    for copy in ins:
        copy.start()
    for arrives, leaves in zip(ins, outs):
        arrives.wait()
        leaves.start()
    for copy in outs:
        copy.wait()


def body(queries, keys, values, out_grad, block_list, block_count):
    rows, width = queries.shape
    frames = lax.axis_size("frames")
    blocked = [x.reshape(HALF, BLOCK, width) for x in (queries, keys, values, out_grad)]
    shape = jax.ShapeDtypeStruct((HALF, BLOCK, width), jnp.bfloat16)
    dma = pltpu.SemaphoreType.DMA
    flops = 6 * 2 * FRAME * SEL * BLOCK * 256 * 256 * GROUPS
    outs = pl.pallas_call(
        lambda *refs: kernel(frames, *refs),
        out_shape=[shape] * 4,
        in_specs=[pl.BlockSpec(memory_space=pltpu.VMEM), pl.BlockSpec(memory_space=pltpu.SMEM)] + [pl.BlockSpec(memory_space=pl.ANY)] * 4,
        out_specs=[pl.BlockSpec(memory_space=pl.ANY)] * 4,
        scratch_shapes=[
            pltpu.VMEM((4, HALF, BLOCK, width), jnp.bfloat16),
            pltpu.VMEM((GROUPS, 2, HALF, BLOCK, 2 * LANES), jnp.bfloat16),
            pltpu.VMEM((GROUPS, WINDOW, BLOCK, 2 * LANES), jnp.bfloat16),
            pltpu.VMEM((GROUPS, FRAME, BLOCK, 2 * LANES), jnp.bfloat16),
            pltpu.VMEM((WINDOW, BLOCK, 2 * LANES), jnp.bfloat16),
            pltpu.VMEM((FRAME, SEL + 1, BLOCK, 2 * LANES), jnp.float32),
            pltpu.VMEM((GROUPS, FRAME, BLOCK, 2 * LANES), jnp.bfloat16),
            pltpu.VMEM((GROUPS, HALF, BLOCK, 2 * LANES), jnp.bfloat16),
            pltpu.VMEM((GROUPS, 2, FRAME, BLOCK, 2 * LANES), jnp.bfloat16),
            pltpu.VMEM((GROUPS, 2, FRAME, BLOCK, 2 * LANES), jnp.bfloat16),
            pltpu.VMEM((2, FRAME, BLOCK, 2 * LANES), jnp.float32),
            pltpu.VMEM((GROUPS, FRAME, BLOCK, 2 * LANES), jnp.bfloat16),
            pltpu.VMEM((GROUPS, HALF, BLOCK, 2 * LANES), jnp.bfloat16),
            pltpu.VMEM((2, GROUPS, HALF, BLOCK, 2 * LANES), jnp.bfloat16),
            pltpu.VMEM((2, 8, LANES), jnp.int32),
            pltpu.SMEM((2, 8, LANES), jnp.int32),
            dma((4,)), dma((GROUPS, 2)), dma((GROUPS, 2)),
            dma((GROUPS, 2, 2)), dma((GROUPS, 2, 2)),
            dma, dma, dma,
            dma((GROUPS,)), dma((GROUPS,)), dma((2 * GROUPS, 2)),
            dma((GROUPS, 2, 2)), dma((GROUPS, 2, 2)),
            dma((GROUPS,)), dma((GROUPS,)), dma((2 * GROUPS, 2)),
            dma((2, GROUPS)), dma((2, GROUPS)), dma,
        ],
        cost_estimate=pl.CostEstimate(
            flops=flops, bytes_accessed=16 * rows * width, transcendentals=FRAME * SEL * BLOCK * LANES * GROUPS
        ),
        compiler_params=pltpu.CompilerParams(
            collective_id=0, has_side_effects=True, vmem_limit_bytes=60 * 1024 * 1024
        ),
    )(block_list, block_count, *blocked)
    outs = pl.pallas_call(
        hand_over,
        out_shape=[shape] * 4,
        in_specs=[pl.BlockSpec(memory_space=pl.ANY)] * 4,
        out_specs=[pl.BlockSpec(memory_space=pl.ANY)] * 4,
        scratch_shapes=[
            pltpu.VMEM((4, HALF, BLOCK, width), jnp.bfloat16), dma((4, HALF)), dma((4, HALF)),
        ],
        compiler_params=pltpu.CompilerParams(vmem_limit_bytes=60 * 1024 * 1024),
    )(*outs)
    return tuple(x.reshape(rows, width) for x in outs)


def solution(mesh):
    split = P(("frames", "strip"), None)
    in_specs = (split, split, split, split, split, P(("frames", "strip")))
    return jax.shard_map(
        body, mesh=mesh, in_specs=in_specs, out_specs=(split,) * 4, check_vma=False
    )
```

```python
import jax
import jax.numpy as jnp
from jax import lax
from jax.experimental import pallas as pl
from jax.experimental.pallas import tpu as pltpu
from jax.sharding import PartitionSpec as P

HD = 64
BLOCK = 64
SEL = 13
HALF = 4
FRAME = 8
WINDOW = 24
GROUPS = 4
LANES = 128
FACTOR = 0.125
MASKED = -1e30
PLACE_AT = 32
RUN = 8
MESH = pl.DeviceIdType.MESH


def kernel(
    frames,
    block_list, block_count, queries, keys, values, out_grad,
    attended, query_grad, key_grad, value_grad,
    loaded, packed, kv, qd, work, tiles, rows_out, rows_in, give, take, own, final, final_in, relay, meta_vm, meta_sm,
    load_sem, in_send, in_recv, pass_send, pass_recv,
    meta_send, meta_recv, meta_local, row_send, row_recv, row_local,
    term_send, term_recv, grad_send, grad_recv, grad_local, relay_send, relay_recv, slant_send,
):
    f, s = lax.axis_index("frames"), lax.axis_index("strip")
    o = 1 - s
    partner, next_dev, prev_dev = (f, o), (f + 1, s), (f - 1, s)

    sources = (keys, values, queries, out_grad)
    loads = [pltpu.make_async_copy(sources[a], loaded.at[a], load_sem.at[a]) for a in range(4)]
    for load in loads:
        load.start()

    place_in_run = lax.rem(f, RUN)
    has_after, has_before = f < frames - 1, f > 0
    edge = ((place_in_run == RUN - 1) & has_after, (place_in_run == 0) & has_before)
    part_column = (3 * s, 1 + s)

    def relay_of(d, column):
        return (f - 2 * column if d == 0 else f + 2 * column, s)

    def relay_to(d, column):
        return (f + 1 + 2 * column if d == 0 else f - 1 - 2 * column, s)

    relay_back = 1 - lax.rem(place_in_run, 2)
    relay_column = lax.select(relay_back == 0, (RUN - 1 - place_in_run) // 2, place_in_run // 2)
    relay_half = lax.rem(relay_column, 2)
    relay_source_frame = f - place_in_run + (1 - relay_back) * (RUN - 1)
    relay_target_frame = relay_source_frame + 1 - 2 * relay_back
    is_relay = ((relay_column == 1) & (s == 0)) | ((relay_column >= 2) & (s == 1))
    is_relay = is_relay & (relay_target_frame >= 0) & (relay_target_frame < frames)
    relay_target, relay_source = (relay_target_frame, s), (relay_source_frame, s)

    barrier = pltpu.get_barrier_semaphore()

    def greet(device):
        pl.semaphore_signal(barrier, inc=1, device_id=device, device_id_type=MESH)

    greet(partner)

    @pl.when(has_after)
    def _():
        greet(next_dev)

    @pl.when(has_before)
    def _():
        greet(prev_dev)

    @pl.when(is_relay)
    def _():
        greet(relay_source)
        greet(relay_target)

    for d in range(2):
        for column in (1, 2, 3):
            @pl.when(edge[d] & (s == (0 if column == 1 else 1)))
            def _():
                greet(relay_of(d, column))
                greet(relay_to(d, column))

    slant = (edge[0] & (s == 1), edge[1] & (s == 0))
    slant_to = ((f + 1, 0), (f - 1, 1))
    for d in range(2):
        @pl.when(slant[d])
        def _():
            greet(slant_to[d])

    at_end = (edge[0] | edge[1]).astype(jnp.int32)
    slants = (slant[0] | slant[1]).astype(jnp.int32)
    beside = has_after.astype(jnp.int32) + has_before.astype(jnp.int32)
    pl.semaphore_wait(barrier, 1 + beside + slants + 2 * is_relay.astype(jnp.int32) + at_end * (2 + 2 * s))

    def remote(src, dst, send, recv, device):
        return pltpu.make_async_remote_copy(
            src_ref=src, dst_ref=dst, send_sem=send, recv_sem=recv,
            device_id=device, device_id_type=MESH,
        )

    def columns(half, g):
        return pl.ds(pl.multiple_of(half * (GROUPS * LANES) + g * LANES, LANES), LANES)

    def landing(g, pair, half):
        if pair == 0:
            return kv.at[g, pl.ds(FRAME + HALF * half, HALF)]
        return qd.at[g, pl.ds(HALF * half, HALF)]

    def swap(g, pair):
        return remote(
            packed.at[g, pair], landing(g, pair, s), in_send.at[g, pair], in_recv.at[g, pair], partner
        )

    def pack(g, pair):
        for a in range(2):
            lanes = slice(a * LANES, (a + 1) * LANES)
            packed[g, pair, :, :, lanes] = loaded[2 * pair + a, :, :, columns(o, g)]

    def keep(g, pair):
        own_rows = landing(g, pair, s)
        for a in range(2):
            lanes = slice(a * LANES, (a + 1) * LANES)
            own_rows[:, :, lanes] = loaded[2 * pair + a, :, :, columns(s, g)]

    neighbours = (next_dev, prev_dev)
    sends_to, hears_from = (has_after, has_before), (has_before, has_after)

    skipped = (edge[0] & (s == 0), edge[1] & (s == 1))

    def start_part(d, part, src, dst, send, recv, phase, g):
        straight = remote(src, dst, send, recv, neighbours[d])
        starts = sends_to[d]
        if part == 0:
            bent = edge[d] & (s == 1)
        elif phase == 0:
            bent = edge[d] & (s != d) & (g > 0)
            starts = starts & jnp.logical_not(skipped[d])
        else:
            bent = edge[d]

        @pl.when(bent)
        def _():
            remote(
                src, relay.at[phase, g], send, relay_recv.at[phase, g], relay_of(d, part_column[part])
            ).start()

        @pl.when(starts & jnp.logical_not(bent))
        def _():
            straight.start()

    def kv_window(g, base, half):
        return kv.at[g, pl.ds(base + HALF * half, HALF)]

    def pass_args(g, d, part):
        half = (s, o)[part]
        return (
            kv_window(g, FRAME, half), kv_window(g, (0, 2 * FRAME)[d], half),
            pass_send.at[g, d, half], pass_recv.at[g, d, half],
        )

    def start_pass(g, d, part):
        start_part(d, part, *pass_args(g, d, part), 0, g)

    def wait_pass(g, d, part):
        return remote(*pass_args(g, d, part), neighbours[d])

    def term_args(g, d, part):
        half = (s, o)[part]
        at = pl.ds(HALF * half, HALF)
        return (
            give.at[g, d, at], take.at[g, d, at], term_send.at[g, d, half], term_recv.at[g, d, half]
        )

    def start_terms(g, d, part):
        start_part(d, part, *term_args(g, d, part), 1, g)

    def wait_terms(g, d, part):
        return remote(*term_args(g, d, part), neighbours[d])

    def relay_on(g, phase):
        if phase == 0:
            target = kv_window(g, relay_back * (2 * FRAME), relay_half)
            recv = pass_recv.at[g, relay_back, relay_half]
        else:
            target = take.at[g, relay_back, pl.ds(HALF * relay_half, HALF)]
            recv = term_recv.at[g, relay_back, relay_half]
        return remote(relay.at[phase, g], target, relay_send.at[phase, g], recv, relay_target)

    def relays(g, phase):
        if phase == 0:
            return is_relay & ((relay_column == 3) | ((relay_column == 2 - relay_back) & (g > 0)))
        return is_relay

    def slant_copy(g, d):
        base = (0, 2 * FRAME)[d]
        return remote(
            packed.at[g, 0], kv_window(g, base, s), slant_send.at[g], pass_recv.at[g, d, s], slant_to[d]
        )

    def relay_step(g, phase):
        @pl.when(relays(g, phase))
        def _():
            remote(
                relay.at[phase, g], relay.at[phase, g], relay_send.at[phase, g],
                relay_recv.at[phase, g], relay_target,
            ).wait_recv()
            relay_on(g, phase).start()

    def rows_across(g):
        return remote(
            rows_out.at[g, pl.ds(HALF * o, HALF)], rows_in.at[g], row_send.at[g], row_recv.at[g], partner
        )

    def grads_across(g):
        return remote(
            final.at[g, pl.ds(HALF * o, HALF)], final_in.at[g], grad_send.at[g], grad_recv.at[g], partner
        )

    row_targets, grad_targets = (query_grad, attended), (key_grad, value_grad)

    def place_copy(staged, targets, local, g, half, a):
        return pltpu.make_async_copy(
            staged.at[:, :, pl.ds(a * LANES, LANES)], targets[a].at[:, :, columns(half, g)], local.at[g, a]
        )

    def rows_along(g, a):
        return place_copy(rows_out.at[g, pl.ds(HALF * s, HALF)], row_targets, row_local, g, s, a)

    def grads_along(g, a):
        return place_copy(final.at[g, pl.ds(HALF * s, HALF)], grad_targets, grad_local, g, s, a)

    def rows_back(g, a):
        return place_copy(rows_in.at[g], row_targets, row_local.at[pl.ds(GROUPS, GROUPS)], g, o, a)

    def grads_back(g, a):
        return place_copy(final_in.at[g], grad_targets, grad_local.at[pl.ds(GROUPS, GROUPS)], g, o, a)

    share_meta = remote(meta_vm.at[s], meta_vm.at[s], meta_send, meta_recv, partner)

    def begin_keys(g):
        swap(g, 0).start()
        for d in range(2):
            start_pass(g, d, 0)

            @pl.when(slant[d])
            def _():
                slant_copy(g, d).start()

    def begin_queries(g):
        swap(g, 1).start()

    def pack_keep(g):
        for pair in range(2):
            pack(g, pair)
            keep(g, pair)

    for pair in range(2):
        loads[2 * pair].wait()
        loads[2 * pair + 1].wait()
        pack(0, pair)
        keep(0, pair)
        if pair == 0:
            begin_keys(0)
        else:
            begin_queries(0)

    listed = block_list[...]
    row_at = lax.broadcasted_iota(jnp.int32, (HALF, LANES), 0)
    lane_at = lax.broadcasted_iota(jnp.int32, (HALF, LANES), 1)
    counts = jnp.zeros((HALF, LANES), jnp.int32)
    for row in range(HALF):
        counts = jnp.where(row_at == row, block_count[row], counts)
    edge_low = jnp.where(f > 0, 0, FRAME)
    edge_high = jnp.where(f < frames - 1, WINDOW, 2 * FRAME)
    usable = (listed >= edge_low) & (listed < edge_high) & (lane_at[:, :SEL] < counts[:, :SEL])
    slots = jnp.where(usable, listed, -1)
    place = jnp.full((HALF, LANES), SEL, jnp.int32)
    for j in range(SEL):
        place = jnp.where(lane_at - PLACE_AT == slots[:, j:j + 1], j, place)
    meta_vm[s, 0:HALF] = place
    meta_vm[s, 0:HALF, 0:SEL] = listed
    meta_vm[s, HALF:] = jnp.zeros((HALF, LANES), jnp.int32)
    meta_vm[s, HALF:, 0:SEL] = usable.astype(jnp.int32)
    share_meta.start()
    pack_keep(1)
    begin_keys(1)
    pack_keep(2)
    tiles[:, SEL] = jnp.zeros((FRAME, BLOCK, 2 * LANES), jnp.float32)

    def forward(g):
        swap(g, 0).wait_recv()
        for d in range(2):
            start_pass(g, d, 1)

    def clear(w, carry):
        @pl.when(jnp.logical_not(has_before))
        def _():
            for g in range(GROUPS):
                kv[g, w] = jnp.zeros((BLOCK, 2 * LANES), jnp.bfloat16)
                take[g, 0, w] = jnp.zeros((BLOCK, 2 * LANES), jnp.bfloat16)

        @pl.when(jnp.logical_not(has_after))
        def _():
            for g in range(GROUPS):
                kv[g, 2 * FRAME + w] = jnp.zeros((BLOCK, 2 * LANES), jnp.bfloat16)
                take[g, 1, w] = jnp.zeros((BLOCK, 2 * LANES), jnp.bfloat16)

        return carry

    lax.fori_loop(0, FRAME, clear, 0)
    relay_step(0, 0)
    forward(0)
    begin_keys(2)
    begin_queries(1)
    share_meta.wait()
    to_scalar = pltpu.make_async_copy(meta_vm, meta_sm, meta_local)
    to_scalar.start()
    to_scalar.wait()
    pack_keep(3)

    row_ids = lax.broadcasted_iota(jnp.int32, (4 * HD, 4 * HD), 0) // HD
    col_ids = lax.broadcasted_iota(jnp.int32, (4 * HD, 4 * HD), 1) // HD
    spread = jnp.where(
        row_ids == col_ids, jnp.where(col_ids < 2, FACTOR, 1.0), 0.0
    ).astype(jnp.bfloat16)
    first_head = lax.broadcasted_iota(jnp.int32, (BLOCK, LANES), 1) < HD

    def heads(full):
        return jnp.where(first_head, full[:HD], full[HD:])

    def fold(array, op):
        return op(array.reshape(array.shape[0] // 8, 8, LANES), axis=0)

    def attend(g, b):
        strip, row = b // HALF, lax.rem(b, HALF)
        chunks = ((0, 4), (4, 8), (8, SEL))
        keep = {"slabs": [None] * SEL, "powers": [None] * SEL}

        def diagonal():
            keep["diagonal"] = jnp.concatenate([qd[g, b]] * 4, axis=0) * spread
            keep["bias"] = [
                jnp.where(meta_sm[strip, HALF + row, j] > 0, 0.0, MASKED).astype(jnp.float32)
                for j in range(SEL)
            ]

        def products(c):
            low, high = chunks[c]
            picked = jnp.concatenate([work[meta_sm[strip, row, j]] for j in range(low, high)], axis=0)
            keep["picked", c] = picked
            both = lax.dot_general(
                picked, keep["diagonal"], (((1,), (1,)), ((), ())), preferred_element_type=jnp.float32
            )
            for j in range(low, high):
                at = slice((j - low) * BLOCK, (j - low + 1) * BLOCK)
                keep["scores", j] = both[at, :LANES]
                keep["grad_weights", j] = both[at, LANES:]

        def peak(c):
            for j in range(*chunks[c]):
                top = fold(keep["scores", j], jnp.max) + keep["bias"][j]
                keep["peak"] = jnp.maximum(keep["peak"], top) if j else top
            if c == len(chunks) - 1:
                keep["peak"] = jnp.max(keep["peak"], axis=0, keepdims=True)

        def power(j):
            powers = jnp.exp(keep["scores", j] - (keep["peak"] - keep["bias"][j]))
            keep["powers"][j] = powers
            total = fold(powers, jnp.sum)
            dots = fold(powers * keep["grad_weights", j], jnp.sum)
            keep["total"] = keep["total"] + total if j else total
            keep["dots"] = keep["dots"] + dots if j else dots
            if j == SEL - 1:
                keep["scale"] = 1.0 / jnp.sum(keep["total"], axis=0, keepdims=True)
                keep["row_dots"] = jnp.sum(keep["dots"], axis=0, keepdims=True) * keep["scale"]

        def slab(j):
            weights = keep["powers"][j] * keep["scale"]
            grad_scores = weights * (keep["grad_weights", j] - keep["row_dots"])
            keep["slabs"][j] = (grad_scores.astype(jnp.bfloat16), weights.astype(jnp.bfloat16))

        def terms(c):
            low, high = chunks[c]
            parts = [jnp.concatenate([pair[k] for pair in keep["slabs"][low:high]], axis=0) for k in range(2)]
            keep["parts", c] = parts
            result = jnp.dot(
                jnp.concatenate(parts, axis=1), keep["diagonal"], preferred_element_type=jnp.float32
            )
            tiles[b, low:high] = result.reshape(high - low, BLOCK, 2 * LANES)

        def mixed(c):
            for k in range(2):
                lanes = slice(k * LANES, (k + 1) * LANES)
                product = lax.dot_general(
                    keep["parts", c][k], keep["picked", c][:, lanes], (((0,), (0,)), ((), ())),
                    preferred_element_type=jnp.float32,
                )
                keep["mixed", k] = keep["mixed", k] + product if c else product
            if c == len(chunks) - 1:
                rows_out[g, b] = jnp.concatenate(
                    [heads(keep["mixed", 0]) * FACTOR, heads(keep["mixed", 1])], axis=1
                ).astype(jnp.bfloat16)

        def call(function, *args):
            return lambda: function(*args)

        count = range(len(chunks))
        return (
            [diagonal] + [call(products, c) for c in count],
            [call(peak, c) for c in count] + [call(power, j) for j in range(SEL)] + [call(slab, j) for j in range(SEL)],
            [call(step, c) for c in count for step in (terms, mixed)],
        )

    def interleave(stages):
        placed = [
            ((k + 0.5) / len(stage), n, step)
            for n, stage in enumerate(stages)
            for k, step in enumerate(stage)
        ]
        for _, _, step in sorted(placed, key=lambda item: item[:2]):
            step()

    def finish(g):
        slot = lax.rem(g, 2)
        for d in range(2):
            @pl.when(hears_from[d])
            def _():
                for part in range(2):
                    wait_terms(g, d, part).wait_recv()

        def add(w, carry):
            total = own[slot, w] + take[g, 0, w].astype(jnp.float32) + take[g, 1, w].astype(jnp.float32)
            final[g, w] = total.astype(jnp.bfloat16)
            return carry

        lax.fori_loop(0, FRAME, add, 0)
        grads_across(g).start()
        for a in range(2):
            grads_along(g, a).start()
        rows_across(g).wait_recv()
        for a in range(2):
            rows_back(g, a).start()

    def one_group(g, carry):
        swap(g, 1).wait_recv()
        for d in range(2):
            @pl.when(hears_from[d])
            def _():
                for part in range(2):
                    wait_pass(g, d, part).wait_recv()

        work[...] = kv[g]

        blocks = [attend(g, lax.rem(HALF * o + i, FRAME)) for i in range(FRAME)]
        for turn in range(FRAME + 2):
            interleave([blocks[turn - k][k] for k in (2, 1, 0) if 0 <= turn - k < FRAME])
            if turn == 3:
                @pl.when(g == 0)
                def _():
                    forward(1)
                    begin_keys(3)
                    begin_queries(2)

                @pl.when((g > 0) & (g + 1 < GROUPS))
                def _():
                    relay_step(g + 1, 0)

                @pl.when(g == GROUPS - 1)
                def _():
                    rows_across(GROUPS - 2).start()

            if turn == 7:
                @pl.when(g == 0)
                def _():
                    begin_queries(3)
                    relay_step(1, 0)

                @pl.when(g + 2 < GROUPS)
                def _():
                    forward(g + 2)

                @pl.when(g > 0)
                def _():
                    relay_step(g - 1, 1)

                @pl.when((g > 0) & (g < GROUPS - 1))
                def _():
                    rows_across(g - 1).start()

                @pl.when(g > 1)
                def _():
                    finish(g - 2)

        for a in range(2):
            rows_along(g, a).start()

        def gather(w, base):
            acc = None
            for b in range(FRAME):
                place = meta_sm[b // HALF, b % HALF, PLACE_AT + base + w]
                tile = tiles[b, place]
                acc = tile if acc is None else acc + tile
            return acc

        def collect(w, inner):
            give[g, 1, w] = gather(w, 0).astype(jnp.bfloat16)
            give[g, 0, w] = gather(w, 2 * FRAME).astype(jnp.bfloat16)
            return inner

        lax.fori_loop(0, FRAME, collect, 0)
        for d in range(2):
            for part in range(2):
                start_terms(g, d, part)

        def collect_own(w, inner):
            own[lax.rem(g, 2), w] = gather(w, FRAME)
            return inner

        lax.fori_loop(0, FRAME, collect_own, 0)

        return carry

    lax.fori_loop(0, GROUPS, one_group, 0)
    relay_step(GROUPS - 1, 1)
    rows_across(GROUPS - 1).start()
    finish(GROUPS - 2)
    finish(GROUPS - 1)

    def land(g, carry):
        grads_across(g).wait_recv()
        for a in range(2):
            grads_back(g, a).start()
        return carry

    lax.fori_loop(0, GROUPS, land, 0)

    def drain(g, carry):
        for pair in range(2):
            swap(g, pair).wait_send()
        for d in range(2):
            @pl.when(sends_to[d])
            def _():
                for part in range(2):
                    wait_terms(g, d, part).wait_send()
                wait_pass(g, d, 0).wait_send()

                @pl.when(jnp.logical_not(skipped[d]))
                def _():
                    wait_pass(g, d, 1).wait_send()

                @pl.when(slant[d])
                def _():
                    slant_copy(g, d).wait_send()

        for phase in range(2):
            @pl.when(relays(g, phase))
            def _():
                relay_on(g, phase).wait_send()

        rows_across(g).wait_send()
        grads_across(g).wait_send()
        for a in range(2):
            rows_along(g, a).wait()
            grads_along(g, a).wait()
            rows_back(g, a).wait()
            grads_back(g, a).wait()
        return carry

    lax.fori_loop(0, GROUPS, drain, 0)


def hand_over(*refs):
    sources, targets, held, in_sems, out_sems = refs[:4], refs[4:8], refs[8], refs[9], refs[10]
    spots = [(i, at) for i in range(4) for at in range(HALF)]
    ins = [pltpu.make_async_copy(sources[i].at[at], held.at[i, at], in_sems.at[i, at]) for i, at in spots]
    outs = [pltpu.make_async_copy(held.at[i, at], targets[i].at[at], out_sems.at[i, at]) for i, at in spots]
    for copy in ins:
        copy.start()
    for arrives, leaves in zip(ins, outs):
        arrives.wait()
        leaves.start()
    for copy in outs:
        copy.wait()


def body(queries, keys, values, out_grad, block_list, block_count):
    rows, width = queries.shape
    frames = lax.axis_size("frames")
    blocked = [x.reshape(HALF, BLOCK, width) for x in (queries, keys, values, out_grad)]
    shape = jax.ShapeDtypeStruct((HALF, BLOCK, width), jnp.bfloat16)
    dma = pltpu.SemaphoreType.DMA
    flops = 6 * 2 * FRAME * SEL * BLOCK * 256 * 256 * GROUPS
    outs = pl.pallas_call(
        lambda *refs: kernel(frames, *refs),
        out_shape=[shape] * 4,
        in_specs=[pl.BlockSpec(memory_space=pltpu.VMEM), pl.BlockSpec(memory_space=pltpu.SMEM)] + [pl.BlockSpec(memory_space=pl.ANY)] * 4,
        out_specs=[pl.BlockSpec(memory_space=pl.ANY)] * 4,
        scratch_shapes=[
            pltpu.VMEM((4, HALF, BLOCK, width), jnp.bfloat16),
            pltpu.VMEM((GROUPS, 2, HALF, BLOCK, 2 * LANES), jnp.bfloat16),
            pltpu.VMEM((GROUPS, WINDOW, BLOCK, 2 * LANES), jnp.bfloat16),
            pltpu.VMEM((GROUPS, FRAME, BLOCK, 2 * LANES), jnp.bfloat16),
            pltpu.VMEM((WINDOW, BLOCK, 2 * LANES), jnp.bfloat16),
            pltpu.VMEM((FRAME, SEL + 1, BLOCK, 2 * LANES), jnp.float32),
            pltpu.VMEM((GROUPS, FRAME, BLOCK, 2 * LANES), jnp.bfloat16),
            pltpu.VMEM((GROUPS, HALF, BLOCK, 2 * LANES), jnp.bfloat16),
            pltpu.VMEM((GROUPS, 2, FRAME, BLOCK, 2 * LANES), jnp.bfloat16),
            pltpu.VMEM((GROUPS, 2, FRAME, BLOCK, 2 * LANES), jnp.bfloat16),
            pltpu.VMEM((2, FRAME, BLOCK, 2 * LANES), jnp.float32),
            pltpu.VMEM((GROUPS, FRAME, BLOCK, 2 * LANES), jnp.bfloat16),
            pltpu.VMEM((GROUPS, HALF, BLOCK, 2 * LANES), jnp.bfloat16),
            pltpu.VMEM((2, GROUPS, HALF, BLOCK, 2 * LANES), jnp.bfloat16),
            pltpu.VMEM((2, 8, LANES), jnp.int32),
            pltpu.SMEM((2, 8, LANES), jnp.int32),
            dma((4,)), dma((GROUPS, 2)), dma((GROUPS, 2)),
            dma((GROUPS, 2, 2)), dma((GROUPS, 2, 2)),
            dma, dma, dma,
            dma((GROUPS,)), dma((GROUPS,)), dma((2 * GROUPS, 2)),
            dma((GROUPS, 2, 2)), dma((GROUPS, 2, 2)),
            dma((GROUPS,)), dma((GROUPS,)), dma((2 * GROUPS, 2)),
            dma((2, GROUPS)), dma((2, GROUPS)), dma((GROUPS,)),
        ],
        cost_estimate=pl.CostEstimate(
            flops=flops, bytes_accessed=16 * rows * width, transcendentals=FRAME * SEL * BLOCK * LANES * GROUPS
        ),
        compiler_params=pltpu.CompilerParams(
            collective_id=0, has_side_effects=True, vmem_limit_bytes=60 * 1024 * 1024
        ),
    )(block_list, block_count, *blocked)
    outs = pl.pallas_call(
        hand_over,
        out_shape=[shape] * 4,
        in_specs=[pl.BlockSpec(memory_space=pl.ANY)] * 4,
        out_specs=[pl.BlockSpec(memory_space=pl.ANY)] * 4,
        scratch_shapes=[
            pltpu.VMEM((4, HALF, BLOCK, width), jnp.bfloat16), dma((4, HALF)), dma((4, HALF)),
        ],
        compiler_params=pltpu.CompilerParams(vmem_limit_bytes=60 * 1024 * 1024),
    )(*outs)
    return tuple(x.reshape(rows, width) for x in outs)


def solution(mesh):
    split = P(("frames", "strip"), None)
    in_specs = (split, split, split, split, split, P(("frames", "strip")))
    return jax.shard_map(
        body, mesh=mesh, in_specs=in_specs, out_specs=(split,) * 4, check_vma=False
    )
```

```python
import jax
import jax.numpy as jnp
from jax import lax
from jax.experimental import pallas as pl
from jax.experimental.pallas import tpu as pltpu
from jax.sharding import PartitionSpec as P

HD = 64
BLOCK = 64
SEL = 13
HALF = 4
FRAME = 8
WINDOW = 24
GROUPS = 4
LANES = 128
FACTOR = 0.125
MASKED = -1e30
PLACE_AT = 32
RUN = 8
MESH = pl.DeviceIdType.MESH


def kernel(
    frames,
    block_list, block_count, queries, keys, values, out_grad,
    attended, query_grad, key_grad, value_grad,
    loaded, packed, kv, qd, work, tiles, rows_out, rows_in, give, take, own, final, final_in, relay, meta_vm, meta_sm,
    load_sem, in_send, in_recv, pass_send, pass_recv,
    meta_send, meta_recv, meta_local, row_send, row_recv, row_local,
    term_send, term_recv, grad_send, grad_recv, grad_local, relay_send, relay_recv, slant_send,
):
    f, s = lax.axis_index("frames"), lax.axis_index("strip")
    o = 1 - s
    partner, next_dev, prev_dev = (f, o), (f + 1, s), (f - 1, s)

    sources = (keys, values, queries, out_grad)
    loads = [pltpu.make_async_copy(sources[a], loaded.at[a], load_sem.at[a]) for a in range(4)]
    for load in loads:
        load.start()

    place_in_run = lax.rem(f, RUN)
    has_after, has_before = f < frames - 1, f > 0
    edge = ((place_in_run == RUN - 1) & has_after, (place_in_run == 0) & has_before)
    part_column = (3 * s, 1 + s)

    def relay_of(d, column):
        return (f - 2 * column if d == 0 else f + 2 * column, s)

    def relay_to(d, column):
        return (f + 1 + 2 * column if d == 0 else f - 1 - 2 * column, s)

    relay_back = 1 - lax.rem(place_in_run, 2)
    relay_column = lax.select(relay_back == 0, (RUN - 1 - place_in_run) // 2, place_in_run // 2)
    relay_half = lax.rem(relay_column, 2)
    relay_source_frame = f - place_in_run + (1 - relay_back) * (RUN - 1)
    relay_target_frame = relay_source_frame + 1 - 2 * relay_back
    is_relay = ((relay_column == 1) & (s == 0)) | ((relay_column >= 2) & (s == 1))
    is_relay = is_relay & (relay_target_frame >= 0) & (relay_target_frame < frames)
    relay_target, relay_source = (relay_target_frame, s), (relay_source_frame, s)

    barrier = pltpu.get_barrier_semaphore()

    def greet(device):
        pl.semaphore_signal(barrier, inc=1, device_id=device, device_id_type=MESH)

    greet(partner)

    @pl.when(has_after)
    def _():
        greet(next_dev)

    @pl.when(has_before)
    def _():
        greet(prev_dev)

    @pl.when(is_relay)
    def _():
        greet(relay_source)
        greet(relay_target)

    for d in range(2):
        for column in (1, 2, 3):
            @pl.when(edge[d] & (s == (0 if column == 1 else 1)))
            def _():
                greet(relay_of(d, column))
                greet(relay_to(d, column))

    slant = (edge[0] & (s == 1), edge[1] & (s == 0))
    slant_to = ((f + 1, 0), (f - 1, 1))
    for d in range(2):
        @pl.when(slant[d])
        def _():
            greet(slant_to[d])

    at_end = (edge[0] | edge[1]).astype(jnp.int32)
    slants = (slant[0] | slant[1]).astype(jnp.int32)
    beside = has_after.astype(jnp.int32) + has_before.astype(jnp.int32)
    pl.semaphore_wait(barrier, 1 + beside + slants + 2 * is_relay.astype(jnp.int32) + at_end * (2 + 2 * s))

    def remote(src, dst, send, recv, device):
        return pltpu.make_async_remote_copy(
            src_ref=src, dst_ref=dst, send_sem=send, recv_sem=recv,
            device_id=device, device_id_type=MESH,
        )

    def columns(half, g):
        return pl.ds(pl.multiple_of(half * (GROUPS * LANES) + g * LANES, LANES), LANES)

    def landing(g, pair, half):
        if pair == 0:
            return kv.at[g, pl.ds(FRAME + HALF * half, HALF)]
        return qd.at[g, pl.ds(HALF * half, HALF)]

    def swap(g, pair):
        return remote(
            packed.at[g, pair], landing(g, pair, s), in_send.at[g, pair], in_recv.at[g, pair], partner
        )

    def pack(g, pair):
        for a in range(2):
            lanes = slice(a * LANES, (a + 1) * LANES)
            packed[g, pair, :, :, lanes] = loaded[2 * pair + a, :, :, columns(o, g)]

    def keep(g, pair):
        own_rows = landing(g, pair, s)
        for a in range(2):
            lanes = slice(a * LANES, (a + 1) * LANES)
            own_rows[:, :, lanes] = loaded[2 * pair + a, :, :, columns(s, g)]

    neighbours = (next_dev, prev_dev)
    sends_to, hears_from = (has_after, has_before), (has_before, has_after)

    skipped = (edge[0] & (s == 0), edge[1] & (s == 1))

    def start_part(d, part, src, dst, send, recv, phase, g):
        straight = remote(src, dst, send, recv, neighbours[d])
        starts = sends_to[d]
        if part == 0:
            bent = edge[d] & (s == 1)
        elif phase == 0:
            bent = edge[d] & (s != d) & (g > 1)
            starts = starts & jnp.logical_not(skipped[d])
        else:
            bent = edge[d]

        @pl.when(bent)
        def _():
            remote(
                src, relay.at[phase, g], send, relay_recv.at[phase, g], relay_of(d, part_column[part])
            ).start()

        @pl.when(starts & jnp.logical_not(bent))
        def _():
            straight.start()

    def kv_window(g, base, half):
        return kv.at[g, pl.ds(base + HALF * half, HALF)]

    def pass_args(g, d, part):
        half = (s, o)[part]
        return (
            kv_window(g, FRAME, half), kv_window(g, (0, 2 * FRAME)[d], half),
            pass_send.at[g, d, half], pass_recv.at[g, d, half],
        )

    def start_pass(g, d, part):
        start_part(d, part, *pass_args(g, d, part), 0, g)

    def wait_pass(g, d, part):
        return remote(*pass_args(g, d, part), neighbours[d])

    def term_args(g, d, part):
        half = (s, o)[part]
        at = pl.ds(HALF * half, HALF)
        return (
            give.at[g, d, at], take.at[g, d, at], term_send.at[g, d, half], term_recv.at[g, d, half]
        )

    def start_terms(g, d, part):
        start_part(d, part, *term_args(g, d, part), 1, g)

    def wait_terms(g, d, part):
        return remote(*term_args(g, d, part), neighbours[d])

    def relay_on(g, phase):
        if phase == 0:
            target = kv_window(g, relay_back * (2 * FRAME), relay_half)
            recv = pass_recv.at[g, relay_back, relay_half]
        else:
            target = take.at[g, relay_back, pl.ds(HALF * relay_half, HALF)]
            recv = term_recv.at[g, relay_back, relay_half]
        return remote(relay.at[phase, g], target, relay_send.at[phase, g], recv, relay_target)

    def relays(g, phase):
        if phase == 0:
            return is_relay & ((relay_column == 3) | ((relay_column == 2 - relay_back) & (g > 1)))
        return is_relay

    def slant_copy(g, d):
        base = (0, 2 * FRAME)[d]
        return remote(
            packed.at[g, 0], kv_window(g, base, s), slant_send.at[g], pass_recv.at[g, d, s], slant_to[d]
        )

    def relay_step(g, phase):
        @pl.when(relays(g, phase))
        def _():
            remote(
                relay.at[phase, g], relay.at[phase, g], relay_send.at[phase, g],
                relay_recv.at[phase, g], relay_target,
            ).wait_recv()
            relay_on(g, phase).start()

    def rows_across(g):
        return remote(
            rows_out.at[g, pl.ds(HALF * o, HALF)], rows_in.at[g], row_send.at[g], row_recv.at[g], partner
        )

    def grads_across(g):
        return remote(
            final.at[g, pl.ds(HALF * o, HALF)], final_in.at[g], grad_send.at[g], grad_recv.at[g], partner
        )

    row_targets, grad_targets = (query_grad, attended), (key_grad, value_grad)

    def place_copy(staged, targets, local, g, half, a):
        return pltpu.make_async_copy(
            staged.at[:, :, pl.ds(a * LANES, LANES)], targets[a].at[:, :, columns(half, g)], local.at[g, a]
        )

    def rows_along(g, a):
        return place_copy(rows_out.at[g, pl.ds(HALF * s, HALF)], row_targets, row_local, g, s, a)

    def grads_along(g, a):
        return place_copy(final.at[g, pl.ds(HALF * s, HALF)], grad_targets, grad_local, g, s, a)

    def rows_back(g, a):
        return place_copy(rows_in.at[g], row_targets, row_local.at[pl.ds(GROUPS, GROUPS)], g, o, a)

    def grads_back(g, a):
        return place_copy(final_in.at[g], grad_targets, grad_local.at[pl.ds(GROUPS, GROUPS)], g, o, a)

    share_meta = remote(meta_vm.at[s], meta_vm.at[s], meta_send, meta_recv, partner)

    def begin_keys(g):
        swap(g, 0).start()
        for d in range(2):
            start_pass(g, d, 0)

            @pl.when(slant[d])
            def _():
                slant_copy(g, d).start()

    def begin_queries(g):
        swap(g, 1).start()

    def pack_keep(g):
        for pair in range(2):
            pack(g, pair)
            keep(g, pair)

    for pair in range(2):
        loads[2 * pair].wait()
        loads[2 * pair + 1].wait()
        pack(0, pair)
        keep(0, pair)
        if pair == 0:
            begin_keys(0)
        else:
            begin_queries(0)

    listed = block_list[...]
    row_at = lax.broadcasted_iota(jnp.int32, (HALF, LANES), 0)
    lane_at = lax.broadcasted_iota(jnp.int32, (HALF, LANES), 1)
    counts = jnp.zeros((HALF, LANES), jnp.int32)
    for row in range(HALF):
        counts = jnp.where(row_at == row, block_count[row], counts)
    edge_low = jnp.where(f > 0, 0, FRAME)
    edge_high = jnp.where(f < frames - 1, WINDOW, 2 * FRAME)
    usable = (listed >= edge_low) & (listed < edge_high) & (lane_at[:, :SEL] < counts[:, :SEL])
    slots = jnp.where(usable, listed, -1)
    place = jnp.full((HALF, LANES), SEL, jnp.int32)
    for j in range(SEL):
        place = jnp.where(lane_at - PLACE_AT == slots[:, j:j + 1], j, place)
    meta_vm[s, 0:HALF] = place
    meta_vm[s, 0:HALF, 0:SEL] = listed
    meta_vm[s, HALF:] = jnp.zeros((HALF, LANES), jnp.int32)
    meta_vm[s, HALF:, 0:SEL] = usable.astype(jnp.int32)
    share_meta.start()
    pack_keep(1)
    begin_keys(1)
    pack_keep(2)
    tiles[:, SEL] = jnp.zeros((FRAME, BLOCK, 2 * LANES), jnp.float32)

    def forward(g):
        swap(g, 0).wait_recv()
        for d in range(2):
            start_pass(g, d, 1)

    def clear(w, carry):
        @pl.when(jnp.logical_not(has_before))
        def _():
            for g in range(GROUPS):
                kv[g, w] = jnp.zeros((BLOCK, 2 * LANES), jnp.bfloat16)
                take[g, 0, w] = jnp.zeros((BLOCK, 2 * LANES), jnp.bfloat16)

        @pl.when(jnp.logical_not(has_after))
        def _():
            for g in range(GROUPS):
                kv[g, 2 * FRAME + w] = jnp.zeros((BLOCK, 2 * LANES), jnp.bfloat16)
                take[g, 1, w] = jnp.zeros((BLOCK, 2 * LANES), jnp.bfloat16)

        return carry

    lax.fori_loop(0, FRAME, clear, 0)
    relay_step(0, 0)
    forward(0)
    begin_keys(2)
    begin_queries(1)
    share_meta.wait()
    to_scalar = pltpu.make_async_copy(meta_vm, meta_sm, meta_local)
    to_scalar.start()
    to_scalar.wait()
    pack_keep(3)

    row_ids = lax.broadcasted_iota(jnp.int32, (4 * HD, 4 * HD), 0) // HD
    col_ids = lax.broadcasted_iota(jnp.int32, (4 * HD, 4 * HD), 1) // HD
    spread = jnp.where(
        row_ids == col_ids, jnp.where(col_ids < 2, FACTOR, 1.0), 0.0
    ).astype(jnp.bfloat16)
    first_head = lax.broadcasted_iota(jnp.int32, (BLOCK, LANES), 1) < HD

    def heads(full):
        return jnp.where(first_head, full[:HD], full[HD:])

    def fold(array, op):
        return op(array.reshape(array.shape[0] // 8, 8, LANES), axis=0)

    def attend(g, b):
        strip, row = b // HALF, lax.rem(b, HALF)
        chunks = ((0, 4), (4, 8), (8, SEL))
        keep = {"slabs": [None] * SEL, "powers": [None] * SEL}

        def diagonal():
            keep["diagonal"] = jnp.concatenate([qd[g, b]] * 4, axis=0) * spread
            keep["bias"] = [
                jnp.where(meta_sm[strip, HALF + row, j] > 0, 0.0, MASKED).astype(jnp.float32)
                for j in range(SEL)
            ]

        def products(c):
            low, high = chunks[c]
            picked = jnp.concatenate([work[meta_sm[strip, row, j]] for j in range(low, high)], axis=0)
            keep["picked", c] = picked
            both = lax.dot_general(
                picked, keep["diagonal"], (((1,), (1,)), ((), ())), preferred_element_type=jnp.float32
            )
            for j in range(low, high):
                at = slice((j - low) * BLOCK, (j - low + 1) * BLOCK)
                keep["scores", j] = both[at, :LANES]
                keep["grad_weights", j] = both[at, LANES:]

        def peak(c):
            for j in range(*chunks[c]):
                top = fold(keep["scores", j], jnp.max) + keep["bias"][j]
                keep["peak"] = jnp.maximum(keep["peak"], top) if j else top
            if c == len(chunks) - 1:
                keep["peak"] = jnp.max(keep["peak"], axis=0, keepdims=True)

        def power(j):
            powers = jnp.exp(keep["scores", j] - (keep["peak"] - keep["bias"][j]))
            keep["powers"][j] = powers
            total = fold(powers, jnp.sum)
            dots = fold(powers * keep["grad_weights", j], jnp.sum)
            keep["total"] = keep["total"] + total if j else total
            keep["dots"] = keep["dots"] + dots if j else dots
            if j == SEL - 1:
                keep["scale"] = 1.0 / jnp.sum(keep["total"], axis=0, keepdims=True)
                keep["row_dots"] = jnp.sum(keep["dots"], axis=0, keepdims=True) * keep["scale"]

        def slab(j):
            weights = keep["powers"][j] * keep["scale"]
            grad_scores = weights * (keep["grad_weights", j] - keep["row_dots"])
            keep["slabs"][j] = (grad_scores.astype(jnp.bfloat16), weights.astype(jnp.bfloat16))

        def terms(c):
            low, high = chunks[c]
            parts = [jnp.concatenate([pair[k] for pair in keep["slabs"][low:high]], axis=0) for k in range(2)]
            keep["parts", c] = parts
            result = jnp.dot(
                jnp.concatenate(parts, axis=1), keep["diagonal"], preferred_element_type=jnp.float32
            )
            tiles[b, low:high] = result.reshape(high - low, BLOCK, 2 * LANES)

        def mixed(c):
            for k in range(2):
                lanes = slice(k * LANES, (k + 1) * LANES)
                product = lax.dot_general(
                    keep["parts", c][k], keep["picked", c][:, lanes], (((0,), (0,)), ((), ())),
                    preferred_element_type=jnp.float32,
                )
                keep["mixed", k] = keep["mixed", k] + product if c else product
            if c == len(chunks) - 1:
                rows_out[g, b] = jnp.concatenate(
                    [heads(keep["mixed", 0]) * FACTOR, heads(keep["mixed", 1])], axis=1
                ).astype(jnp.bfloat16)

        def call(function, *args):
            return lambda: function(*args)

        count = range(len(chunks))
        return (
            [diagonal] + [call(products, c) for c in count],
            [call(peak, c) for c in count] + [call(power, j) for j in range(SEL)] + [call(slab, j) for j in range(SEL)],
            [call(step, c) for c in count for step in (terms, mixed)],
        )

    def interleave(stages):
        placed = [
            ((k + 0.5) / len(stage), n, step)
            for n, stage in enumerate(stages)
            for k, step in enumerate(stage)
        ]
        for _, _, step in sorted(placed, key=lambda item: item[:2]):
            step()

    def finish(g):
        slot = lax.rem(g, 2)
        for d in range(2):
            @pl.when(hears_from[d])
            def _():
                for part in range(2):
                    wait_terms(g, d, part).wait_recv()

        def add(w, carry):
            total = own[slot, w] + take[g, 0, w].astype(jnp.float32) + take[g, 1, w].astype(jnp.float32)
            final[g, w] = total.astype(jnp.bfloat16)
            return carry

        lax.fori_loop(0, FRAME, add, 0)
        grads_across(g).start()
        for a in range(2):
            grads_along(g, a).start()
        rows_across(g).wait_recv()
        for a in range(2):
            rows_back(g, a).start()

    def one_group(g, carry):
        swap(g, 1).wait_recv()
        for d in range(2):
            @pl.when(hears_from[d])
            def _():
                for part in range(2):
                    wait_pass(g, d, part).wait_recv()

        work[...] = kv[g]

        blocks = [attend(g, lax.rem(HALF * o + i, FRAME)) for i in range(FRAME)]
        for turn in range(FRAME + 2):
            interleave([blocks[turn - k][k] for k in (2, 1, 0) if 0 <= turn - k < FRAME])
            if turn == 3:
                @pl.when(g == 0)
                def _():
                    forward(1)
                    relay_step(1, 0)
                    begin_keys(3)
                    begin_queries(2)

                @pl.when((g > 0) & (g + 1 < GROUPS))
                def _():
                    relay_step(g + 1, 0)

                @pl.when(g == GROUPS - 1)
                def _():
                    rows_across(GROUPS - 2).start()

            if turn == 7:
                @pl.when(g == 0)
                def _():
                    begin_queries(3)

                @pl.when(g + 2 < GROUPS)
                def _():
                    forward(g + 2)

                @pl.when(g > 0)
                def _():
                    relay_step(g - 1, 1)

                @pl.when((g > 0) & (g < GROUPS - 1))
                def _():
                    rows_across(g - 1).start()

                @pl.when(g > 1)
                def _():
                    finish(g - 2)

        for a in range(2):
            rows_along(g, a).start()

        def gather(w, base):
            acc = None
            for b in range(FRAME):
                place = meta_sm[b // HALF, b % HALF, PLACE_AT + base + w]
                tile = tiles[b, place]
                acc = tile if acc is None else acc + tile
            return acc

        def collect(w, inner):
            give[g, 1, w] = gather(w, 0).astype(jnp.bfloat16)
            give[g, 0, w] = gather(w, 2 * FRAME).astype(jnp.bfloat16)
            return inner

        lax.fori_loop(0, FRAME, collect, 0)
        for d in range(2):
            for part in range(2):
                start_terms(g, d, part)

        def collect_own(w, inner):
            own[lax.rem(g, 2), w] = gather(w, FRAME)
            return inner

        lax.fori_loop(0, FRAME, collect_own, 0)

        return carry

    lax.fori_loop(0, GROUPS, one_group, 0)
    relay_step(GROUPS - 1, 1)
    rows_across(GROUPS - 1).start()
    finish(GROUPS - 2)
    finish(GROUPS - 1)

    def land(g, carry):
        grads_across(g).wait_recv()
        for a in range(2):
            grads_back(g, a).start()
        return carry

    lax.fori_loop(0, GROUPS, land, 0)

    def drain(g, carry):
        for pair in range(2):
            swap(g, pair).wait_send()
        for d in range(2):
            @pl.when(sends_to[d])
            def _():
                for part in range(2):
                    wait_terms(g, d, part).wait_send()
                wait_pass(g, d, 0).wait_send()

                @pl.when(jnp.logical_not(skipped[d]))
                def _():
                    wait_pass(g, d, 1).wait_send()

                @pl.when(slant[d])
                def _():
                    slant_copy(g, d).wait_send()

        for phase in range(2):
            @pl.when(relays(g, phase))
            def _():
                relay_on(g, phase).wait_send()

        rows_across(g).wait_send()
        grads_across(g).wait_send()
        for a in range(2):
            rows_along(g, a).wait()
            grads_along(g, a).wait()
            rows_back(g, a).wait()
            grads_back(g, a).wait()
        return carry

    lax.fori_loop(0, GROUPS, drain, 0)


def hand_over(*refs):
    sources, targets, held, in_sems, out_sems = refs[:4], refs[4:8], refs[8], refs[9], refs[10]
    spots = [(i, at) for i in range(4) for at in range(HALF)]
    ins = [pltpu.make_async_copy(sources[i].at[at], held.at[i, at], in_sems.at[i, at]) for i, at in spots]
    outs = [pltpu.make_async_copy(held.at[i, at], targets[i].at[at], out_sems.at[i, at]) for i, at in spots]
    for copy in ins:
        copy.start()
    for arrives, leaves in zip(ins, outs):
        arrives.wait()
        leaves.start()
    for copy in outs:
        copy.wait()


def body(queries, keys, values, out_grad, block_list, block_count):
    rows, width = queries.shape
    frames = lax.axis_size("frames")
    blocked = [x.reshape(HALF, BLOCK, width) for x in (queries, keys, values, out_grad)]
    shape = jax.ShapeDtypeStruct((HALF, BLOCK, width), jnp.bfloat16)
    dma = pltpu.SemaphoreType.DMA
    flops = 6 * 2 * FRAME * SEL * BLOCK * 256 * 256 * GROUPS
    outs = pl.pallas_call(
        lambda *refs: kernel(frames, *refs),
        out_shape=[shape] * 4,
        in_specs=[pl.BlockSpec(memory_space=pltpu.VMEM), pl.BlockSpec(memory_space=pltpu.SMEM)] + [pl.BlockSpec(memory_space=pl.ANY)] * 4,
        out_specs=[pl.BlockSpec(memory_space=pl.ANY)] * 4,
        scratch_shapes=[
            pltpu.VMEM((4, HALF, BLOCK, width), jnp.bfloat16),
            pltpu.VMEM((GROUPS, 2, HALF, BLOCK, 2 * LANES), jnp.bfloat16),
            pltpu.VMEM((GROUPS, WINDOW, BLOCK, 2 * LANES), jnp.bfloat16),
            pltpu.VMEM((GROUPS, FRAME, BLOCK, 2 * LANES), jnp.bfloat16),
            pltpu.VMEM((WINDOW, BLOCK, 2 * LANES), jnp.bfloat16),
            pltpu.VMEM((FRAME, SEL + 1, BLOCK, 2 * LANES), jnp.float32),
            pltpu.VMEM((GROUPS, FRAME, BLOCK, 2 * LANES), jnp.bfloat16),
            pltpu.VMEM((GROUPS, HALF, BLOCK, 2 * LANES), jnp.bfloat16),
            pltpu.VMEM((GROUPS, 2, FRAME, BLOCK, 2 * LANES), jnp.bfloat16),
            pltpu.VMEM((GROUPS, 2, FRAME, BLOCK, 2 * LANES), jnp.bfloat16),
            pltpu.VMEM((2, FRAME, BLOCK, 2 * LANES), jnp.float32),
            pltpu.VMEM((GROUPS, FRAME, BLOCK, 2 * LANES), jnp.bfloat16),
            pltpu.VMEM((GROUPS, HALF, BLOCK, 2 * LANES), jnp.bfloat16),
            pltpu.VMEM((2, GROUPS, HALF, BLOCK, 2 * LANES), jnp.bfloat16),
            pltpu.VMEM((2, 8, LANES), jnp.int32),
            pltpu.SMEM((2, 8, LANES), jnp.int32),
            dma((4,)), dma((GROUPS, 2)), dma((GROUPS, 2)),
            dma((GROUPS, 2, 2)), dma((GROUPS, 2, 2)),
            dma, dma, dma,
            dma((GROUPS,)), dma((GROUPS,)), dma((2 * GROUPS, 2)),
            dma((GROUPS, 2, 2)), dma((GROUPS, 2, 2)),
            dma((GROUPS,)), dma((GROUPS,)), dma((2 * GROUPS, 2)),
            dma((2, GROUPS)), dma((2, GROUPS)), dma((GROUPS,)),
        ],
        cost_estimate=pl.CostEstimate(
            flops=flops, bytes_accessed=16 * rows * width, transcendentals=FRAME * SEL * BLOCK * LANES * GROUPS
        ),
        compiler_params=pltpu.CompilerParams(
            collective_id=0, has_side_effects=True, vmem_limit_bytes=60 * 1024 * 1024
        ),
    )(block_list, block_count, *blocked)
    outs = pl.pallas_call(
        hand_over,
        out_shape=[shape] * 4,
        in_specs=[pl.BlockSpec(memory_space=pl.ANY)] * 4,
        out_specs=[pl.BlockSpec(memory_space=pl.ANY)] * 4,
        scratch_shapes=[
            pltpu.VMEM((4, HALF, BLOCK, width), jnp.bfloat16), dma((4, HALF)), dma((4, HALF)),
        ],
        compiler_params=pltpu.CompilerParams(vmem_limit_bytes=60 * 1024 * 1024),
    )(*outs)
    return tuple(x.reshape(rows, width) for x in outs)


def solution(mesh):
    split = P(("frames", "strip"), None)
    in_specs = (split, split, split, split, split, P(("frames", "strip")))
    return jax.shard_map(
        body, mesh=mesh, in_specs=in_specs, out_specs=(split,) * 4, check_vma=False
    )
```

```python
import jax
import jax.numpy as jnp
from jax import lax
from jax.experimental import pallas as pl
from jax.experimental.pallas import tpu as pltpu
from jax.sharding import PartitionSpec as P

HD = 64
BLOCK = 64
SEL = 13
HALF = 4
FRAME = 8
WINDOW = 24
GROUPS = 4
LANES = 128
FACTOR = 0.125
MASKED = -1e30
PLACE_AT = 32
RUN = 8
MESH = pl.DeviceIdType.MESH


def kernel(
    frames,
    block_list, block_count, queries, keys, values, out_grad,
    attended, query_grad, key_grad, value_grad,
    loaded, packed, kv, qd, work, tiles, rows_out, rows_in, give, take, own, final, final_in, relay, meta_vm, meta_sm,
    load_sem, in_send, in_recv, pass_send, pass_recv,
    meta_send, meta_recv, meta_local, row_send, row_recv, row_local,
    term_send, term_recv, grad_send, grad_recv, grad_local, relay_send, relay_recv, slant_send,
):
    f, s = lax.axis_index("frames"), lax.axis_index("strip")
    o = 1 - s
    partner, next_dev, prev_dev = (f, o), (f + 1, s), (f - 1, s)

    sources = (keys, values, queries, out_grad)
    loads = [pltpu.make_async_copy(sources[a], loaded.at[a], load_sem.at[a]) for a in range(4)]
    for load in loads:
        load.start()

    place_in_run = lax.rem(f, RUN)
    has_after, has_before = f < frames - 1, f > 0
    edge = ((place_in_run == RUN - 1) & has_after, (place_in_run == 0) & has_before)
    part_column = (3 * s, 1 + s)

    def relay_of(d, column):
        return (f - 2 * column if d == 0 else f + 2 * column, s)

    def relay_to(d, column):
        return (f + 1 + 2 * column if d == 0 else f - 1 - 2 * column, s)

    relay_back = 1 - lax.rem(place_in_run, 2)
    relay_column = lax.select(relay_back == 0, (RUN - 1 - place_in_run) // 2, place_in_run // 2)
    relay_half = lax.rem(relay_column, 2)
    relay_source_frame = f - place_in_run + (1 - relay_back) * (RUN - 1)
    relay_target_frame = relay_source_frame + 1 - 2 * relay_back
    is_relay = ((relay_column == 1) & (s == 0)) | ((relay_column >= 2) & (s == 1))
    is_relay = is_relay & (relay_target_frame >= 0) & (relay_target_frame < frames)
    relay_target, relay_source = (relay_target_frame, s), (relay_source_frame, s)

    barrier = pltpu.get_barrier_semaphore()

    def greet(device):
        pl.semaphore_signal(barrier, inc=1, device_id=device, device_id_type=MESH)

    greet(partner)

    @pl.when(has_after)
    def _():
        greet(next_dev)

    @pl.when(has_before)
    def _():
        greet(prev_dev)

    @pl.when(is_relay)
    def _():
        greet(relay_source)
        greet(relay_target)

    for d in range(2):
        for column in (1, 2, 3):
            @pl.when(edge[d] & (s == (0 if column == 1 else 1)))
            def _():
                greet(relay_of(d, column))
                greet(relay_to(d, column))

    slant = (edge[0] & (s == 1), edge[1] & (s == 0))
    slant_to = ((f + 1, 0), (f - 1, 1))
    for d in range(2):
        @pl.when(slant[d])
        def _():
            greet(slant_to[d])

    at_end = (edge[0] | edge[1]).astype(jnp.int32)
    slants = (slant[0] | slant[1]).astype(jnp.int32)
    beside = has_after.astype(jnp.int32) + has_before.astype(jnp.int32)
    pl.semaphore_wait(barrier, 1 + beside + slants + 2 * is_relay.astype(jnp.int32) + at_end * (2 + 2 * s))

    def remote(src, dst, send, recv, device):
        return pltpu.make_async_remote_copy(
            src_ref=src, dst_ref=dst, send_sem=send, recv_sem=recv,
            device_id=device, device_id_type=MESH,
        )

    def columns(half, g):
        return pl.ds(pl.multiple_of(half * (GROUPS * LANES) + g * LANES, LANES), LANES)

    def landing(g, pair, half):
        if pair == 0:
            return kv.at[g, pl.ds(FRAME + HALF * half, HALF)]
        return qd.at[g, pl.ds(HALF * half, HALF)]

    def swap(g, pair):
        return remote(
            packed.at[g, pair], landing(g, pair, s), in_send.at[g, pair], in_recv.at[g, pair], partner
        )

    def pack(g, pair):
        for a in range(2):
            lanes = slice(a * LANES, (a + 1) * LANES)
            packed[g, pair, :, :, lanes] = loaded[2 * pair + a, :, :, columns(o, g)]

    def keep(g, pair):
        own_rows = landing(g, pair, s)
        for a in range(2):
            lanes = slice(a * LANES, (a + 1) * LANES)
            own_rows[:, :, lanes] = loaded[2 * pair + a, :, :, columns(s, g)]

    neighbours = (next_dev, prev_dev)
    sends_to, hears_from = (has_after, has_before), (has_before, has_after)

    skipped = (edge[0] & (s == 0), edge[1] & (s == 1))

    def start_part(d, part, src, dst, send, recv, phase, g):
        straight = remote(src, dst, send, recv, neighbours[d])
        starts = sends_to[d]
        if part == 0:
            bent = edge[d] & (s == 1)
        elif phase == 0:
            bent = edge[d] & (s != d) & (g > 0)
            starts = starts & jnp.logical_not(skipped[d])
        else:
            bent = edge[d]

        @pl.when(bent)
        def _():
            remote(
                src, relay.at[phase, g], send, relay_recv.at[phase, g], relay_of(d, part_column[part])
            ).start()

        @pl.when(starts & jnp.logical_not(bent))
        def _():
            straight.start()

    def kv_window(g, base, half):
        return kv.at[g, pl.ds(base + HALF * half, HALF)]

    def pass_args(g, d, part):
        half = (s, o)[part]
        return (
            kv_window(g, FRAME, half), kv_window(g, (0, 2 * FRAME)[d], half),
            pass_send.at[g, d, half], pass_recv.at[g, d, half],
        )

    def start_pass(g, d, part):
        start_part(d, part, *pass_args(g, d, part), 0, g)

    def wait_pass(g, d, part):
        return remote(*pass_args(g, d, part), neighbours[d])

    def term_args(g, d, part):
        half = (s, o)[part]
        at = pl.ds(HALF * half, HALF)
        return (
            give.at[g, d, at], take.at[g, d, at], term_send.at[g, d, half], term_recv.at[g, d, half]
        )

    def start_terms(g, d, part):
        start_part(d, part, *term_args(g, d, part), 1, g)

    def wait_terms(g, d, part):
        return remote(*term_args(g, d, part), neighbours[d])

    def relay_on(g, phase):
        if phase == 0:
            target = kv_window(g, relay_back * (2 * FRAME), relay_half)
            recv = pass_recv.at[g, relay_back, relay_half]
        else:
            target = take.at[g, relay_back, pl.ds(HALF * relay_half, HALF)]
            recv = term_recv.at[g, relay_back, relay_half]
        return remote(relay.at[phase, g], target, relay_send.at[phase, g], recv, relay_target)

    def relays(g, phase):
        if phase == 0:
            return is_relay & ((relay_column == 3) | ((relay_column == 2 - relay_back) & (g > 0)))
        return is_relay

    def slant_copy(g, d):
        base = (0, 2 * FRAME)[d]
        return remote(
            packed.at[g, 0], kv_window(g, base, s), slant_send.at[g], pass_recv.at[g, d, s], slant_to[d]
        )

    def relay_step(g, phase):
        @pl.when(relays(g, phase))
        def _():
            remote(
                relay.at[phase, g], relay.at[phase, g], relay_send.at[phase, g],
                relay_recv.at[phase, g], relay_target,
            ).wait_recv()
            relay_on(g, phase).start()

    def rows_across(g):
        return remote(
            rows_out.at[g, pl.ds(HALF * o, HALF)], rows_in.at[g], row_send.at[g], row_recv.at[g], partner
        )

    def grads_across(g):
        return remote(
            final.at[g, pl.ds(HALF * o, HALF)], final_in.at[g], grad_send.at[g], grad_recv.at[g], partner
        )

    row_targets, grad_targets = (query_grad, attended), (key_grad, value_grad)

    def place_copy(staged, targets, local, g, half, a):
        return pltpu.make_async_copy(
            staged.at[:, :, pl.ds(a * LANES, LANES)], targets[a].at[:, :, columns(half, g)], local.at[g, a]
        )

    def rows_along(g, a):
        return place_copy(rows_out.at[g, pl.ds(HALF * s, HALF)], row_targets, row_local, g, s, a)

    def grads_along(g, a):
        return place_copy(final.at[g, pl.ds(HALF * s, HALF)], grad_targets, grad_local, g, s, a)

    def rows_back(g, a):
        return place_copy(rows_in.at[g], row_targets, row_local.at[pl.ds(GROUPS, GROUPS)], g, o, a)

    def grads_back(g, a):
        return place_copy(final_in.at[g], grad_targets, grad_local.at[pl.ds(GROUPS, GROUPS)], g, o, a)

    share_meta = remote(meta_vm.at[s], meta_vm.at[s], meta_send, meta_recv, partner)

    def begin_keys(g):
        swap(g, 0).start()
        for d in range(2):
            start_pass(g, d, 0)

            @pl.when(slant[d])
            def _():
                slant_copy(g, d).start()

    def begin_queries(g):
        swap(g, 1).start()

    def pack_keep(g):
        for pair in range(2):
            pack(g, pair)
            keep(g, pair)

    for pair in range(2):
        loads[2 * pair].wait()
        loads[2 * pair + 1].wait()
        pack(0, pair)
        keep(0, pair)
        if pair == 0:
            begin_keys(0)
        else:
            begin_queries(0)

    listed = block_list[...]
    row_at = lax.broadcasted_iota(jnp.int32, (HALF, LANES), 0)
    lane_at = lax.broadcasted_iota(jnp.int32, (HALF, LANES), 1)
    counts = jnp.zeros((HALF, LANES), jnp.int32)
    for row in range(HALF):
        counts = jnp.where(row_at == row, block_count[row], counts)
    edge_low = jnp.where(f > 0, 0, FRAME)
    edge_high = jnp.where(f < frames - 1, WINDOW, 2 * FRAME)
    usable = (listed >= edge_low) & (listed < edge_high) & (lane_at[:, :SEL] < counts[:, :SEL])
    slots = jnp.where(usable, listed, -1)
    place = jnp.full((HALF, LANES), SEL, jnp.int32)
    for j in range(SEL):
        place = jnp.where(lane_at - PLACE_AT == slots[:, j:j + 1], j, place)
    meta_vm[s, 0:HALF] = place
    meta_vm[s, 0:HALF, 0:SEL] = listed
    meta_vm[s, HALF:] = jnp.zeros((HALF, LANES), jnp.int32)
    meta_vm[s, HALF:, 0:SEL] = usable.astype(jnp.int32)
    share_meta.start()
    pack_keep(1)
    begin_keys(1)
    pack_keep(2)
    tiles[:, SEL] = jnp.zeros((FRAME, BLOCK, 2 * LANES), jnp.float32)

    def forward(g):
        swap(g, 0).wait_recv()
        for d in range(2):
            start_pass(g, d, 1)

    def clear(w, carry):
        @pl.when(jnp.logical_not(has_before))
        def _():
            for g in range(GROUPS):
                kv[g, w] = jnp.zeros((BLOCK, 2 * LANES), jnp.bfloat16)
                take[g, 0, w] = jnp.zeros((BLOCK, 2 * LANES), jnp.bfloat16)

        @pl.when(jnp.logical_not(has_after))
        def _():
            for g in range(GROUPS):
                kv[g, 2 * FRAME + w] = jnp.zeros((BLOCK, 2 * LANES), jnp.bfloat16)
                take[g, 1, w] = jnp.zeros((BLOCK, 2 * LANES), jnp.bfloat16)

        return carry

    lax.fori_loop(0, FRAME, clear, 0)
    relay_step(0, 0)
    forward(0)
    begin_keys(2)
    begin_queries(1)
    share_meta.wait()
    to_scalar = pltpu.make_async_copy(meta_vm, meta_sm, meta_local)
    to_scalar.start()
    to_scalar.wait()
    pack_keep(3)

    row_ids = lax.broadcasted_iota(jnp.int32, (4 * HD, 4 * HD), 0) // HD
    col_ids = lax.broadcasted_iota(jnp.int32, (4 * HD, 4 * HD), 1) // HD
    spread = jnp.where(
        row_ids == col_ids, jnp.where(col_ids < 2, FACTOR, 1.0), 0.0
    ).astype(jnp.bfloat16)
    first_head = lax.broadcasted_iota(jnp.int32, (BLOCK, LANES), 1) < HD

    def heads(full):
        return jnp.where(first_head, full[:HD], full[HD:])

    def fold(array, op):
        return op(array.reshape(array.shape[0] // 8, 8, LANES), axis=0)

    def attend(g, b):
        strip, row = b // HALF, lax.rem(b, HALF)
        chunks = ((0, 4), (4, 8), (8, SEL))
        keep = {"slabs": [None] * SEL, "powers": [None] * SEL}

        def diagonal():
            keep["diagonal"] = jnp.concatenate([qd[g, b]] * 4, axis=0) * spread
            keep["bias"] = [
                jnp.where(meta_sm[strip, HALF + row, j] > 0, 0.0, MASKED).astype(jnp.float32)
                for j in range(SEL)
            ]

        def products(c):
            low, high = chunks[c]
            picked = jnp.concatenate([work[meta_sm[strip, row, j]] for j in range(low, high)], axis=0)
            keep["picked", c] = picked
            both = lax.dot_general(
                picked, keep["diagonal"], (((1,), (1,)), ((), ())), preferred_element_type=jnp.float32
            )
            for j in range(low, high):
                at = slice((j - low) * BLOCK, (j - low + 1) * BLOCK)
                keep["scores", j] = both[at, :LANES]
                keep["grad_weights", j] = both[at, LANES:]

        def peak(c):
            for j in range(*chunks[c]):
                top = fold(keep["scores", j], jnp.max) + keep["bias"][j]
                keep["peak"] = jnp.maximum(keep["peak"], top) if j else top
            if c == len(chunks) - 1:
                keep["peak"] = jnp.max(keep["peak"], axis=0, keepdims=True)

        def power(j):
            powers = jnp.exp(keep["scores", j] - (keep["peak"] - keep["bias"][j]))
            keep["powers"][j] = powers
            total = fold(powers, jnp.sum)
            dots = fold(powers * keep["grad_weights", j], jnp.sum)
            keep["total"] = keep["total"] + total if j else total
            keep["dots"] = keep["dots"] + dots if j else dots
            if j == SEL - 1:
                keep["scale"] = 1.0 / jnp.sum(keep["total"], axis=0, keepdims=True)
                keep["row_dots"] = jnp.sum(keep["dots"], axis=0, keepdims=True) * keep["scale"]

        def slab(j):
            weights = keep["powers"][j] * keep["scale"]
            grad_scores = weights * (keep["grad_weights", j] - keep["row_dots"])
            keep["slabs"][j] = (grad_scores.astype(jnp.bfloat16), weights.astype(jnp.bfloat16))

        def terms(c):
            low, high = chunks[c]
            parts = [jnp.concatenate([pair[k] for pair in keep["slabs"][low:high]], axis=0) for k in range(2)]
            keep["parts", c] = parts
            result = jnp.dot(
                jnp.concatenate(parts, axis=1), keep["diagonal"], preferred_element_type=jnp.float32
            )
            tiles[b, low:high] = result.reshape(high - low, BLOCK, 2 * LANES)

        def mixed(c):
            for k in range(2):
                lanes = slice(k * LANES, (k + 1) * LANES)
                product = lax.dot_general(
                    keep["parts", c][k], keep["picked", c][:, lanes], (((0,), (0,)), ((), ())),
                    preferred_element_type=jnp.float32,
                )
                keep["mixed", k] = keep["mixed", k] + product if c else product
            if c == len(chunks) - 1:
                rows_out[g, b] = jnp.concatenate(
                    [heads(keep["mixed", 0]) * FACTOR, heads(keep["mixed", 1])], axis=1
                ).astype(jnp.bfloat16)

        def call(function, *args):
            return lambda: function(*args)

        count = range(len(chunks))
        return (
            [diagonal] + [call(products, c) for c in count],
            [call(peak, c) for c in count] + [call(power, j) for j in range(SEL)] + [call(slab, j) for j in range(SEL)],
            [call(step, c) for c in count for step in (terms, mixed)],
        )

    def interleave(stages):
        placed = [
            ((k + 0.5) / len(stage), n, step)
            for n, stage in enumerate(stages)
            for k, step in enumerate(stage)
        ]
        for _, _, step in sorted(placed, key=lambda item: item[:2]):
            step()

    def finish(g):
        slot = lax.rem(g, 2)
        for d in range(2):
            @pl.when(hears_from[d])
            def _():
                for part in range(2):
                    wait_terms(g, d, part).wait_recv()

        def add(w, carry):
            total = own[slot, w] + take[g, 0, w].astype(jnp.float32) + take[g, 1, w].astype(jnp.float32)
            final[g, w] = total.astype(jnp.bfloat16)
            return carry

        lax.fori_loop(0, FRAME, add, 0)
        grads_across(g).start()
        for a in range(2):
            grads_along(g, a).start()
        rows_across(g).wait_recv()
        for a in range(2):
            rows_back(g, a).start()

    def one_group(g, carry):
        swap(g, 1).wait_recv()
        for d in range(2):
            @pl.when(hears_from[d])
            def _():
                for part in range(2):
                    wait_pass(g, d, part).wait_recv()

        work[...] = kv[g]

        blocks = [attend(g, lax.rem(HALF * o + i, FRAME)) for i in range(FRAME)]
        for turn in range(FRAME + 2):
            interleave([blocks[turn - k][k] for k in (2, 1, 0) if 0 <= turn - k < FRAME])
            if turn == 3:
                @pl.when(g == 0)
                def _():
                    forward(1)
                    begin_keys(3)
                    begin_queries(2)

                @pl.when((g > 0) & (g + 1 < GROUPS))
                def _():
                    relay_step(g + 1, 0)

                @pl.when(g == GROUPS - 1)
                def _():
                    rows_across(GROUPS - 2).start()

            if turn == 7:
                @pl.when(g == 0)
                def _():
                    begin_queries(3)
                    relay_step(1, 0)

                @pl.when(g + 2 < GROUPS)
                def _():
                    forward(g + 2)

                @pl.when(g > 0)
                def _():
                    relay_step(g - 1, 1)

                @pl.when((g > 0) & (g < GROUPS - 1))
                def _():
                    rows_across(g - 1).start()

                @pl.when(g > 1)
                def _():
                    finish(g - 2)

        for a in range(2):
            rows_along(g, a).start()

        def gather(w, base):
            acc = None
            for b in range(FRAME):
                place = meta_sm[b // HALF, b % HALF, PLACE_AT + base + w]
                tile = tiles[b, place]
                acc = tile if acc is None else acc + tile
            return acc

        def collect(w, inner):
            give[g, 1, w] = gather(w, 0).astype(jnp.bfloat16)
            give[g, 0, w] = gather(w, 2 * FRAME).astype(jnp.bfloat16)
            return inner

        for part, half in ((1, o), (0, s)):
            lax.fori_loop(HALF * half, HALF * half + HALF, collect, 0)
            for d in range(2):
                start_terms(g, d, part)

        def collect_own(w, inner):
            own[lax.rem(g, 2), w] = gather(w, FRAME)
            return inner

        lax.fori_loop(0, FRAME, collect_own, 0)

        return carry

    lax.fori_loop(0, GROUPS, one_group, 0)
    relay_step(GROUPS - 1, 1)
    rows_across(GROUPS - 1).start()
    finish(GROUPS - 2)
    finish(GROUPS - 1)

    def land(g, carry):
        grads_across(g).wait_recv()
        for a in range(2):
            grads_back(g, a).start()
        return carry

    lax.fori_loop(0, GROUPS, land, 0)

    def drain(g, carry):
        for pair in range(2):
            swap(g, pair).wait_send()
        for d in range(2):
            @pl.when(sends_to[d])
            def _():
                for part in range(2):
                    wait_terms(g, d, part).wait_send()
                wait_pass(g, d, 0).wait_send()

                @pl.when(jnp.logical_not(skipped[d]))
                def _():
                    wait_pass(g, d, 1).wait_send()

                @pl.when(slant[d])
                def _():
                    slant_copy(g, d).wait_send()

        for phase in range(2):
            @pl.when(relays(g, phase))
            def _():
                relay_on(g, phase).wait_send()

        rows_across(g).wait_send()
        grads_across(g).wait_send()
        for a in range(2):
            rows_along(g, a).wait()
            grads_along(g, a).wait()
            rows_back(g, a).wait()
            grads_back(g, a).wait()
        return carry

    lax.fori_loop(0, GROUPS, drain, 0)


def hand_over(*refs):
    sources, targets, held, in_sems, out_sems = refs[:4], refs[4:8], refs[8], refs[9], refs[10]
    spots = [(i, at) for i in range(4) for at in range(HALF)]
    ins = [pltpu.make_async_copy(sources[i].at[at], held.at[i, at], in_sems.at[i, at]) for i, at in spots]
    outs = [pltpu.make_async_copy(held.at[i, at], targets[i].at[at], out_sems.at[i, at]) for i, at in spots]
    for copy in ins:
        copy.start()
    for arrives, leaves in zip(ins, outs):
        arrives.wait()
        leaves.start()
    for copy in outs:
        copy.wait()


def body(queries, keys, values, out_grad, block_list, block_count):
    rows, width = queries.shape
    frames = lax.axis_size("frames")
    blocked = [x.reshape(HALF, BLOCK, width) for x in (queries, keys, values, out_grad)]
    shape = jax.ShapeDtypeStruct((HALF, BLOCK, width), jnp.bfloat16)
    dma = pltpu.SemaphoreType.DMA
    flops = 6 * 2 * FRAME * SEL * BLOCK * 256 * 256 * GROUPS
    outs = pl.pallas_call(
        lambda *refs: kernel(frames, *refs),
        out_shape=[shape] * 4,
        in_specs=[pl.BlockSpec(memory_space=pltpu.VMEM), pl.BlockSpec(memory_space=pltpu.SMEM)] + [pl.BlockSpec(memory_space=pl.ANY)] * 4,
        out_specs=[pl.BlockSpec(memory_space=pl.ANY)] * 4,
        scratch_shapes=[
            pltpu.VMEM((4, HALF, BLOCK, width), jnp.bfloat16),
            pltpu.VMEM((GROUPS, 2, HALF, BLOCK, 2 * LANES), jnp.bfloat16),
            pltpu.VMEM((GROUPS, WINDOW, BLOCK, 2 * LANES), jnp.bfloat16),
            pltpu.VMEM((GROUPS, FRAME, BLOCK, 2 * LANES), jnp.bfloat16),
            pltpu.VMEM((WINDOW, BLOCK, 2 * LANES), jnp.bfloat16),
            pltpu.VMEM((FRAME, SEL + 1, BLOCK, 2 * LANES), jnp.float32),
            pltpu.VMEM((GROUPS, FRAME, BLOCK, 2 * LANES), jnp.bfloat16),
            pltpu.VMEM((GROUPS, HALF, BLOCK, 2 * LANES), jnp.bfloat16),
            pltpu.VMEM((GROUPS, 2, FRAME, BLOCK, 2 * LANES), jnp.bfloat16),
            pltpu.VMEM((GROUPS, 2, FRAME, BLOCK, 2 * LANES), jnp.bfloat16),
            pltpu.VMEM((2, FRAME, BLOCK, 2 * LANES), jnp.float32),
            pltpu.VMEM((GROUPS, FRAME, BLOCK, 2 * LANES), jnp.bfloat16),
            pltpu.VMEM((GROUPS, HALF, BLOCK, 2 * LANES), jnp.bfloat16),
            pltpu.VMEM((2, GROUPS, HALF, BLOCK, 2 * LANES), jnp.bfloat16),
            pltpu.VMEM((2, 8, LANES), jnp.int32),
            pltpu.SMEM((2, 8, LANES), jnp.int32),
            dma((4,)), dma((GROUPS, 2)), dma((GROUPS, 2)),
            dma((GROUPS, 2, 2)), dma((GROUPS, 2, 2)),
            dma, dma, dma,
            dma((GROUPS,)), dma((GROUPS,)), dma((2 * GROUPS, 2)),
            dma((GROUPS, 2, 2)), dma((GROUPS, 2, 2)),
            dma((GROUPS,)), dma((GROUPS,)), dma((2 * GROUPS, 2)),
            dma((2, GROUPS)), dma((2, GROUPS)), dma((GROUPS,)),
        ],
        cost_estimate=pl.CostEstimate(
            flops=flops, bytes_accessed=16 * rows * width, transcendentals=FRAME * SEL * BLOCK * LANES * GROUPS
        ),
        compiler_params=pltpu.CompilerParams(
            collective_id=0, has_side_effects=True, vmem_limit_bytes=60 * 1024 * 1024
        ),
    )(block_list, block_count, *blocked)
    outs = pl.pallas_call(
        hand_over,
        out_shape=[shape] * 4,
        in_specs=[pl.BlockSpec(memory_space=pl.ANY)] * 4,
        out_specs=[pl.BlockSpec(memory_space=pl.ANY)] * 4,
        scratch_shapes=[
            pltpu.VMEM((4, HALF, BLOCK, width), jnp.bfloat16), dma((4, HALF)), dma((4, HALF)),
        ],
        compiler_params=pltpu.CompilerParams(vmem_limit_bytes=60 * 1024 * 1024),
    )(*outs)
    return tuple(x.reshape(rows, width) for x in outs)


def solution(mesh):
    split = P(("frames", "strip"), None)
    in_specs = (split, split, split, split, split, P(("frames", "strip")))
    return jax.shard_map(
        body, mesh=mesh, in_specs=in_specs, out_specs=(split,) * 4, check_vma=False
    )
```
